128 devices in a mesh: gy: 8 (over x, core), gz: 16 (over y, z).
Axes of the slice: x: 4, y: 4, z: 4, core: 2. Of those that a mesh axis runs over, the one named last changes fastest.
Arguments:
- right_side: float32 [5, 8, 256, 4096], P(None, None, 'gy', 'gz'), may hold values from -6 to 6
- speeds: float32 [3, 8, 256, 4096], P(None, None, 'gy', 'gz'), may hold values from -1 to 1
- porosity: float32 [8, 256, 4096], P(None, 'gy', 'gz'), may hold values from 0 to 1
- coupling: float32 [3, 5, 5], replicated, may hold values from -3 to 3
- momentum: float32 [3, 8, 256, 4096], P(None, None, 'gy', 'gz'), may hold values from -6 to 6
- design_ids: int32 [2, 64, 1024], P(None, 'gy', 'gz'), may hold values from 0 to 32767, as said below
Outputs:
- adjoint: float32 [5, 8, 256, 4096], P(None, None, 'gy', 'gz')
- sensitivity: float32 [32768], P(('gy', 'gz'))
The draws below stay inside these ranges and needn't reach their ends.
Inputs may be any that keep to these rules, and one draw needn't show every extreme that they name: `design_ids`: of the blocks that one device holds, at most 16 name variables owned by any one device, and in every draw each device sends exactly 16 to some owner.
All inputs are finite; a program needn't handle non-finite values.
Results may differ from the reference program's by a relative error of at most 0.00019.
Values sent between devices are 32-bit elements; how exact they have to be, the bound alone decides.
A program may use at most 64 MiB of HBM per device.

```python
import jax
import jax.numpy as jnp
from jax import lax

VARS = 5
POWERS = 3
CY = 32
CZ = 256
NX = 8
NY = 256
NZ = 4096
NDES = 32768


def draw_design_ids(key, part):
    key = jax.random.fold_in(key, 11)
    along_y = NY // CY
    along_z = NZ // CZ
    devices = along_y * along_z
    blocks_x = NX // 4
    blocks_y = CY // 4
    blocks_z = CZ // 4
    number = blocks_x * blocks_y * blocks_z
    capacity = max(2, 2 * number // devices)
    half = number // 2
    per_owner = number // 4
    key_place, key_owner, key_local = jax.random.split(key, 3)
    place = jax.vmap(lambda sub: jax.random.permutation(sub, number))(jax.random.split(key_place, devices))
    ranks = jnp.where(place < half, place // capacity, half // capacity + (place - half) // (capacity // 2))
    shuffled = jax.vmap(lambda sub: jax.random.permutation(sub, devices))(jax.random.split(key_owner, devices))
    owners = jnp.take_along_axis(shuffled, ranks, axis=1)
    labels = owners * per_owner + jax.random.randint(key_local, (devices, number), 0, per_owner)
    labels = labels.reshape(along_y, along_z, blocks_x, blocks_y, blocks_z)
    labels = labels.transpose(2, 0, 3, 1, 4).reshape(NX // 4, NY // 4, NZ // 4)
    return labels.astype(jnp.int32)


def block_levels(own_key, extent, cuts, smallest, largest):
    gain, own = 1.0, jax.random.fold_in(own_key, 6)
    for axis_at, parts in cuts:
        draws = jnp.exp(jax.random.uniform(jax.random.fold_in(own, axis_at), (parts,), jnp.float32, smallest / len(cuts), largest / len(cuts)))
        gain = gain * jnp.repeat(draws, extent[axis_at] // parts).reshape([-1 if axis == axis_at else 1 for axis in range(len(extent))])
    return gain


def centred(key, shape, deviation, limit, shards=(), held_as=jnp.bfloat16):
    gain = block_levels(key, shape, shards, -0.22, 0.18) if shards else 1.0
    entries = jax.random.normal(key, shape, jnp.float32) * deviation * gain
    return jnp.minimum(jnp.maximum(entries, -limit), limit).astype(held_as)


def setup_inputs(seed: int = 0) -> dict:
    seeds = jax.random.split(jax.random.key(seed), 7)
    right_side = centred(seeds[0], (VARS, NX, NY, NZ), 1.0, 6.0, ((2, 8), (3, 16)), jnp.float32)
    speeds = jnp.clip(jax.random.uniform(seeds[1], (3, NX, NY, NZ), jnp.float32, -1.0, 1.0) * block_levels(seeds[1], (3, NX, NY, NZ), ((2, 8), (3, 16)), -0.4, 0.0), -1.0, 1.0)
    porosity = jnp.clip(1.0 * jax.random.uniform(seeds[2], (NX, NY, NZ), jnp.float32) ** block_levels(seeds[2], (NX, NY, NZ), ((1, 8), (2, 16)), -0.2, 0.2), 0.0, 1.0)
    coupling = centred(seeds[3], (3, VARS, VARS), 0.5, 3.0, (), jnp.float32)
    momentum = centred(seeds[4], (3, NX, NY, NZ), 1.0, 6.0, ((2, 8), (3, 16)), jnp.float32)
    design_ids = draw_design_ids(jax.random.fold_in(seeds[6], 71), 0)
    return {"right_side": right_side, "speeds": speeds, "porosity": porosity, "coupling": coupling, "momentum": momentum, "design_ids": design_ids}


PENALTY = 1.0
COURANT = 0.3

def shifted(field, direction, start):
    sizes = field.shape
    index = [slice(None), slice(1, sizes[1] - 1), slice(1, sizes[2] - 1), slice(1, sizes[3] - 1)]
    length = sizes[direction + 1]
    index[direction + 1] = slice(start, length - 2 + start)
    return field[tuple(index)]

def transpose_sweep(values, speeds, porosity, coupling):
    interior = shifted(values, 0, 1)
    total = PENALTY * porosity[1:-1, 1:-1, 1:-1][None] * interior
    for direction in range(3):
        speed = speeds[direction][None]
        forward = jnp.maximum(speed, 0.0) * values
        backward = jnp.maximum(-speed, 0.0) * values
        flux = jnp.abs(shifted(speed, 0, 1)) * interior - shifted(forward, direction, 2) - shifted(backward, direction, 0)
        total = total + COURANT * jnp.einsum('ij,ixyz->jxyz', coupling[direction], flux, precision=lax.Precision.HIGHEST)
    return total

def pad_cells(field):
    widths = [(0, 0)] * (field.ndim - 3) + [(1, 1), (1, 1), (1, 1)]
    return jnp.pad(field, widths)

def least_squares(upper):
    hess = upper[:, 1:] + upper[:, :-1]
    normal = jnp.dot(hess.T, hess, precision=lax.Precision.HIGHEST)
    target = jnp.dot(hess.T, upper[:, 0], precision=lax.Precision.HIGHEST)
    factor = jnp.linalg.cholesky(normal)
    count = normal.shape[0]
    forward = []
    for place in range(count):
        value = target[place]
        for inner in range(place):
            value = value - factor[place, inner] * forward[inner]
        forward.append(value / factor[place, place])
    backward = [None] * count
    for place in reversed(range(count)):
        value = forward[place]
        for inner in range(place + 1, count):
            value = value - factor[inner, place] * backward[inner]
        backward[place] = value / factor[place, place]
    return backward

def gram_matrix(basis):
    count = len(basis)
    rows_list = []
    for first in range(count):
        rows_list.append(jnp.stack([jnp.sum(basis[first] * basis[second]) for second in range(count)]))
    return jnp.stack(rows_list)

def reference(right_side, speeds, porosity, coupling, momentum, design_ids):
    padded_speeds = pad_cells(speeds)
    padded_porosity = pad_cells(porosity)
    basis = [right_side]
    for step in range(POWERS):
        basis.append(transpose_sweep(pad_cells(basis[-1]), padded_speeds, padded_porosity, coupling))
    gram = gram_matrix(basis)
    upper = jnp.linalg.cholesky(gram).T
    coeffs = least_squares(upper)
    adjoint = coeffs[0] * basis[0]
    for step in range(1, POWERS):
        adjoint = adjoint + coeffs[step] * basis[step]
    cell_term = -PENALTY * jnp.sum(adjoint[1:4] * momentum, axis=0)
    blocks = cell_term.reshape(NX // 4, 4, NY // 4, 4, NZ // 4, 4).sum(axis=(1, 3, 5))
    sensitivity = jax.ops.segment_sum(blocks.reshape(-1), design_ids.reshape(-1), num_segments=NDES)
    return (adjoint, sensitivity)
```

```python
import functools

import jax
import jax.numpy as jnp
from jax import lax
from jax.experimental import pallas as pl
from jax.experimental.pallas import tpu as pltpu
from jax.sharding import PartitionSpec as P

PENALTY = 1.0
COURANT = 0.3
VARS = 5
SLOTS = 16
MESH = pl.DeviceIdType.MESH
F32 = jnp.float32
BF16 = jnp.bfloat16


def pieces(value):
    high = value.astype(BF16)
    rest = value - high.astype(F32)
    mid = rest.astype(BF16)
    low = (rest - mid.astype(F32)).astype(BF16)
    return high, mid, low


def dot(a, b):
    return jnp.dot(a, b, preferred_element_type=F32)


def dot_nt(a, b):
    return lax.dot_general(a, b, (((1,), (1,)), ((), ())), preferred_element_type=F32)


def iota(shape, axis):
    return lax.broadcasted_iota(jnp.int32, shape, axis)


def fold(product):
    rows = product[0:8] + product[8:16] + product[16:24] + product[24:32]
    return rows[:, 0:128] + rows[:, 128:256]


def solve(gram):
    low = [[None] * 4 for _ in range(4)]
    for col in range(4):
        diag = gram[col][col]
        for inner in range(col):
            diag = diag - low[col][inner] * low[col][inner]
        low[col][col] = jnp.sqrt(diag)
        for row in range(col + 1, 4):
            value = gram[row][col]
            for inner in range(col):
                value = value - low[row][inner] * low[col][inner]
            low[row][col] = value / low[col][col]
    zero = jnp.zeros_like(gram[0][0])
    upper = [[low[c][r] if c >= r else None for c in range(4)] for r in range(4)]

    def add(a, b):
        return b if a is None else (a if b is None else a + b)

    hess = [[add(upper[r][c + 1], upper[r][c]) for c in range(3)] for r in range(4)]

    def inner_sum(terms):
        total = None
        for a, b in terms:
            if a is not None and b is not None:
                total = add(total, a * b)
        return zero if total is None else total

    normal = [[inner_sum([(hess[r][a], hess[r][b]) for r in range(4)]) for b in range(3)] for a in range(3)]
    target = [inner_sum([(hess[r][a], upper[r][0]) for r in range(4)]) for a in range(3)]
    fac = [[None] * 3 for _ in range(3)]
    for col in range(3):
        diag = normal[col][col]
        for inner in range(col):
            diag = diag - fac[col][inner] * fac[col][inner]
        fac[col][col] = jnp.sqrt(diag)
        for row in range(col + 1, 3):
            value = normal[row][col]
            for inner in range(col):
                value = value - fac[row][inner] * fac[col][inner]
            fac[row][col] = value / fac[col][col]
    forward = []
    for place in range(3):
        value = target[place]
        for inner in range(place):
            value = value - fac[place][inner] * forward[inner]
        forward.append(value / fac[place][place])
    backward = [None] * 3
    for place in reversed(range(3)):
        value = forward[place]
        for inner in range(place + 1, 3):
            value = value - fac[inner][place] * backward[inner]
        backward[place] = value / fac[place][place]
    return backward


def kernel(ny, nz, per_owner,
           rs_hbm, sp_hbm, po_hbm, cp, mo_hbm, ids_ref,
           adj_hbm, sens_ref,
           b0, b1, b2, b3, sp, po, mo, wmat, wz, w, cf, sface,
           ysend, yrecv, zsend, zrecv,
           owner_hot, rank_hot, local_row, dsend, recv1, turned, recv2,
           gsend, grecv1, gsend2, grecv2,
           in_sem, out_sem, ysend_sem, yrecv_sem, zsend_sem, zrecv_sem,
           a1_send, a1_recv, a2_send, a2_recv, g1_send, g1_recv, g2_send, g2_recv):
    gy = lax.axis_index("gy")
    gz = lax.axis_index("gz")

    def gy_at(delta):
        return lax.rem(gy + (delta + ny), ny)

    def gz_at(delta):
        return lax.rem(gz + (delta + nz), nz)

    barrier = pltpu.get_barrier_semaphore()
    for delta in range(1, ny):
        pl.semaphore_signal(barrier, inc=1, device_id={"gy": gy_at(delta)}, device_id_type=MESH)
    for delta in range(1, nz):
        pl.semaphore_signal(barrier, inc=1, device_id={"gz": gz_at(delta)}, device_id_type=MESH)

    loads = [pltpu.make_async_copy(src, dst, in_sem.at[place]) for place, (src, dst) in enumerate(
        [(sp_hbm, sp), (rs_hbm, b0), (po_hbm, po), (mo_hbm, mo)])]
    for load in loads:
        load.start()

    basis = [b0, b1, b2, b3]

    lane = iota((16, 256), 1)
    row = iota((16, 256), 0)
    group = lane >> 4
    piece = jnp.where(group >= 10, 2, jnp.where(group >= 5, 1, 0))
    which = group - 5 * piece
    same = (lane & 15) == row
    for d in range(3):
        for j in range(VARS):
            value = jnp.zeros((16, 256), F32)
            for i in range(VARS):
                value = jnp.where(which == i, COURANT * cp[d, i, j], value)
            high = value.astype(BF16).astype(F32)
            value = jnp.where(same, jnp.where(piece == 2, value - high, high), 0.0)
            at = (d * VARS + j) * 16
            wmat[at:at + 16, :] = value[:, 0:240].astype(BF16)
    lane = iota((8, 128), 1)
    row = iota((8, 128), 0)
    for i in range(VARS):
        value = jnp.zeros((8, 128), F32)
        for j in range(VARS):
            value = jnp.where((lane >> 3) == j, -COURANT * cp[2, i, j], value)
        wz[8 * i:8 * i + 8, :] = jnp.where((lane & 7) == row, value, 0.0)
    wz[40:128, :] = jnp.zeros((88, 128), F32)

    ids = jnp.concatenate([ids_ref[0], ids_ref[1]], axis=1)
    owners = lax.div(ids, per_owner)
    local_row[...] = (ids - owners * per_owner + 1).astype(F32)
    tri = jnp.where(iota((128, 128), 0) < iota((128, 128), 1), 1.0, 0.0).astype(BF16)
    ones = jnp.ones((128, 128), BF16)
    number = ny * nz
    sub = iota((number, 128), 0)
    before = jnp.zeros((number, 128), F32)
    for p in range(8):
        hot = jnp.where(sub == owners[p:p + 1, :], 1.0, 0.0)
        hot16 = hot.astype(BF16)
        count = dot(hot16, tri) + dot(before.astype(BF16), ones)
        before = before + hot
        owner_hot[:, p * 128:(p + 1) * 128] = hot16
        rank = jnp.sum(hot * count, axis=0, keepdims=True)
        rank_hot[:, p * 128:(p + 1) * 128] = jnp.where(rank == iota((SLOTS, 128), 0).astype(F32), 1.0, 0.0)

    loads[0].wait()
    keep_low = jnp.where(gy > 0, 1.0, 0.0)
    keep_high = jnp.where(gy < ny - 1, 1.0, 0.0)
    keep_near = jnp.where(gz > 0, 1.0, 0.0)
    keep_far = jnp.where(gz < nz - 1, 1.0, 0.0)

    lanes = iota((32, 128), 1)
    near = jnp.zeros((32, 128), F32)
    far = jnp.zeros((32, 128), F32)
    for x in range(8):
        at_near = sp[2, x, :, 0:128]
        at_far = sp[2, x, :, 128:256]
        for i in range(VARS):
            s = i * 8 + x
            near = jnp.where(lanes == s, pltpu.roll(at_near, s, axis=1) if s else at_near, near)
            far = jnp.where(lanes == s, pltpu.roll(at_far, s + 1, axis=1), far)
    sface[0] = jnp.maximum(near, 0.0) * keep_near
    sface[1] = jnp.maximum(-far, 0.0) * keep_far

    def pack_z(k, fix):
        b = basis[k]
        near = jnp.zeros((32, 128), F32)
        far = jnp.zeros((32, 128), F32)
        if fix:
            from_near = zrecv[k - 1, 0]
            from_far = zrecv[k - 1, 1]
        for i in range(VARS):
            for x in range(8):
                s = i * 8 + x
                at_near = b[i, x, :, 0:128]
                at_far = b[i, x, :, 128:256]
                if fix:
                    at_near = at_near + jnp.where(lanes == 0, pltpu.roll(from_near, (128 - s) % 128, axis=1), 0.0)
                    at_far = at_far + jnp.where(lanes == 127, pltpu.roll(from_far, 127 - s, axis=1), 0.0)
                    b[i, x, :, 0:128] = at_near
                    b[i, x, :, 128:256] = at_far
                if k < 3:
                    near = jnp.where(lanes == s, pltpu.roll(at_near, s, axis=1) if s else at_near, near)
                    far = jnp.where(lanes == s, pltpu.roll(at_far, s + 1, axis=1), far)
        if k < 3:
            both = jnp.concatenate([near * sface[0], far * sface[1]], axis=0)
            out = jnp.dot(both, wz[...], preferred_element_type=F32, precision=lax.Precision.HIGHEST)
            zsend[k, 0] = out[0:32]
            zsend[k, 1] = out[32:64]

    def fix_y(k):
        b = basis[k]
        for i in range(VARS):
            for x in range(8):
                b[i, x, 0:1, :] = b[i, x, 0:1, :] + yrecv[k - 1, 0, i, x:x + 1, :]
                b[i, x, 31:32, :] = b[i, x, 31:32, :] + yrecv[k - 1, 1, i, x:x + 1, :]

    def pack_y(k):
        b = basis[k]
        for side, y in ((0, 0), (1, 31)):
            speed = sp[1, :, y, :]
            speed = jnp.maximum(speed, 0.0) * keep_low if side == 0 else jnp.maximum(-speed, 0.0) * keep_high
            faces = [b[i, :, y, :] * speed for i in range(VARS)]
            for j in range(VARS):
                total = faces[0] * (-COURANT * cp[1, 0, j])
                for i in range(1, VARS):
                    total = total + faces[i] * (-COURANT * cp[1, i, j])
                ysend[k, side, j] = total

    def halo_copies(k):
        copies = []
        for side, delta in ((0, -1), (1, 1)):
            copies.append(pltpu.make_async_remote_copy(
                src_ref=ysend.at[k, side], dst_ref=yrecv.at[k, 1 - side],
                send_sem=ysend_sem.at[k, side], recv_sem=yrecv_sem.at[k, 1 - side],
                device_id={"gy": gy_at(delta)}, device_id_type=MESH))
            copies.append(pltpu.make_async_remote_copy(
                src_ref=zsend.at[k, side], dst_ref=zrecv.at[k, 1 - side],
                send_sem=zsend_sem.at[k, side], recv_sem=zrecv_sem.at[k, 1 - side],
                device_id={"gz": gz_at(delta)}, device_id_type=MESH))
        return copies

    def couple(k, x):
        for h in (0, 16):
            high, low = [], []
            for i in range(VARS):
                v = basis[k][i, x, h:h + 16, :]
                top = v.astype(BF16)
                high.append(top)
                low.append((v - top.astype(F32)).astype(BF16))
            out = dot(wmat[...], jnp.concatenate(high + low + high, axis=0))
            for place in range(3 * VARS):
                w[place, x, h:h + 16, :] = out[place * 16:place * 16 + 16]

    def sweep(k):
        couple(k, 0)

        def body(x, sums):
            after = jnp.minimum(x + 1, 7)
            prior = jnp.maximum(x - 1, 0)
            couple(k, after)
            sums = list(sums)
            for j in range(VARS):
                v = basis[k][j, x]
                for l in range(k + 1):
                    sums[l] = sums[l] + fold(v * basis[l][j, x])
                acc = po[x] * v
                wx = w[j, x]
                wy = w[VARS + j, x]
                wv = w[2 * VARS + j, x]
                acc = acc + cf[0, x] * wx + cf[3, x] * wy + cf[6, x] * wv
                acc = acc + cf[4, x] * pltpu.roll(wy, 31, axis=0) + cf[5, x] * pltpu.roll(wy, 1, axis=0)
                acc = acc + cf[7, x] * pltpu.roll(wv, 255, axis=1) + cf[8, x] * pltpu.roll(wv, 1, axis=1)
                acc = acc + cf[1, x] * w[j, after] + cf[2, x] * w[j, prior]
                basis[k + 1][j, x] = acc
            return tuple(sums)

        return lax.fori_loop(0, 8, body, tuple(jnp.zeros((8, 128), F32) for _ in range(k + 1)))

    gram = [[None] * 4 for _ in range(4)]

    loads[1].wait()
    pack_y(0)
    pack_z(0, False)
    pl.semaphore_wait(barrier, (ny - 1) + (nz - 1))
    halos = halo_copies(0)
    for copy in halos:
        copy.start()

    row = iota((32, 256), 0)
    lane = iota((32, 256), 1)

    def coefficients(x, carry):
        after = jnp.minimum(x + 1, 7)
        prior = jnp.maximum(x - 1, 0)
        cf[0, x] = jnp.abs(sp[0, x])
        cf[1, x] = -jnp.maximum(sp[0, after], 0.0) * jnp.where(x < 7, 1.0, 0.0)
        cf[2, x] = -jnp.maximum(-sp[0, prior], 0.0) * jnp.where(x > 0, 1.0, 0.0)
        s = sp[1, x]
        cf[3, x] = jnp.abs(s)
        cf[4, x] = jnp.where(row == 31, 0.0, -jnp.maximum(pltpu.roll(s, 31, axis=0), 0.0))
        cf[5, x] = jnp.where(row == 0, 0.0, -jnp.maximum(-pltpu.roll(s, 1, axis=0), 0.0))
        s = sp[2, x]
        cf[6, x] = jnp.abs(s)
        cf[7, x] = jnp.where(lane == 255, 0.0, -jnp.maximum(pltpu.roll(s, 255, axis=1), 0.0))
        cf[8, x] = jnp.where(lane == 0, 0.0, -jnp.maximum(-pltpu.roll(s, 1, axis=1), 0.0))
        return carry

    lax.fori_loop(0, 8, coefficients, 0)
    loads[2].wait()

    for k in range(2):
        sums = sweep(k)
        for l in range(k + 1):
            gram[l][k] = sums[l]
        for copy in halos:
            copy.wait()
        fix_y(k + 1)
        pack_z(k + 1, True)
        pack_y(k + 1)
        halos = halo_copies(k + 1)
        for copy in halos:
            copy.start()

    loads[3].wait()
    low8 = iota((16, 192), 0)
    col = iota((16, 192), 1)
    within = jnp.where(col >= 96, col - 96, col) & 31
    half = jnp.where(col >= 96, 1, 0)
    ysel = jnp.where((low8 >> 3 == half) & ((low8 & 7) == (within >> 2)), 1.0, 0.0).astype(BF16)
    zrow = iota((512, 128), 0)
    zsel = jnp.where(((zrow & 255) >> 2) + (zrow >> 8) * 64 == iota((512, 128), 1), 1.0, 0.0).astype(BF16)
    parts = []
    for k in range(3):
        stack = []
        for half_x in range(2):
            total = None
            for x in range(4 * half_x, 4 * half_x + 4):
                for i in range(3):
                    term = basis[k][1 + i, x] * mo[i, x]
                    total = term if total is None else total + term
            stack.extend(pieces(total))
        t = dot(ysel, jnp.concatenate(stack, axis=0))
        for part in pieces(jnp.concatenate([t[0:8], t[8:16]], axis=1)):
            parts.append(part.astype(F32))
    t = dot(jnp.concatenate(parts, axis=0).astype(BF16), zsel)
    values = [-PENALTY * (t[24 * k:24 * k + 8] + t[24 * k + 8:24 * k + 16] + t[24 * k + 16:24 * k + 24])
              for k in range(3)]
    empty = jnp.zeros((SLOTS, 128), F32)
    chunks = [[], [], []]
    for p in range(8):
        hot = rank_hot[:, p * 128:(p + 1) * 128]
        spread = [(hot * local_row[p:p + 1, :]).astype(BF16).astype(F32), empty, empty]
        rows = [[spread[q]] for q in range(3)]
        for k in range(3):
            for q, part in enumerate(pieces(hot * values[k][p:p + 1, :])):
                rows[q].append(part.astype(F32))
        for q in range(3):
            chunks[q].append(jnp.concatenate(rows[q] + [empty] * 4, axis=0).astype(BF16))
    total = None
    for q in range(3):
        term = dot_nt(owner_hot[...], jnp.concatenate(chunks[q], axis=1))
        total = term if total is None else total + term
    dsend[...] = total.reshape(ny, nz, 128)

    def a1_copy(delta):
        return pltpu.make_async_remote_copy(
            src_ref=dsend.at[gy_at(delta)], dst_ref=recv1.at[delta],
            send_sem=a1_send.at[delta], recv_sem=a1_recv.at[delta],
            device_id={"gy": gy_at(delta)}, device_id_type=MESH)

    first = [a1_copy(delta) for delta in range(1, ny)]
    for copy in first:
        copy.start()
    recv1[0] = dsend[gy]

    sums = sweep(2)
    for l in range(3):
        gram[l][2] = sums[l]
    for copy in halos:
        copy.wait()
    fix_y(3)
    pack_z(3, True)

    def last(x, sums):
        sums = list(sums)
        for j in range(VARS):
            v = b3[j, x]
            for l in range(4):
                sums[l] = sums[l] + fold(v * basis[l][j, x])
        return tuple(sums)

    sums = lax.fori_loop(0, 8, last, tuple(jnp.zeros((8, 128), F32) for _ in range(4)))
    for l in range(4):
        gram[l][3] = sums[l]

    entries = [(l, k) for k in range(4) for l in range(k + 1)]
    lane = iota((8, 128), 1)
    packed = jnp.zeros((8, 128), F32)
    for e, (l, k) in enumerate(entries):
        value = gram[l][k]
        for shift in (64, 32, 16, 8):
            value = value + pltpu.roll(value, shift, axis=1)
        packed = jnp.where((lane >> 3) == e, value, packed)
    own = jnp.sum(packed, axis=0, keepdims=True)
    gsend[...] = own

    def g1_copy(delta):
        return pltpu.make_async_remote_copy(
            src_ref=gsend, dst_ref=grecv1.at[delta],
            send_sem=g1_send.at[delta], recv_sem=g1_recv.at[delta],
            device_id={"gy": gy_at(delta)}, device_id_type=MESH)

    gram1 = [g1_copy(delta) for delta in range(1, ny)]
    for copy in gram1:
        copy.start()

    for copy in first:
        copy.wait()
    for g in range(nz):
        turned[g] = recv1[:, g, :]

    def a2_copy(delta):
        return pltpu.make_async_remote_copy(
            src_ref=turned.at[gz_at(delta)], dst_ref=recv2.at[delta],
            send_sem=a2_send.at[delta], recv_sem=a2_recv.at[delta],
            device_id={"gz": gz_at(delta)}, device_id_type=MESH)

    second = [a2_copy(delta) for delta in range(1, nz)]
    for copy in second:
        copy.start()
    recv2[0] = turned[gz]

    for copy in gram1:
        copy.wait()
    own = gsend[...]
    for delta in range(1, ny):
        own = own + grecv1[delta]
    gsend2[...] = own

    def g2_copy(delta):
        return pltpu.make_async_remote_copy(
            src_ref=gsend2, dst_ref=grecv2.at[delta],
            send_sem=g2_send.at[delta], recv_sem=g2_recv.at[delta],
            device_id={"gz": gz_at(delta)}, device_id_type=MESH)

    gram2 = [g2_copy(delta) for delta in range(1, nz)]
    for copy in gram2:
        copy.start()

    for copy in second:
        copy.wait()
    bins = iota((8, per_owner), 1).astype(F32) + 1.0

    def collect(t, sums):
        tile = recv2[t]
        sums = list(sums)
        for r in range(SLOTS):
            hit = tile[:, r:r + 1] == bins
            for k in range(3):
                at = SLOTS * (k + 1) + r
                sums[k] = sums[k] + jnp.where(hit, tile[:, at:at + 1], 0.0)
        return tuple(sums)

    sums = lax.fori_loop(0, nz, collect, tuple(jnp.zeros((8, per_owner), F32) for _ in range(3)))
    bin_sums = [jnp.sum(value, axis=0, keepdims=True) for value in sums]

    for copy in gram2:
        copy.wait()
    own = gsend2[...]
    for delta in range(1, nz):
        own = own + grecv2[delta]
    for shift in (4, 2, 1):
        own = own + pltpu.roll(own, shift, axis=1)
    own = jnp.broadcast_to(own, (8, 128))
    splat = {}
    for e, (l, k) in enumerate(entries):
        splat[l, k] = jnp.broadcast_to(own[:, 8 * e + 7:8 * e + 8], (8, 128))
    coeffs = solve([[splat[min(a, b), max(a, b)] for b in range(4)] for a in range(4)])

    sens = None
    for k in range(3):
        c = coeffs[k][0:1]
        term = bin_sums[k] * jnp.concatenate([c] * (per_owner // 128), axis=1)
        sens = term if sens is None else sens + term
    sens_ref[...] = sens

    wide = [jnp.concatenate([jnp.concatenate([c, c], axis=1)] * 4, axis=0) for c in coeffs]
    stores = []
    for j in range(VARS):
        def combine(x, carry):
            b0[j, x] = wide[0] * b0[j, x] + wide[1] * b1[j, x] + wide[2] * b2[j, x]
            return carry
        lax.fori_loop(0, 8, combine, 0)
        store = pltpu.make_async_copy(b0.at[j], adj_hbm.at[j], out_sem.at[j])
        store.start()
        stores.append(store)
    for store in stores:
        store.wait()


def local(right_side, speeds, porosity, coupling, momentum, design_ids):
    ny = lax.axis_size("gy")
    nz = lax.axis_size("gz")
    _, nx, cy, cz = right_side.shape
    per_owner = design_ids.size // 4
    field = (VARS, nx, cy, cz)
    dma = pltpu.SemaphoreType.DMA
    any_spec = pl.BlockSpec(memory_space=pl.ANY)
    vmem_spec = pl.BlockSpec(memory_space=pltpu.VMEM)
    adjoint, sensitivity = pl.pallas_call(
        functools.partial(kernel, ny, nz, per_owner),
        out_shape=[jax.ShapeDtypeStruct(field, F32), jax.ShapeDtypeStruct((1, per_owner), F32)],
        in_specs=[any_spec, any_spec, any_spec, pl.BlockSpec(memory_space=pltpu.SMEM), any_spec, vmem_spec],
        out_specs=[any_spec, vmem_spec],
        scratch_shapes=[
            pltpu.VMEM(field, F32), pltpu.VMEM(field, F32), pltpu.VMEM(field, F32), pltpu.VMEM(field, F32),
            pltpu.VMEM((3, nx, cy, cz), F32),
            pltpu.VMEM((nx, cy, cz), F32),
            pltpu.VMEM((3, nx, cy, cz), F32),
            pltpu.VMEM((240, 240), BF16),
            pltpu.VMEM((128, 128), F32),
            pltpu.VMEM((3 * VARS, nx, cy, cz), F32),
            pltpu.VMEM((9, nx, cy, cz), F32),
            pltpu.VMEM((2, 32, 128), F32),
            pltpu.VMEM((3, 2, VARS, nx, cz), F32),
            pltpu.VMEM((3, 2, VARS, nx, cz), F32),
            pltpu.VMEM((3, 2, 32, 128), F32),
            pltpu.VMEM((3, 2, 32, 128), F32),
            pltpu.VMEM((ny * nz, 1024), BF16),
            pltpu.VMEM((SLOTS, 1024), F32),
            pltpu.VMEM((8, 128), F32),
            pltpu.VMEM((ny, nz, 128), F32),
            pltpu.VMEM((ny, nz, 128), F32),
            pltpu.VMEM((nz, ny, 128), F32),
            pltpu.VMEM((nz, ny, 128), F32),
            pltpu.VMEM((1, 128), F32),
            pltpu.VMEM((ny, 1, 128), F32),
            pltpu.VMEM((1, 128), F32),
            pltpu.VMEM((nz, 1, 128), F32),
            dma((4,)), dma((VARS,)),
            dma((3, 2)), dma((3, 2)), dma((3, 2)), dma((3, 2)),
            dma((ny,)), dma((ny,)), dma((nz,)), dma((nz,)),
            dma((ny,)), dma((ny,)), dma((nz,)), dma((nz,)),
        ],
        compiler_params=pltpu.CompilerParams(
            collective_id=0, has_side_effects=True, vmem_limit_bytes=48 * 1024 * 1024),
    )(right_side, speeds, porosity, coupling, momentum, design_ids)
    return adjoint, sensitivity.reshape(per_owner)


def solution(mesh):
    in_specs = (
        P(None, None, "gy", "gz"),
        P(None, None, "gy", "gz"),
        P(None, "gy", "gz"),
        P(),
        P(None, None, "gy", "gz"),
        P(None, "gy", "gz"),
    )
    out_specs = (P(None, None, "gy", "gz"), P(("gy", "gz")))
    return jax.shard_map(local, mesh=mesh, in_specs=in_specs, out_specs=out_specs, check_vma=False)
```

```python
import functools

import jax
import jax.numpy as jnp
from jax import lax
from jax.experimental import pallas as pl
from jax.experimental.pallas import tpu as pltpu
from jax.sharding import PartitionSpec as P

PENALTY = 1.0
COURANT = 0.3
VARS = 5
SLOTS = 16
MESH = pl.DeviceIdType.MESH
F32 = jnp.float32
BF16 = jnp.bfloat16


def pieces(value):
    high = value.astype(BF16)
    rest = value - high.astype(F32)
    mid = rest.astype(BF16)
    low = (rest - mid.astype(F32)).astype(BF16)
    return high, mid, low


def dot(a, b):
    return jnp.dot(a, b, preferred_element_type=F32)


def dot_nt(a, b):
    return lax.dot_general(a, b, (((1,), (1,)), ((), ())), preferred_element_type=F32)


def iota(shape, axis):
    return lax.broadcasted_iota(jnp.int32, shape, axis)


def fold(product):
    rows = product[0:8] + product[8:16] + product[16:24] + product[24:32]
    return rows[:, 0:128] + rows[:, 128:256]


def solve(gram):
    low = [[None] * 4 for _ in range(4)]
    for col in range(4):
        diag = gram[col][col]
        for inner in range(col):
            diag = diag - low[col][inner] * low[col][inner]
        low[col][col] = jnp.sqrt(diag)
        for row in range(col + 1, 4):
            value = gram[row][col]
            for inner in range(col):
                value = value - low[row][inner] * low[col][inner]
            low[row][col] = value / low[col][col]
    zero = jnp.zeros_like(gram[0][0])
    upper = [[low[c][r] if c >= r else None for c in range(4)] for r in range(4)]

    def add(a, b):
        return b if a is None else (a if b is None else a + b)

    hess = [[add(upper[r][c + 1], upper[r][c]) for c in range(3)] for r in range(4)]

    def inner_sum(terms):
        total = None
        for a, b in terms:
            if a is not None and b is not None:
                total = add(total, a * b)
        return zero if total is None else total

    normal = [[inner_sum([(hess[r][a], hess[r][b]) for r in range(4)]) for b in range(3)] for a in range(3)]
    target = [inner_sum([(hess[r][a], upper[r][0]) for r in range(4)]) for a in range(3)]
    fac = [[None] * 3 for _ in range(3)]
    for col in range(3):
        diag = normal[col][col]
        for inner in range(col):
            diag = diag - fac[col][inner] * fac[col][inner]
        fac[col][col] = jnp.sqrt(diag)
        for row in range(col + 1, 3):
            value = normal[row][col]
            for inner in range(col):
                value = value - fac[row][inner] * fac[col][inner]
            fac[row][col] = value / fac[col][col]
    forward = []
    for place in range(3):
        value = target[place]
        for inner in range(place):
            value = value - fac[place][inner] * forward[inner]
        forward.append(value / fac[place][place])
    backward = [None] * 3
    for place in reversed(range(3)):
        value = forward[place]
        for inner in range(place + 1, 3):
            value = value - fac[inner][place] * backward[inner]
        backward[place] = value / fac[place][place]
    return backward


def kernel(ny, nz, per_owner,
           rs_hbm, sp_hbm, po_hbm, cp, mo_hbm, ids_ref,
           adj_hbm, sens_ref,
           basis, cur, nxt, sp, po, mo, wmat, wz, wa, wb, cpos, cneg, part, fprev, low_shift, high_shift, sface,
           halo_out, halo_in, yfix, block,
           owner_hot, rank_hot, owner_row, local_row, spread, dsend, recv1, turned, recv2, picked,
           gsend, grecv1, gsend2, grecv2,
           in_sem, out_sem, halo_send, halo_recv, a1_sem, a2_sem, g1_sem, g2_sem):
    gy = lax.axis_index("gy")
    gz = lax.axis_index("gz")

    def gy_at(delta):
        return lax.rem(gy + (delta + ny), ny)

    def gz_at(delta):
        return lax.rem(gz + (delta + nz), nz)

    def each(count, step, start=0):
        def body(t, carry):
            step(t)
            return carry
        lax.fori_loop(start, count, body, 0)

    barrier = pltpu.get_barrier_semaphore()

    @functools.partial(each, ny, start=1)
    def _(delta):
        pl.semaphore_signal(barrier, inc=1, device_id={"gy": gy_at(delta)}, device_id_type=MESH)

    @functools.partial(each, nz, start=1)
    def _(delta):
        pl.semaphore_signal(barrier, inc=1, device_id={"gz": gz_at(delta)}, device_id_type=MESH)

    loads = [pltpu.make_async_copy(src, dst, in_sem.at[place]) for place, (src, dst) in enumerate(
        [(sp_hbm, sp), (rs_hbm, nxt), (po_hbm, po), (mo_hbm, mo)])]
    for load in loads:
        load.start()

    lane = iota((16, 256), 1)
    row = iota((16, 256), 0)
    group = lane >> 4
    piece = jnp.where(group >= 10, 2, jnp.where(group >= 5, 1, 0))
    which = group - 5 * piece
    same = (lane & 15) == row

    @functools.partial(each, 3 * VARS)
    def _(place):
        d = lax.div(place, VARS)
        j = place - d * VARS
        value = jnp.zeros((16, 256), F32)
        for i in range(VARS):
            value = jnp.where(which == i, COURANT * cp[i, d, j], value)
        high = value.astype(BF16).astype(F32)
        value = jnp.where(same, jnp.where(piece == 2, value - high, high), 0.0)
        wmat[pl.ds(pl.multiple_of(place * 16, 16), 16), :] = value[:, 0:240].astype(BF16)

    lane = iota((16, 128), 1)
    row = iota((16, 128), 0)

    wz[80:128, :] = jnp.zeros((48, 128), F32)

    @functools.partial(each, VARS)
    def _(i):
        value = jnp.zeros((16, 128), F32)
        for j in range(VARS):
            value = jnp.where((lane >> 4) == j, -COURANT * cp[i, 2, j], value)
        wz[pl.ds(pl.multiple_of(16 * i, 16), 16), :] = jnp.where((lane & 15) == row, value, 0.0)

    ids = jnp.concatenate([ids_ref[0], ids_ref[1]], axis=1)
    owners = lax.div(ids, per_owner)
    local_row[...] = (ids - owners * per_owner + 1).astype(F32)
    number = ny * nz
    tri = jnp.where(iota((256, 128), 0) < jnp.where(iota((256, 128), 0) >= 128, 256, iota((256, 128), 1)), 1.0, 0.0).astype(BF16)
    sub = iota((number, 128), 0)
    before = jnp.zeros((number, 128), F32)
    for p in range(8):
        hot = jnp.where(sub == owners[p:p + 1, :], 1.0, 0.0)
        hot16 = hot.astype(BF16)
        count = dot(jnp.concatenate([hot16, before.astype(BF16)], axis=1), tri)
        before = before + hot
        owner_hot[:, p * 128:(p + 1) * 128] = hot16
        rank = jnp.sum(hot * count, axis=0, keepdims=True)
        rank_hot[:, p * 128:(p + 1) * 128] = jnp.where(rank == iota((SLOTS, 128), 0).astype(F32), 1.0, 0.0)

    loads[0].wait()

    @functools.partial(each, 8)
    def _(x):
        for d in range(3):
            s = sp[d, x]
            cpos[d, x] = jnp.maximum(s, 0.0)
            cneg[d, x] = jnp.maximum(-s, 0.0)

    lanes = iota((32, 128), 1)
    odd = (lanes & 1) == 1
    faces = jnp.zeros((32, 128), F32)
    for x in range(8):
        ends = jnp.where(lanes == 0, sp[2, x, :, 0:128], sp[2, x, :, 128:256])
        faces = jnp.where((lanes >> 1) == x, pltpu.roll(ends, 2 * x + 1, axis=1), faces)
    total = faces
    for i in range(1, VARS):
        total = jnp.where((lanes >> 4) == i, pltpu.roll(faces, 16 * i, axis=1), total)
    total = jnp.where((lanes >> 4) < VARS, total, 0.0)
    sface[...] = jnp.where(odd, jnp.maximum(total, 0.0), jnp.maximum(-total, 0.0))

    keep_low = jnp.where(gy > 0, 1.0, 0.0)
    keep_high = jnp.where(gy < ny - 1, 1.0, 0.0)
    keep_near = jnp.where(gz > 0, 1.0, 0.0)
    keep_far = jnp.where(gz < nz - 1, 1.0, 0.0)

    YROWS = VARS * 16
    ZAT = 2 * YROWS

    def y_at(side, j, half):
        return side * YROWS + j * 16 + half * 8

    def halo_copies(par):
        copies = []
        for side, delta in ((0, -1), (1, 1)):
            rows = pl.ds(side * YROWS, YROWS)
            other = pl.ds((1 - side) * YROWS, YROWS)
            copies.append(pltpu.make_async_remote_copy(
                src_ref=halo_out.at[par, rows], dst_ref=halo_in.at[par, other],
                send_sem=halo_send.at[par], recv_sem=halo_recv.at[par],
                device_id={"gy": gy_at(delta)}, device_id_type=MESH))
            copies.append(pltpu.make_async_remote_copy(
                src_ref=halo_out.at[par, pl.ds(ZAT, 32)], dst_ref=halo_in.at[par, pl.ds(ZAT + 32 * (1 - side), 32)],
                send_sem=halo_send.at[par], recv_sem=halo_recv.at[par],
                device_id={"gz": gz_at(delta)}, device_id_type=MESH))
        return copies

    def wait_all(ref, sem):
        pltpu.make_async_copy(ref, ref, sem).wait()

    halves = (slice(0, 128), slice(128, 256))

    def fix_and_pack(k, par, ufix):
        for i in range(VARS):
            for x in range(8):
                for side, y in ((0, 0), (1, 31)):
                    for half in range(2):
                        at = y_at(side, i, half) + x
                        nxt[i, x, y:y + 1, halves[half]] = nxt[i, x, y:y + 1, halves[half]] + yfix[at:at + 1, :]
        packed = jnp.zeros((32, 128), F32)
        for i in range(VARS):
            for x in range(8):
                s = i * 8 + x
                fix = pltpu.roll(ufix, 127 - 2 * s, axis=1)
                near = nxt[i, x, :, 0:128] + jnp.where(lanes == 0, fix, 0.0)
                far = nxt[i, x, :, 128:256] + jnp.where(lanes == 127, fix, 0.0)
                cur[i, x, :, 0:128] = near
                cur[i, x, :, 128:256] = far
                basis[k, i, x, :, 0:128] = near
                basis[k, i, x, :, 128:256] = far
                ends = jnp.where(lanes == 0, near, far)
                packed = jnp.where((lanes >> 1) == s, pltpu.roll(ends, 2 * s + 1, axis=1), packed)
        halo_out[par, ZAT:ZAT + 32, :] = jnp.dot(
            packed * sface[...], wz[...], preferred_element_type=F32, precision=lax.Precision.HIGHEST)
        for side, y in ((0, 0), (1, 31)):
            for half in range(2):
                speed = sp[1, :, y, halves[half]]
                speed = jnp.maximum(speed, 0.0) if side == 0 else jnp.maximum(-speed, 0.0)
                flux = [cur[i, :, y, halves[half]] * speed for i in range(VARS)]
                for j in range(VARS):
                    total = flux[0] * (-COURANT * cp[0, 1, j])
                    for i in range(1, VARS):
                        total = total + flux[i] * (-COURANT * cp[i, 1, j])
                    at = y_at(side, j, half)
                    halo_out[par, at:at + 8, :] = total

    def receive(par):
        wait_all(halo_in.at[par], halo_recv.at[par])
        wait_all(halo_in.at[par], halo_send.at[par])
        yfix[0:YROWS, :] = keep_low * halo_in[par, 0:YROWS, :] - halo_out[par, YROWS:ZAT, :]
        yfix[YROWS:ZAT, :] = keep_high * halo_in[par, YROWS:ZAT, :] - halo_out[par, 0:YROWS, :]
        own = halo_out[par, ZAT:ZAT + 32, :]
        from_near = pltpu.roll(keep_near * halo_in[par, ZAT:ZAT + 32, :] - own, 1, axis=1)
        from_far = pltpu.roll(keep_far * halo_in[par, ZAT + 32:ZAT + 64, :] - own, 127, axis=1)
        yfix[ZAT:ZAT + 32, :] = jnp.where(odd, from_near, from_far)

    def couple(x, w):
        for h in (0, 16):
            high, low = [], []
            for i in range(VARS):
                v = cur[i, x, h:h + 16, :]
                top = v.astype(BF16)
                high.append(top)
                low.append((v - top.astype(F32)).astype(BF16))
            out = dot(wmat[...], jnp.concatenate(high + low + high, axis=0))
            for place in range(3 * VARS):
                w[place, h:h + 16, :] = out[place * 16:place * 16 + 16]

    def stencil(x, w):
        prior = jnp.maximum(x - 1, 0)
        for j in range(VARS):
            wx = w[j]
            flux = cpos[0, x] * wx - fprev[j]
            nxt[j, prior] = part[j] - flux
            fprev[j] = cneg[0, x] * wx
            acc = po[x] * cur[j, x] + flux
            wv = w[2 * VARS + j]
            flux = cpos[2, x] * wv - pltpu.roll(cneg[2, x] * wv, 1, axis=1)
            acc = acc + flux - pltpu.roll(flux, 255, axis=1)
            for half in range(2):
                at = halves[half]
                wy = w[VARS + j, :, at]
                minus = cneg[1, x, :, at] * wy
                low_shift[j, half, 8:40, :] = minus
                low_shift[j, half, 0:8, :] = minus[24:32]
                flux = cpos[1, x, :, at] * wy - low_shift[j, half, 7:39, :]
                high_shift[j, half, 0:32, :] = flux
                high_shift[j, half, 32:40, :] = flux[0:8]
                part[j, :, at] = acc[:, at] + flux - high_shift[j, half, 1:33, :]

    def sweep():
        fprev[...] = jnp.zeros(fprev.shape, F32)
        couple(0, wa)

        @functools.partial(each, 4)
        def _(t):
            x = 2 * t
            couple(x + 1, wb)
            stencil(x, wa)
            couple(jnp.minimum(x + 2, 7), wa)
            stencil(x + 1, wb)

        for j in range(VARS):
            nxt[j, 7] = part[j] + fprev[j]

    def dispatch():
        loads[3].wait()

        @functools.partial(each, 2)
        def _(half_x):
            for k in range(3):
                total = None
                for x in range(4):
                    for i in range(3):
                        term = basis[k, 1 + i, 4 * half_x + x] * mo[i, 4 * half_x + x]
                        total = term if total is None else total + term
                block[k, half_x] = total

        low8 = iota((16, 192), 0)
        col = iota((16, 192), 1)
        within = jnp.where(col >= 96, col - 96, col) & 31
        half = jnp.where(col >= 96, 1, 0)
        ysel = jnp.where((low8 >> 3 == half) & ((low8 & 7) == (within >> 2)), 1.0, 0.0).astype(BF16)
        zrow = iota((512, 128), 0)
        zsel = jnp.where(((zrow & 255) >> 2) + (zrow >> 8) * 64 == iota((512, 128), 1), 1.0, 0.0).astype(BF16)
        parts = []
        for k in range(3):
            t = dot(ysel, jnp.concatenate(list(pieces(block[k, 0])) + list(pieces(block[k, 1])), axis=0))
            for part_ in pieces(jnp.concatenate([t[0:8], t[8:16]], axis=1)):
                parts.append(part_.astype(F32))
        t = dot(jnp.concatenate(parts, axis=0).astype(BF16), zsel)
        values = [-PENALTY * (t[24 * k:24 * k + 8] + t[24 * k + 8:24 * k + 16] + t[24 * k + 16:24 * k + 24])
                  for k in range(3)]
        tops = [value.astype(BF16).astype(F32) for value in values]
        rests = [value - top for value, top in zip(values, tops)]
        empty = jnp.zeros((SLOTS, 128), BF16)
        for p in range(8):
            hot = rank_hot[:, p * 128:(p + 1) * 128]
            rows = [local_row[...]] + tops + rests
            rows = [(hot * value[p:p + 1, :]).astype(BF16) for value in rows]
            spread[:, p * 128:(p + 1) * 128] = jnp.concatenate(rows + [empty], axis=0)
        dsend[...] = dot_nt(owner_hot[...], spread[...]).reshape(ny, nz, 128)

        @functools.partial(each, ny, start=1)
        def _(delta):
            pltpu.make_async_remote_copy(
                src_ref=dsend.at[gy_at(delta)], dst_ref=recv1.at[delta],
                send_sem=a1_sem.at[0], recv_sem=a1_sem.at[1],
                device_id={"gy": gy_at(delta)}, device_id_type=MESH).start()
        recv1[0] = dsend[gy]

    yfix[...] = jnp.zeros(yfix.shape, F32)
    loads[1].wait()
    loads[2].wait()

    @functools.partial(each, 4)
    def _(k):
        par = k & 1

        @pl.when(k > 0)
        def _():
            receive(1 - par)

        fix_and_pack(k, par, yfix[ZAT:ZAT + 32, :])

        @pl.when(k == 0)
        def _():
            pl.semaphore_wait(barrier, (ny - 1) + (nz - 1))

        @pl.when(k < 3)
        def _():
            for copy in halo_copies(par):
                copy.start()

            @pl.when(k == 2)
            def _():
                dispatch()

            sweep()

    pairs = [(l, k) for k in range(4) for l in range(k + 1)]

    def products(x, sums):
        sums = list(sums)
        for j in range(VARS):
            v = [basis[k, j, x] for k in range(4)]
            for e, (l, k) in enumerate(pairs):
                sums[e] = sums[e] + fold(v[l] * v[k])
        return tuple(sums)

    sums = lax.fori_loop(0, 8, products, tuple(jnp.zeros((8, 128), F32) for _ in pairs))

    lane = iota((8, 128), 1)
    packed = jnp.zeros((8, 128), F32)
    for e, value in enumerate(sums):
        for shift in (64, 32, 16, 8):
            value = value + pltpu.roll(value, shift, axis=1)
        packed = jnp.where((lane >> 3) == e, value, packed)
    gsend[...] = jnp.sum(packed, axis=0, keepdims=True)

    @functools.partial(each, ny, start=1)
    def _(delta):
        pltpu.make_async_remote_copy(
            src_ref=gsend, dst_ref=grecv1.at[delta], send_sem=g1_sem.at[0], recv_sem=g1_sem.at[1],
            device_id={"gy": gy_at(delta)}, device_id_type=MESH).start()

    wait_all(recv1.at[pl.ds(1, ny - 1)], a1_sem.at[1])
    wait_all(recv1.at[pl.ds(1, ny - 1)], a1_sem.at[0])
    for g in range(nz):
        turned[g] = recv1[:, g, :]

    @functools.partial(each, nz, start=1)
    def _(delta):
        pltpu.make_async_remote_copy(
            src_ref=turned.at[gz_at(delta)], dst_ref=recv2.at[delta], send_sem=a2_sem.at[0], recv_sem=a2_sem.at[1],
            device_id={"gz": gz_at(delta)}, device_id_type=MESH).start()
    recv2[0] = turned[gz]

    wait_all(grecv1.at[pl.ds(1, ny - 1)], g1_sem.at[1])
    wait_all(grecv1.at[pl.ds(1, ny - 1)], g1_sem.at[0])
    own = gsend[...]
    for delta in range(1, ny):
        own = own + grecv1[delta]
    gsend2[...] = own

    @functools.partial(each, nz, start=1)
    def _(delta):
        pltpu.make_async_remote_copy(
            src_ref=gsend2, dst_ref=grecv2.at[delta], send_sem=g2_sem.at[0], recv_sem=g2_sem.at[1],
            device_id={"gz": gz_at(delta)}, device_id_type=MESH).start()

    wait_all(recv2.at[pl.ds(1, nz - 1)], a2_sem.at[1])
    wait_all(recv2.at[pl.ds(1, nz - 1)], a2_sem.at[0])
    picked[...] = recv2[...].reshape(number, 128).T
    digit = iota((16, 128), 0)
    left, right = [], []
    for r in range(SLOTS):
        number_r = picked[r:r + 1, :].astype(jnp.int32) - 1
        high = (number_r >> 4) == digit
        right.append(jnp.where((number_r & 15) == digit, 1.0, 0.0).astype(BF16))
        left.append(jnp.concatenate(
            [jnp.where(high, picked[SLOTS * (q + 1) + r:SLOTS * (q + 1) + r + 1, :], 0.0).astype(BF16) for q in range(6)], axis=0))
    bins = dot_nt(jnp.concatenate(left, axis=1), jnp.concatenate(right, axis=1))
    bins = bins[0:48] + bins[48:96]
    wide = jnp.where((iota((16, 256), 1) & 15) == iota((16, 256), 0), 1.0, 0.0).astype(BF16)
    bins = sum(dot(part_, wide) for part_ in pieces(bins))
    bins = jnp.where((iota((48, 256), 1) >> 4) == (iota((48, 256), 0) & 15), bins, 0.0)
    bin_sums = [jnp.sum(bins[16 * k:16 * k + 16], axis=0, keepdims=True) for k in range(3)]

    wait_all(grecv2.at[pl.ds(1, nz - 1)], g2_sem.at[1])
    wait_all(grecv2.at[pl.ds(1, nz - 1)], g2_sem.at[0])
    own = gsend2[...]
    for delta in range(1, nz):
        own = own + grecv2[delta]
    for shift in (4, 2, 1):
        own = own + pltpu.roll(own, shift, axis=1)
    own = jnp.broadcast_to(own, (8, 128))
    splat = {}
    for e, (l, k) in enumerate(pairs):
        splat[l, k] = jnp.broadcast_to(own[:, 8 * e + 7:8 * e + 8], (8, 128))
    coeffs = solve([[splat[min(a, b), max(a, b)] for b in range(4)] for a in range(4)])

    sens = None
    for k in range(3):
        term = bin_sums[k] * jnp.concatenate([coeffs[k][0:1]] * (per_owner // 128), axis=1)
        sens = term if sens is None else sens + term
    sens_ref[...] = sens

    full = [jnp.concatenate([jnp.concatenate([c, c], axis=1)] * 4, axis=0) for c in coeffs]

    @functools.partial(each, VARS)
    def _(j):
        for x in range(8):
            nxt[j, x] = full[0] * basis[0, j, x] + full[1] * basis[1, j, x] + full[2] * basis[2, j, x]
        pltpu.make_async_copy(nxt.at[j], adj_hbm.at[j], out_sem).start()

    wait_all(nxt, out_sem)


def local(right_side, speeds, porosity, coupling, momentum, design_ids):
    ny = lax.axis_size("gy")
    nz = lax.axis_size("gz")
    _, nx, cy, cz = right_side.shape
    per_owner = design_ids.size // 4
    field = (VARS, nx, cy, cz)
    dma = pltpu.SemaphoreType.DMA
    hbm = pl.BlockSpec(memory_space=pltpu.HBM)
    vmem = pl.BlockSpec(memory_space=pltpu.VMEM)
    adjoint, sensitivity = pl.pallas_call(
        functools.partial(kernel, ny, nz, per_owner),
        out_shape=[jax.ShapeDtypeStruct(field, F32), jax.ShapeDtypeStruct((1, per_owner), F32)],
        in_specs=[hbm, hbm, hbm, pl.BlockSpec(memory_space=pltpu.SMEM), hbm, vmem],
        out_specs=[hbm, vmem],
        scratch_shapes=[
            pltpu.VMEM((4,) + field, F32), pltpu.VMEM(field, F32), pltpu.VMEM(field, F32),
            pltpu.VMEM((3, nx, cy, cz), F32),
            pltpu.VMEM((nx, cy, cz), F32),
            pltpu.VMEM((3, nx, cy, cz), F32),
            pltpu.VMEM((240, 240), BF16),
            pltpu.VMEM((128, 128), F32),
            pltpu.VMEM((3 * VARS, cy, cz), F32), pltpu.VMEM((3 * VARS, cy, cz), F32),
            pltpu.VMEM((3, nx, cy, cz), F32), pltpu.VMEM((3, nx, cy, cz), F32),
            pltpu.VMEM((VARS, cy, cz), F32), pltpu.VMEM((VARS, cy, cz), F32),
            pltpu.VMEM((VARS, 2, 40, 128), F32), pltpu.VMEM((VARS, 2, 40, 128), F32),
            pltpu.VMEM((32, 128), F32),
            pltpu.VMEM((2, 192, 128), F32), pltpu.VMEM((2, 224, 128), F32), pltpu.VMEM((192, 128), F32),
            pltpu.VMEM((3, 2, cy, cz), F32),
            pltpu.VMEM((ny * nz, 1024), BF16),
            pltpu.VMEM((SLOTS, 1024), F32),
            pltpu.VMEM((8, 128), F32),
            pltpu.VMEM((8, 128), F32),
            pltpu.VMEM((128, 1024), BF16),
            pltpu.VMEM((ny, nz, 128), F32),
            pltpu.VMEM((ny, nz, 128), F32),
            pltpu.VMEM((nz, ny, 128), F32),
            pltpu.VMEM((nz, ny, 128), F32),
            pltpu.VMEM((128, 128), F32),
            pltpu.VMEM((1, 128), F32),
            pltpu.VMEM((ny, 1, 128), F32),
            pltpu.VMEM((1, 128), F32),
            pltpu.VMEM((nz, 1, 128), F32),
            dma((4,)), dma, dma((2,)), dma((2,)), dma((2,)), dma((2,)), dma((2,)), dma((2,)),
        ],
        compiler_params=pltpu.CompilerParams(
            collective_id=0, has_side_effects=True, vmem_limit_bytes=48 * 1024 * 1024),
    )(right_side, speeds, porosity, coupling.transpose(1, 0, 2), momentum, design_ids)
    return adjoint, sensitivity.reshape(per_owner)


def solution(mesh):
    in_specs = (
        P(None, None, "gy", "gz"),
        P(None, None, "gy", "gz"),
        P(None, "gy", "gz"),
        P(),
        P(None, None, "gy", "gz"),
        P(None, "gy", "gz"),
    )
    out_specs = (P(None, None, "gy", "gz"), P(("gy", "gz")))
    return jax.shard_map(local, mesh=mesh, in_specs=in_specs, out_specs=out_specs, check_vma=False)
```

```python
import functools

import jax
import jax.numpy as jnp
from jax import lax
from jax.experimental import pallas as pl
from jax.experimental.pallas import tpu as pltpu
from jax.sharding import PartitionSpec as P

PENALTY = 1.0
COURANT = 0.3
VARS = 5
SLOTS = 16
MESH = pl.DeviceIdType.MESH
F32 = jnp.float32
BF16 = jnp.bfloat16


def pieces(value):
    high = value.astype(BF16)
    rest = value - high.astype(F32)
    mid = rest.astype(BF16)
    low = (rest - mid.astype(F32)).astype(BF16)
    return high, mid, low


def dot(a, b):
    return jnp.dot(a, b, preferred_element_type=F32)


def dot_nt(a, b):
    return lax.dot_general(a, b, (((1,), (1,)), ((), ())), preferred_element_type=F32)


def iota(shape, axis):
    return lax.broadcasted_iota(jnp.int32, shape, axis)


def fold(product):
    rows = product[0:8] + product[8:16] + product[16:24] + product[24:32]
    return rows[:, 0:128] + rows[:, 128:256]


def solve(gram):
    low = [[None] * 4 for _ in range(4)]
    for col in range(4):
        diag = gram[col][col]
        for inner in range(col):
            diag = diag - low[col][inner] * low[col][inner]
        low[col][col] = jnp.sqrt(diag)
        for row in range(col + 1, 4):
            value = gram[row][col]
            for inner in range(col):
                value = value - low[row][inner] * low[col][inner]
            low[row][col] = value / low[col][col]
    zero = jnp.zeros_like(gram[0][0])
    upper = [[low[c][r] if c >= r else None for c in range(4)] for r in range(4)]

    def add(a, b):
        return b if a is None else (a if b is None else a + b)

    hess = [[add(upper[r][c + 1], upper[r][c]) for c in range(3)] for r in range(4)]

    def inner_sum(terms):
        total = None
        for a, b in terms:
            if a is not None and b is not None:
                total = add(total, a * b)
        return zero if total is None else total

    normal = [[inner_sum([(hess[r][a], hess[r][b]) for r in range(4)]) for b in range(3)] for a in range(3)]
    target = [inner_sum([(hess[r][a], upper[r][0]) for r in range(4)]) for a in range(3)]
    fac = [[None] * 3 for _ in range(3)]
    for col in range(3):
        diag = normal[col][col]
        for inner in range(col):
            diag = diag - fac[col][inner] * fac[col][inner]
        fac[col][col] = jnp.sqrt(diag)
        for row in range(col + 1, 3):
            value = normal[row][col]
            for inner in range(col):
                value = value - fac[row][inner] * fac[col][inner]
            fac[row][col] = value / fac[col][col]
    forward = []
    for place in range(3):
        value = target[place]
        for inner in range(place):
            value = value - fac[place][inner] * forward[inner]
        forward.append(value / fac[place][place])
    backward = [None] * 3
    for place in reversed(range(3)):
        value = forward[place]
        for inner in range(place + 1, 3):
            value = value - fac[inner][place] * backward[inner]
        backward[place] = value / fac[place][place]
    return backward


def kernel(ny, nz, per_owner,
           rs_hbm, sp_hbm, po_hbm, cp, mo_hbm, ids_ref,
           adj_hbm, sens_ref,
           basis, cur, nxt, sp, po, mo, wmat, wz, wa, wb, cpos, cneg, part, fprev, low_shift, high_shift, sface,
           halo_out, halo_in, yfix, block, prods,
           owner_hot, rank_hot, owner_row, local_row, spread, dsend, recv1, turned, recv2, picked,
           gsend, grecv1, gsend2, grecv2,
           in_sem, out_sem, halo_send, halo_recv, a1_sem, a2_sem, g1_sem, g2_sem):
    gy = lax.axis_index("gy")
    gz = lax.axis_index("gz")

    number = ny * nz

    def gy_at(delta):
        return lax.rem(gy + (delta + ny), ny)

    def gz_at(delta):
        return lax.rem(gz + (delta + nz), nz)

    def each(count, step, start=0):
        def body(t, carry):
            step(t)
            return carry
        lax.fori_loop(start, count, body, 0)

    barrier = pltpu.get_barrier_semaphore()

    @functools.partial(each, ny, start=1)
    def _(delta):
        pl.semaphore_signal(barrier, inc=1, device_id={"gy": gy_at(delta)}, device_id_type=MESH)

    @functools.partial(each, nz, start=1)
    def _(delta):
        pl.semaphore_signal(barrier, inc=1, device_id={"gz": gz_at(delta)}, device_id_type=MESH)

    loads = [pltpu.make_async_copy(src, dst, in_sem.at[place]) for place, (src, dst) in enumerate(
        [(sp_hbm, sp), (rs_hbm, nxt), (po_hbm, po), (mo_hbm, mo)])]
    for load in loads:
        load.start()

    lane = iota((16, 128), 1)
    row = iota((16, 128), 0)

    wz[80:128, :] = jnp.zeros((48, 128), F32)

    @functools.partial(each, VARS)
    def _(i):
        value = jnp.zeros((16, 128), F32)
        for j in range(VARS):
            value = jnp.where((lane >> 4) == j, -COURANT * cp[i, 2, j], value)
        wz[pl.ds(pl.multiple_of(16 * i, 16), 16), :] = jnp.where((lane & 15) == row, value, 0.0)

    loads[0].wait()

    lanes = iota((32, 128), 1)
    odd = (lanes & 1) == 1
    faces = jnp.zeros((32, 128), F32)
    for x in range(8):
        ends = jnp.where(lanes == 0, sp[2, x, :, 0:128], sp[2, x, :, 128:256])
        faces = jnp.where((lanes >> 1) == x, pltpu.roll(ends, 2 * x + 1, axis=1), faces)
    total = faces
    for i in range(1, VARS):
        total = jnp.where((lanes >> 4) == i, pltpu.roll(faces, 16 * i, axis=1), total)
    total = jnp.where((lanes >> 4) < VARS, total, 0.0)
    sface[...] = jnp.where(odd, jnp.maximum(total, 0.0), jnp.maximum(-total, 0.0))

    inside = (gy > 0, gy < ny - 1, gz > 0, gz < nz - 1)

    YROWS = VARS * 16
    ZAT = 2 * YROWS

    def y_at(side, j, half):
        return side * YROWS + j * 16 + half * 8

    def in_rows(place):
        return pl.ds(place * YROWS, YROWS) if place < 2 else pl.ds(ZAT + 32 * (place - 2), 32)

    def send_halo(par):
        for place, (axis, delta) in enumerate((("y", -1), ("y", 1), ("z", -1), ("z", 1))):
            rows = in_rows(place) if axis == "y" else pl.ds(ZAT, 32)
            target = {"gy": gy_at(delta)} if axis == "y" else {"gz": gz_at(delta)}
            copy = pltpu.make_async_remote_copy(
                src_ref=halo_out.at[par, rows], dst_ref=halo_in.at[par, in_rows(place ^ 1)],
                send_sem=halo_send.at[par, place], recv_sem=halo_recv.at[par, place ^ 1],
                device_id=target, device_id_type=MESH)
            pl.when(inside[place])(copy.start)

    for place in range(4):
        @pl.when(jnp.logical_not(inside[place]))
        def _():
            for par in range(2):
                halo_in[par, in_rows(place), :] = jnp.zeros((YROWS if place < 2 else 32, 128), F32)

    def wait_all(ref, sem):
        pltpu.make_async_copy(ref, ref, sem).wait()

    halves = (slice(0, 128), slice(128, 256))

    def fix_and_pack(k, par, ufix):
        for i in range(VARS):
            for x in range(8):
                for side, y in ((0, 0), (1, 31)):
                    for half in range(2):
                        at = y_at(side, i, half) + x
                        nxt[i, x, y:y + 1, halves[half]] = nxt[i, x, y:y + 1, halves[half]] + yfix[at:at + 1, :]
        packed = jnp.zeros((32, 128), F32)
        for i in range(VARS):
            for x in range(8):
                s = i * 8 + x
                fix = pltpu.roll(ufix, 127 - 2 * s, axis=1)
                near = nxt[i, x, :, 0:128] + jnp.where(lanes == 0, fix, 0.0)
                far = nxt[i, x, :, 128:256] + jnp.where(lanes == 127, fix, 0.0)
                cur[i, x, :, 0:128] = near
                cur[i, x, :, 128:256] = far
                basis[k, i, x, :, 0:128] = near
                basis[k, i, x, :, 128:256] = far
                ends = jnp.where(lanes == 0, near, far)
                packed = jnp.where((lanes >> 1) == s, pltpu.roll(ends, 2 * s + 1, axis=1), packed)
        halo_out[par, ZAT:ZAT + 32, :] = jnp.dot(
            packed * sface[...], wz[...], preferred_element_type=F32, precision=lax.Precision.HIGHEST)
        for side, y in ((0, 0), (1, 31)):
            for half in range(2):
                speed = sp[1, :, y, halves[half]]
                speed = jnp.maximum(speed, 0.0) if side == 0 else jnp.maximum(-speed, 0.0)
                flux = [cur[i, :, y, halves[half]] * speed for i in range(VARS)]
                for j in range(VARS):
                    total = flux[0] * (-COURANT * cp[0, 1, j])
                    for i in range(1, VARS):
                        total = total + flux[i] * (-COURANT * cp[i, 1, j])
                    at = y_at(side, j, half)
                    halo_out[par, at:at + 8, :] = total

    def receive(par):
        for place in range(4):
            @pl.when(inside[place])
            def _():
                ref = halo_in.at[par, in_rows(place)]
                wait_all(ref, halo_recv.at[par, place])
                wait_all(ref, halo_send.at[par, place])
        yfix[0:YROWS, :] = halo_in[par, 0:YROWS, :] - halo_out[par, YROWS:ZAT, :]
        yfix[YROWS:ZAT, :] = halo_in[par, YROWS:ZAT, :] - halo_out[par, 0:YROWS, :]
        own = halo_out[par, ZAT:ZAT + 32, :]
        from_near = pltpu.roll(halo_in[par, ZAT:ZAT + 32, :] - own, 1, axis=1)
        from_far = pltpu.roll(halo_in[par, ZAT + 32:ZAT + 64, :] - own, 127, axis=1)
        yfix[ZAT:ZAT + 32, :] = jnp.where(odd, from_near, from_far)

    def prepare():
        @functools.partial(each, 8)
        def _(x):
            for d in range(3):
                s = sp[d, x]
                cpos[d, x] = jnp.maximum(s, 0.0)
                cneg[d, x] = jnp.maximum(-s, 0.0)

        lane = iota((16, 256), 1)
        row = iota((16, 256), 0)
        group = lane >> 4
        piece = jnp.where(group >= 10, 2, jnp.where(group >= 5, 1, 0))
        which = group - 5 * piece
        same = (lane & 15) == row

        @functools.partial(each, 3 * VARS)
        def _(place):
            d = lax.div(place, VARS)
            j = place - d * VARS
            value = jnp.zeros((16, 256), F32)
            for i in range(VARS):
                value = jnp.where(which == i, COURANT * cp[i, d, j], value)
            high = value.astype(BF16).astype(F32)
            value = jnp.where(same, jnp.where(piece == 2, value - high, high), 0.0)
            wmat[pl.ds(pl.multiple_of(place * 16, 16), 16), :] = value[:, 0:240].astype(BF16)

        ids = jnp.concatenate([ids_ref[0], ids_ref[1]], axis=1)
        owners = lax.div(ids, per_owner)
        local_row[...] = (ids - owners * per_owner + 1).astype(F32)
        tri = jnp.where(iota((256, 128), 0) < jnp.where(iota((256, 128), 0) >= 128, 256, iota((256, 128), 1)), 1.0, 0.0).astype(BF16)
        sub = iota((number, 128), 0)
        before = jnp.zeros((number, 128), F32)
        for p in range(8):
            hot = jnp.where(sub == owners[p:p + 1, :], 1.0, 0.0)
            hot16 = hot.astype(BF16)
            count = dot(jnp.concatenate([hot16, before.astype(BF16)], axis=1), tri)
            before = before + hot
            owner_hot[:, p * 128:(p + 1) * 128] = hot16
            rank = jnp.sum(hot * count, axis=0, keepdims=True)
            rank_hot[:, p * 128:(p + 1) * 128] = jnp.where(rank == iota((SLOTS, 128), 0).astype(F32), 1.0, 0.0)


    def couple(x, w):
        for h in (0, 16):
            high, low = [], []
            for i in range(VARS):
                v = cur[i, x, h:h + 16, :]
                top = v.astype(BF16)
                high.append(top)
                low.append((v - top.astype(F32)).astype(BF16))
            out = dot(wmat[...], jnp.concatenate(high + low + high, axis=0))
            for place in range(3 * VARS):
                w[place, h:h + 16, :] = out[place * 16:place * 16 + 16]

    def stencil(x, w):
        prior = jnp.maximum(x - 1, 0)
        for j in range(VARS):
            wx = w[j]
            flux = cpos[0, x] * wx - fprev[j]
            nxt[j, prior] = part[j] - flux
            fprev[j] = cneg[0, x] * wx
            acc = po[x] * cur[j, x] + flux
            wv = w[2 * VARS + j]
            flux = cpos[2, x] * wv - pltpu.roll(cneg[2, x] * wv, 1, axis=1)
            acc = acc + flux - pltpu.roll(flux, 255, axis=1)
            for half in range(2):
                at = halves[half]
                wy = w[VARS + j, :, at]
                minus = cneg[1, x, :, at] * wy
                low_shift[j, half, 8:40, :] = minus
                low_shift[j, half, 0:8, :] = minus[24:32]
                flux = cpos[1, x, :, at] * wy - low_shift[j, half, 7:39, :]
                high_shift[j, half, 0:32, :] = flux
                high_shift[j, half, 32:40, :] = flux[0:8]
                part[j, :, at] = acc[:, at] + flux - high_shift[j, half, 1:33, :]

    def sweep():
        fprev[...] = jnp.zeros(fprev.shape, F32)
        couple(0, wa)

        @functools.partial(each, 4)
        def _(t):
            x = 2 * t
            couple(x + 1, wb)
            stencil(x, wa)
            couple(jnp.minimum(x + 2, 7), wa)
            stencil(x + 1, wb)

        for j in range(VARS):
            nxt[j, 7] = part[j] + fprev[j]

    def dispatch():
        loads[3].wait()

        @functools.partial(each, 2)
        def _(half_x):
            for k in range(3):
                total = None
                for x in range(4):
                    for i in range(3):
                        term = basis[k, 1 + i, 4 * half_x + x] * mo[i, 4 * half_x + x]
                        total = term if total is None else total + term
                block[k, half_x] = total

        low8 = iota((16, 192), 0)
        col = iota((16, 192), 1)
        within = jnp.where(col >= 96, col - 96, col) & 31
        half = jnp.where(col >= 96, 1, 0)
        ysel = jnp.where((low8 >> 3 == half) & ((low8 & 7) == (within >> 2)), 1.0, 0.0).astype(BF16)
        zrow = iota((512, 128), 0)
        zsel = jnp.where(((zrow & 255) >> 2) + (zrow >> 8) * 64 == iota((512, 128), 1), 1.0, 0.0).astype(BF16)
        parts = []
        for k in range(3):
            t = dot(ysel, jnp.concatenate(list(pieces(block[k, 0])) + list(pieces(block[k, 1])), axis=0))
            for part_ in pieces(jnp.concatenate([t[0:8], t[8:16]], axis=1)):
                parts.append(part_.astype(F32))
        t = dot(jnp.concatenate(parts, axis=0).astype(BF16), zsel)
        values = [-PENALTY * (t[24 * k:24 * k + 8] + t[24 * k + 8:24 * k + 16] + t[24 * k + 16:24 * k + 24])
                  for k in range(3)]
        tops = [value.astype(BF16).astype(F32) for value in values]
        rests = [value - top for value, top in zip(values, tops)]
        empty = jnp.zeros((SLOTS, 128), BF16)
        for p in range(8):
            hot = rank_hot[:, p * 128:(p + 1) * 128]
            rows = [local_row[...]] + tops + rests
            rows = [(hot * value[p:p + 1, :]).astype(BF16) for value in rows]
            spread[:, p * 128:(p + 1) * 128] = jnp.concatenate(rows + [empty], axis=0)
        dsend[...] = dot_nt(owner_hot[...], spread[...]).reshape(ny, nz, 128)

        @functools.partial(each, ny, start=1)
        def _(delta):
            pltpu.make_async_remote_copy(
                src_ref=dsend.at[gy_at(delta)], dst_ref=recv1.at[delta],
                send_sem=a1_sem.at[0], recv_sem=a1_sem.at[1],
                device_id={"gy": gy_at(delta)}, device_id_type=MESH).start()
        recv1[0] = dsend[gy]

    pairs = [(l, k) for k in range(4) for l in range(k + 1)]

    def early(x, sums):
        sums = list(sums)
        for j in range(VARS):
            v = [basis[k, j, x] for k in range(3)]
            for e, (l, k) in enumerate(pairs[:6]):
                sums[e] = sums[e] + fold(v[l] * v[k])
        return tuple(sums)

    yfix[...] = jnp.zeros(yfix.shape, F32)
    loads[1].wait()

    @functools.partial(each, 3)
    def _(k):
        par = k & 1

        @pl.when(k > 0)
        def _():
            receive(1 - par)

        fix_and_pack(k, par, yfix[ZAT:ZAT + 32, :])

        @pl.when(k == 0)
        def _():
            pl.semaphore_wait(barrier, (ny - 1) + (nz - 1))

        send_halo(par)

        @pl.when(k == 0)
        def _():
            prepare()
            loads[2].wait()

        @pl.when(k == 2)
        def _():
            dispatch()
            done = lax.fori_loop(0, 8, early, tuple(jnp.zeros((8, 128), F32) for _ in range(6)))
            for e in range(6):
                prods[e] = done[e]

        sweep()

    receive(0)

    def late(j, sums):
        sums = list(sums)
        for x in range(8):
            for side, y in ((0, 0), (1, 31)):
                for half in range(2):
                    at = pl.ds(side * YROWS + j * 16 + half * 8 + x, 1)
                    nxt[j, x, y:y + 1, halves[half]] = nxt[j, x, y:y + 1, halves[half]] + yfix[at, :]
        ufix = yfix[ZAT:ZAT + 32, :]
        for x in range(8):
            fix = pltpu.roll(ufix, 127 - 16 * j - 2 * x, axis=1)
            near = nxt[j, x, :, 0:128] + jnp.where(lanes == 0, fix, 0.0)
            far = nxt[j, x, :, 128:256] + jnp.where(lanes == 127, fix, 0.0)
            for l in range(4):
                if l < 3:
                    product = basis[l, j, x, :, 0:128] * near + basis[l, j, x, :, 128:256] * far
                else:
                    product = near * near + far * far
                sums[l] = sums[l] + (product[0:8] + product[8:16] + product[16:24] + product[24:32])
        return tuple(sums)

    sums = lax.fori_loop(0, VARS, late, tuple(jnp.zeros((8, 128), F32) for _ in range(4)))
    sums = [prods[e] for e in range(6)] + list(sums)

    lane = iota((8, 128), 1)
    packed = jnp.zeros((8, 128), F32)
    for e, value in enumerate(sums):
        for shift in (64, 32, 16, 8):
            value = value + pltpu.roll(value, shift, axis=1)
        packed = jnp.where((lane >> 3) == e, value, packed)
    gsend[...] = jnp.sum(packed, axis=0, keepdims=True)

    @functools.partial(each, ny, start=1)
    def _(delta):
        pltpu.make_async_remote_copy(
            src_ref=gsend, dst_ref=grecv1.at[delta], send_sem=g1_sem.at[0], recv_sem=g1_sem.at[1],
            device_id={"gy": gy_at(delta)}, device_id_type=MESH).start()

    wait_all(recv1.at[pl.ds(1, ny - 1)], a1_sem.at[1])
    wait_all(recv1.at[pl.ds(1, ny - 1)], a1_sem.at[0])
    for g in range(nz):
        turned[g] = recv1[:, g, :]

    @functools.partial(each, nz, start=1)
    def _(delta):
        pltpu.make_async_remote_copy(
            src_ref=turned.at[gz_at(delta)], dst_ref=recv2.at[delta], send_sem=a2_sem.at[0], recv_sem=a2_sem.at[1],
            device_id={"gz": gz_at(delta)}, device_id_type=MESH).start()
    recv2[0] = turned[gz]

    wait_all(grecv1.at[pl.ds(1, ny - 1)], g1_sem.at[1])
    wait_all(grecv1.at[pl.ds(1, ny - 1)], g1_sem.at[0])
    own = gsend[...]
    for delta in range(1, ny):
        own = own + grecv1[delta]
    gsend2[...] = own

    @functools.partial(each, nz, start=1)
    def _(delta):
        pltpu.make_async_remote_copy(
            src_ref=gsend2, dst_ref=grecv2.at[delta], send_sem=g2_sem.at[0], recv_sem=g2_sem.at[1],
            device_id={"gz": gz_at(delta)}, device_id_type=MESH).start()

    wait_all(recv2.at[pl.ds(1, nz - 1)], a2_sem.at[1])
    wait_all(recv2.at[pl.ds(1, nz - 1)], a2_sem.at[0])
    picked[...] = recv2[...].reshape(number, 128).T
    digit = iota((16, 128), 0)
    left, right = [], []
    for r in range(SLOTS):
        number_r = picked[r:r + 1, :].astype(jnp.int32) - 1
        high = (number_r >> 4) == digit
        right.append(jnp.where((number_r & 15) == digit, 1.0, 0.0).astype(BF16))
        left.append(jnp.concatenate(
            [jnp.where(high, picked[SLOTS * (q + 1) + r:SLOTS * (q + 1) + r + 1, :], 0.0).astype(BF16) for q in range(6)], axis=0))
    bins = dot_nt(jnp.concatenate(left, axis=1), jnp.concatenate(right, axis=1))
    bins = bins[0:48] + bins[48:96]
    wide = jnp.where((iota((16, 256), 1) & 15) == iota((16, 256), 0), 1.0, 0.0).astype(BF16)
    bins = sum(dot(part_, wide) for part_ in pieces(bins))
    bins = jnp.where((iota((48, 256), 1) >> 4) == (iota((48, 256), 0) & 15), bins, 0.0)
    bin_sums = [jnp.sum(bins[16 * k:16 * k + 16], axis=0, keepdims=True) for k in range(3)]

    wait_all(grecv2.at[pl.ds(1, nz - 1)], g2_sem.at[1])
    wait_all(grecv2.at[pl.ds(1, nz - 1)], g2_sem.at[0])
    own = gsend2[...]
    for delta in range(1, nz):
        own = own + grecv2[delta]
    for shift in (4, 2, 1):
        own = own + pltpu.roll(own, shift, axis=1)
    own = jnp.broadcast_to(own, (8, 128))
    splat = {}
    for e, (l, k) in enumerate(pairs):
        splat[l, k] = jnp.broadcast_to(own[:, 8 * e + 7:8 * e + 8], (8, 128))
    coeffs = solve([[splat[min(a, b), max(a, b)] for b in range(4)] for a in range(4)])

    sens = None
    for k in range(3):
        term = bin_sums[k] * jnp.concatenate([coeffs[k][0:1]] * (per_owner // 128), axis=1)
        sens = term if sens is None else sens + term
    sens_ref[...] = sens

    full = [jnp.concatenate([jnp.concatenate([c, c], axis=1)] * 4, axis=0) for c in coeffs]

    @functools.partial(each, VARS)
    def _(j):
        for x in range(8):
            nxt[j, x] = full[0] * basis[0, j, x] + full[1] * basis[1, j, x] + full[2] * basis[2, j, x]
        pltpu.make_async_copy(nxt.at[j], adj_hbm.at[j], out_sem).start()

    wait_all(nxt, out_sem)


def local(right_side, speeds, porosity, coupling, momentum, design_ids):
    ny = lax.axis_size("gy")
    nz = lax.axis_size("gz")
    _, nx, cy, cz = right_side.shape
    per_owner = design_ids.size // 4
    field = (VARS, nx, cy, cz)
    dma = pltpu.SemaphoreType.DMA
    hbm = pl.BlockSpec(memory_space=pltpu.HBM)
    vmem = pl.BlockSpec(memory_space=pltpu.VMEM)
    adjoint, sensitivity = pl.pallas_call(
        functools.partial(kernel, ny, nz, per_owner),
        out_shape=[jax.ShapeDtypeStruct(field, F32), jax.ShapeDtypeStruct((1, per_owner), F32)],
        in_specs=[hbm, hbm, hbm, pl.BlockSpec(memory_space=pltpu.SMEM), hbm, vmem],
        out_specs=[hbm, vmem],
        scratch_shapes=[
            pltpu.VMEM((3,) + field, F32), pltpu.VMEM(field, F32), pltpu.VMEM(field, F32),
            pltpu.VMEM((3, nx, cy, cz), F32),
            pltpu.VMEM((nx, cy, cz), F32),
            pltpu.VMEM((3, nx, cy, cz), F32),
            pltpu.VMEM((240, 240), BF16),
            pltpu.VMEM((128, 128), F32),
            pltpu.VMEM((3 * VARS, cy, cz), F32), pltpu.VMEM((3 * VARS, cy, cz), F32),
            pltpu.VMEM((3, nx, cy, cz), F32), pltpu.VMEM((3, nx, cy, cz), F32),
            pltpu.VMEM((VARS, cy, cz), F32), pltpu.VMEM((VARS, cy, cz), F32),
            pltpu.VMEM((VARS, 2, 40, 128), F32), pltpu.VMEM((VARS, 2, 40, 128), F32),
            pltpu.VMEM((32, 128), F32),
            pltpu.VMEM((2, 192, 128), F32), pltpu.VMEM((2, 224, 128), F32), pltpu.VMEM((192, 128), F32),
            pltpu.VMEM((3, 2, cy, cz), F32),
            pltpu.VMEM((6, 8, 128), F32),
            pltpu.VMEM((ny * nz, 1024), BF16),
            pltpu.VMEM((SLOTS, 1024), F32),
            pltpu.VMEM((8, 128), F32),
            pltpu.VMEM((8, 128), F32),
            pltpu.VMEM((128, 1024), BF16),
            pltpu.VMEM((ny, nz, 128), F32),
            pltpu.VMEM((ny, nz, 128), F32),
            pltpu.VMEM((nz, ny, 128), F32),
            pltpu.VMEM((nz, ny, 128), F32),
            pltpu.VMEM((128, 128), F32),
            pltpu.VMEM((1, 128), F32),
            pltpu.VMEM((ny, 1, 128), F32),
            pltpu.VMEM((1, 128), F32),
            pltpu.VMEM((nz, 1, 128), F32),
            dma((4,)), dma, dma((2, 4)), dma((2, 4)), dma((2,)), dma((2,)), dma((2,)), dma((2,)),
        ],
        compiler_params=pltpu.CompilerParams(
            collective_id=0, has_side_effects=True, vmem_limit_bytes=62 * 1024 * 1024),
    )(right_side, speeds, porosity, coupling.transpose(1, 0, 2), momentum, design_ids)
    return adjoint, sensitivity.reshape(per_owner)


def solution(mesh):
    in_specs = (
        P(None, None, "gy", "gz"),
        P(None, None, "gy", "gz"),
        P(None, "gy", "gz"),
        P(),
        P(None, None, "gy", "gz"),
        P(None, "gy", "gz"),
    )
    out_specs = (P(None, None, "gy", "gz"), P(("gy", "gz")))
    return jax.shard_map(local, mesh=mesh, in_specs=in_specs, out_specs=out_specs, check_vma=False)
```

```python
import functools

import jax
import jax.numpy as jnp
from jax import lax
from jax.experimental import pallas as pl
from jax.experimental.pallas import tpu as pltpu
from jax.sharding import PartitionSpec as P

PENALTY = 1.0
COURANT = 0.3
VARS = 5
SLOTS = 16
MESH = pl.DeviceIdType.MESH
F32 = jnp.float32
BF16 = jnp.bfloat16


def pieces(value):
    high = value.astype(BF16)
    rest = value - high.astype(F32)
    mid = rest.astype(BF16)
    low = (rest - mid.astype(F32)).astype(BF16)
    return high, mid, low


def dot(a, b):
    return jnp.dot(a, b, preferred_element_type=F32)


def dot_nt(a, b):
    return lax.dot_general(a, b, (((1,), (1,)), ((), ())), preferred_element_type=F32)


def iota(shape, axis):
    return lax.broadcasted_iota(jnp.int32, shape, axis)


def fold(product):
    rows = product[0:8] + product[8:16] + product[16:24] + product[24:32]
    return rows[:, 0:128] + rows[:, 128:256]


def solve(gram):
    low = [[None] * 4 for _ in range(4)]
    for col in range(4):
        diag = gram[col][col]
        for inner in range(col):
            diag = diag - low[col][inner] * low[col][inner]
        low[col][col] = jnp.sqrt(diag)
        for row in range(col + 1, 4):
            value = gram[row][col]
            for inner in range(col):
                value = value - low[row][inner] * low[col][inner]
            low[row][col] = value / low[col][col]
    zero = jnp.zeros_like(gram[0][0])
    upper = [[low[c][r] if c >= r else None for c in range(4)] for r in range(4)]

    def add(a, b):
        return b if a is None else (a if b is None else a + b)

    hess = [[add(upper[r][c + 1], upper[r][c]) for c in range(3)] for r in range(4)]

    def inner_sum(terms):
        total = None
        for a, b in terms:
            if a is not None and b is not None:
                total = add(total, a * b)
        return zero if total is None else total

    normal = [[inner_sum([(hess[r][a], hess[r][b]) for r in range(4)]) for b in range(3)] for a in range(3)]
    target = [inner_sum([(hess[r][a], upper[r][0]) for r in range(4)]) for a in range(3)]
    fac = [[None] * 3 for _ in range(3)]
    for col in range(3):
        diag = normal[col][col]
        for inner in range(col):
            diag = diag - fac[col][inner] * fac[col][inner]
        fac[col][col] = jnp.sqrt(diag)
        for row in range(col + 1, 3):
            value = normal[row][col]
            for inner in range(col):
                value = value - fac[row][inner] * fac[col][inner]
            fac[row][col] = value / fac[col][col]
    forward = []
    for place in range(3):
        value = target[place]
        for inner in range(place):
            value = value - fac[place][inner] * forward[inner]
        forward.append(value / fac[place][place])
    backward = [None] * 3
    for place in reversed(range(3)):
        value = forward[place]
        for inner in range(place + 1, 3):
            value = value - fac[inner][place] * backward[inner]
        backward[place] = value / fac[place][place]
    return backward


def kernel(ny, nz, per_owner,
           rs_hbm, sp_hbm, po_hbm, cp_hbm, mo_hbm, ids_hbm,
           adj_hbm, sens_hbm,
           basis, cur, nxt, sp, po, mo, wmat, wz, wa, wb, cpos, cneg, part, fprev, low_shift, high_shift, sface,
           halo_out, halo_in, yfix, zfix, ypart, zpart, yheld, zheld, corner, turn, block, prods, cp, ids_ref, sens_ref,
           owner_hot, rank_hot, owner_row, local_row, spread, dsend, recv1, turned, recv2, picked,
           gsend, grecv1, gsend2, grecv2,
           in_sem, out_sem, sens_sem, halo_send, halo_recv, a1_sem, a2_sem, g1_sem, g2_sem):
    gy = lax.axis_index("gy")
    gz = lax.axis_index("gz")

    number = ny * nz

    def gy_at(delta):
        return lax.rem(gy + (delta + ny), ny)

    def gz_at(delta):
        return lax.rem(gz + (delta + nz), nz)

    def each(count, step, start=0):
        def body(t, carry):
            step(t)
            return carry
        lax.fori_loop(start, count, body, 0)

    barrier = pltpu.get_barrier_semaphore()

    def greet(target):
        pl.semaphore_signal(barrier, inc=1, device_id=target, device_id_type=MESH)

    for delta in (1, -1):
        greet({"gz": gz_at(delta)})
        greet({"gy": gy_at(delta)})

    @functools.partial(each, ny - 1, start=2)
    def _(delta):
        greet({"gy": gy_at(delta)})

    @functools.partial(each, nz - 1, start=2)
    def _(delta):
        greet({"gz": gz_at(delta)})

    loads = [pltpu.make_async_copy(src, dst, in_sem.at[place]) for place, (src, dst) in enumerate(
        [(sp_hbm, sp), (rs_hbm, nxt), (po_hbm, po), (mo_hbm, mo), (cp_hbm, cp), (ids_hbm, ids_ref)])]
    for place in (4, 0, 1, 5, 2, 3):
        loads[place].start()

    loads[4].wait()
    lane = iota((8, 128), 1)
    row = iota((8, 128), 0)
    wz[40:128, :] = jnp.zeros((88, 128), F32)

    @functools.partial(each, VARS)
    def _(i):
        value = jnp.zeros((8, 128), F32)
        for j in range(VARS):
            value = jnp.where((lane >> 3) == j, -COURANT * cp[i, 2, j], value)
        wz[pl.ds(pl.multiple_of(8 * i, 8), 8), :] = jnp.where((lane & 7) == row, value, 0.0)

    loads[0].wait()

    lanes = iota((32, 128), 1)
    near = jnp.zeros((32, 128), F32)
    far = jnp.zeros((32, 128), F32)
    for x in range(8):
        ends = pltpu.roll(jnp.where(lanes == 0, sp[2, x, :, 0:128], sp[2, x, :, 128:256]), x + 1, axis=1)
        near = jnp.where(lanes == x + 1, ends, near)
        far = jnp.where(lanes == x, ends, far)
    near = pltpu.roll(near, 127, axis=1)
    for side, face in ((0, jnp.maximum(near, 0.0)), (1, jnp.maximum(-far, 0.0))):
        total = face
        for i in range(1, VARS):
            total = jnp.where((lanes >> 3) == i, pltpu.roll(face, 8 * i, axis=1), total)
        sface[32 * side:32 * side + 32, :] = jnp.where(lanes < 8 * VARS, total, 0.0)

    inside = (gy > 0, gy < ny - 1, gz > 0, gz < nz - 1)

    YROWS = VARS * 16
    ZAT = 2 * YROWS

    def y_at(side, j, half):
        return side * YROWS + j * 16 + half * 8

    def in_rows(place):
        return pl.ds(place * YROWS, YROWS) if place < 2 else pl.ds(ZAT + 32 * (place - 2), 32)

    def send_halo(par):
        for place, (axis, delta) in enumerate((("y", -1), ("y", 1), ("z", -1), ("z", 1))):
            rows = in_rows(place)
            target = {"gy": gy_at(delta)} if axis == "y" else {"gz": gz_at(delta)}
            copy = pltpu.make_async_remote_copy(
                src_ref=halo_out.at[par, rows], dst_ref=halo_in.at[par, in_rows(place ^ 1)],
                send_sem=halo_send.at[par, place], recv_sem=halo_recv.at[par, place ^ 1],
                device_id=target, device_id_type=MESH)
            pl.when(inside[place])(copy.start)

    for place in range(4):
        @pl.when(jnp.logical_not(inside[place]))
        def _():
            for par in range(2):
                halo_in[par, in_rows(place), :] = jnp.zeros((YROWS if place < 2 else 32, 128), F32)

    def wait_all(ref, sem):
        pltpu.make_async_copy(ref, ref, sem).wait()

    halves = (slice(0, 128), slice(128, 256))

    def pack():
        near = jnp.zeros((32, 128), F32)
        far = jnp.zeros((32, 128), F32)
        for i in range(VARS):
            for x in range(8):
                s = i * 8 + x
                ends = jnp.where(lanes == 0, nxt[i, x, :, 0:128], nxt[i, x, :, 128:256])
                ends = pltpu.roll(ends, s + 1, axis=1)
                near = jnp.where(lanes == s + 1, ends, near)
                far = jnp.where(lanes == s, ends, far)
        zpart[0:32, :] = pltpu.roll(near, 127, axis=1)
        zpart[32:64, :] = far
        for side, y in ((0, 0), (1, 31)):
            for half in range(2):
                for i in range(VARS):
                    at = y_at(side, i, half)
                    ypart[at:at + 8, :] = nxt[i, :, y, halves[half]]

    lane8 = iota((8, 128), 1)
    rows32 = iota((32, 128), 0)

    def y_corners():
        for side in range(2):
            for i in range(VARS):
                corner[side * 64 + i * 8:side * 64 + i * 8 + 8, :] = jnp.where(
                    lane8 == 0, yfix[y_at(side, i, 0):y_at(side, i, 0) + 8, :],
                    yfix[y_at(side, i, 1):y_at(side, i, 1) + 8, :])
        turn[...] = corner[...].T
        parts = []
        for at in (0, 127):
            both = jnp.broadcast_to(turn[at:at + 1, :], (32, 128))
            parts.append(jnp.where(rows32 == 0, both, jnp.where(rows32 == 31, pltpu.roll(both, 64, axis=1), 0.0)))
        return jnp.where(jnp.concatenate([lanes, lanes], axis=0) < 8 * VARS, jnp.concatenate(parts, axis=0), 0.0)

    def finish(k, par):
        faces = zpart[...] + zfix[...] + y_corners()
        zheld[k] = faces
        halo_out[par, ZAT:ZAT + 64, :] = jnp.dot(
            faces * sface[...], wz[...], preferred_element_type=F32, precision=lax.Precision.HIGHEST)
        turned_z = jnp.concatenate([zfix[...], jnp.zeros((64, 128), F32)], axis=0).T
        for side, y in ((0, 0), (1, 31)):
            for half in range(2):
                speed = sp[1, :, y, halves[half]]
                speed = jnp.maximum(speed, 0.0) if side == 0 else jnp.maximum(-speed, 0.0)
                flux = []
                for i in range(VARS):
                    extra = turned_z[8 * i:8 * i + 8]
                    shift = ((0, 95), (97, 64))[side][half]
                    extra = pltpu.roll(extra, shift, axis=1) if shift else extra
                    at = y_at(side, i, half)
                    value = ypart[at:at + 8, :] + yfix[at:at + 8, :] + jnp.where(lane8 == 127 * half, extra, 0.0)
                    yheld[k, at:at + 8, :] = value
                    flux.append(value * speed)
                for j in range(VARS):
                    total = flux[0] * (-COURANT * cp[0, 1, j])
                    for i in range(1, VARS):
                        total = total + flux[i] * (-COURANT * cp[i, 1, j])
                    at = y_at(side, j, half)
                    halo_out[par, at:at + 8, :] = total

    def settle(k):
        @functools.partial(each, VARS)
        def _(i):
            for x in range(8):
                for side, y in ((0, 0), (1, 31)):
                    for half in range(2):
                        at = pl.ds(side * YROWS + i * 16 + half * 8 + x, 1)
                        nxt[i, x, y:y + 1, halves[half]] = nxt[i, x, y:y + 1, halves[half]] + yfix[at, :]
            for x in range(8):
                near = nxt[i, x, :, 0:128] + jnp.where(
                    lanes == 0, pltpu.roll(zfix[0:32, :], 128 - 8 * i - x, axis=1), 0.0)
                far = nxt[i, x, :, 128:256] + jnp.where(
                    lanes == 127, pltpu.roll(zfix[32:64, :], 127 - 8 * i - x, axis=1), 0.0)
                cur[i, x, :, 0:128] = near
                cur[i, x, :, 128:256] = far
                basis[k, i, x, :, 0:128] = near
                basis[k, i, x, :, 128:256] = far

    def receive(par):
        for place in range(4):
            @pl.when(inside[place])
            def _():
                ref = halo_in.at[par, in_rows(place)]
                wait_all(ref, halo_recv.at[par, place])
                wait_all(ref, halo_send.at[par, place])
        yfix[0:YROWS, :] = halo_in[par, 0:YROWS, :] - halo_out[par, YROWS:ZAT, :]
        yfix[YROWS:ZAT, :] = halo_in[par, YROWS:ZAT, :] - halo_out[par, 0:YROWS, :]
        zfix[0:32, :] = halo_in[par, ZAT:ZAT + 32, :] - halo_out[par, ZAT + 32:ZAT + 64, :]
        zfix[32:64, :] = halo_in[par, ZAT + 32:ZAT + 64, :] - halo_out[par, ZAT:ZAT + 32, :]

    def prepare():
        @functools.partial(each, 8)
        def _(x):
            for d in range(3):
                s = sp[d, x]
                cpos[d, x] = jnp.maximum(s, 0.0)
                cneg[d, x] = jnp.maximum(-s, 0.0)

        lane = iota((16, 256), 1)
        row = iota((16, 256), 0)
        group = lane >> 4
        piece = jnp.where(group >= 10, 2, jnp.where(group >= 5, 1, 0))
        which = group - 5 * piece
        same = (lane & 15) == row

        @functools.partial(each, 3 * VARS)
        def _(place):
            d = lax.div(place, VARS)
            j = place - d * VARS
            value = jnp.zeros((16, 256), F32)
            for i in range(VARS):
                value = jnp.where(which == i, COURANT * cp[i, d, j], value)
            high = value.astype(BF16).astype(F32)
            value = jnp.where(same, jnp.where(piece == 2, value - high, high), 0.0)
            wmat[pl.ds(pl.multiple_of(place * 16, 16), 16), :] = value[:, 0:240].astype(BF16)

        loads[5].wait()
        ids = jnp.concatenate([ids_ref[0], ids_ref[1]], axis=1)
        owners = lax.div(ids, per_owner)
        local_row[...] = (ids - owners * per_owner + 1).astype(F32)
        tri = jnp.where(iota((256, 128), 0) < jnp.where(iota((256, 128), 0) >= 128, 256, iota((256, 128), 1)), 1.0, 0.0).astype(BF16)
        sub = iota((number, 128), 0)
        before = jnp.zeros((number, 128), F32)
        for p in range(8):
            hot = jnp.where(sub == owners[p:p + 1, :], 1.0, 0.0)
            hot16 = hot.astype(BF16)
            count = dot(jnp.concatenate([hot16, before.astype(BF16)], axis=1), tri)
            before = before + hot
            owner_hot[:, p * 128:(p + 1) * 128] = hot16
            rank = jnp.sum(hot * count, axis=0, keepdims=True)
            rank_hot[:, p * 128:(p + 1) * 128] = jnp.where(rank == iota((SLOTS, 128), 0).astype(F32), 1.0, 0.0)


    def couple(x, w):
        for h in (0, 16):
            high, low = [], []
            for i in range(VARS):
                v = cur[i, x, h:h + 16, :]
                top = v.astype(BF16)
                high.append(top)
                low.append((v - top.astype(F32)).astype(BF16))
            out = dot(wmat[...], jnp.concatenate(high + low + high, axis=0))
            for place in range(3 * VARS):
                w[place, h:h + 16, :] = out[place * 16:place * 16 + 16]

    def stencil(x, w):
        prior = jnp.maximum(x - 1, 0)
        for j in range(VARS):
            wx = w[j]
            flux = cpos[0, x] * wx - fprev[j]
            nxt[j, prior] = part[j] - flux
            fprev[j] = cneg[0, x] * wx
            acc = po[x] * cur[j, x] + flux
            wv = w[2 * VARS + j]
            flux = cpos[2, x] * wv - pltpu.roll(cneg[2, x] * wv, 1, axis=1)
            acc = acc + flux - pltpu.roll(flux, 255, axis=1)
            for half in range(2):
                at = halves[half]
                wy = w[VARS + j, :, at]
                minus = cneg[1, x, :, at] * wy
                low_shift[j, half, 8:40, :] = minus
                low_shift[j, half, 0:8, :] = minus[24:32]
                flux = cpos[1, x, :, at] * wy - low_shift[j, half, 7:39, :]
                high_shift[j, half, 0:32, :] = flux
                high_shift[j, half, 32:40, :] = flux[0:8]
                part[j, :, at] = acc[:, at] + flux - high_shift[j, half, 1:33, :]

    def sweep():
        fprev[...] = jnp.zeros(fprev.shape, F32)
        couple(0, wa)

        @functools.partial(each, 4)
        def _(t):
            x = 2 * t
            couple(x + 1, wb)
            stencil(x, wa)
            couple(jnp.minimum(x + 2, 7), wa)
            stencil(x + 1, wb)

        for j in range(VARS):
            nxt[j, 7] = part[j] + fprev[j]

    def dispatch():
        loads[3].wait()

        @functools.partial(each, 2)
        def _(half_x):
            for k in range(3):
                total = None
                for x in range(4):
                    for i in range(3):
                        term = basis[k, 1 + i, 4 * half_x + x] * mo[i, 4 * half_x + x]
                        total = term if total is None else total + term
                block[k, half_x] = total

        low8 = iota((16, 192), 0)
        col = iota((16, 192), 1)
        within = jnp.where(col >= 96, col - 96, col) & 31
        half = jnp.where(col >= 96, 1, 0)
        ysel = jnp.where((low8 >> 3 == half) & ((low8 & 7) == (within >> 2)), 1.0, 0.0).astype(BF16)
        zrow = iota((512, 128), 0)
        zsel = jnp.where(((zrow & 255) >> 2) + (zrow >> 8) * 64 == iota((512, 128), 1), 1.0, 0.0).astype(BF16)
        parts = []
        for k in range(3):
            t = dot(ysel, jnp.concatenate(list(pieces(block[k, 0])) + list(pieces(block[k, 1])), axis=0))
            for part_ in pieces(jnp.concatenate([t[0:8], t[8:16]], axis=1)):
                parts.append(part_.astype(F32))
        t = dot(jnp.concatenate(parts, axis=0).astype(BF16), zsel)
        values = [-PENALTY * (t[24 * k:24 * k + 8] + t[24 * k + 8:24 * k + 16] + t[24 * k + 16:24 * k + 24])
                  for k in range(3)]
        tops = [value.astype(BF16).astype(F32) for value in values]
        rests = [value - top for value, top in zip(values, tops)]
        empty = jnp.zeros((SLOTS, 128), BF16)
        for p in range(8):
            hot = rank_hot[:, p * 128:(p + 1) * 128]
            rows = [local_row[...]] + tops + rests
            rows = [(hot * value[p:p + 1, :]).astype(BF16) for value in rows]
            spread[:, p * 128:(p + 1) * 128] = jnp.concatenate(rows + [empty], axis=0)
        dsend[...] = dot_nt(owner_hot[...], spread[...]).reshape(ny, nz, 128)

        @functools.partial(each, ny, start=1)
        def _(delta):
            pltpu.make_async_remote_copy(
                src_ref=dsend.at[gy_at(delta)], dst_ref=recv1.at[delta],
                send_sem=a1_sem.at[0], recv_sem=a1_sem.at[1],
                device_id={"gy": gy_at(delta)}, device_id_type=MESH).start()
        recv1[0] = dsend[gy]

    pairs = [(l, k) for k in range(4) for l in range(k + 1)]

    def products(entries, vectors):
        def body(x, sums):
            sums = list(sums)
            for j in range(VARS):
                v = [nxt[j, x] if k == 3 else basis[k, j, x] for k in range(vectors)]
                for place, e in enumerate(entries):
                    l, k = pairs[e]
                    sums[place] = sums[place] + fold(v[l] * v[k])
            return tuple(sums)

        sums = lax.fori_loop(0, 8, body, tuple(jnp.zeros((8, 128), F32) for _ in entries))
        for place, e in enumerate(entries):
            prods[e] = sums[place]

    def corrections():
        sums = [jnp.zeros((8, 128), F32) for _ in range(4)]
        for at in range(0, 2 * YROWS, 8):
            add = yfix[at:at + 8, :]
            for l in range(3):
                sums[l] = sums[l] + yheld[l, at:at + 8, :] * add
            sums[3] = sums[3] + (2.0 * ypart[at:at + 8, :] + add) * add
        both = y_corners()
        for at in range(0, 64, 8):
            add = zfix[at:at + 8, :]
            for l in range(3):
                sums[l] = sums[l] + zheld[l, at:at + 8, :] * add
            sums[3] = sums[3] + (2.0 * (zpart[at:at + 8, :] + both[at:at + 8]) + add) * add
        for l in range(4):
            prods[6 + l] = prods[6 + l] + sums[l]

    yfix[...] = jnp.zeros(yfix.shape, F32)
    zfix[...] = jnp.zeros(zfix.shape, F32)
    corner[...] = jnp.zeros(corner.shape, F32)
    loads[1].wait()

    @functools.partial(each, 4)
    def _(k):
        par = k & 1
        pack()

        @pl.when(k == 3)
        def _():
            products((6, 7, 8, 9), 4)

        @pl.when(k > 0)
        def _():
            receive(1 - par)

        @pl.when(k == 3)
        def _():
            corrections()

        @pl.when(k < 3)
        def _():
            finish(k, par)

            @pl.when(k == 0)
            def _():
                pl.semaphore_wait(barrier, (ny - 1) + (nz - 1))

            send_halo(par)
            settle(k)

            @pl.when(k == 0)
            def _():
                prepare()
                loads[2].wait()

            @pl.when(k == 1)
            def _():
                products((0, 1, 2), 2)

            @pl.when(k == 2)
            def _():
                dispatch()
                products((3, 4, 5), 3)

            sweep()

    sums = [prods[e] for e in range(10)]

    lane = iota((8, 128), 1)
    packed = jnp.zeros((8, 128), F32)
    for e, value in enumerate(sums):
        for shift in (64, 32, 16, 8):
            value = value + pltpu.roll(value, shift, axis=1)
        packed = jnp.where((lane >> 3) == e, value, packed)
    gsend[...] = jnp.sum(packed, axis=0, keepdims=True)

    @functools.partial(each, ny, start=1)
    def _(delta):
        pltpu.make_async_remote_copy(
            src_ref=gsend, dst_ref=grecv1.at[delta], send_sem=g1_sem.at[0], recv_sem=g1_sem.at[1],
            device_id={"gy": gy_at(delta)}, device_id_type=MESH).start()

    wait_all(recv1.at[pl.ds(1, ny - 1)], a1_sem.at[1])
    wait_all(recv1.at[pl.ds(1, ny - 1)], a1_sem.at[0])
    for g in range(nz):
        turned[g] = recv1[:, g, :]

    @functools.partial(each, nz, start=1)
    def _(delta):
        pltpu.make_async_remote_copy(
            src_ref=turned.at[gz_at(delta)], dst_ref=recv2.at[delta], send_sem=a2_sem.at[0], recv_sem=a2_sem.at[1],
            device_id={"gz": gz_at(delta)}, device_id_type=MESH).start()
    recv2[0] = turned[gz]

    wait_all(grecv1.at[pl.ds(1, ny - 1)], g1_sem.at[1])
    wait_all(grecv1.at[pl.ds(1, ny - 1)], g1_sem.at[0])
    own = gsend[...]
    for delta in range(1, ny):
        own = own + grecv1[delta]
    gsend2[...] = own

    @functools.partial(each, nz, start=1)
    def _(delta):
        pltpu.make_async_remote_copy(
            src_ref=gsend2, dst_ref=grecv2.at[delta], send_sem=g2_sem.at[0], recv_sem=g2_sem.at[1],
            device_id={"gz": gz_at(delta)}, device_id_type=MESH).start()

    wait_all(recv2.at[pl.ds(1, nz - 1)], a2_sem.at[1])
    wait_all(recv2.at[pl.ds(1, nz - 1)], a2_sem.at[0])
    picked[...] = recv2[...].reshape(number, 128).T
    digit = iota((16, 128), 0)
    left, right = [], []
    for r in range(SLOTS):
        number_r = picked[r:r + 1, :].astype(jnp.int32) - 1
        high = (number_r >> 4) == digit
        right.append(jnp.where((number_r & 15) == digit, 1.0, 0.0).astype(BF16))
        left.append(jnp.concatenate(
            [jnp.where(high, picked[SLOTS * (q + 1) + r:SLOTS * (q + 1) + r + 1, :], 0.0).astype(BF16) for q in range(6)], axis=0))
    bins = dot_nt(jnp.concatenate(left, axis=1), jnp.concatenate(right, axis=1))
    bins = bins[0:48] + bins[48:96]
    wide = jnp.where((iota((16, 256), 1) & 15) == iota((16, 256), 0), 1.0, 0.0).astype(BF16)
    bins = sum(dot(part_, wide) for part_ in pieces(bins))
    bins = jnp.where((iota((48, 256), 1) >> 4) == (iota((48, 256), 0) & 15), bins, 0.0)
    bin_sums = [jnp.sum(bins[16 * k:16 * k + 16], axis=0, keepdims=True) for k in range(3)]

    wait_all(grecv2.at[pl.ds(1, nz - 1)], g2_sem.at[1])
    wait_all(grecv2.at[pl.ds(1, nz - 1)], g2_sem.at[0])
    own = gsend2[...]
    for delta in range(1, nz):
        own = own + grecv2[delta]
    for shift in (4, 2, 1):
        own = own + pltpu.roll(own, shift, axis=1)
    own = jnp.broadcast_to(own, (8, 128))
    splat = {}
    for e, (l, k) in enumerate(pairs):
        splat[l, k] = jnp.broadcast_to(own[:, 8 * e + 7:8 * e + 8], (8, 128))
    coeffs = solve([[splat[min(a, b), max(a, b)] for b in range(4)] for a in range(4)])

    sens = None
    for k in range(3):
        term = bin_sums[k] * jnp.concatenate([coeffs[k][0:1]] * (per_owner // 128), axis=1)
        sens = term if sens is None else sens + term
    sens_ref[...] = sens
    sens_copy = pltpu.make_async_copy(sens_ref, sens_hbm, sens_sem)
    sens_copy.start()

    full = [jnp.concatenate([jnp.concatenate([c, c], axis=1)] * 4, axis=0) for c in coeffs]

    @functools.partial(each, VARS)
    def _(j):
        for x in range(8):
            nxt[j, x] = full[0] * basis[0, j, x] + full[1] * basis[1, j, x] + full[2] * basis[2, j, x]
        pltpu.make_async_copy(nxt.at[j], adj_hbm.at[j], out_sem).start()

    wait_all(nxt, out_sem)
    sens_copy.wait()


def local(right_side, speeds, porosity, coupling, momentum, design_ids):
    ny = lax.axis_size("gy")
    nz = lax.axis_size("gz")
    _, nx, cy, cz = right_side.shape
    per_owner = design_ids.size // 4
    field = (VARS, nx, cy, cz)
    dma = pltpu.SemaphoreType.DMA
    hbm = pl.BlockSpec(memory_space=pltpu.HBM)
    adjoint, sensitivity = pl.pallas_call(
        functools.partial(kernel, ny, nz, per_owner),
        out_shape=[jax.ShapeDtypeStruct(field, F32), jax.ShapeDtypeStruct((1, per_owner), F32)],
        in_specs=[hbm] * 6,
        out_specs=[hbm, hbm],
        scratch_shapes=[
            pltpu.VMEM((3,) + field, F32), pltpu.VMEM(field, F32), pltpu.VMEM(field, F32),
            pltpu.VMEM((3, nx, cy, cz), F32),
            pltpu.VMEM((nx, cy, cz), F32),
            pltpu.VMEM((3, nx, cy, cz), F32),
            pltpu.VMEM((240, 240), BF16),
            pltpu.VMEM((128, 128), F32),
            pltpu.VMEM((3 * VARS, cy, cz), F32), pltpu.VMEM((3 * VARS, cy, cz), F32),
            pltpu.VMEM((3, nx, cy, cz), F32), pltpu.VMEM((3, nx, cy, cz), F32),
            pltpu.VMEM((VARS, cy, cz), F32), pltpu.VMEM((VARS, cy, cz), F32),
            pltpu.VMEM((VARS, 2, 40, 128), F32), pltpu.VMEM((VARS, 2, 40, 128), F32),
            pltpu.VMEM((64, 128), F32),
            pltpu.VMEM((2, 224, 128), F32), pltpu.VMEM((2, 224, 128), F32), pltpu.VMEM((160, 128), F32), pltpu.VMEM((64, 128), F32),
            pltpu.VMEM((160, 128), F32), pltpu.VMEM((64, 128), F32), pltpu.VMEM((3, 160, 128), F32), pltpu.VMEM((3, 64, 128), F32),
            pltpu.VMEM((128, 128), F32), pltpu.VMEM((128, 128), F32),
            pltpu.VMEM((3, 2, cy, cz), F32),
            pltpu.VMEM((10, 8, 128), F32),
            pltpu.SMEM((VARS, 3, VARS), F32),
            pltpu.VMEM(design_ids.shape, jnp.int32),
            pltpu.VMEM((1, per_owner), F32),
            pltpu.VMEM((ny * nz, 1024), BF16),
            pltpu.VMEM((SLOTS, 1024), F32),
            pltpu.VMEM((8, 128), F32),
            pltpu.VMEM((8, 128), F32),
            pltpu.VMEM((128, 1024), BF16),
            pltpu.VMEM((ny, nz, 128), F32),
            pltpu.VMEM((ny, nz, 128), F32),
            pltpu.VMEM((nz, ny, 128), F32),
            pltpu.VMEM((nz, ny, 128), F32),
            pltpu.VMEM((128, 128), F32),
            pltpu.VMEM((1, 128), F32),
            pltpu.VMEM((ny, 1, 128), F32),
            pltpu.VMEM((1, 128), F32),
            pltpu.VMEM((nz, 1, 128), F32),
            dma((6,)), dma, dma, dma((2, 4)), dma((2, 4)), dma((2,)), dma((2,)), dma((2,)), dma((2,)),
        ],
        compiler_params=pltpu.CompilerParams(
            collective_id=0, has_side_effects=True, vmem_limit_bytes=62 * 1024 * 1024),
    )(right_side, speeds, porosity, coupling.transpose(1, 0, 2), momentum, design_ids)
    return adjoint, sensitivity.reshape(per_owner)


def solution(mesh):
    in_specs = (
        P(None, None, "gy", "gz"),
        P(None, None, "gy", "gz"),
        P(None, "gy", "gz"),
        P(),
        P(None, None, "gy", "gz"),
        P(None, "gy", "gz"),
    )
    out_specs = (P(None, None, "gy", "gz"), P(("gy", "gz")))
    return jax.shard_map(local, mesh=mesh, in_specs=in_specs, out_specs=out_specs, check_vma=False)
```

```python
import functools

import jax
import jax.numpy as jnp
from jax import lax
from jax.experimental import pallas as pl
from jax.experimental.pallas import tpu as pltpu
from jax.sharding import PartitionSpec as P

PENALTY = 1.0
COURANT = 0.3
VARS = 5
SLOTS = 16
MESH = pl.DeviceIdType.MESH
F32 = jnp.float32
BF16 = jnp.bfloat16


def pieces(value):
    high = value.astype(BF16)
    rest = value - high.astype(F32)
    mid = rest.astype(BF16)
    low = (rest - mid.astype(F32)).astype(BF16)
    return high, mid, low


def dot(a, b):
    return jnp.dot(a, b, preferred_element_type=F32)


def dot_nt(a, b):
    return lax.dot_general(a, b, (((1,), (1,)), ((), ())), preferred_element_type=F32)


def iota(shape, axis):
    return lax.broadcasted_iota(jnp.int32, shape, axis)


def fold(product):
    rows = product[0:8] + product[8:16] + product[16:24] + product[24:32]
    return rows[:, 0:128] + rows[:, 128:256]


def solve(gram):
    low = [[None] * 4 for _ in range(4)]
    for col in range(4):
        diag = gram[col][col]
        for inner in range(col):
            diag = diag - low[col][inner] * low[col][inner]
        low[col][col] = jnp.sqrt(diag)
        for row in range(col + 1, 4):
            value = gram[row][col]
            for inner in range(col):
                value = value - low[row][inner] * low[col][inner]
            low[row][col] = value / low[col][col]
    zero = jnp.zeros_like(gram[0][0])
    upper = [[low[c][r] if c >= r else None for c in range(4)] for r in range(4)]

    def add(a, b):
        return b if a is None else (a if b is None else a + b)

    hess = [[add(upper[r][c + 1], upper[r][c]) for c in range(3)] for r in range(4)]

    def inner_sum(terms):
        total = None
        for a, b in terms:
            if a is not None and b is not None:
                total = add(total, a * b)
        return zero if total is None else total

    normal = [[inner_sum([(hess[r][a], hess[r][b]) for r in range(4)]) for b in range(3)] for a in range(3)]
    target = [inner_sum([(hess[r][a], upper[r][0]) for r in range(4)]) for a in range(3)]
    fac = [[None] * 3 for _ in range(3)]
    for col in range(3):
        diag = normal[col][col]
        for inner in range(col):
            diag = diag - fac[col][inner] * fac[col][inner]
        fac[col][col] = jnp.sqrt(diag)
        for row in range(col + 1, 3):
            value = normal[row][col]
            for inner in range(col):
                value = value - fac[row][inner] * fac[col][inner]
            fac[row][col] = value / fac[col][col]
    forward = []
    for place in range(3):
        value = target[place]
        for inner in range(place):
            value = value - fac[place][inner] * forward[inner]
        forward.append(value / fac[place][place])
    backward = [None] * 3
    for place in reversed(range(3)):
        value = forward[place]
        for inner in range(place + 1, 3):
            value = value - fac[inner][place] * backward[inner]
        backward[place] = value / fac[place][place]
    return backward


def kernel(ny, nz, per_owner,
           rs_hbm, sp_hbm, po_hbm, cp_hbm, mo_hbm, ids_hbm,
           held_hbm, small_hbm,
           basis, cur, nxt, sp, po, mo, wmat, wz, wa, wb, cpos, cneg, part, fprev, low_shift, high_shift, sface,
           halo_out, halo_in, yfix, zfix, ypart, zpart, yheld, zheld, corner, turn, block, prods, cp, ids_ref, small,
           owner_hot, rank_hot, owner_row, local_row, spread, dsend, recv1, turned, recv2, picked,
           gsend, grecv1, gsend2, grecv2,
           in_sem, out_sem, small_sem, halo_send, halo_recv, a1_sem, a2_sem, g1_sem, g2_sem):
    gy = lax.axis_index("gy")
    gz = lax.axis_index("gz")

    number = ny * nz

    def gy_at(delta):
        return lax.rem(gy + (delta + ny), ny)

    def gz_at(delta):
        return lax.rem(gz + (delta + nz), nz)

    def each(count, step, start=0):
        def body(t, carry):
            step(t)
            return carry
        lax.fori_loop(start, count, body, 0)

    barrier = pltpu.get_barrier_semaphore()

    def greet(target):
        pl.semaphore_signal(barrier, inc=1, device_id=target, device_id_type=MESH)

    for delta in (1, -1):
        greet({"gz": gz_at(delta)})
        greet({"gy": gy_at(delta)})

    @functools.partial(each, ny - 1, start=2)
    def _(delta):
        greet({"gy": gy_at(delta)})

    @functools.partial(each, nz - 1, start=2)
    def _(delta):
        greet({"gz": gz_at(delta)})

    loads = [pltpu.make_async_copy(src, dst, in_sem.at[place]) for place, (src, dst) in enumerate(
        [(sp_hbm, sp), (rs_hbm, nxt), (po_hbm, po), (mo_hbm, mo), (cp_hbm, cp), (ids_hbm, ids_ref)])]
    for place in (4, 0, 1, 5, 2, 3):
        loads[place].start()

    loads[4].wait()
    lane = iota((8, 128), 1)
    row = iota((8, 128), 0)
    wz[40:128, :] = jnp.zeros((88, 128), F32)

    @functools.partial(each, VARS)
    def _(i):
        value = jnp.zeros((8, 128), F32)
        for j in range(VARS):
            value = jnp.where((lane >> 3) == j, -COURANT * cp[i, 2, j], value)
        wz[pl.ds(pl.multiple_of(8 * i, 8), 8), :] = jnp.where((lane & 7) == row, value, 0.0)

    loads[0].wait()

    lanes = iota((32, 128), 1)
    near = jnp.zeros((32, 128), F32)
    far = jnp.zeros((32, 128), F32)
    for x in range(8):
        ends = pltpu.roll(jnp.where(lanes == 0, sp[2, x, :, 0:128], sp[2, x, :, 128:256]), x + 1, axis=1)
        near = jnp.where(lanes == x + 1, ends, near)
        far = jnp.where(lanes == x, ends, far)
    near = pltpu.roll(near, 127, axis=1)
    for side, face in ((0, jnp.maximum(near, 0.0)), (1, jnp.maximum(-far, 0.0))):
        total = face
        for i in range(1, VARS):
            total = jnp.where((lanes >> 3) == i, pltpu.roll(face, 8 * i, axis=1), total)
        sface[32 * side:32 * side + 32, :] = jnp.where(lanes < 8 * VARS, total, 0.0)

    inside = (gy > 0, gy < ny - 1, gz > 0, gz < nz - 1)

    YROWS = VARS * 16
    ZAT = 2 * YROWS

    def y_at(side, j, half):
        return side * YROWS + j * 16 + half * 8

    def in_rows(place):
        return pl.ds(place * YROWS, YROWS) if place < 2 else pl.ds(ZAT + 32 * (place - 2), 32)

    def send_halo(par):
        for place, (axis, delta) in enumerate((("y", -1), ("y", 1), ("z", -1), ("z", 1))):
            rows = in_rows(place)
            target = {"gy": gy_at(delta)} if axis == "y" else {"gz": gz_at(delta)}
            copy = pltpu.make_async_remote_copy(
                src_ref=halo_out.at[par, rows], dst_ref=halo_in.at[par, in_rows(place ^ 1)],
                send_sem=halo_send.at[par, place], recv_sem=halo_recv.at[par, place ^ 1],
                device_id=target, device_id_type=MESH)
            pl.when(inside[place])(copy.start)

    for place in range(4):
        @pl.when(jnp.logical_not(inside[place]))
        def _():
            for par in range(2):
                halo_in[par, in_rows(place), :] = jnp.zeros((YROWS if place < 2 else 32, 128), F32)

    def wait_all(ref, sem):
        pltpu.make_async_copy(ref, ref, sem).wait()

    halves = (slice(0, 128), slice(128, 256))

    def pack():
        near = jnp.zeros((32, 128), F32)
        far = jnp.zeros((32, 128), F32)
        for i in range(VARS):
            for x in range(8):
                s = i * 8 + x
                ends = jnp.where(lanes == 0, nxt[i, x, :, 0:128], nxt[i, x, :, 128:256])
                ends = pltpu.roll(ends, s + 1, axis=1)
                near = jnp.where(lanes == s + 1, ends, near)
                far = jnp.where(lanes == s, ends, far)
        zpart[0:32, :] = pltpu.roll(near, 127, axis=1)
        zpart[32:64, :] = far
        for side, y in ((0, 0), (1, 31)):
            for half in range(2):
                for i in range(VARS):
                    at = y_at(side, i, half)
                    ypart[at:at + 8, :] = nxt[i, :, y, halves[half]]

    lane8 = iota((8, 128), 1)
    rows32 = iota((32, 128), 0)

    def y_corners():
        for side in range(2):
            for i in range(VARS):
                corner[side * 64 + i * 8:side * 64 + i * 8 + 8, :] = jnp.where(
                    lane8 == 0, yfix[y_at(side, i, 0):y_at(side, i, 0) + 8, :],
                    yfix[y_at(side, i, 1):y_at(side, i, 1) + 8, :])
        turn[...] = corner[...].T
        parts = []
        for at in (0, 127):
            both = jnp.broadcast_to(turn[at:at + 1, :], (32, 128))
            parts.append(jnp.where(rows32 == 0, both, jnp.where(rows32 == 31, pltpu.roll(both, 64, axis=1), 0.0)))
        return jnp.where(jnp.concatenate([lanes, lanes], axis=0) < 8 * VARS, jnp.concatenate(parts, axis=0), 0.0)

    def finish(k, par):
        faces = zpart[...] + zfix[...] + y_corners()
        zheld[k] = faces
        halo_out[par, ZAT:ZAT + 64, :] = jnp.dot(
            faces * sface[...], wz[...], preferred_element_type=F32, precision=lax.Precision.HIGHEST)
        turned_z = jnp.concatenate([zfix[...], jnp.zeros((64, 128), F32)], axis=0).T
        for side, y in ((0, 0), (1, 31)):
            for half in range(2):
                speed = sp[1, :, y, halves[half]]
                speed = jnp.maximum(speed, 0.0) if side == 0 else jnp.maximum(-speed, 0.0)
                flux = []
                for i in range(VARS):
                    extra = turned_z[8 * i:8 * i + 8]
                    shift = ((0, 95), (97, 64))[side][half]
                    extra = pltpu.roll(extra, shift, axis=1) if shift else extra
                    at = y_at(side, i, half)
                    value = ypart[at:at + 8, :] + yfix[at:at + 8, :] + jnp.where(lane8 == 127 * half, extra, 0.0)
                    yheld[k, at:at + 8, :] = value
                    flux.append(value * speed)
                for j in range(VARS):
                    total = flux[0] * (-COURANT * cp[0, 1, j])
                    for i in range(1, VARS):
                        total = total + flux[i] * (-COURANT * cp[i, 1, j])
                    at = y_at(side, j, half)
                    halo_out[par, at:at + 8, :] = total

    def settle(k):
        @functools.partial(each, VARS)
        def _(i):
            for x in range(8):
                for side, y in ((0, 0), (1, 31)):
                    for half in range(2):
                        at = pl.ds(side * YROWS + i * 16 + half * 8 + x, 1)
                        nxt[i, x, y:y + 1, halves[half]] = nxt[i, x, y:y + 1, halves[half]] + yfix[at, :]
            for x in range(8):
                near = nxt[i, x, :, 0:128] + jnp.where(
                    lanes == 0, pltpu.roll(zfix[0:32, :], 128 - 8 * i - x, axis=1), 0.0)
                far = nxt[i, x, :, 128:256] + jnp.where(
                    lanes == 127, pltpu.roll(zfix[32:64, :], 127 - 8 * i - x, axis=1), 0.0)
                cur[i, x, :, 0:128] = near
                cur[i, x, :, 128:256] = far
                basis[k, i, x, :, 0:128] = near
                basis[k, i, x, :, 128:256] = far

    def receive(par):
        for place in range(4):
            @pl.when(inside[place])
            def _():
                ref = halo_in.at[par, in_rows(place)]
                wait_all(ref, halo_recv.at[par, place])
                wait_all(ref, halo_send.at[par, place])
        yfix[0:YROWS, :] = halo_in[par, 0:YROWS, :] - halo_out[par, YROWS:ZAT, :]
        yfix[YROWS:ZAT, :] = halo_in[par, YROWS:ZAT, :] - halo_out[par, 0:YROWS, :]
        zfix[0:32, :] = halo_in[par, ZAT:ZAT + 32, :] - halo_out[par, ZAT + 32:ZAT + 64, :]
        zfix[32:64, :] = halo_in[par, ZAT + 32:ZAT + 64, :] - halo_out[par, ZAT:ZAT + 32, :]

    def prepare():
        @functools.partial(each, 8)
        def _(x):
            for d in range(3):
                s = sp[d, x]
                cpos[d, x] = jnp.maximum(s, 0.0)
                cneg[d, x] = jnp.maximum(-s, 0.0)

        lane = iota((16, 256), 1)
        row = iota((16, 256), 0)
        group = lane >> 4
        piece = jnp.where(group >= 10, 2, jnp.where(group >= 5, 1, 0))
        which = group - 5 * piece
        same = (lane & 15) == row

        @functools.partial(each, 3 * VARS)
        def _(place):
            d = lax.div(place, VARS)
            j = place - d * VARS
            value = jnp.zeros((16, 256), F32)
            for i in range(VARS):
                value = jnp.where(which == i, COURANT * cp[i, d, j], value)
            high = value.astype(BF16).astype(F32)
            value = jnp.where(same, jnp.where(piece == 2, value - high, high), 0.0)
            wmat[pl.ds(pl.multiple_of(place * 16, 16), 16), :] = value[:, 0:240].astype(BF16)

        loads[5].wait()
        ids = jnp.concatenate([ids_ref[0], ids_ref[1]], axis=1)
        owners = lax.div(ids, per_owner)
        local_row[...] = (ids - owners * per_owner + 1).astype(F32)
        tri = jnp.where(iota((256, 128), 0) < jnp.where(iota((256, 128), 0) >= 128, 256, iota((256, 128), 1)), 1.0, 0.0).astype(BF16)
        sub = iota((number, 128), 0)
        before = jnp.zeros((number, 128), F32)
        for p in range(8):
            hot = jnp.where(sub == owners[p:p + 1, :], 1.0, 0.0)
            hot16 = hot.astype(BF16)
            count = dot(jnp.concatenate([hot16, before.astype(BF16)], axis=1), tri)
            before = before + hot
            owner_hot[:, p * 128:(p + 1) * 128] = hot16
            rank = jnp.sum(hot * count, axis=0, keepdims=True)
            rank_hot[:, p * 128:(p + 1) * 128] = jnp.where(rank == iota((SLOTS, 128), 0).astype(F32), 1.0, 0.0)


    def couple(x, w):
        for h in (0, 16):
            high, low = [], []
            for i in range(VARS):
                v = cur[i, x, h:h + 16, :]
                top = v.astype(BF16)
                high.append(top)
                low.append((v - top.astype(F32)).astype(BF16))
            out = dot(wmat[...], jnp.concatenate(high + low + high, axis=0))
            for place in range(3 * VARS):
                w[place, h:h + 16, :] = out[place * 16:place * 16 + 16]

    def stencil(x, w):
        prior = jnp.maximum(x - 1, 0)
        for j in range(VARS):
            wx = w[j]
            flux = cpos[0, x] * wx - fprev[j]
            nxt[j, prior] = part[j] - flux
            fprev[j] = cneg[0, x] * wx
            acc = po[x] * cur[j, x] + flux
            wv = w[2 * VARS + j]
            flux = cpos[2, x] * wv - pltpu.roll(cneg[2, x] * wv, 1, axis=1)
            acc = acc + flux - pltpu.roll(flux, 255, axis=1)
            for half in range(2):
                at = halves[half]
                wy = w[VARS + j, :, at]
                minus = cneg[1, x, :, at] * wy
                low_shift[j, half, 8:40, :] = minus
                low_shift[j, half, 0:8, :] = minus[24:32]
                flux = cpos[1, x, :, at] * wy - low_shift[j, half, 7:39, :]
                high_shift[j, half, 0:32, :] = flux
                high_shift[j, half, 32:40, :] = flux[0:8]
                part[j, :, at] = acc[:, at] + flux - high_shift[j, half, 1:33, :]

    def sweep():
        fprev[...] = jnp.zeros(fprev.shape, F32)
        couple(0, wa)

        @functools.partial(each, 4)
        def _(t):
            x = 2 * t
            couple(x + 1, wb)
            stencil(x, wa)
            couple(jnp.minimum(x + 2, 7), wa)
            stencil(x + 1, wb)

        for j in range(VARS):
            nxt[j, 7] = part[j] + fprev[j]

    def dispatch():
        loads[3].wait()

        @functools.partial(each, 2)
        def _(half_x):
            for k in range(3):
                total = None
                for x in range(4):
                    for i in range(3):
                        term = basis[k, 1 + i, 4 * half_x + x] * mo[i, 4 * half_x + x]
                        total = term if total is None else total + term
                block[k, half_x] = total

        low8 = iota((16, 192), 0)
        col = iota((16, 192), 1)
        within = jnp.where(col >= 96, col - 96, col) & 31
        half = jnp.where(col >= 96, 1, 0)
        ysel = jnp.where((low8 >> 3 == half) & ((low8 & 7) == (within >> 2)), 1.0, 0.0).astype(BF16)
        zrow = iota((512, 128), 0)
        zsel = jnp.where(((zrow & 255) >> 2) + (zrow >> 8) * 64 == iota((512, 128), 1), 1.0, 0.0).astype(BF16)
        parts = []
        for k in range(3):
            t = dot(ysel, jnp.concatenate(list(pieces(block[k, 0])) + list(pieces(block[k, 1])), axis=0))
            for part_ in pieces(jnp.concatenate([t[0:8], t[8:16]], axis=1)):
                parts.append(part_.astype(F32))
        t = dot(jnp.concatenate(parts, axis=0).astype(BF16), zsel)
        values = [-PENALTY * (t[24 * k:24 * k + 8] + t[24 * k + 8:24 * k + 16] + t[24 * k + 16:24 * k + 24])
                  for k in range(3)]
        tops = [value.astype(BF16).astype(F32) for value in values]
        rests = [value - top for value, top in zip(values, tops)]
        empty = jnp.zeros((SLOTS, 128), BF16)
        for p in range(8):
            hot = rank_hot[:, p * 128:(p + 1) * 128]
            rows = [local_row[...]] + tops + rests
            rows = [(hot * value[p:p + 1, :]).astype(BF16) for value in rows]
            spread[:, p * 128:(p + 1) * 128] = jnp.concatenate(rows + [empty], axis=0)
        dsend[...] = dot_nt(owner_hot[...], spread[...]).reshape(ny, nz, 128)

        @functools.partial(each, ny, start=1)
        def _(delta):
            pltpu.make_async_remote_copy(
                src_ref=dsend.at[gy_at(delta)], dst_ref=recv1.at[delta],
                send_sem=a1_sem.at[0], recv_sem=a1_sem.at[1],
                device_id={"gy": gy_at(delta)}, device_id_type=MESH).start()
        recv1[0] = dsend[gy]

    pairs = [(l, k) for k in range(4) for l in range(k + 1)]

    def products(entries, vectors):
        def body(x, sums):
            sums = list(sums)
            for j in range(VARS):
                v = [nxt[j, x] if k == 3 else basis[k, j, x] for k in range(vectors)]
                for place, e in enumerate(entries):
                    l, k = pairs[e]
                    sums[place] = sums[place] + fold(v[l] * v[k])
            return tuple(sums)

        sums = lax.fori_loop(0, 8, body, tuple(jnp.zeros((8, 128), F32) for _ in entries))
        for place, e in enumerate(entries):
            prods[e] = sums[place]

    def corrections():
        sums = [jnp.zeros((8, 128), F32) for _ in range(4)]
        for at in range(0, 2 * YROWS, 8):
            add = yfix[at:at + 8, :]
            for l in range(3):
                sums[l] = sums[l] + yheld[l, at:at + 8, :] * add
            sums[3] = sums[3] + (2.0 * ypart[at:at + 8, :] + add) * add
        both = y_corners()
        for at in range(0, 64, 8):
            add = zfix[at:at + 8, :]
            for l in range(3):
                sums[l] = sums[l] + zheld[l, at:at + 8, :] * add
            sums[3] = sums[3] + (2.0 * (zpart[at:at + 8, :] + both[at:at + 8]) + add) * add
        for l in range(4):
            prods[6 + l] = prods[6 + l] + sums[l]

    yfix[...] = jnp.zeros(yfix.shape, F32)
    zfix[...] = jnp.zeros(zfix.shape, F32)
    corner[...] = jnp.zeros(corner.shape, F32)
    loads[1].wait()

    @functools.partial(each, 4)
    def _(k):
        par = k & 1
        pack()

        @pl.when(k == 3)
        def _():
            products((6, 7, 8, 9), 4)

        @pl.when(k > 0)
        def _():
            receive(1 - par)

        @pl.when(k == 3)
        def _():
            corrections()

        @pl.when(k < 3)
        def _():
            finish(k, par)

            @pl.when(k == 0)
            def _():
                pl.semaphore_wait(barrier, (ny - 1) + (nz - 1))

            send_halo(par)
            settle(k)

            @pl.when(k > 0)
            def _():
                pltpu.make_async_copy(basis.at[k], held_hbm.at[k - 1], out_sem).start()

            @pl.when(k == 0)
            def _():
                prepare()
                loads[2].wait()

            @pl.when(k == 1)
            def _():
                products((0, 1, 2), 2)

            @pl.when(k == 2)
            def _():
                dispatch()
                products((3, 4, 5), 3)

            sweep()

    sums = [prods[e] for e in range(10)]

    lane = iota((8, 128), 1)
    packed = jnp.zeros((8, 128), F32)
    for e, value in enumerate(sums):
        for shift in (64, 32, 16, 8):
            value = value + pltpu.roll(value, shift, axis=1)
        packed = jnp.where((lane >> 3) == e, value, packed)
    gsend[...] = jnp.sum(packed, axis=0, keepdims=True)

    @functools.partial(each, ny, start=1)
    def _(delta):
        pltpu.make_async_remote_copy(
            src_ref=gsend, dst_ref=grecv1.at[delta], send_sem=g1_sem.at[0], recv_sem=g1_sem.at[1],
            device_id={"gy": gy_at(delta)}, device_id_type=MESH).start()

    wait_all(recv1.at[pl.ds(1, ny - 1)], a1_sem.at[1])
    wait_all(recv1.at[pl.ds(1, ny - 1)], a1_sem.at[0])
    for g in range(nz):
        turned[g] = recv1[:, g, :]

    @functools.partial(each, nz, start=1)
    def _(delta):
        pltpu.make_async_remote_copy(
            src_ref=turned.at[gz_at(delta)], dst_ref=recv2.at[delta], send_sem=a2_sem.at[0], recv_sem=a2_sem.at[1],
            device_id={"gz": gz_at(delta)}, device_id_type=MESH).start()
    recv2[0] = turned[gz]

    wait_all(grecv1.at[pl.ds(1, ny - 1)], g1_sem.at[1])
    wait_all(grecv1.at[pl.ds(1, ny - 1)], g1_sem.at[0])
    own = gsend[...]
    for delta in range(1, ny):
        own = own + grecv1[delta]
    gsend2[...] = own

    @functools.partial(each, nz, start=1)
    def _(delta):
        pltpu.make_async_remote_copy(
            src_ref=gsend2, dst_ref=grecv2.at[delta], send_sem=g2_sem.at[0], recv_sem=g2_sem.at[1],
            device_id={"gz": gz_at(delta)}, device_id_type=MESH).start()

    wait_all(recv2.at[pl.ds(1, nz - 1)], a2_sem.at[1])
    wait_all(recv2.at[pl.ds(1, nz - 1)], a2_sem.at[0])
    picked[...] = recv2[...].reshape(number, 128).T
    digit = iota((16, 128), 0)
    left, right = [], []
    for r in range(SLOTS):
        number_r = picked[r:r + 1, :].astype(jnp.int32) - 1
        high = (number_r >> 4) == digit
        right.append(jnp.where((number_r & 15) == digit, 1.0, 0.0).astype(BF16))
        left.append(jnp.concatenate(
            [jnp.where(high, picked[SLOTS * (q + 1) + r:SLOTS * (q + 1) + r + 1, :], 0.0).astype(BF16) for q in range(6)], axis=0))
    bins = dot_nt(jnp.concatenate(left, axis=1), jnp.concatenate(right, axis=1))
    bins = bins[0:48] + bins[48:96]
    wide = jnp.where((iota((16, 256), 1) & 15) == iota((16, 256), 0), 1.0, 0.0).astype(BF16)
    bins = sum(dot(part_, wide) for part_ in pieces(bins))
    bins = jnp.where((iota((48, 256), 1) >> 4) == (iota((48, 256), 0) & 15), bins, 0.0)
    bin_sums = [jnp.sum(bins[16 * k:16 * k + 16], axis=0, keepdims=True) for k in range(3)]

    wait_all(grecv2.at[pl.ds(1, nz - 1)], g2_sem.at[1])
    wait_all(grecv2.at[pl.ds(1, nz - 1)], g2_sem.at[0])
    own = gsend2[...]
    for delta in range(1, nz):
        own = own + grecv2[delta]
    for shift in (4, 2, 1):
        own = own + pltpu.roll(own, shift, axis=1)
    own = jnp.broadcast_to(own, (8, 128))
    splat = {}
    for e, (l, k) in enumerate(pairs):
        splat[l, k] = jnp.broadcast_to(own[:, 8 * e + 7:8 * e + 8], (8, 128))
    coeffs = solve([[splat[min(a, b), max(a, b)] for b in range(4)] for a in range(4)])

    sens = None
    for k in range(3):
        term = bin_sums[k] * jnp.concatenate([coeffs[k][0:1]] * (per_owner // 128), axis=1)
        sens = term if sens is None else sens + term
    small[0:1, :] = sens
    for k in range(3):
        small[8 + 8 * k:16 + 8 * k, :] = jnp.concatenate([coeffs[k]] * (per_owner // 128), axis=1)
    copy = pltpu.make_async_copy(small, small_hbm, small_sem)
    copy.start()
    wait_all(basis.at[pl.ds(1, 2)], out_sem)
    copy.wait()


def combine(rs_hbm, held_hbm, small_hbm, adj_hbm, sens_hbm, vectors, result, small, load_sem, small_sem, out_sem, sens_sem):
    get_small = pltpu.make_async_copy(small_hbm, small, small_sem)
    get_small.start()
    for j in range(VARS):
        pltpu.make_async_copy(rs_hbm.at[j], vectors.at[j, 0], load_sem.at[j]).start()
        for k in range(2):
            pltpu.make_async_copy(held_hbm.at[k, j], vectors.at[j, 1 + k], load_sem.at[j]).start()
    get_small.wait()
    put_sens = pltpu.make_async_copy(small.at[0:1], sens_hbm, sens_sem)
    put_sens.start()
    full = [jnp.concatenate([small[8 + 8 * k:16 + 8 * k, :]] * 4, axis=0) for k in range(3)]

    def body(j, carry):
        pltpu.make_async_copy(vectors.at[j], vectors.at[j], load_sem.at[j]).wait()
        for x in range(8):
            result[j, x] = full[0] * vectors[j, 0, x] + full[1] * vectors[j, 1, x] + full[2] * vectors[j, 2, x]
        pltpu.make_async_copy(result.at[j], adj_hbm.at[j], out_sem).start()
        return carry

    lax.fori_loop(0, VARS, body, 0)
    pltpu.make_async_copy(result, result, out_sem).wait()
    put_sens.wait()


def local(right_side, speeds, porosity, coupling, momentum, design_ids):
    ny = lax.axis_size("gy")
    nz = lax.axis_size("gz")
    _, nx, cy, cz = right_side.shape
    per_owner = design_ids.size // 4
    field = (VARS, nx, cy, cz)
    dma = pltpu.SemaphoreType.DMA
    hbm = pl.BlockSpec(memory_space=pltpu.HBM)
    held, small = pl.pallas_call(
        functools.partial(kernel, ny, nz, per_owner),
        out_shape=[jax.ShapeDtypeStruct((2,) + field, F32), jax.ShapeDtypeStruct((32, per_owner), F32)],
        in_specs=[hbm] * 6,
        out_specs=[hbm, hbm],
        scratch_shapes=[
            pltpu.VMEM((3,) + field, F32), pltpu.VMEM(field, F32), pltpu.VMEM(field, F32),
            pltpu.VMEM((3, nx, cy, cz), F32),
            pltpu.VMEM((nx, cy, cz), F32),
            pltpu.VMEM((3, nx, cy, cz), F32),
            pltpu.VMEM((240, 240), BF16),
            pltpu.VMEM((128, 128), F32),
            pltpu.VMEM((3 * VARS, cy, cz), F32), pltpu.VMEM((3 * VARS, cy, cz), F32),
            pltpu.VMEM((3, nx, cy, cz), F32), pltpu.VMEM((3, nx, cy, cz), F32),
            pltpu.VMEM((VARS, cy, cz), F32), pltpu.VMEM((VARS, cy, cz), F32),
            pltpu.VMEM((VARS, 2, 40, 128), F32), pltpu.VMEM((VARS, 2, 40, 128), F32),
            pltpu.VMEM((64, 128), F32),
            pltpu.VMEM((2, 224, 128), F32), pltpu.VMEM((2, 224, 128), F32), pltpu.VMEM((160, 128), F32), pltpu.VMEM((64, 128), F32),
            pltpu.VMEM((160, 128), F32), pltpu.VMEM((64, 128), F32), pltpu.VMEM((3, 160, 128), F32), pltpu.VMEM((3, 64, 128), F32),
            pltpu.VMEM((128, 128), F32), pltpu.VMEM((128, 128), F32),
            pltpu.VMEM((3, 2, cy, cz), F32),
            pltpu.VMEM((10, 8, 128), F32),
            pltpu.SMEM((VARS, 3, VARS), F32),
            pltpu.VMEM(design_ids.shape, jnp.int32),
            pltpu.VMEM((32, per_owner), F32),
            pltpu.VMEM((ny * nz, 1024), BF16),
            pltpu.VMEM((SLOTS, 1024), F32),
            pltpu.VMEM((8, 128), F32),
            pltpu.VMEM((8, 128), F32),
            pltpu.VMEM((128, 1024), BF16),
            pltpu.VMEM((ny, nz, 128), F32),
            pltpu.VMEM((ny, nz, 128), F32),
            pltpu.VMEM((nz, ny, 128), F32),
            pltpu.VMEM((nz, ny, 128), F32),
            pltpu.VMEM((128, 128), F32),
            pltpu.VMEM((1, 128), F32),
            pltpu.VMEM((ny, 1, 128), F32),
            pltpu.VMEM((1, 128), F32),
            pltpu.VMEM((nz, 1, 128), F32),
            dma((6,)), dma, dma, dma((2, 4)), dma((2, 4)), dma((2,)), dma((2,)), dma((2,)), dma((2,)),
        ],
        compiler_params=pltpu.CompilerParams(
            collective_id=0, has_side_effects=True, vmem_limit_bytes=62 * 1024 * 1024),
    )(right_side, speeds, porosity, coupling.transpose(1, 0, 2), momentum, design_ids)
    adjoint, sensitivity = pl.pallas_call(
        combine,
        out_shape=[jax.ShapeDtypeStruct(field, F32), jax.ShapeDtypeStruct((1, per_owner), F32)],
        in_specs=[hbm] * 3,
        out_specs=[hbm, hbm],
        scratch_shapes=[
            pltpu.VMEM((VARS, 3, nx, cy, cz), F32), pltpu.VMEM(field, F32), pltpu.VMEM((32, per_owner), F32),
            dma((VARS,)), dma, dma, dma,
        ],
        compiler_params=pltpu.CompilerParams(vmem_limit_bytes=62 * 1024 * 1024),
    )(right_side, held, small)
    return adjoint, sensitivity.reshape(per_owner)


def solution(mesh):
    in_specs = (
        P(None, None, "gy", "gz"),
        P(None, None, "gy", "gz"),
        P(None, "gy", "gz"),
        P(),
        P(None, None, "gy", "gz"),
        P(None, "gy", "gz"),
    )
    out_specs = (P(None, None, "gy", "gz"), P(("gy", "gz")))
    return jax.shard_map(local, mesh=mesh, in_specs=in_specs, out_specs=out_specs, check_vma=False)
```

```python
import functools

import jax
import jax.numpy as jnp
from jax import lax
from jax.experimental import pallas as pl
from jax.experimental.pallas import tpu as pltpu
from jax.sharding import PartitionSpec as P

PENALTY = 1.0
COURANT = 0.3
VARS = 5
SLOTS = 16
MESH = pl.DeviceIdType.MESH
F32 = jnp.float32
BF16 = jnp.bfloat16


def pieces(value):
    high = value.astype(BF16)
    rest = value - high.astype(F32)
    mid = rest.astype(BF16)
    low = (rest - mid.astype(F32)).astype(BF16)
    return high, mid, low


def dot(a, b):
    return jnp.dot(a, b, preferred_element_type=F32)


def dot_nt(a, b):
    return lax.dot_general(a, b, (((1,), (1,)), ((), ())), preferred_element_type=F32)


def iota(shape, axis):
    return lax.broadcasted_iota(jnp.int32, shape, axis)


def fold(product):
    rows = product[0:8] + product[8:16] + product[16:24] + product[24:32]
    return rows[:, 0:128] + rows[:, 128:256]


def solve(gram):
    low = [[None] * 4 for _ in range(4)]
    for col in range(4):
        diag = gram[col][col]
        for inner in range(col):
            diag = diag - low[col][inner] * low[col][inner]
        low[col][col] = jnp.sqrt(diag)
        for row in range(col + 1, 4):
            value = gram[row][col]
            for inner in range(col):
                value = value - low[row][inner] * low[col][inner]
            low[row][col] = value / low[col][col]
    zero = jnp.zeros_like(gram[0][0])
    upper = [[low[c][r] if c >= r else None for c in range(4)] for r in range(4)]

    def add(a, b):
        return b if a is None else (a if b is None else a + b)

    hess = [[add(upper[r][c + 1], upper[r][c]) for c in range(3)] for r in range(4)]

    def inner_sum(terms):
        total = None
        for a, b in terms:
            if a is not None and b is not None:
                total = add(total, a * b)
        return zero if total is None else total

    normal = [[inner_sum([(hess[r][a], hess[r][b]) for r in range(4)]) for b in range(3)] for a in range(3)]
    target = [inner_sum([(hess[r][a], upper[r][0]) for r in range(4)]) for a in range(3)]
    fac = [[None] * 3 for _ in range(3)]
    for col in range(3):
        diag = normal[col][col]
        for inner in range(col):
            diag = diag - fac[col][inner] * fac[col][inner]
        fac[col][col] = jnp.sqrt(diag)
        for row in range(col + 1, 3):
            value = normal[row][col]
            for inner in range(col):
                value = value - fac[row][inner] * fac[col][inner]
            fac[row][col] = value / fac[col][col]
    forward = []
    for place in range(3):
        value = target[place]
        for inner in range(place):
            value = value - fac[place][inner] * forward[inner]
        forward.append(value / fac[place][place])
    backward = [None] * 3
    for place in reversed(range(3)):
        value = forward[place]
        for inner in range(place + 1, 3):
            value = value - fac[inner][place] * backward[inner]
        backward[place] = value / fac[place][place]
    return backward


def kernel(ny, nz, per_owner,
           rs_hbm, sp_hbm, po_hbm, cp_hbm, mo_hbm, ids_hbm,
           held_hbm, small_hbm,
           basis, cur, nxt, sp, po, mo, wmat, wz, wa, wb, cpos, cneg, part, fprev, low_shift, high_shift, sface,
           halo_out, halo_in, yfix, zfix, ypart, zpart, yheld, zheld, corner, turn, block, prods, cp, ids_ref, small,
           owner_hot, rank_hot, owner_row, local_row, spread, dsend, recv1, turned, recv2, picked,
           gsend, grecv1, gsend2, grecv2,
           in_sem, out_sem, small_sem, halo_send, halo_recv, a1_sem, a2_sem, g1_sem, g2_sem):
    gy = lax.axis_index("gy")
    gz = lax.axis_index("gz")

    number = ny * nz

    def gy_at(delta):
        return lax.rem(gy + (delta + ny), ny)

    def gz_at(delta):
        return lax.rem(gz + (delta + nz), nz)

    def each(count, step, start=0):
        def body(t, carry):
            step(t)
            return carry
        lax.fori_loop(start, count, body, 0)

    barrier = pltpu.get_barrier_semaphore()

    def greet(target):
        pl.semaphore_signal(barrier, inc=1, device_id=target, device_id_type=MESH)

    for delta in (1, -1):
        greet({"gz": gz_at(delta)})
        greet({"gy": gy_at(delta)})

    @functools.partial(each, ny - 1, start=2)
    def _(delta):
        greet({"gy": gy_at(delta)})

    @functools.partial(each, nz - 1, start=2)
    def _(delta):
        greet({"gz": gz_at(delta)})

    loads = [pltpu.make_async_copy(src, dst, in_sem.at[place]) for place, (src, dst) in enumerate(
        [(sp_hbm, sp), (rs_hbm, nxt), (po_hbm, po), (mo_hbm, mo), (cp_hbm, cp), (ids_hbm, ids_ref)])]
    for place in (4, 0, 1, 5, 2, 3):
        loads[place].start()

    loads[4].wait()
    lane = iota((8, 128), 1)
    row = iota((8, 128), 0)
    wz[40:128, :] = jnp.zeros((88, 128), F32)

    @functools.partial(each, VARS)
    def _(i):
        value = jnp.zeros((8, 128), F32)
        for j in range(VARS):
            value = jnp.where((lane >> 3) == j, -COURANT * cp[i, 2, j], value)
        wz[pl.ds(pl.multiple_of(8 * i, 8), 8), :] = jnp.where((lane & 7) == row, value, 0.0)

    loads[0].wait()

    lanes = iota((32, 128), 1)
    near = jnp.zeros((32, 128), F32)
    far = jnp.zeros((32, 128), F32)
    for x in range(8):
        ends = pltpu.roll(jnp.where(lanes == 0, sp[2, x, :, 0:128], sp[2, x, :, 128:256]), x + 1, axis=1)
        near = jnp.where(lanes == x + 1, ends, near)
        far = jnp.where(lanes == x, ends, far)
    near = pltpu.roll(near, 127, axis=1)
    for side, face in ((0, jnp.maximum(near, 0.0)), (1, jnp.maximum(-far, 0.0))):
        total = face
        for i in range(1, VARS):
            total = jnp.where((lanes >> 3) == i, pltpu.roll(face, 8 * i, axis=1), total)
        sface[32 * side:32 * side + 32, :] = jnp.where(lanes < 8 * VARS, total, 0.0)

    inside = (gy > 0, gy < ny - 1, gz > 0, gz < nz - 1)

    YROWS = VARS * 16
    ZAT = 2 * YROWS

    def y_at(side, j, half):
        return side * YROWS + j * 16 + half * 8

    def in_rows(place):
        return pl.ds(place * YROWS, YROWS) if place < 2 else pl.ds(ZAT + 32 * (place - 2), 32)

    def send_halo(par):
        for place, (axis, delta) in enumerate((("y", -1), ("y", 1), ("z", -1), ("z", 1))):
            rows = in_rows(place)
            target = {"gy": gy_at(delta)} if axis == "y" else {"gz": gz_at(delta)}
            copy = pltpu.make_async_remote_copy(
                src_ref=halo_out.at[par, rows], dst_ref=halo_in.at[par, in_rows(place ^ 1)],
                send_sem=halo_send.at[par, place], recv_sem=halo_recv.at[par, place ^ 1],
                device_id=target, device_id_type=MESH)
            pl.when(inside[place])(copy.start)

    for place in range(4):
        @pl.when(jnp.logical_not(inside[place]))
        def _():
            for par in range(2):
                halo_in[par, in_rows(place), :] = jnp.zeros((YROWS if place < 2 else 32, 128), F32)

    def wait_all(ref, sem):
        pltpu.make_async_copy(ref, ref, sem).wait()

    halves = (slice(0, 128), slice(128, 256))

    def pack():
        near = jnp.zeros((32, 128), F32)
        far = jnp.zeros((32, 128), F32)
        for i in range(VARS):
            for x in range(8):
                s = i * 8 + x
                ends = jnp.where(lanes == 0, nxt[i, x, :, 0:128], nxt[i, x, :, 128:256])
                ends = pltpu.roll(ends, s + 1, axis=1)
                near = jnp.where(lanes == s + 1, ends, near)
                far = jnp.where(lanes == s, ends, far)
        zpart[0:32, :] = pltpu.roll(near, 127, axis=1)
        zpart[32:64, :] = far
        for side, y in ((0, 0), (1, 31)):
            for half in range(2):
                for i in range(VARS):
                    at = y_at(side, i, half)
                    ypart[at:at + 8, :] = nxt[i, :, y, halves[half]]

    lane8 = iota((8, 128), 1)
    rows32 = iota((32, 128), 0)

    def y_corners():
        for side in range(2):
            for i in range(VARS):
                corner[side * 64 + i * 8:side * 64 + i * 8 + 8, :] = jnp.where(
                    lane8 == 0, yfix[y_at(side, i, 0):y_at(side, i, 0) + 8, :],
                    yfix[y_at(side, i, 1):y_at(side, i, 1) + 8, :])
        turn[...] = corner[...].T
        parts = []
        for at in (0, 127):
            both = jnp.broadcast_to(turn[at:at + 1, :], (32, 128))
            parts.append(jnp.where(rows32 == 0, both, jnp.where(rows32 == 31, pltpu.roll(both, 64, axis=1), 0.0)))
        return jnp.where(jnp.concatenate([lanes, lanes], axis=0) < 8 * VARS, jnp.concatenate(parts, axis=0), 0.0)

    def finish(k, par):
        faces = zpart[...] + zfix[...] + y_corners()
        zheld[k] = faces
        halo_out[par, ZAT:ZAT + 64, :] = jnp.dot(
            faces * sface[...], wz[...], preferred_element_type=F32, precision=lax.Precision.HIGHEST)
        turned_z = jnp.concatenate([zfix[...], jnp.zeros((64, 128), F32)], axis=0).T
        for side, y in ((0, 0), (1, 31)):
            for half in range(2):
                speed = sp[1, :, y, halves[half]]
                speed = jnp.maximum(speed, 0.0) if side == 0 else jnp.maximum(-speed, 0.0)
                flux = []
                for i in range(VARS):
                    extra = turned_z[8 * i:8 * i + 8]
                    shift = ((0, 95), (97, 64))[side][half]
                    extra = pltpu.roll(extra, shift, axis=1) if shift else extra
                    at = y_at(side, i, half)
                    value = ypart[at:at + 8, :] + yfix[at:at + 8, :] + jnp.where(lane8 == 127 * half, extra, 0.0)
                    yheld[k, at:at + 8, :] = value
                    flux.append(value * speed)
                for j in range(VARS):
                    total = flux[0] * (-COURANT * cp[0, 1, j])
                    for i in range(1, VARS):
                        total = total + flux[i] * (-COURANT * cp[i, 1, j])
                    at = y_at(side, j, half)
                    halo_out[par, at:at + 8, :] = total

    def settle(k):
        @functools.partial(each, VARS)
        def _(i):
            for x in range(8):
                for side, y in ((0, 0), (1, 31)):
                    for half in range(2):
                        at = pl.ds(side * YROWS + i * 16 + half * 8 + x, 1)
                        nxt[i, x, y:y + 1, halves[half]] = nxt[i, x, y:y + 1, halves[half]] + yfix[at, :]
            for x in range(8):
                near = nxt[i, x, :, 0:128] + jnp.where(
                    lanes == 0, pltpu.roll(zfix[0:32, :], 128 - 8 * i - x, axis=1), 0.0)
                far = nxt[i, x, :, 128:256] + jnp.where(
                    lanes == 127, pltpu.roll(zfix[32:64, :], 127 - 8 * i - x, axis=1), 0.0)
                cur[i, x, :, 0:128] = near
                cur[i, x, :, 128:256] = far
                basis[k, i, x, :, 0:128] = near
                basis[k, i, x, :, 128:256] = far

    def receive(par):
        for place in range(4):
            @pl.when(inside[place])
            def _():
                ref = halo_in.at[par, in_rows(place)]
                wait_all(ref, halo_recv.at[par, place])
                wait_all(ref, halo_send.at[par, place])
        yfix[0:YROWS, :] = halo_in[par, 0:YROWS, :] - halo_out[par, YROWS:ZAT, :]
        yfix[YROWS:ZAT, :] = halo_in[par, YROWS:ZAT, :] - halo_out[par, 0:YROWS, :]
        zfix[0:32, :] = halo_in[par, ZAT:ZAT + 32, :] - halo_out[par, ZAT + 32:ZAT + 64, :]
        zfix[32:64, :] = halo_in[par, ZAT + 32:ZAT + 64, :] - halo_out[par, ZAT:ZAT + 32, :]

    def prepare():
        @functools.partial(each, 8)
        def _(x):
            for d in range(3):
                s = sp[d, x]
                cpos[d, x] = jnp.maximum(s, 0.0)
                cneg[d, x] = jnp.maximum(-s, 0.0)

        lane = iota((16, 256), 1)
        row = iota((16, 256), 0)
        group = lane >> 4
        piece = jnp.where(group >= 10, 2, jnp.where(group >= 5, 1, 0))
        which = group - 5 * piece
        same = (lane & 15) == row

        @functools.partial(each, 3 * VARS)
        def _(place):
            d = lax.div(place, VARS)
            j = place - d * VARS
            value = jnp.zeros((16, 256), F32)
            for i in range(VARS):
                value = jnp.where(which == i, COURANT * cp[i, d, j], value)
            high = value.astype(BF16).astype(F32)
            value = jnp.where(same, jnp.where(piece == 2, value - high, high), 0.0)
            wmat[pl.ds(pl.multiple_of(place * 16, 16), 16), :] = value[:, 0:240].astype(BF16)

        loads[5].wait()
        ids = jnp.concatenate([ids_ref[0], ids_ref[1]], axis=1)
        owners = lax.div(ids, per_owner)
        local_row[...] = (ids - owners * per_owner + 1).astype(F32)
        tri = jnp.where(iota((256, 128), 0) < jnp.where(iota((256, 128), 0) >= 128, 256, iota((256, 128), 1)), 1.0, 0.0).astype(BF16)
        sub = iota((number, 128), 0)
        before = jnp.zeros((number, 128), F32)
        for p in range(8):
            hot = jnp.where(sub == owners[p:p + 1, :], 1.0, 0.0)
            hot16 = hot.astype(BF16)
            count = dot(jnp.concatenate([hot16, before.astype(BF16)], axis=1), tri)
            before = before + hot
            owner_hot[:, p * 128:(p + 1) * 128] = hot16
            rank = jnp.sum(hot * count, axis=0, keepdims=True)
            rank_hot[:, p * 128:(p + 1) * 128] = jnp.where(rank == iota((SLOTS, 128), 0).astype(F32), 1.0, 0.0)


    def couple(x, w):
        for h in (0, 16):
            high, low = [], []
            for i in range(VARS):
                v = cur[i, x, h:h + 16, :]
                top = v.astype(BF16)
                high.append(top)
                low.append((v - top.astype(F32)).astype(BF16))
            out = dot(wmat[...], jnp.concatenate(high + low + high, axis=0))
            for place in range(3 * VARS):
                w[place, h:h + 16, :] = out[place * 16:place * 16 + 16]

    def stencil(x, w):
        prior = jnp.maximum(x - 1, 0)
        for j in range(VARS):
            wx = w[j]
            flux = cpos[0, x] * wx - fprev[j]
            nxt[j, prior] = part[j] - flux
            fprev[j] = cneg[0, x] * wx
            acc = po[x] * cur[j, x] + flux
            wv = w[2 * VARS + j]
            flux = cpos[2, x] * wv - pltpu.roll(cneg[2, x] * wv, 1, axis=1)
            acc = acc + flux - pltpu.roll(flux, 255, axis=1)
            for half in range(2):
                at = halves[half]
                wy = w[VARS + j, :, at]
                minus = cneg[1, x, :, at] * wy
                low_shift[j, half, 8:40, :] = minus
                low_shift[j, half, 0:8, :] = minus[24:32]
                flux = cpos[1, x, :, at] * wy - low_shift[j, half, 7:39, :]
                high_shift[j, half, 0:32, :] = flux
                high_shift[j, half, 32:40, :] = flux[0:8]
                part[j, :, at] = acc[:, at] + flux - high_shift[j, half, 1:33, :]

    def sweep():
        fprev[...] = jnp.zeros(fprev.shape, F32)
        couple(0, wa)

        @functools.partial(each, 4)
        def _(t):
            x = 2 * t
            couple(x + 1, wb)
            stencil(x, wa)
            couple(jnp.minimum(x + 2, 7), wa)
            stencil(x + 1, wb)

        for j in range(VARS):
            nxt[j, 7] = part[j] + fprev[j]

    def dispatch():
        loads[3].wait()

        @functools.partial(each, 2)
        def _(half_x):
            for k in range(3):
                total = None
                for x in range(4):
                    for i in range(3):
                        term = basis[k, 1 + i, 4 * half_x + x] * mo[i, 4 * half_x + x]
                        total = term if total is None else total + term
                block[k, half_x] = total

        low8 = iota((16, 192), 0)
        col = iota((16, 192), 1)
        within = jnp.where(col >= 96, col - 96, col) & 31
        half = jnp.where(col >= 96, 1, 0)
        ysel = jnp.where((low8 >> 3 == half) & ((low8 & 7) == (within >> 2)), 1.0, 0.0).astype(BF16)
        zrow = iota((512, 128), 0)
        zsel = jnp.where(((zrow & 255) >> 2) + (zrow >> 8) * 64 == iota((512, 128), 1), 1.0, 0.0).astype(BF16)
        parts = []
        for k in range(3):
            t = dot(ysel, jnp.concatenate(list(pieces(block[k, 0])) + list(pieces(block[k, 1])), axis=0))
            for part_ in pieces(jnp.concatenate([t[0:8], t[8:16]], axis=1)):
                parts.append(part_.astype(F32))
        t = dot(jnp.concatenate(parts, axis=0).astype(BF16), zsel)
        values = [-PENALTY * (t[24 * k:24 * k + 8] + t[24 * k + 8:24 * k + 16] + t[24 * k + 16:24 * k + 24])
                  for k in range(3)]
        tops = [value.astype(BF16).astype(F32) for value in values]
        rests = [value - top for value, top in zip(values, tops)]
        empty = jnp.zeros((SLOTS, 128), BF16)
        for p in range(8):
            hot = rank_hot[:, p * 128:(p + 1) * 128]
            rows = [local_row[...]] + tops + rests
            rows = [(hot * value[p:p + 1, :]).astype(BF16) for value in rows]
            spread[:, p * 128:(p + 1) * 128] = jnp.concatenate(rows + [empty], axis=0)
        dsend[...] = dot_nt(owner_hot[...], spread[...]).reshape(ny, nz, 128)

        @functools.partial(each, ny, start=1)
        def _(delta):
            pltpu.make_async_remote_copy(
                src_ref=dsend.at[gy_at(delta)], dst_ref=recv1.at[delta],
                send_sem=a1_sem.at[0], recv_sem=a1_sem.at[1],
                device_id={"gy": gy_at(delta)}, device_id_type=MESH).start()
        recv1[0] = dsend[gy]

    pairs = [(l, k) for k in range(4) for l in range(k + 1)]

    def products(entries, vectors):
        def body(x, sums):
            sums = list(sums)
            for j in range(VARS):
                v = [nxt[j, x] if k == 3 else basis[k, j, x] for k in range(vectors)]
                for place, e in enumerate(entries):
                    l, k = pairs[e]
                    sums[place] = sums[place] + fold(v[l] * v[k])
            return tuple(sums)

        sums = lax.fori_loop(0, 8, body, tuple(jnp.zeros((8, 128), F32) for _ in entries))
        for place, e in enumerate(entries):
            prods[e] = sums[place]

    def corrections():
        sums = [jnp.zeros((8, 128), F32) for _ in range(4)]
        for at in range(0, 2 * YROWS, 8):
            add = yfix[at:at + 8, :]
            for l in range(3):
                sums[l] = sums[l] + yheld[l, at:at + 8, :] * add
            sums[3] = sums[3] + (2.0 * ypart[at:at + 8, :] + add) * add
        both = y_corners()
        for at in range(0, 64, 8):
            add = zfix[at:at + 8, :]
            for l in range(3):
                sums[l] = sums[l] + zheld[l, at:at + 8, :] * add
            sums[3] = sums[3] + (2.0 * (zpart[at:at + 8, :] + both[at:at + 8]) + add) * add
        for l in range(4):
            prods[6 + l] = prods[6 + l] + sums[l]

    yfix[...] = jnp.zeros(yfix.shape, F32)
    zfix[...] = jnp.zeros(zfix.shape, F32)
    corner[...] = jnp.zeros(corner.shape, F32)
    loads[1].wait()

    @functools.partial(each, 4)
    def _(k):
        par = k & 1
        pack()

        @pl.when(k == 3)
        def _():
            products((6, 7, 8, 9), 4)

        @pl.when(k > 0)
        def _():
            receive(1 - par)

        @pl.when(k == 3)
        def _():
            corrections()

        @pl.when(k < 3)
        def _():
            finish(k, par)

            @pl.when(k == 0)
            def _():
                pl.semaphore_wait(barrier, (ny - 1) + (nz - 1))

            send_halo(par)
            settle(k)

            @pl.when(k > 0)
            def _():
                pltpu.make_async_copy(basis.at[k], held_hbm.at[k - 1], out_sem).start()

            @pl.when(k == 0)
            def _():
                prepare()
                loads[2].wait()

            @pl.when(k == 1)
            def _():
                products((0, 1, 2), 2)

            @pl.when(k == 2)
            def _():
                dispatch()
                products((3, 4, 5), 3)

            sweep()

    sums = [prods[e] for e in range(10)]

    lane = iota((8, 128), 1)
    packed = jnp.zeros((8, 128), F32)
    for e, value in enumerate(sums):
        for shift in (64, 32, 16, 8):
            value = value + pltpu.roll(value, shift, axis=1)
        packed = jnp.where((lane >> 3) == e, value, packed)
    gsend[...] = jnp.sum(packed, axis=0, keepdims=True)

    @functools.partial(each, ny, start=1)
    def _(delta):
        pltpu.make_async_remote_copy(
            src_ref=gsend, dst_ref=grecv1.at[delta], send_sem=g1_sem.at[0], recv_sem=g1_sem.at[1],
            device_id={"gy": gy_at(delta)}, device_id_type=MESH).start()

    wait_all(recv1.at[pl.ds(1, ny - 1)], a1_sem.at[1])
    wait_all(recv1.at[pl.ds(1, ny - 1)], a1_sem.at[0])
    for g in range(nz):
        turned[g] = recv1[:, g, :]

    @functools.partial(each, nz, start=1)
    def _(delta):
        pltpu.make_async_remote_copy(
            src_ref=turned.at[gz_at(delta)], dst_ref=recv2.at[delta], send_sem=a2_sem.at[0], recv_sem=a2_sem.at[1],
            device_id={"gz": gz_at(delta)}, device_id_type=MESH).start()
    recv2[0] = turned[gz]

    wait_all(grecv1.at[pl.ds(1, ny - 1)], g1_sem.at[1])
    wait_all(grecv1.at[pl.ds(1, ny - 1)], g1_sem.at[0])
    own = gsend[...]
    for delta in range(1, ny):
        own = own + grecv1[delta]
    gsend2[...] = own

    @functools.partial(each, nz, start=1)
    def _(delta):
        pltpu.make_async_remote_copy(
            src_ref=gsend2, dst_ref=grecv2.at[delta], send_sem=g2_sem.at[0], recv_sem=g2_sem.at[1],
            device_id={"gz": gz_at(delta)}, device_id_type=MESH).start()

    wait_all(recv2.at[pl.ds(1, nz - 1)], a2_sem.at[1])
    wait_all(recv2.at[pl.ds(1, nz - 1)], a2_sem.at[0])
    picked[...] = recv2[...].reshape(number, 128).T
    digit = iota((16, 128), 0)
    left, right = [], []
    for r in range(SLOTS):
        number_r = picked[r:r + 1, :].astype(jnp.int32) - 1
        high = (number_r >> 4) == digit
        right.append(jnp.where((number_r & 15) == digit, 1.0, 0.0).astype(BF16))
        left.append(jnp.concatenate(
            [jnp.where(high, picked[SLOTS * (q + 1) + r:SLOTS * (q + 1) + r + 1, :], 0.0).astype(BF16) for q in range(6)], axis=0))
    bins = dot_nt(jnp.concatenate(left, axis=1), jnp.concatenate(right, axis=1))
    bins = bins[0:48] + bins[48:96]
    wide = jnp.where((iota((16, 256), 1) & 15) == iota((16, 256), 0), 1.0, 0.0).astype(BF16)
    bins = sum(dot(part_, wide) for part_ in pieces(bins))
    bins = jnp.where((iota((48, 256), 1) >> 4) == (iota((48, 256), 0) & 15), bins, 0.0)
    bin_sums = [jnp.sum(bins[16 * k:16 * k + 16], axis=0, keepdims=True) for k in range(3)]

    wait_all(grecv2.at[pl.ds(1, nz - 1)], g2_sem.at[1])
    wait_all(grecv2.at[pl.ds(1, nz - 1)], g2_sem.at[0])
    own = gsend2[...]
    for delta in range(1, nz):
        own = own + grecv2[delta]
    for shift in (4, 2, 1):
        own = own + pltpu.roll(own, shift, axis=1)
    own = jnp.broadcast_to(own, (8, 128))
    splat = {}
    for e, (l, k) in enumerate(pairs):
        splat[l, k] = jnp.broadcast_to(own[:, 8 * e + 7:8 * e + 8], (8, 128))
    coeffs = solve([[splat[min(a, b), max(a, b)] for b in range(4)] for a in range(4)])

    sens = None
    for k in range(3):
        term = bin_sums[k] * jnp.concatenate([coeffs[k][0:1]] * (per_owner // 128), axis=1)
        sens = term if sens is None else sens + term
    small[0:1, :] = sens
    for k in range(3):
        small[8 + 8 * k:16 + 8 * k, :] = jnp.concatenate([coeffs[k]] * (per_owner // 128), axis=1)
    copy = pltpu.make_async_copy(small, small_hbm, small_sem)
    copy.start()
    wait_all(basis.at[pl.ds(1, 2)], out_sem)
    copy.wait()


def combine(rs, held, small, adj_hbm, sens_hbm, result, sens, out_sem, sens_sem):
    sens[...] = small[0:1, :]
    put_sens = pltpu.make_async_copy(sens, sens_hbm, sens_sem)
    put_sens.start()
    full = [jnp.concatenate([small[8 + 8 * k:16 + 8 * k, :]] * 4, axis=0) for k in range(3)]

    def body(j, carry):
        for x in range(8):
            result[j, x] = full[0] * rs[j, x] + full[1] * held[0, j, x] + full[2] * held[1, j, x]
        pltpu.make_async_copy(result.at[j], adj_hbm.at[j], out_sem).start()
        return carry

    lax.fori_loop(0, VARS, body, 0)
    pltpu.make_async_copy(result, result, out_sem).wait()
    put_sens.wait()


def local(right_side, speeds, porosity, coupling, momentum, design_ids):
    ny = lax.axis_size("gy")
    nz = lax.axis_size("gz")
    _, nx, cy, cz = right_side.shape
    per_owner = design_ids.size // 4
    field = (VARS, nx, cy, cz)
    dma = pltpu.SemaphoreType.DMA
    hbm = pl.BlockSpec(memory_space=pltpu.HBM)
    held, small = pl.pallas_call(
        functools.partial(kernel, ny, nz, per_owner),
        out_shape=[jax.ShapeDtypeStruct((2,) + field, F32), jax.ShapeDtypeStruct((32, per_owner), F32)],
        in_specs=[hbm] * 6,
        out_specs=[pl.BlockSpec(memory_space=pl.ANY)] * 2,
        scratch_shapes=[
            pltpu.VMEM((3,) + field, F32), pltpu.VMEM(field, F32), pltpu.VMEM(field, F32),
            pltpu.VMEM((3, nx, cy, cz), F32),
            pltpu.VMEM((nx, cy, cz), F32),
            pltpu.VMEM((3, nx, cy, cz), F32),
            pltpu.VMEM((240, 240), BF16),
            pltpu.VMEM((128, 128), F32),
            pltpu.VMEM((3 * VARS, cy, cz), F32), pltpu.VMEM((3 * VARS, cy, cz), F32),
            pltpu.VMEM((3, nx, cy, cz), F32), pltpu.VMEM((3, nx, cy, cz), F32),
            pltpu.VMEM((VARS, cy, cz), F32), pltpu.VMEM((VARS, cy, cz), F32),
            pltpu.VMEM((VARS, 2, 40, 128), F32), pltpu.VMEM((VARS, 2, 40, 128), F32),
            pltpu.VMEM((64, 128), F32),
            pltpu.VMEM((2, 224, 128), F32), pltpu.VMEM((2, 224, 128), F32), pltpu.VMEM((160, 128), F32), pltpu.VMEM((64, 128), F32),
            pltpu.VMEM((160, 128), F32), pltpu.VMEM((64, 128), F32), pltpu.VMEM((3, 160, 128), F32), pltpu.VMEM((3, 64, 128), F32),
            pltpu.VMEM((128, 128), F32), pltpu.VMEM((128, 128), F32),
            pltpu.VMEM((3, 2, cy, cz), F32),
            pltpu.VMEM((10, 8, 128), F32),
            pltpu.SMEM((VARS, 3, VARS), F32),
            pltpu.VMEM(design_ids.shape, jnp.int32),
            pltpu.VMEM((32, per_owner), F32),
            pltpu.VMEM((ny * nz, 1024), BF16),
            pltpu.VMEM((SLOTS, 1024), F32),
            pltpu.VMEM((8, 128), F32),
            pltpu.VMEM((8, 128), F32),
            pltpu.VMEM((128, 1024), BF16),
            pltpu.VMEM((ny, nz, 128), F32),
            pltpu.VMEM((ny, nz, 128), F32),
            pltpu.VMEM((nz, ny, 128), F32),
            pltpu.VMEM((nz, ny, 128), F32),
            pltpu.VMEM((128, 128), F32),
            pltpu.VMEM((1, 128), F32),
            pltpu.VMEM((ny, 1, 128), F32),
            pltpu.VMEM((1, 128), F32),
            pltpu.VMEM((nz, 1, 128), F32),
            dma((6,)), dma, dma, dma((2, 4)), dma((2, 4)), dma((2,)), dma((2,)), dma((2,)), dma((2,)),
        ],
        compiler_params=pltpu.CompilerParams(
            collective_id=0, has_side_effects=True, vmem_limit_bytes=40 * 1024 * 1024),
    )(*[pltpu.with_memory_space_constraint(value, pltpu.HBM) for value in (
        right_side, speeds, porosity, coupling.transpose(1, 0, 2), momentum, design_ids)])
    adjoint, sensitivity = pl.pallas_call(
        combine,
        out_shape=[jax.ShapeDtypeStruct(field, F32), jax.ShapeDtypeStruct((1, per_owner), F32)],
        in_specs=[pl.BlockSpec(memory_space=pltpu.VMEM)] * 3,
        out_specs=[hbm, hbm],
        scratch_shapes=[pltpu.VMEM(field, F32), pltpu.VMEM((1, per_owner), F32), dma, dma],
        compiler_params=pltpu.CompilerParams(vmem_limit_bytes=24 * 1024 * 1024),
    )(right_side, held, small)
    return adjoint, sensitivity.reshape(per_owner)


def solution(mesh):
    in_specs = (
        P(None, None, "gy", "gz"),
        P(None, None, "gy", "gz"),
        P(None, "gy", "gz"),
        P(),
        P(None, None, "gy", "gz"),
        P(None, "gy", "gz"),
    )
    out_specs = (P(None, None, "gy", "gz"), P(("gy", "gz")))
    return jax.shard_map(local, mesh=mesh, in_specs=in_specs, out_specs=out_specs, check_vma=False)
```

```python
import functools

import jax
import jax.numpy as jnp
from jax import lax
from jax.experimental import pallas as pl
from jax.experimental.pallas import tpu as pltpu
from jax.sharding import PartitionSpec as P

PENALTY = 1.0
COURANT = 0.3
VARS = 5
SLOTS = 16
MESH = pl.DeviceIdType.MESH
F32 = jnp.float32
BF16 = jnp.bfloat16


def pieces(value):
    high = value.astype(BF16)
    rest = value - high.astype(F32)
    mid = rest.astype(BF16)
    low = (rest - mid.astype(F32)).astype(BF16)
    return high, mid, low


def dot(a, b):
    return jnp.dot(a, b, preferred_element_type=F32)


def dot_nt(a, b):
    return lax.dot_general(a, b, (((1,), (1,)), ((), ())), preferred_element_type=F32)


def iota(shape, axis):
    return lax.broadcasted_iota(jnp.int32, shape, axis)


def fold(product):
    rows = product[0:8] + product[8:16] + product[16:24] + product[24:32]
    return rows[:, 0:128] + rows[:, 128:256]


def solve(gram):
    low = [[None] * 4 for _ in range(4)]
    for col in range(4):
        diag = gram[col][col]
        for inner in range(col):
            diag = diag - low[col][inner] * low[col][inner]
        low[col][col] = jnp.sqrt(diag)
        for row in range(col + 1, 4):
            value = gram[row][col]
            for inner in range(col):
                value = value - low[row][inner] * low[col][inner]
            low[row][col] = value / low[col][col]
    zero = jnp.zeros_like(gram[0][0])
    upper = [[low[c][r] if c >= r else None for c in range(4)] for r in range(4)]

    def add(a, b):
        return b if a is None else (a if b is None else a + b)

    hess = [[add(upper[r][c + 1], upper[r][c]) for c in range(3)] for r in range(4)]

    def inner_sum(terms):
        total = None
        for a, b in terms:
            if a is not None and b is not None:
                total = add(total, a * b)
        return zero if total is None else total

    normal = [[inner_sum([(hess[r][a], hess[r][b]) for r in range(4)]) for b in range(3)] for a in range(3)]
    target = [inner_sum([(hess[r][a], upper[r][0]) for r in range(4)]) for a in range(3)]
    fac = [[None] * 3 for _ in range(3)]
    for col in range(3):
        diag = normal[col][col]
        for inner in range(col):
            diag = diag - fac[col][inner] * fac[col][inner]
        fac[col][col] = jnp.sqrt(diag)
        for row in range(col + 1, 3):
            value = normal[row][col]
            for inner in range(col):
                value = value - fac[row][inner] * fac[col][inner]
            fac[row][col] = value / fac[col][col]
    forward = []
    for place in range(3):
        value = target[place]
        for inner in range(place):
            value = value - fac[place][inner] * forward[inner]
        forward.append(value / fac[place][place])
    backward = [None] * 3
    for place in reversed(range(3)):
        value = forward[place]
        for inner in range(place + 1, 3):
            value = value - fac[inner][place] * backward[inner]
        backward[place] = value / fac[place][place]
    return backward


def kernel(ny, nz, per_owner,
           rs_hbm, sp_hbm, po_hbm, cp_hbm, mo_hbm, ids_hbm,
           held_hbm, small,
           basis, cur, nxt, sp, po, mo, wmat, wz, wa, wb, cpos, cneg, part, fprev, low_shift, high_shift, sface,
           halo_out, halo_in, yfix, zfix, ypart, zpart, yheld, zheld, corner, turn, block, prods, cp, ids_ref,
           owner_hot, rank_hot, owner_row, local_row, spread, dsend, recv1, turned, recv2, picked,
           gsend, grecv1, gsend2, grecv2,
           in_sem, out_sem, halo_send, halo_recv, a1_sem, a2_sem, g1_sem, g2_sem):
    gy = lax.axis_index("gy")
    gz = lax.axis_index("gz")

    number = ny * nz

    def gy_at(delta):
        return lax.rem(gy + (delta + ny), ny)

    def gz_at(delta):
        return lax.rem(gz + (delta + nz), nz)

    def each(count, step, start=0):
        def body(t, carry):
            step(t)
            return carry
        lax.fori_loop(start, count, body, 0)

    barrier = pltpu.get_barrier_semaphore()

    def greet(target):
        pl.semaphore_signal(barrier, inc=1, device_id=target, device_id_type=MESH)

    for delta in (1, -1):
        greet({"gz": gz_at(delta)})
        greet({"gy": gy_at(delta)})

    loads = [pltpu.make_async_copy(src, dst, in_sem.at[place]) for place, (src, dst) in enumerate(
        [(sp_hbm, sp), (rs_hbm, nxt), (po_hbm, po), (mo_hbm, mo), (cp_hbm, cp), (ids_hbm, ids_ref)])]
    for place in (4, 0, 1):
        loads[place].start()

    @functools.partial(each, ny - 1, start=2)
    def _(delta):
        greet({"gy": gy_at(delta)})

    @functools.partial(each, nz - 1, start=2)
    def _(delta):
        greet({"gz": gz_at(delta)})

    for place in (2, 5, 3):
        loads[place].start()

    loads[4].wait()
    lane = iota((8, 128), 1)
    row = iota((8, 128), 0)
    wz[40:128, :] = jnp.zeros((88, 128), F32)

    @functools.partial(each, VARS)
    def _(i):
        value = jnp.zeros((8, 128), F32)
        for j in range(VARS):
            value = jnp.where((lane >> 3) == j, -COURANT * cp[i, 2, j], value)
        wz[pl.ds(pl.multiple_of(8 * i, 8), 8), :] = jnp.where((lane & 7) == row, value, 0.0)

    loads[0].wait()

    lanes = iota((32, 128), 1)
    near = jnp.zeros((32, 128), F32)
    far = jnp.zeros((32, 128), F32)
    for x in range(8):
        ends = pltpu.roll(jnp.where(lanes == 0, sp[2, x, :, 0:128], sp[2, x, :, 128:256]), x + 1, axis=1)
        near = jnp.where(lanes == x + 1, ends, near)
        far = jnp.where(lanes == x, ends, far)
    near = pltpu.roll(near, 127, axis=1)
    for side, face in ((0, jnp.maximum(near, 0.0)), (1, jnp.maximum(-far, 0.0))):
        total = face
        for i in range(1, VARS):
            total = jnp.where((lanes >> 3) == i, pltpu.roll(face, 8 * i, axis=1), total)
        sface[32 * side:32 * side + 32, :] = jnp.where(lanes < 8 * VARS, total, 0.0)

    inside = (gy > 0, gy < ny - 1, gz > 0, gz < nz - 1)

    YROWS = VARS * 16
    ZAT = 2 * YROWS

    def y_at(side, j, half):
        return side * YROWS + j * 16 + half * 8

    def in_rows(place):
        return pl.ds(place * YROWS, YROWS) if place < 2 else pl.ds(ZAT + 32 * (place - 2), 32)

    def send_halo(par):
        for place, (axis, delta) in enumerate((("y", -1), ("y", 1), ("z", -1), ("z", 1))):
            rows = in_rows(place)
            target = {"gy": gy_at(delta)} if axis == "y" else {"gz": gz_at(delta)}
            copy = pltpu.make_async_remote_copy(
                src_ref=halo_out.at[par, rows], dst_ref=halo_in.at[par, in_rows(place ^ 1)],
                send_sem=halo_send.at[par, place], recv_sem=halo_recv.at[par, place ^ 1],
                device_id=target, device_id_type=MESH)
            pl.when(inside[place])(copy.start)

    for place in range(4):
        @pl.when(jnp.logical_not(inside[place]))
        def _():
            for par in range(2):
                halo_in[par, in_rows(place), :] = jnp.zeros((YROWS if place < 2 else 32, 128), F32)

    def wait_all(ref, sem):
        pltpu.make_async_copy(ref, ref, sem).wait()

    halves = (slice(0, 128), slice(128, 256))

    def pack():
        near = jnp.zeros((32, 128), F32)
        far = jnp.zeros((32, 128), F32)
        for i in range(VARS):
            for x in range(8):
                s = i * 8 + x
                ends = jnp.where(lanes == 0, nxt[i, x, :, 0:128], nxt[i, x, :, 128:256])
                ends = pltpu.roll(ends, s + 1, axis=1)
                near = jnp.where(lanes == s + 1, ends, near)
                far = jnp.where(lanes == s, ends, far)
        zpart[0:32, :] = pltpu.roll(near, 127, axis=1)
        zpart[32:64, :] = far
        for side, y in ((0, 0), (1, 31)):
            for half in range(2):
                for i in range(VARS):
                    at = y_at(side, i, half)
                    ypart[at:at + 8, :] = nxt[i, :, y, halves[half]]

    lane8 = iota((8, 128), 1)
    rows32 = iota((32, 128), 0)

    def y_corners():
        for side in range(2):
            for i in range(VARS):
                corner[side * 64 + i * 8:side * 64 + i * 8 + 8, :] = jnp.where(
                    lane8 == 0, yfix[y_at(side, i, 0):y_at(side, i, 0) + 8, :],
                    yfix[y_at(side, i, 1):y_at(side, i, 1) + 8, :])
        turn[...] = corner[...].T
        parts = []
        for at in (0, 127):
            both = jnp.broadcast_to(turn[at:at + 1, :], (32, 128))
            parts.append(jnp.where(rows32 == 0, both, jnp.where(rows32 == 31, pltpu.roll(both, 64, axis=1), 0.0)))
        return jnp.where(jnp.concatenate([lanes, lanes], axis=0) < 8 * VARS, jnp.concatenate(parts, axis=0), 0.0)

    def finish(k, par):
        faces = zpart[...] + zfix[...] + y_corners()
        zheld[k] = faces
        halo_out[par, ZAT:ZAT + 64, :] = jnp.dot(
            faces * sface[...], wz[...], preferred_element_type=F32, precision=lax.Precision.HIGHEST)
        turned_z = jnp.concatenate([zfix[...], jnp.zeros((64, 128), F32)], axis=0).T
        for side, y in ((0, 0), (1, 31)):
            for half in range(2):
                speed = sp[1, :, y, halves[half]]
                speed = jnp.maximum(speed, 0.0) if side == 0 else jnp.maximum(-speed, 0.0)
                flux = []
                for i in range(VARS):
                    extra = turned_z[8 * i:8 * i + 8]
                    shift = ((0, 95), (97, 64))[side][half]
                    extra = pltpu.roll(extra, shift, axis=1) if shift else extra
                    at = y_at(side, i, half)
                    value = ypart[at:at + 8, :] + yfix[at:at + 8, :] + jnp.where(lane8 == 127 * half, extra, 0.0)
                    yheld[k, at:at + 8, :] = value
                    flux.append(value * speed)
                for j in range(VARS):
                    total = flux[0] * (-COURANT * cp[0, 1, j])
                    for i in range(1, VARS):
                        total = total + flux[i] * (-COURANT * cp[i, 1, j])
                    at = y_at(side, j, half)
                    halo_out[par, at:at + 8, :] = total

    def settle(k):
        @functools.partial(each, VARS)
        def _(i):
            for x in range(8):
                for side, y in ((0, 0), (1, 31)):
                    for half in range(2):
                        at = pl.ds(side * YROWS + i * 16 + half * 8 + x, 1)
                        nxt[i, x, y:y + 1, halves[half]] = nxt[i, x, y:y + 1, halves[half]] + yfix[at, :]
            for x in range(8):
                near = nxt[i, x, :, 0:128] + jnp.where(
                    lanes == 0, pltpu.roll(zfix[0:32, :], 128 - 8 * i - x, axis=1), 0.0)
                far = nxt[i, x, :, 128:256] + jnp.where(
                    lanes == 127, pltpu.roll(zfix[32:64, :], 127 - 8 * i - x, axis=1), 0.0)
                cur[i, x, :, 0:128] = near
                cur[i, x, :, 128:256] = far
                basis[k, i, x, :, 0:128] = near
                basis[k, i, x, :, 128:256] = far

    def receive(par):
        for place in range(4):
            @pl.when(inside[place])
            def _():
                ref = halo_in.at[par, in_rows(place)]
                wait_all(ref, halo_recv.at[par, place])
                wait_all(ref, halo_send.at[par, place])
        yfix[0:YROWS, :] = halo_in[par, 0:YROWS, :] - halo_out[par, YROWS:ZAT, :]
        yfix[YROWS:ZAT, :] = halo_in[par, YROWS:ZAT, :] - halo_out[par, 0:YROWS, :]
        zfix[0:32, :] = halo_in[par, ZAT:ZAT + 32, :] - halo_out[par, ZAT + 32:ZAT + 64, :]
        zfix[32:64, :] = halo_in[par, ZAT + 32:ZAT + 64, :] - halo_out[par, ZAT:ZAT + 32, :]

    def prepare():
        @functools.partial(each, 8)
        def _(x):
            for d in range(3):
                s = sp[d, x]
                cpos[d, x] = jnp.maximum(s, 0.0)
                cneg[d, x] = jnp.maximum(-s, 0.0)

        lane = iota((16, 256), 1)
        row = iota((16, 256), 0)
        group = lane >> 4
        piece = jnp.where(group >= 10, 2, jnp.where(group >= 5, 1, 0))
        which = group - 5 * piece
        same = (lane & 15) == row

        @functools.partial(each, 3 * VARS)
        def _(place):
            d = lax.div(place, VARS)
            j = place - d * VARS
            value = jnp.zeros((16, 256), F32)
            for i in range(VARS):
                value = jnp.where(which == i, COURANT * cp[i, d, j], value)
            high = value.astype(BF16).astype(F32)
            value = jnp.where(same, jnp.where(piece == 2, value - high, high), 0.0)
            wmat[pl.ds(pl.multiple_of(place * 16, 16), 16), :] = value[:, 0:240].astype(BF16)

    def rank_slots():
        loads[5].wait()
        ids = jnp.concatenate([ids_ref[0], ids_ref[1]], axis=1)
        owners = lax.div(ids, per_owner)
        local_row[...] = (ids - owners * per_owner + 1).astype(F32)
        tri = jnp.where(iota((256, 128), 0) < jnp.where(iota((256, 128), 0) >= 128, 256, iota((256, 128), 1)), 1.0, 0.0).astype(BF16)
        sub = iota((number, 128), 0)
        before = jnp.zeros((number, 128), F32)
        for p in range(8):
            hot = jnp.where(sub == owners[p:p + 1, :], 1.0, 0.0)
            hot16 = hot.astype(BF16)
            count = dot(jnp.concatenate([hot16, before.astype(BF16)], axis=1), tri)
            before = before + hot
            owner_hot[:, p * 128:(p + 1) * 128] = hot16
            rank = jnp.sum(hot * count, axis=0, keepdims=True)
            rank_hot[:, p * 128:(p + 1) * 128] = jnp.where(rank == iota((SLOTS, 128), 0).astype(F32), 1.0, 0.0)


    def couple(x, w):
        for h in (0, 16):
            high, low = [], []
            for i in range(VARS):
                v = cur[i, x, h:h + 16, :]
                top = v.astype(BF16)
                high.append(top)
                low.append((v - top.astype(F32)).astype(BF16))
            out = dot(wmat[...], jnp.concatenate(high + low + high, axis=0))
            for place in range(3 * VARS):
                w[place, h:h + 16, :] = out[place * 16:place * 16 + 16]

    def stencil(x, w):
        prior = jnp.maximum(x - 1, 0)
        for j in range(VARS):
            wx = w[j]
            flux = cpos[0, x] * wx - fprev[j]
            nxt[j, prior] = part[j] - flux
            fprev[j] = cneg[0, x] * wx
            acc = po[x] * cur[j, x] + flux
            wv = w[2 * VARS + j]
            flux = cpos[2, x] * wv - pltpu.roll(cneg[2, x] * wv, 1, axis=1)
            acc = acc + flux - pltpu.roll(flux, 255, axis=1)
            for half in range(2):
                at = halves[half]
                wy = w[VARS + j, :, at]
                minus = cneg[1, x, :, at] * wy
                low_shift[j, half, 8:40, :] = minus
                low_shift[j, half, 0:8, :] = minus[24:32]
                flux = cpos[1, x, :, at] * wy - low_shift[j, half, 7:39, :]
                high_shift[j, half, 0:32, :] = flux
                high_shift[j, half, 32:40, :] = flux[0:8]
                part[j, :, at] = acc[:, at] + flux - high_shift[j, half, 1:33, :]

    def sweep():
        fprev[...] = jnp.zeros(fprev.shape, F32)
        couple(0, wa)

        @functools.partial(each, 4)
        def _(t):
            x = 2 * t
            couple(x + 1, wb)
            stencil(x, wa)
            couple(jnp.minimum(x + 2, 7), wa)
            stencil(x + 1, wb)

        for j in range(VARS):
            nxt[j, 7] = part[j] + fprev[j]

    def dispatch():
        loads[3].wait()

        @functools.partial(each, 2)
        def _(half_x):
            for k in range(3):
                total = None
                for x in range(4):
                    for i in range(3):
                        term = basis[k, 1 + i, 4 * half_x + x] * mo[i, 4 * half_x + x]
                        total = term if total is None else total + term
                block[k, half_x] = total

        low8 = iota((16, 192), 0)
        col = iota((16, 192), 1)
        within = jnp.where(col >= 96, col - 96, col) & 31
        half = jnp.where(col >= 96, 1, 0)
        ysel = jnp.where((low8 >> 3 == half) & ((low8 & 7) == (within >> 2)), 1.0, 0.0).astype(BF16)
        zrow = iota((512, 128), 0)
        zsel = jnp.where(((zrow & 255) >> 2) + (zrow >> 8) * 64 == iota((512, 128), 1), 1.0, 0.0).astype(BF16)
        parts = []
        for k in range(3):
            t = dot(ysel, jnp.concatenate(list(pieces(block[k, 0])) + list(pieces(block[k, 1])), axis=0))
            for part_ in pieces(jnp.concatenate([t[0:8], t[8:16]], axis=1)):
                parts.append(part_.astype(F32))
        t = dot(jnp.concatenate(parts, axis=0).astype(BF16), zsel)
        values = [-PENALTY * (t[24 * k:24 * k + 8] + t[24 * k + 8:24 * k + 16] + t[24 * k + 16:24 * k + 24])
                  for k in range(3)]
        tops = [value.astype(BF16).astype(F32) for value in values]
        rests = [value - top for value, top in zip(values, tops)]
        empty = jnp.zeros((SLOTS, 128), BF16)
        for p in range(8):
            hot = rank_hot[:, p * 128:(p + 1) * 128]
            rows = [local_row[...]] + tops + rests
            rows = [(hot * value[p:p + 1, :]).astype(BF16) for value in rows]
            spread[:, p * 128:(p + 1) * 128] = jnp.concatenate(rows + [empty], axis=0)
        dsend[...] = dot_nt(owner_hot[...], spread[...]).reshape(ny, nz, 128)

        @functools.partial(each, ny, start=1)
        def _(delta):
            pltpu.make_async_remote_copy(
                src_ref=dsend.at[gy_at(delta)], dst_ref=recv1.at[delta],
                send_sem=a1_sem.at[0], recv_sem=a1_sem.at[1],
                device_id={"gy": gy_at(delta)}, device_id_type=MESH).start()
        recv1[0] = dsend[gy]

    pairs = [(l, k) for k in range(4) for l in range(k + 1)]

    def products(entries, vectors):
        def body(x, sums):
            sums = list(sums)
            for j in range(VARS):
                v = [nxt[j, x] if k == 3 else basis[k, j, x] for k in range(vectors)]
                for place, e in enumerate(entries):
                    l, k = pairs[e]
                    sums[place] = sums[place] + fold(v[l] * v[k])
            return tuple(sums)

        sums = lax.fori_loop(0, 8, body, tuple(jnp.zeros((8, 128), F32) for _ in entries))
        for place, e in enumerate(entries):
            prods[e] = sums[place]

    def corrections():
        sums = [jnp.zeros((8, 128), F32) for _ in range(4)]
        for at in range(0, 2 * YROWS, 8):
            add = yfix[at:at + 8, :]
            for l in range(3):
                sums[l] = sums[l] + yheld[l, at:at + 8, :] * add
            sums[3] = sums[3] + (2.0 * ypart[at:at + 8, :] + add) * add
        both = y_corners()
        for at in range(0, 64, 8):
            add = zfix[at:at + 8, :]
            for l in range(3):
                sums[l] = sums[l] + zheld[l, at:at + 8, :] * add
            sums[3] = sums[3] + (2.0 * (zpart[at:at + 8, :] + both[at:at + 8]) + add) * add
        for l in range(4):
            prods[6 + l] = prods[6 + l] + sums[l]

    yfix[...] = jnp.zeros(yfix.shape, F32)
    zfix[...] = jnp.zeros(zfix.shape, F32)
    corner[...] = jnp.zeros(corner.shape, F32)
    loads[1].wait()

    @functools.partial(each, 4)
    def _(k):
        par = k & 1
        pack()

        @pl.when(k == 3)
        def _():
            products((6, 7, 8, 9), 4)

        @pl.when(k > 0)
        def _():
            receive(1 - par)

        @pl.when(k == 3)
        def _():
            corrections()

        @pl.when(k < 3)
        def _():
            finish(k, par)

            @pl.when(k == 0)
            def _():
                pl.semaphore_wait(barrier, (ny - 1) + (nz - 1))

            send_halo(par)
            settle(k)

            @pl.when(k > 0)
            def _():
                pltpu.make_async_copy(basis.at[k], held_hbm.at[k - 1], out_sem).start()

            @pl.when(k == 0)
            def _():
                prepare()
                loads[2].wait()

            @pl.when(k == 1)
            def _():
                products((0, 1, 2), 2)
                rank_slots()

            @pl.when(k == 2)
            def _():
                dispatch()
                products((3, 4, 5), 3)

            sweep()

    sums = [prods[e] for e in range(10)]

    lane = iota((8, 128), 1)
    packed = jnp.zeros((8, 128), F32)
    for e, value in enumerate(sums):
        for shift in (64, 32, 16, 8):
            value = value + pltpu.roll(value, shift, axis=1)
        packed = jnp.where((lane >> 3) == e, value, packed)
    gsend[...] = jnp.sum(packed, axis=0, keepdims=True)

    @functools.partial(each, ny, start=1)
    def _(delta):
        pltpu.make_async_remote_copy(
            src_ref=gsend, dst_ref=grecv1.at[delta], send_sem=g1_sem.at[0], recv_sem=g1_sem.at[1],
            device_id={"gy": gy_at(delta)}, device_id_type=MESH).start()

    wait_all(recv1.at[pl.ds(1, ny - 1)], a1_sem.at[1])
    wait_all(recv1.at[pl.ds(1, ny - 1)], a1_sem.at[0])
    for g in range(nz):
        turned[g] = recv1[:, g, :]

    @functools.partial(each, nz, start=1)
    def _(delta):
        pltpu.make_async_remote_copy(
            src_ref=turned.at[gz_at(delta)], dst_ref=recv2.at[delta], send_sem=a2_sem.at[0], recv_sem=a2_sem.at[1],
            device_id={"gz": gz_at(delta)}, device_id_type=MESH).start()
    recv2[0] = turned[gz]

    wait_all(grecv1.at[pl.ds(1, ny - 1)], g1_sem.at[1])
    wait_all(grecv1.at[pl.ds(1, ny - 1)], g1_sem.at[0])
    own = gsend[...]
    for delta in range(1, ny):
        own = own + grecv1[delta]
    gsend2[...] = own

    @functools.partial(each, nz, start=1)
    def _(delta):
        pltpu.make_async_remote_copy(
            src_ref=gsend2, dst_ref=grecv2.at[delta], send_sem=g2_sem.at[0], recv_sem=g2_sem.at[1],
            device_id={"gz": gz_at(delta)}, device_id_type=MESH).start()

    wait_all(recv2.at[pl.ds(1, nz - 1)], a2_sem.at[1])
    wait_all(recv2.at[pl.ds(1, nz - 1)], a2_sem.at[0])
    picked[...] = recv2[...].reshape(number, 128).T
    digit = iota((16, 128), 0)
    left, right = [], []
    for r in range(SLOTS):
        number_r = picked[r:r + 1, :].astype(jnp.int32) - 1
        high = (number_r >> 4) == digit
        right.append(jnp.where((number_r & 15) == digit, 1.0, 0.0).astype(BF16))
        left.append(jnp.concatenate(
            [jnp.where(high, picked[SLOTS * (q + 1) + r:SLOTS * (q + 1) + r + 1, :], 0.0).astype(BF16) for q in range(6)], axis=0))
    bins = dot_nt(jnp.concatenate(left, axis=1), jnp.concatenate(right, axis=1))
    bins = bins[0:48] + bins[48:96]
    wide = jnp.where((iota((16, 256), 1) & 15) == iota((16, 256), 0), 1.0, 0.0).astype(BF16)
    bins = sum(dot(part_, wide) for part_ in pieces(bins))
    bins = jnp.where((iota((48, 256), 1) >> 4) == (iota((48, 256), 0) & 15), bins, 0.0)
    bin_sums = [jnp.sum(bins[16 * k:16 * k + 16], axis=0, keepdims=True) for k in range(3)]

    wait_all(grecv2.at[pl.ds(1, nz - 1)], g2_sem.at[1])
    wait_all(grecv2.at[pl.ds(1, nz - 1)], g2_sem.at[0])
    own = gsend2[...]
    for delta in range(1, nz):
        own = own + grecv2[delta]
    for shift in (4, 2, 1):
        own = own + pltpu.roll(own, shift, axis=1)
    own = jnp.broadcast_to(own, (8, 128))
    splat = {}
    for e, (l, k) in enumerate(pairs):
        splat[l, k] = jnp.broadcast_to(own[:, 8 * e + 7:8 * e + 8], (8, 128))
    coeffs = solve([[splat[min(a, b), max(a, b)] for b in range(4)] for a in range(4)])

    sens = None
    for k in range(3):
        term = bin_sums[k] * jnp.concatenate([coeffs[k][0:1]] * (per_owner // 128), axis=1)
        sens = term if sens is None else sens + term
    small[0:1, :] = sens
    for k in range(3):
        small[8 + 8 * k:16 + 8 * k, :] = jnp.concatenate([coeffs[k]] * (per_owner // 128), axis=1)
    wait_all(basis.at[pl.ds(1, 2)], out_sem)


def combine(rs, held, small, adj_hbm, sens_hbm, result, sens, out_sem, sens_sem):
    sens[...] = small[0:1, :]
    put_sens = pltpu.make_async_copy(sens, sens_hbm, sens_sem)
    put_sens.start()
    full = [jnp.concatenate([small[8 + 8 * k:16 + 8 * k, :]] * 4, axis=0) for k in range(3)]

    def body(j, carry):
        for x in range(8):
            result[j, x] = full[0] * rs[j, x] + full[1] * held[0, j, x] + full[2] * held[1, j, x]
        pltpu.make_async_copy(result.at[j], adj_hbm.at[j], out_sem).start()
        return carry

    lax.fori_loop(0, VARS, body, 0)
    pltpu.make_async_copy(result, result, out_sem).wait()
    put_sens.wait()


def local(right_side, speeds, porosity, coupling, momentum, design_ids):
    ny = lax.axis_size("gy")
    nz = lax.axis_size("gz")
    _, nx, cy, cz = right_side.shape
    per_owner = design_ids.size // 4
    field = (VARS, nx, cy, cz)
    dma = pltpu.SemaphoreType.DMA
    hbm = pl.BlockSpec(memory_space=pltpu.HBM)
    held, small = pl.pallas_call(
        functools.partial(kernel, ny, nz, per_owner),
        out_shape=[jax.ShapeDtypeStruct((2,) + field, F32), jax.ShapeDtypeStruct((32, per_owner), F32)],
        in_specs=[hbm] * 6,
        out_specs=[pl.BlockSpec(memory_space=pl.ANY), pl.BlockSpec(memory_space=pltpu.VMEM)],
        scratch_shapes=[
            pltpu.VMEM((3,) + field, F32), pltpu.VMEM(field, F32), pltpu.VMEM(field, F32),
            pltpu.VMEM((3, nx, cy, cz), F32),
            pltpu.VMEM((nx, cy, cz), F32),
            pltpu.VMEM((3, nx, cy, cz), F32),
            pltpu.VMEM((240, 240), BF16),
            pltpu.VMEM((128, 128), F32),
            pltpu.VMEM((3 * VARS, cy, cz), F32), pltpu.VMEM((3 * VARS, cy, cz), F32),
            pltpu.VMEM((3, nx, cy, cz), F32), pltpu.VMEM((3, nx, cy, cz), F32),
            pltpu.VMEM((VARS, cy, cz), F32), pltpu.VMEM((VARS, cy, cz), F32),
            pltpu.VMEM((VARS, 2, 40, 128), F32), pltpu.VMEM((VARS, 2, 40, 128), F32),
            pltpu.VMEM((64, 128), F32),
            pltpu.VMEM((2, 224, 128), F32), pltpu.VMEM((2, 224, 128), F32), pltpu.VMEM((160, 128), F32), pltpu.VMEM((64, 128), F32),
            pltpu.VMEM((160, 128), F32), pltpu.VMEM((64, 128), F32), pltpu.VMEM((3, 160, 128), F32), pltpu.VMEM((3, 64, 128), F32),
            pltpu.VMEM((128, 128), F32), pltpu.VMEM((128, 128), F32),
            pltpu.VMEM((3, 2, cy, cz), F32),
            pltpu.VMEM((10, 8, 128), F32),
            pltpu.SMEM((VARS, 3, VARS), F32),
            pltpu.VMEM(design_ids.shape, jnp.int32),
            pltpu.VMEM((ny * nz, 1024), BF16),
            pltpu.VMEM((SLOTS, 1024), F32),
            pltpu.VMEM((8, 128), F32),
            pltpu.VMEM((8, 128), F32),
            pltpu.VMEM((128, 1024), BF16),
            pltpu.VMEM((ny, nz, 128), F32),
            pltpu.VMEM((ny, nz, 128), F32),
            pltpu.VMEM((nz, ny, 128), F32),
            pltpu.VMEM((nz, ny, 128), F32),
            pltpu.VMEM((128, 128), F32),
            pltpu.VMEM((1, 128), F32),
            pltpu.VMEM((ny, 1, 128), F32),
            pltpu.VMEM((1, 128), F32),
            pltpu.VMEM((nz, 1, 128), F32),
            dma((6,)), dma, dma((2, 4)), dma((2, 4)), dma((2,)), dma((2,)), dma((2,)), dma((2,)),
        ],
        compiler_params=pltpu.CompilerParams(
            collective_id=0, has_side_effects=True, vmem_limit_bytes=40 * 1024 * 1024),
    )(*[pltpu.with_memory_space_constraint(value, pltpu.HBM) for value in (
        right_side, speeds, porosity, coupling.transpose(1, 0, 2), momentum, design_ids)])
    adjoint, sensitivity = pl.pallas_call(
        combine,
        out_shape=[jax.ShapeDtypeStruct(field, F32), jax.ShapeDtypeStruct((1, per_owner), F32)],
        in_specs=[pl.BlockSpec(memory_space=pltpu.VMEM)] * 3,
        out_specs=[hbm, hbm],
        scratch_shapes=[pltpu.VMEM(field, F32), pltpu.VMEM((1, per_owner), F32), dma, dma],
        compiler_params=pltpu.CompilerParams(vmem_limit_bytes=24 * 1024 * 1024),
    )(right_side, held, small)
    return adjoint, sensitivity.reshape(per_owner)


def solution(mesh):
    in_specs = (
        P(None, None, "gy", "gz"),
        P(None, None, "gy", "gz"),
        P(None, "gy", "gz"),
        P(),
        P(None, None, "gy", "gz"),
        P(None, "gy", "gz"),
    )
    out_specs = (P(None, None, "gy", "gz"), P(("gy", "gz")))
    return jax.shard_map(local, mesh=mesh, in_specs=in_specs, out_specs=out_specs, check_vma=False)
```

```python
import functools

import jax
import jax.numpy as jnp
from jax import lax
from jax.experimental import pallas as pl
from jax.experimental.pallas import tpu as pltpu
from jax.sharding import PartitionSpec as P

PENALTY = 1.0
COURANT = 0.3
VARS = 5
SLOTS = 16
MESH = pl.DeviceIdType.MESH
F32 = jnp.float32
BF16 = jnp.bfloat16


def pieces(value):
    high = value.astype(BF16)
    rest = value - high.astype(F32)
    mid = rest.astype(BF16)
    low = (rest - mid.astype(F32)).astype(BF16)
    return high, mid, low


def dot(a, b):
    return jnp.dot(a, b, preferred_element_type=F32)


def dot_nt(a, b):
    return lax.dot_general(a, b, (((1,), (1,)), ((), ())), preferred_element_type=F32)


def iota(shape, axis):
    return lax.broadcasted_iota(jnp.int32, shape, axis)


def fold(product):
    rows = product[0:8] + product[8:16] + product[16:24] + product[24:32]
    return rows[:, 0:128] + rows[:, 128:256]


def solve(gram):
    low = [[None] * 4 for _ in range(4)]
    for col in range(4):
        diag = gram[col][col]
        for inner in range(col):
            diag = diag - low[col][inner] * low[col][inner]
        low[col][col] = jnp.sqrt(diag)
        for row in range(col + 1, 4):
            value = gram[row][col]
            for inner in range(col):
                value = value - low[row][inner] * low[col][inner]
            low[row][col] = value / low[col][col]
    zero = jnp.zeros_like(gram[0][0])
    upper = [[low[c][r] if c >= r else None for c in range(4)] for r in range(4)]

    def add(a, b):
        return b if a is None else (a if b is None else a + b)

    hess = [[add(upper[r][c + 1], upper[r][c]) for c in range(3)] for r in range(4)]

    def inner_sum(terms):
        total = None
        for a, b in terms:
            if a is not None and b is not None:
                total = add(total, a * b)
        return zero if total is None else total

    normal = [[inner_sum([(hess[r][a], hess[r][b]) for r in range(4)]) for b in range(3)] for a in range(3)]
    target = [inner_sum([(hess[r][a], upper[r][0]) for r in range(4)]) for a in range(3)]
    fac = [[None] * 3 for _ in range(3)]
    for col in range(3):
        diag = normal[col][col]
        for inner in range(col):
            diag = diag - fac[col][inner] * fac[col][inner]
        fac[col][col] = jnp.sqrt(diag)
        for row in range(col + 1, 3):
            value = normal[row][col]
            for inner in range(col):
                value = value - fac[row][inner] * fac[col][inner]
            fac[row][col] = value / fac[col][col]
    forward = []
    for place in range(3):
        value = target[place]
        for inner in range(place):
            value = value - fac[place][inner] * forward[inner]
        forward.append(value / fac[place][place])
    backward = [None] * 3
    for place in reversed(range(3)):
        value = forward[place]
        for inner in range(place + 1, 3):
            value = value - fac[inner][place] * backward[inner]
        backward[place] = value / fac[place][place]
    return backward


def kernel(ny, nz, per_owner,
           rs_hbm, sp_hbm, po_hbm, cp_hbm, mo_hbm, ids_hbm,
           held_hbm, small,
           basis, cur, nxt, sp, po, mo, wmat, wz, wa, wb, cpos, cneg, part, fprev, low_shift, high_shift, sface,
           halo_out, halo_in, yfix, zfix, ypart, zpart, yheld, zheld, corner, turn, block, prods, cp, ids_ref,
           owner_hot, rank_hot, owner_row, local_row, spread, dsend, recv1, turned, recv2, picked,
           gsend, grecv,
           in_sem, out_sem, halo_send, halo_recv, a1_sem, a2_sem, g_sem, known_sem):
    gy = lax.axis_index("gy")
    gz = lax.axis_index("gz")

    number = ny * nz

    def gy_at(delta):
        return lax.rem(gy + (delta + ny), ny)

    def gz_at(delta):
        return lax.rem(gz + (delta + nz), nz)

    def each(count, step, start=0):
        def body(t, carry):
            step(t)
            return carry
        lax.fori_loop(start, count, body, 0)

    barrier = pltpu.get_barrier_semaphore()

    def greet(target):
        pl.semaphore_signal(barrier, inc=1, device_id=target, device_id_type=MESH)

    for delta in (1, -1):
        greet({"gz": gz_at(delta)})
        greet({"gy": gy_at(delta)})

    loads = [pltpu.make_async_copy(src, dst, in_sem.at[place]) for place, (src, dst) in enumerate(
        [(sp_hbm, sp), (rs_hbm, nxt), (po_hbm, po), (mo_hbm, mo), (cp_hbm, cp), (ids_hbm, ids_ref)])]
    for place in (4, 0, 1):
        loads[place].start()

    @functools.partial(each, ny - 1, start=2)
    def _(delta):
        greet({"gy": gy_at(delta)})

    @functools.partial(each, nz - 1, start=2)
    def _(delta):
        greet({"gz": gz_at(delta)})

    for place in (2, 5, 3):
        loads[place].start()

    loads[4].wait()
    lane = iota((8, 128), 1)
    row = iota((8, 128), 0)
    wz[40:128, :] = jnp.zeros((88, 128), F32)

    @functools.partial(each, VARS)
    def _(i):
        value = jnp.zeros((8, 128), F32)
        for j in range(VARS):
            value = jnp.where((lane >> 3) == j, -COURANT * cp[i, 2, j], value)
        wz[pl.ds(pl.multiple_of(8 * i, 8), 8), :] = jnp.where((lane & 7) == row, value, 0.0)

    loads[0].wait()

    lanes = iota((32, 128), 1)
    near = jnp.zeros((32, 128), F32)
    far = jnp.zeros((32, 128), F32)
    for x in range(8):
        ends = pltpu.roll(jnp.where(lanes == 0, sp[2, x, :, 0:128], sp[2, x, :, 128:256]), x + 1, axis=1)
        near = jnp.where(lanes == x + 1, ends, near)
        far = jnp.where(lanes == x, ends, far)
    near = pltpu.roll(near, 127, axis=1)
    for side, face in ((0, jnp.maximum(near, 0.0)), (1, jnp.maximum(-far, 0.0))):
        total = face
        for i in range(1, VARS):
            total = jnp.where((lanes >> 3) == i, pltpu.roll(face, 8 * i, axis=1), total)
        sface[32 * side:32 * side + 32, :] = jnp.where(lanes < 8 * VARS, total, 0.0)

    inside = (gy > 0, gy < ny - 1, gz > 0, gz < nz - 1)

    YROWS = VARS * 16
    ZAT = 2 * YROWS

    def y_at(side, j, half):
        return side * YROWS + j * 16 + half * 8

    def in_rows(place):
        return pl.ds(place * YROWS, YROWS) if place < 2 else pl.ds(ZAT + 32 * (place - 2), 32)

    def send_halo(par):
        for place, (axis, delta) in enumerate((("y", -1), ("y", 1), ("z", -1), ("z", 1))):
            rows = in_rows(place)
            target = {"gy": gy_at(delta)} if axis == "y" else {"gz": gz_at(delta)}
            copy = pltpu.make_async_remote_copy(
                src_ref=halo_out.at[par, rows], dst_ref=halo_in.at[par, in_rows(place ^ 1)],
                send_sem=halo_send.at[par, place], recv_sem=halo_recv.at[par, place ^ 1],
                device_id=target, device_id_type=MESH)
            pl.when(inside[place])(copy.start)

    for place in range(4):
        @pl.when(jnp.logical_not(inside[place]))
        def _():
            for par in range(2):
                halo_in[par, in_rows(place), :] = jnp.zeros((YROWS if place < 2 else 32, 128), F32)

    def wait_all(ref, sem):
        pltpu.make_async_copy(ref, ref, sem).wait()

    halves = (slice(0, 128), slice(128, 256))

    def pack():
        near = jnp.zeros((32, 128), F32)
        far = jnp.zeros((32, 128), F32)
        for i in range(VARS):
            for x in range(8):
                s = i * 8 + x
                ends = jnp.where(lanes == 0, nxt[i, x, :, 0:128], nxt[i, x, :, 128:256])
                ends = pltpu.roll(ends, s + 1, axis=1)
                near = jnp.where(lanes == s + 1, ends, near)
                far = jnp.where(lanes == s, ends, far)
        zpart[0:32, :] = pltpu.roll(near, 127, axis=1)
        zpart[32:64, :] = far
        for side, y in ((0, 0), (1, 31)):
            for half in range(2):
                for i in range(VARS):
                    at = y_at(side, i, half)
                    ypart[at:at + 8, :] = nxt[i, :, y, halves[half]]

    lane8 = iota((8, 128), 1)
    rows32 = iota((32, 128), 0)

    def y_corners():
        for side in range(2):
            for i in range(VARS):
                corner[side * 64 + i * 8:side * 64 + i * 8 + 8, :] = jnp.where(
                    lane8 == 0, yfix[y_at(side, i, 0):y_at(side, i, 0) + 8, :],
                    yfix[y_at(side, i, 1):y_at(side, i, 1) + 8, :])
        turn[...] = corner[...].T
        parts = []
        for at in (0, 127):
            both = jnp.broadcast_to(turn[at:at + 1, :], (32, 128))
            parts.append(jnp.where(rows32 == 0, both, jnp.where(rows32 == 31, pltpu.roll(both, 64, axis=1), 0.0)))
        return jnp.where(jnp.concatenate([lanes, lanes], axis=0) < 8 * VARS, jnp.concatenate(parts, axis=0), 0.0)

    def finish(k, par):
        faces = zpart[...] + zfix[...] + y_corners()
        zheld[k] = faces
        halo_out[par, ZAT:ZAT + 64, :] = jnp.dot(
            faces * sface[...], wz[...], preferred_element_type=F32, precision=lax.Precision.HIGHEST)
        turned_z = jnp.concatenate([zfix[...], jnp.zeros((64, 128), F32)], axis=0).T
        for side, y in ((0, 0), (1, 31)):
            for half in range(2):
                speed = sp[1, :, y, halves[half]]
                speed = jnp.maximum(speed, 0.0) if side == 0 else jnp.maximum(-speed, 0.0)
                flux = []
                for i in range(VARS):
                    extra = turned_z[8 * i:8 * i + 8]
                    shift = ((0, 95), (97, 64))[side][half]
                    extra = pltpu.roll(extra, shift, axis=1) if shift else extra
                    at = y_at(side, i, half)
                    value = ypart[at:at + 8, :] + yfix[at:at + 8, :] + jnp.where(lane8 == 127 * half, extra, 0.0)
                    yheld[k, at:at + 8, :] = value
                    flux.append(value * speed)
                for j in range(VARS):
                    total = flux[0] * (-COURANT * cp[0, 1, j])
                    for i in range(1, VARS):
                        total = total + flux[i] * (-COURANT * cp[i, 1, j])
                    at = y_at(side, j, half)
                    halo_out[par, at:at + 8, :] = total

    def settle(k):
        @functools.partial(each, VARS)
        def _(i):
            for x in range(8):
                for side, y in ((0, 0), (1, 31)):
                    for half in range(2):
                        at = pl.ds(side * YROWS + i * 16 + half * 8 + x, 1)
                        nxt[i, x, y:y + 1, halves[half]] = nxt[i, x, y:y + 1, halves[half]] + yfix[at, :]
            for x in range(8):
                near = nxt[i, x, :, 0:128] + jnp.where(
                    lanes == 0, pltpu.roll(zfix[0:32, :], 128 - 8 * i - x, axis=1), 0.0)
                far = nxt[i, x, :, 128:256] + jnp.where(
                    lanes == 127, pltpu.roll(zfix[32:64, :], 127 - 8 * i - x, axis=1), 0.0)
                cur[i, x, :, 0:128] = near
                cur[i, x, :, 128:256] = far
                basis[k, i, x, :, 0:128] = near
                basis[k, i, x, :, 128:256] = far

    def receive(par):
        for place in range(4):
            @pl.when(inside[place])
            def _():
                ref = halo_in.at[par, in_rows(place)]
                wait_all(ref, halo_recv.at[par, place])
                wait_all(ref, halo_send.at[par, place])
        yfix[0:YROWS, :] = halo_in[par, 0:YROWS, :] - halo_out[par, YROWS:ZAT, :]
        yfix[YROWS:ZAT, :] = halo_in[par, YROWS:ZAT, :] - halo_out[par, 0:YROWS, :]
        zfix[0:32, :] = halo_in[par, ZAT:ZAT + 32, :] - halo_out[par, ZAT + 32:ZAT + 64, :]
        zfix[32:64, :] = halo_in[par, ZAT + 32:ZAT + 64, :] - halo_out[par, ZAT:ZAT + 32, :]

    def prepare():
        @functools.partial(each, 8)
        def _(x):
            for d in range(3):
                s = sp[d, x]
                cpos[d, x] = jnp.maximum(s, 0.0)
                cneg[d, x] = jnp.maximum(-s, 0.0)

        lane = iota((16, 256), 1)
        row = iota((16, 256), 0)
        group = lane >> 4
        piece = jnp.where(group >= 10, 2, jnp.where(group >= 5, 1, 0))
        which = group - 5 * piece
        same = (lane & 15) == row

        @functools.partial(each, 3 * VARS)
        def _(place):
            d = lax.div(place, VARS)
            j = place - d * VARS
            value = jnp.zeros((16, 256), F32)
            for i in range(VARS):
                value = jnp.where(which == i, COURANT * cp[i, d, j], value)
            high = value.astype(BF16).astype(F32)
            value = jnp.where(same, jnp.where(piece == 2, value - high, high), 0.0)
            wmat[pl.ds(pl.multiple_of(place * 16, 16), 16), :] = value[:, 0:240].astype(BF16)

    def rank_slots():
        loads[5].wait()
        ids = jnp.concatenate([ids_ref[0], ids_ref[1]], axis=1)
        owners = lax.div(ids, per_owner)
        local_row[...] = (ids - owners * per_owner + 1).astype(F32)
        tri = jnp.where(iota((256, 128), 0) < jnp.where(iota((256, 128), 0) >= 128, 256, iota((256, 128), 1)), 1.0, 0.0).astype(BF16)
        sub = iota((number, 128), 0)
        before = jnp.zeros((number, 128), F32)
        for p in range(8):
            hot = jnp.where(sub == owners[p:p + 1, :], 1.0, 0.0)
            hot16 = hot.astype(BF16)
            count = dot(jnp.concatenate([hot16, before.astype(BF16)], axis=1), tri)
            before = before + hot
            owner_hot[:, p * 128:(p + 1) * 128] = hot16
            rank = jnp.sum(hot * count, axis=0, keepdims=True)
            rank_hot[:, p * 128:(p + 1) * 128] = jnp.where(rank == iota((SLOTS, 128), 0).astype(F32), 1.0, 0.0)


    def couple(x, w):
        for h in (0, 16):
            high, low = [], []
            for i in range(VARS):
                v = cur[i, x, h:h + 16, :]
                top = v.astype(BF16)
                high.append(top)
                low.append((v - top.astype(F32)).astype(BF16))
            out = dot(wmat[...], jnp.concatenate(high + low + high, axis=0))
            for place in range(3 * VARS):
                w[place, h:h + 16, :] = out[place * 16:place * 16 + 16]

    def stencil(x, w):
        prior = jnp.maximum(x - 1, 0)
        for j in range(VARS):
            wx = w[j]
            flux = cpos[0, x] * wx - fprev[j]
            nxt[j, prior] = part[j] - flux
            fprev[j] = cneg[0, x] * wx
            acc = po[x] * cur[j, x] + flux
            wv = w[2 * VARS + j]
            flux = cpos[2, x] * wv - pltpu.roll(cneg[2, x] * wv, 1, axis=1)
            acc = acc + flux - pltpu.roll(flux, 255, axis=1)
            for half in range(2):
                at = halves[half]
                wy = w[VARS + j, :, at]
                minus = cneg[1, x, :, at] * wy
                low_shift[j, half, 8:40, :] = minus
                low_shift[j, half, 0:8, :] = minus[24:32]
                flux = cpos[1, x, :, at] * wy - low_shift[j, half, 7:39, :]
                high_shift[j, half, 0:32, :] = flux
                high_shift[j, half, 32:40, :] = flux[0:8]
                part[j, :, at] = acc[:, at] + flux - high_shift[j, half, 1:33, :]

    def sweep():
        fprev[...] = jnp.zeros(fprev.shape, F32)
        couple(0, wa)

        @functools.partial(each, 4)
        def _(t):
            x = 2 * t
            couple(x + 1, wb)
            stencil(x, wa)
            couple(jnp.minimum(x + 2, 7), wa)
            stencil(x + 1, wb)

        for j in range(VARS):
            nxt[j, 7] = part[j] + fprev[j]

    def dispatch():
        loads[3].wait()

        @functools.partial(each, 2)
        def _(half_x):
            for k in range(3):
                total = None
                for x in range(4):
                    for i in range(3):
                        term = basis[k, 1 + i, 4 * half_x + x] * mo[i, 4 * half_x + x]
                        total = term if total is None else total + term
                block[k, half_x] = total

        low8 = iota((16, 192), 0)
        col = iota((16, 192), 1)
        within = jnp.where(col >= 96, col - 96, col) & 31
        half = jnp.where(col >= 96, 1, 0)
        ysel = jnp.where((low8 >> 3 == half) & ((low8 & 7) == (within >> 2)), 1.0, 0.0).astype(BF16)
        zrow = iota((512, 128), 0)
        zsel = jnp.where(((zrow & 255) >> 2) + (zrow >> 8) * 64 == iota((512, 128), 1), 1.0, 0.0).astype(BF16)
        parts = []
        for k in range(3):
            t = dot(ysel, jnp.concatenate(list(pieces(block[k, 0])) + list(pieces(block[k, 1])), axis=0))
            for part_ in pieces(jnp.concatenate([t[0:8], t[8:16]], axis=1)):
                parts.append(part_.astype(F32))
        t = dot(jnp.concatenate(parts, axis=0).astype(BF16), zsel)
        values = [-PENALTY * (t[24 * k:24 * k + 8] + t[24 * k + 8:24 * k + 16] + t[24 * k + 16:24 * k + 24])
                  for k in range(3)]
        tops = [value.astype(BF16).astype(F32) for value in values]
        rests = [value - top for value, top in zip(values, tops)]
        empty = jnp.zeros((SLOTS, 128), BF16)
        for p in range(8):
            hot = rank_hot[:, p * 128:(p + 1) * 128]
            rows = [local_row[...]] + tops + rests
            rows = [(hot * value[p:p + 1, :]).astype(BF16) for value in rows]
            spread[:, p * 128:(p + 1) * 128] = jnp.concatenate(rows + [empty], axis=0)
        dsend[...] = dot_nt(owner_hot[...], spread[...]).reshape(ny, nz, 128)

        @functools.partial(each, ny, start=1)
        def _(delta):
            pltpu.make_async_remote_copy(
                src_ref=dsend.at[gy_at(delta)], dst_ref=recv1.at[delta],
                send_sem=a1_sem.at[0], recv_sem=a1_sem.at[1],
                device_id={"gy": gy_at(delta)}, device_id_type=MESH).start()
        recv1[0] = dsend[gy]

    pairs = [(l, k) for k in range(4) for l in range(k + 1)]

    def products(entries, vectors):
        def body(x, sums):
            sums = list(sums)
            for j in range(VARS):
                v = [nxt[j, x] if k == 3 else basis[k, j, x] for k in range(vectors)]
                for place, e in enumerate(entries):
                    l, k = pairs[e]
                    sums[place] = sums[place] + fold(v[l] * v[k])
            return tuple(sums)

        sums = lax.fori_loop(0, 8, body, tuple(jnp.zeros((8, 128), F32) for _ in entries))
        for place, e in enumerate(entries):
            prods[e] = sums[place]

    def corrections():
        sums = [jnp.zeros((8, 128), F32) for _ in range(4)]
        for at in range(0, 2 * YROWS, 8):
            add = yfix[at:at + 8, :]
            for l in range(3):
                sums[l] = sums[l] + yheld[l, at:at + 8, :] * add
            sums[3] = sums[3] + (2.0 * ypart[at:at + 8, :] + add) * add
        both = y_corners()
        for at in range(0, 64, 8):
            add = zfix[at:at + 8, :]
            for l in range(3):
                sums[l] = sums[l] + zheld[l, at:at + 8, :] * add
            sums[3] = sums[3] + (2.0 * (zpart[at:at + 8, :] + both[at:at + 8]) + add) * add
        for l in range(4):
            prods[6 + l] = prods[6 + l] + sums[l]

    yfix[...] = jnp.zeros(yfix.shape, F32)
    zfix[...] = jnp.zeros(zfix.shape, F32)
    corner[...] = jnp.zeros(corner.shape, F32)
    loads[1].wait()

    @functools.partial(each, 4)
    def _(k):
        par = k & 1
        pack()

        @pl.when(k == 3)
        def _():
            products((6, 7, 8, 9), 4)

        @pl.when(k > 0)
        def _():
            receive(1 - par)

        @pl.when(k == 3)
        def _():
            corrections()

        @pl.when(k < 3)
        def _():
            finish(k, par)

            @pl.when(k == 0)
            def _():
                pl.semaphore_wait(barrier, (ny - 1) + (nz - 1))

            send_halo(par)

            @pl.when(k == 0)
            def _():
                @functools.partial(each, nz, start=1)
                def _(delta):
                    pl.semaphore_signal(known_sem, inc=1, device_id={"gz": gz_at(delta)}, device_id_type=MESH)

            settle(k)

            @pl.when(k > 0)
            def _():
                pltpu.make_async_copy(basis.at[k], held_hbm.at[k - 1], out_sem).start()

            @pl.when(k == 0)
            def _():
                prepare()
                loads[2].wait()

            @pl.when(k == 1)
            def _():
                products((0, 1, 2), 2)
                rank_slots()

            @pl.when(k == 2)
            def _():
                dispatch()
                products((3, 4, 5), 3)

            sweep()

    sums = [prods[e] for e in range(10)]

    lane = iota((8, 128), 1)
    packed = jnp.zeros((8, 128), F32)
    for e, value in enumerate(sums):
        for shift in (64, 32, 16, 8):
            value = value + pltpu.roll(value, shift, axis=1)
        packed = jnp.where((lane >> 3) == e, value, packed)
    gsend[...] = jnp.sum(packed, axis=0, keepdims=True)

    pl.semaphore_wait(known_sem, nz - 1)

    def send_gram(a):
        @functools.partial(each, nz, start=0 if a else 1)
        def _(b):
            pltpu.make_async_remote_copy(
                src_ref=gsend, dst_ref=grecv.at[pl.ds(a * nz + b, 1)], send_sem=g_sem.at[0], recv_sem=g_sem.at[1],
                device_id={"gy": gy_at(a), "gz": gz_at(b)}, device_id_type=MESH).start()

    order = sorted(range(ny), key=lambda a: -min(a, ny - a))
    for a in order[:ny // 2]:
        send_gram(a)

    wait_all(recv1.at[pl.ds(1, ny - 1)], a1_sem.at[1])
    wait_all(recv1.at[pl.ds(1, ny - 1)], a1_sem.at[0])
    for g in range(nz):
        turned[g] = recv1[:, g, :]

    @functools.partial(each, nz, start=1)
    def _(delta):
        pltpu.make_async_remote_copy(
            src_ref=turned.at[gz_at(delta)], dst_ref=recv2.at[delta], send_sem=a2_sem.at[0], recv_sem=a2_sem.at[1],
            device_id={"gz": gz_at(delta)}, device_id_type=MESH).start()
    recv2[0] = turned[gz]

    for a in order[ny // 2:]:
        send_gram(a)

    wait_all(recv2.at[pl.ds(1, nz - 1)], a2_sem.at[1])
    wait_all(recv2.at[pl.ds(1, nz - 1)], a2_sem.at[0])
    picked[...] = recv2[...].reshape(number, 128).T
    digit = iota((16, 128), 0)
    left, right = [], []
    for r in range(SLOTS):
        number_r = picked[r:r + 1, :].astype(jnp.int32) - 1
        high = (number_r >> 4) == digit
        right.append(jnp.where((number_r & 15) == digit, 1.0, 0.0).astype(BF16))
        left.append(jnp.concatenate(
            [jnp.where(high, picked[SLOTS * (q + 1) + r:SLOTS * (q + 1) + r + 1, :], 0.0).astype(BF16) for q in range(6)], axis=0))
    bins = dot_nt(jnp.concatenate(left, axis=1), jnp.concatenate(right, axis=1))
    bins = bins[0:48] + bins[48:96]
    wide = jnp.where((iota((16, 256), 1) & 15) == iota((16, 256), 0), 1.0, 0.0).astype(BF16)
    bins = sum(dot(part_, wide) for part_ in pieces(bins))
    bins = jnp.where((iota((48, 256), 1) >> 4) == (iota((48, 256), 0) & 15), bins, 0.0)
    bin_sums = [jnp.sum(bins[16 * k:16 * k + 16], axis=0, keepdims=True) for k in range(3)]

    wait_all(grecv.at[pl.ds(1, number - 1)], g_sem.at[1])
    wait_all(grecv.at[pl.ds(1, number - 1)], g_sem.at[0])
    own = jnp.where(iota((8, 128), 0) == 0, gsend[...], grecv[0:8, :])
    for at in range(8, number, 8):
        own = own + grecv[at:at + 8, :]
    own = jnp.sum(own, axis=0, keepdims=True)
    for shift in (4, 2, 1):
        own = own + pltpu.roll(own, shift, axis=1)
    own = jnp.broadcast_to(own, (8, 128))
    splat = {}
    for e, (l, k) in enumerate(pairs):
        splat[l, k] = jnp.broadcast_to(own[:, 8 * e + 7:8 * e + 8], (8, 128))
    coeffs = solve([[splat[min(a, b), max(a, b)] for b in range(4)] for a in range(4)])

    sens = None
    for k in range(3):
        term = bin_sums[k] * jnp.concatenate([coeffs[k][0:1]] * (per_owner // 128), axis=1)
        sens = term if sens is None else sens + term
    small[0:1, :] = sens
    for k in range(3):
        small[8 + 8 * k:16 + 8 * k, :] = jnp.concatenate([coeffs[k]] * (per_owner // 128), axis=1)
    wait_all(basis.at[pl.ds(1, 2)], out_sem)


def combine(rs, held, small, adj_hbm, sens_hbm, result, sens, out_sem, sens_sem):
    sens[...] = small[0:1, :]
    put_sens = pltpu.make_async_copy(sens, sens_hbm, sens_sem)
    put_sens.start()
    full = [jnp.concatenate([small[8 + 8 * k:16 + 8 * k, :]] * 4, axis=0) for k in range(3)]

    def body(j, carry):
        for x in range(8):
            result[j, x] = full[0] * rs[j, x] + full[1] * held[0, j, x] + full[2] * held[1, j, x]
        pltpu.make_async_copy(result.at[j], adj_hbm.at[j], out_sem).start()
        return carry

    lax.fori_loop(0, VARS, body, 0)
    pltpu.make_async_copy(result, result, out_sem).wait()
    put_sens.wait()


def local(right_side, speeds, porosity, coupling, momentum, design_ids):
    ny = lax.axis_size("gy")
    nz = lax.axis_size("gz")
    _, nx, cy, cz = right_side.shape
    per_owner = design_ids.size // 4
    field = (VARS, nx, cy, cz)
    dma = pltpu.SemaphoreType.DMA
    hbm = pl.BlockSpec(memory_space=pltpu.HBM)
    held, small = pl.pallas_call(
        functools.partial(kernel, ny, nz, per_owner),
        out_shape=[jax.ShapeDtypeStruct((2,) + field, F32), jax.ShapeDtypeStruct((32, per_owner), F32)],
        in_specs=[hbm] * 6,
        out_specs=[pl.BlockSpec(memory_space=pl.ANY), pl.BlockSpec(memory_space=pltpu.VMEM)],
        scratch_shapes=[
            pltpu.VMEM((3,) + field, F32), pltpu.VMEM(field, F32), pltpu.VMEM(field, F32),
            pltpu.VMEM((3, nx, cy, cz), F32),
            pltpu.VMEM((nx, cy, cz), F32),
            pltpu.VMEM((3, nx, cy, cz), F32),
            pltpu.VMEM((240, 240), BF16),
            pltpu.VMEM((128, 128), F32),
            pltpu.VMEM((3 * VARS, cy, cz), F32), pltpu.VMEM((3 * VARS, cy, cz), F32),
            pltpu.VMEM((3, nx, cy, cz), F32), pltpu.VMEM((3, nx, cy, cz), F32),
            pltpu.VMEM((VARS, cy, cz), F32), pltpu.VMEM((VARS, cy, cz), F32),
            pltpu.VMEM((VARS, 2, 40, 128), F32), pltpu.VMEM((VARS, 2, 40, 128), F32),
            pltpu.VMEM((64, 128), F32),
            pltpu.VMEM((2, 224, 128), F32), pltpu.VMEM((2, 224, 128), F32), pltpu.VMEM((160, 128), F32), pltpu.VMEM((64, 128), F32),
            pltpu.VMEM((160, 128), F32), pltpu.VMEM((64, 128), F32), pltpu.VMEM((3, 160, 128), F32), pltpu.VMEM((3, 64, 128), F32),
            pltpu.VMEM((128, 128), F32), pltpu.VMEM((128, 128), F32),
            pltpu.VMEM((3, 2, cy, cz), F32),
            pltpu.VMEM((10, 8, 128), F32),
            pltpu.SMEM((VARS, 3, VARS), F32),
            pltpu.VMEM(design_ids.shape, jnp.int32),
            pltpu.VMEM((ny * nz, 1024), BF16),
            pltpu.VMEM((SLOTS, 1024), F32),
            pltpu.VMEM((8, 128), F32),
            pltpu.VMEM((8, 128), F32),
            pltpu.VMEM((128, 1024), BF16),
            pltpu.VMEM((ny, nz, 128), F32),
            pltpu.VMEM((ny, nz, 128), F32),
            pltpu.VMEM((nz, ny, 128), F32),
            pltpu.VMEM((nz, ny, 128), F32),
            pltpu.VMEM((128, 128), F32),
            pltpu.VMEM((1, 128), F32),
            pltpu.VMEM((ny * nz, 128), F32),
            dma((6,)), dma, dma((2, 4)), dma((2, 4)), dma((2,)), dma((2,)), dma((2,)), pltpu.SemaphoreType.REGULAR,
        ],
        compiler_params=pltpu.CompilerParams(
            collective_id=0, has_side_effects=True, vmem_limit_bytes=40 * 1024 * 1024),
    )(*[pltpu.with_memory_space_constraint(value, pltpu.HBM) for value in (
        right_side, speeds, porosity, coupling.transpose(1, 0, 2), momentum, design_ids)])
    adjoint, sensitivity = pl.pallas_call(
        combine,
        out_shape=[jax.ShapeDtypeStruct(field, F32), jax.ShapeDtypeStruct((1, per_owner), F32)],
        in_specs=[pl.BlockSpec(memory_space=pltpu.VMEM)] * 3,
        out_specs=[hbm, hbm],
        scratch_shapes=[pltpu.VMEM(field, F32), pltpu.VMEM((1, per_owner), F32), dma, dma],
        compiler_params=pltpu.CompilerParams(vmem_limit_bytes=24 * 1024 * 1024),
    )(right_side, held, small)
    return adjoint, sensitivity.reshape(per_owner)


def solution(mesh):
    in_specs = (
        P(None, None, "gy", "gz"),
        P(None, None, "gy", "gz"),
        P(None, "gy", "gz"),
        P(),
        P(None, None, "gy", "gz"),
        P(None, "gy", "gz"),
    )
    out_specs = (P(None, None, "gy", "gz"), P(("gy", "gz")))
    return jax.shard_map(local, mesh=mesh, in_specs=in_specs, out_specs=out_specs, check_vma=False)
```

```python
import functools

import jax
import jax.numpy as jnp
from jax import lax
from jax.experimental import pallas as pl
from jax.experimental.pallas import tpu as pltpu
from jax.sharding import PartitionSpec as P

PENALTY = 1.0
COURANT = 0.3
VARS = 5
SLOTS = 16
MESH = pl.DeviceIdType.MESH
F32 = jnp.float32
BF16 = jnp.bfloat16


def pieces(value):
    high = value.astype(BF16)
    rest = value - high.astype(F32)
    mid = rest.astype(BF16)
    low = (rest - mid.astype(F32)).astype(BF16)
    return high, mid, low


def dot(a, b):
    return jnp.dot(a, b, preferred_element_type=F32)


def dot_nt(a, b):
    return lax.dot_general(a, b, (((1,), (1,)), ((), ())), preferred_element_type=F32)


def iota(shape, axis):
    return lax.broadcasted_iota(jnp.int32, shape, axis)


def fold(product):
    rows = product[0:8] + product[8:16] + product[16:24] + product[24:32]
    return rows[:, 0:128] + rows[:, 128:256]


def solve(gram):
    low = [[None] * 4 for _ in range(4)]
    for col in range(4):
        diag = gram[col][col]
        for inner in range(col):
            diag = diag - low[col][inner] * low[col][inner]
        low[col][col] = jnp.sqrt(diag)
        for row in range(col + 1, 4):
            value = gram[row][col]
            for inner in range(col):
                value = value - low[row][inner] * low[col][inner]
            low[row][col] = value / low[col][col]
    zero = jnp.zeros_like(gram[0][0])
    upper = [[low[c][r] if c >= r else None for c in range(4)] for r in range(4)]

    def add(a, b):
        return b if a is None else (a if b is None else a + b)

    hess = [[add(upper[r][c + 1], upper[r][c]) for c in range(3)] for r in range(4)]

    def inner_sum(terms):
        total = None
        for a, b in terms:
            if a is not None and b is not None:
                total = add(total, a * b)
        return zero if total is None else total

    normal = [[inner_sum([(hess[r][a], hess[r][b]) for r in range(4)]) for b in range(3)] for a in range(3)]
    target = [inner_sum([(hess[r][a], upper[r][0]) for r in range(4)]) for a in range(3)]
    fac = [[None] * 3 for _ in range(3)]
    for col in range(3):
        diag = normal[col][col]
        for inner in range(col):
            diag = diag - fac[col][inner] * fac[col][inner]
        fac[col][col] = jnp.sqrt(diag)
        for row in range(col + 1, 3):
            value = normal[row][col]
            for inner in range(col):
                value = value - fac[row][inner] * fac[col][inner]
            fac[row][col] = value / fac[col][col]
    forward = []
    for place in range(3):
        value = target[place]
        for inner in range(place):
            value = value - fac[place][inner] * forward[inner]
        forward.append(value / fac[place][place])
    backward = [None] * 3
    for place in reversed(range(3)):
        value = forward[place]
        for inner in range(place + 1, 3):
            value = value - fac[inner][place] * backward[inner]
        backward[place] = value / fac[place][place]
    return backward


def kernel(ny, nz, per_owner,
           rs_hbm, sp_hbm, po_hbm, cp_hbm, mo_hbm, ids_hbm,
           held_hbm, small,
           basis, cur, nxt, sp, po, mo, wmat, wz, wa, wb, cpos, cneg, part, fprev, low_shift, high_shift, sface,
           halo_out, halo_in, yfix, zfix, ypart, zpart, yheld, zheld, corner, turn, block, prods, cp, ids_ref,
           owner_hot, rank_hot, owner_row, local_row, spread, dsend, recv1, turned, recv2, picked,
           gsend, grecv,
           in_sem, out_sem, halo_send, halo_recv, a1_sem, a2_sem, g_sem, known_sem):
    gy = lax.axis_index("gy")
    gz = lax.axis_index("gz")

    number = ny * nz

    def gy_at(delta):
        return (gy + (delta + ny)) & (ny - 1)

    def gz_at(delta):
        return (gz + (delta + nz)) & (nz - 1)

    def each(count, step, start=0, unroll=1):
        def body(t, carry):
            step(t)
            return carry
        lax.fori_loop(start, count, body, 0, unroll=unroll)

    barrier = pltpu.get_barrier_semaphore()

    def greet(target):
        pl.semaphore_signal(barrier, inc=1, device_id=target, device_id_type=MESH)

    for delta in (1, -1):
        greet({"gz": gz_at(delta)})
        greet({"gy": gy_at(delta)})

    loads = [pltpu.make_async_copy(src, dst, in_sem.at[place]) for place, (src, dst) in enumerate(
        [(sp_hbm, sp), (rs_hbm, nxt), (po_hbm, po), (mo_hbm, mo), (cp_hbm, cp), (ids_hbm, ids_ref)])]
    for place in (4, 0, 1):
        loads[place].start()

    @functools.partial(each, ny - 1, start=2)
    def _(delta):
        greet({"gy": gy_at(delta)})

    @functools.partial(each, nz - 1, start=2)
    def _(delta):
        greet({"gz": gz_at(delta)})

    for place in (2, 5, 3):
        loads[place].start()

    loads[4].wait()
    lane = iota((8, 128), 1)
    row = iota((8, 128), 0)
    wz[40:128, :] = jnp.zeros((88, 128), F32)

    @functools.partial(each, VARS)
    def _(i):
        value = jnp.zeros((8, 128), F32)
        for j in range(VARS):
            value = jnp.where((lane >> 3) == j, -COURANT * cp[i, 2, j], value)
        wz[pl.ds(pl.multiple_of(8 * i, 8), 8), :] = jnp.where((lane & 7) == row, value, 0.0)

    loads[0].wait()

    lanes = iota((32, 128), 1)
    near = jnp.zeros((32, 128), F32)
    far = jnp.zeros((32, 128), F32)
    for x in range(8):
        ends = pltpu.roll(jnp.where(lanes == 0, sp[2, x, :, 0:128], sp[2, x, :, 128:256]), x + 1, axis=1)
        near = jnp.where(lanes == x + 1, ends, near)
        far = jnp.where(lanes == x, ends, far)
    near = pltpu.roll(near, 127, axis=1)
    for side, face in ((0, jnp.maximum(near, 0.0)), (1, jnp.maximum(-far, 0.0))):
        total = face
        for i in range(1, VARS):
            total = jnp.where((lanes >> 3) == i, pltpu.roll(face, 8 * i, axis=1), total)
        sface[32 * side:32 * side + 32, :] = jnp.where(lanes < 8 * VARS, total, 0.0)

    inside = (gy > 0, gy < ny - 1, gz > 0, gz < nz - 1)

    YROWS = VARS * 16
    ZAT = 2 * YROWS

    def y_at(side, j, half):
        return side * YROWS + j * 16 + half * 8

    def in_rows(place):
        return pl.ds(place * YROWS, YROWS) if place < 2 else pl.ds(ZAT + 32 * (place - 2), 32)

    def send_halo(par):
        for place, (axis, delta) in enumerate((("y", -1), ("y", 1), ("z", -1), ("z", 1))):
            rows = in_rows(place)
            target = {"gy": gy_at(delta)} if axis == "y" else {"gz": gz_at(delta)}
            copy = pltpu.make_async_remote_copy(
                src_ref=halo_out.at[par, rows], dst_ref=halo_in.at[par, in_rows(place ^ 1)],
                send_sem=halo_send.at[par, place], recv_sem=halo_recv.at[par, place ^ 1],
                device_id=target, device_id_type=MESH)
            pl.when(inside[place])(copy.start)

    for place in range(4):
        @pl.when(jnp.logical_not(inside[place]))
        def _():
            for par in range(2):
                halo_in[par, in_rows(place), :] = jnp.zeros((YROWS if place < 2 else 32, 128), F32)

    def wait_all(ref, sem):
        pltpu.make_async_copy(ref, ref, sem).wait()

    halves = (slice(0, 128), slice(128, 256))

    def pack():
        near = jnp.zeros((32, 128), F32)
        far = jnp.zeros((32, 128), F32)
        for i in range(VARS):
            for x in range(8):
                s = i * 8 + x
                ends = jnp.where(lanes == 0, nxt[i, x, :, 0:128], nxt[i, x, :, 128:256])
                ends = pltpu.roll(ends, s + 1, axis=1)
                near = jnp.where(lanes == s + 1, ends, near)
                far = jnp.where(lanes == s, ends, far)
        zpart[0:32, :] = pltpu.roll(near, 127, axis=1)
        zpart[32:64, :] = far
        for side, y in ((0, 0), (1, 31)):
            for half in range(2):
                for i in range(VARS):
                    at = y_at(side, i, half)
                    ypart[at:at + 8, :] = nxt[i, :, y, halves[half]]

    lane8 = iota((8, 128), 1)
    rows32 = iota((32, 128), 0)

    def y_corners():
        for side in range(2):
            for i in range(VARS):
                corner[side * 64 + i * 8:side * 64 + i * 8 + 8, :] = jnp.where(
                    lane8 == 0, yfix[y_at(side, i, 0):y_at(side, i, 0) + 8, :],
                    yfix[y_at(side, i, 1):y_at(side, i, 1) + 8, :])
        turn[...] = corner[...].T
        parts = []
        for at in (0, 127):
            both = jnp.broadcast_to(turn[at:at + 1, :], (32, 128))
            parts.append(jnp.where(rows32 == 0, both, jnp.where(rows32 == 31, pltpu.roll(both, 64, axis=1), 0.0)))
        return jnp.where(jnp.concatenate([lanes, lanes], axis=0) < 8 * VARS, jnp.concatenate(parts, axis=0), 0.0)

    def finish(k, par):
        faces = zpart[...] + zfix[...] + y_corners()
        zheld[k] = faces
        halo_out[par, ZAT:ZAT + 64, :] = jnp.dot(
            faces * sface[...], wz[...], preferred_element_type=F32, precision=lax.Precision.HIGHEST)
        turned_z = jnp.concatenate([zfix[...], jnp.zeros((64, 128), F32)], axis=0).T
        for side, y in ((0, 0), (1, 31)):
            for half in range(2):
                speed = sp[1, :, y, halves[half]]
                speed = jnp.maximum(speed, 0.0) if side == 0 else jnp.maximum(-speed, 0.0)
                flux = []
                for i in range(VARS):
                    extra = turned_z[8 * i:8 * i + 8]
                    shift = ((0, 95), (97, 64))[side][half]
                    extra = pltpu.roll(extra, shift, axis=1) if shift else extra
                    at = y_at(side, i, half)
                    value = ypart[at:at + 8, :] + yfix[at:at + 8, :] + jnp.where(lane8 == 127 * half, extra, 0.0)
                    yheld[k, at:at + 8, :] = value
                    flux.append(value * speed)
                for j in range(VARS):
                    total = flux[0] * (-COURANT * cp[0, 1, j])
                    for i in range(1, VARS):
                        total = total + flux[i] * (-COURANT * cp[i, 1, j])
                    at = y_at(side, j, half)
                    halo_out[par, at:at + 8, :] = total

    def settle(k):
        even = (lanes & 1) == 0
        near_columns = zfix[0:32, :]
        far_columns = pltpu.roll(zfix[32:64, :], 127, axis=1)
        columns = [jnp.where(even, near_columns, far_columns), jnp.where(even, far_columns, near_columns)]
        row8 = iota((8, 128), 0)
        for i in range(VARS):
            for x in range(8):
                s = i * 8 + x
                fix = pltpu.roll(columns[s & 1], 128 - s, axis=1) if s else columns[0]
                for half in range(2):
                    at = y_at(0, i, half) + x
                    top = jnp.where(row8 == 0, yfix[at:at + 1, :], 0.0)
                    at = y_at(1, i, half) + x
                    bottom = jnp.where(row8 == 7, yfix[at:at + 1, :], 0.0)
                    side = jnp.where(lanes == 127 * half, fix, 0.0)
                    value = jnp.concatenate([
                        nxt[i, x, 0:8, halves[half]] + top, nxt[i, x, 8:24, halves[half]],
                        nxt[i, x, 24:32, halves[half]] + bottom], axis=0) + side
                    cur[i, x, :, halves[half]] = value
                    basis[k, i, x, :, halves[half]] = value

    def receive(par):
        for place in range(4):
            @pl.when(inside[place])
            def _():
                ref = halo_in.at[par, in_rows(place)]
                wait_all(ref, halo_recv.at[par, place])
                wait_all(ref, halo_send.at[par, place])
        yfix[0:YROWS, :] = halo_in[par, 0:YROWS, :] - halo_out[par, YROWS:ZAT, :]
        yfix[YROWS:ZAT, :] = halo_in[par, YROWS:ZAT, :] - halo_out[par, 0:YROWS, :]
        zfix[0:32, :] = halo_in[par, ZAT:ZAT + 32, :] - halo_out[par, ZAT + 32:ZAT + 64, :]
        zfix[32:64, :] = halo_in[par, ZAT + 32:ZAT + 64, :] - halo_out[par, ZAT:ZAT + 32, :]

    def prepare():
        @functools.partial(each, 8)
        def _(x):
            for d in range(3):
                s = sp[d, x]
                cpos[d, x] = jnp.maximum(s, 0.0)
                cneg[d, x] = jnp.maximum(-s, 0.0)

        lane = iota((16, 256), 1)
        row = iota((16, 256), 0)
        group = lane >> 4
        piece = jnp.where(group >= 10, 2, jnp.where(group >= 5, 1, 0))
        which = group - 5 * piece
        same = (lane & 15) == row

        @functools.partial(each, 3 * VARS)
        def _(place):
            d = lax.div(place, VARS)
            j = place - d * VARS
            value = jnp.zeros((16, 256), F32)
            for i in range(VARS):
                value = jnp.where(which == i, COURANT * cp[i, d, j], value)
            high = value.astype(BF16).astype(F32)
            value = jnp.where(same, jnp.where(piece == 2, value - high, high), 0.0)
            wmat[pl.ds(pl.multiple_of(place * 16, 16), 16), :] = value[:, 0:240].astype(BF16)

    def rank_slots():
        loads[5].wait()
        ids = jnp.concatenate([ids_ref[0], ids_ref[1]], axis=1)
        owners = lax.div(ids, per_owner)
        local_row[...] = (ids - owners * per_owner + 1).astype(F32)
        tri = jnp.where(iota((256, 128), 0) < jnp.where(iota((256, 128), 0) >= 128, 256, iota((256, 128), 1)), 1.0, 0.0).astype(BF16)
        sub = iota((number, 128), 0)
        before = jnp.zeros((number, 128), F32)
        for p in range(8):
            hot = jnp.where(sub == owners[p:p + 1, :], 1.0, 0.0)
            hot16 = hot.astype(BF16)
            count = dot(jnp.concatenate([hot16, before.astype(BF16)], axis=1), tri)
            before = before + hot
            owner_hot[:, p * 128:(p + 1) * 128] = hot16
            rank = jnp.sum(hot * count, axis=0, keepdims=True)
            rank_hot[:, p * 128:(p + 1) * 128] = jnp.where(rank == iota((SLOTS, 128), 0).astype(F32), 1.0, 0.0)


    def couple(x, w):
        for h in (0, 16):
            high, low = [], []
            for i in range(VARS):
                v = cur[i, x, h:h + 16, :]
                top = v.astype(BF16)
                high.append(top)
                low.append((v - top.astype(F32)).astype(BF16))
            out = dot(wmat[...], jnp.concatenate(high + low + high, axis=0))
            for place in range(3 * VARS):
                w[place, h:h + 16, :] = out[place * 16:place * 16 + 16]

    def stencil(x, w):
        prior = jnp.maximum(x - 1, 0)
        for j in range(VARS):
            wx = w[j]
            flux = cpos[0, x] * wx - fprev[j]
            nxt[j, prior] = part[j] - flux
            fprev[j] = cneg[0, x] * wx
            acc = po[x] * cur[j, x] + flux
            wv = w[2 * VARS + j]
            flux = cpos[2, x] * wv - pltpu.roll(cneg[2, x] * wv, 1, axis=1)
            acc = acc + flux - pltpu.roll(flux, 255, axis=1)
            for half in range(2):
                at = halves[half]
                wy = w[VARS + j, :, at]
                minus = cneg[1, x, :, at] * wy
                low_shift[j, half, 8:40, :] = minus
                low_shift[j, half, 0:8, :] = minus[24:32]
                flux = cpos[1, x, :, at] * wy - low_shift[j, half, 7:39, :]
                high_shift[j, half, 0:32, :] = flux
                high_shift[j, half, 32:40, :] = flux[0:8]
                part[j, :, at] = acc[:, at] + flux - high_shift[j, half, 1:33, :]

    def sweep():
        fprev[...] = jnp.zeros(fprev.shape, F32)
        couple(0, wa)

        @functools.partial(each, 4)
        def _(t):
            x = 2 * t
            couple(x + 1, wb)
            stencil(x, wa)
            couple(jnp.minimum(x + 2, 7), wa)
            stencil(x + 1, wb)

        for j in range(VARS):
            nxt[j, 7] = part[j] + fprev[j]

    def dispatch():
        loads[3].wait()

        @functools.partial(each, 2)
        def _(half_x):
            for k in range(3):
                total = None
                for x in range(4):
                    for i in range(3):
                        term = basis[k, 1 + i, 4 * half_x + x] * mo[i, 4 * half_x + x]
                        total = term if total is None else total + term
                block[k, half_x] = total

        low8 = iota((16, 192), 0)
        col = iota((16, 192), 1)
        within = jnp.where(col >= 96, col - 96, col) & 31
        half = jnp.where(col >= 96, 1, 0)
        ysel = jnp.where((low8 >> 3 == half) & ((low8 & 7) == (within >> 2)), 1.0, 0.0).astype(BF16)
        zrow = iota((512, 128), 0)
        zsel = jnp.where(((zrow & 255) >> 2) + (zrow >> 8) * 64 == iota((512, 128), 1), 1.0, 0.0).astype(BF16)
        parts = []
        for k in range(3):
            t = dot(ysel, jnp.concatenate(list(pieces(block[k, 0])) + list(pieces(block[k, 1])), axis=0))
            for part_ in pieces(jnp.concatenate([t[0:8], t[8:16]], axis=1)):
                parts.append(part_.astype(F32))
        t = dot(jnp.concatenate(parts, axis=0).astype(BF16), zsel)
        values = [-PENALTY * (t[24 * k:24 * k + 8] + t[24 * k + 8:24 * k + 16] + t[24 * k + 16:24 * k + 24])
                  for k in range(3)]
        tops = [value.astype(BF16).astype(F32) for value in values]
        rests = [value - top for value, top in zip(values, tops)]
        empty = jnp.zeros((SLOTS, 128), BF16)
        for p in range(8):
            hot = rank_hot[:, p * 128:(p + 1) * 128]
            rows = [local_row[...]] + tops + rests
            rows = [(hot * value[p:p + 1, :]).astype(BF16) for value in rows]
            spread[:, p * 128:(p + 1) * 128] = jnp.concatenate(rows + [empty], axis=0)
        dsend[...] = dot_nt(owner_hot[...], spread[...]).reshape(ny, nz, 128)

        @functools.partial(each, ny, start=1)
        def _(delta):
            pltpu.make_async_remote_copy(
                src_ref=dsend.at[gy_at(delta)], dst_ref=recv1.at[delta],
                send_sem=a1_sem.at[0], recv_sem=a1_sem.at[1],
                device_id={"gy": gy_at(delta)}, device_id_type=MESH).start()
        recv1[0] = dsend[gy]

    pairs = [(l, k) for k in range(4) for l in range(k + 1)]

    def products(entries, vectors):
        def body(x, sums):
            sums = list(sums)
            for j in range(VARS):
                v = [nxt[j, x] if k == 3 else basis[k, j, x] for k in range(vectors)]
                for place, e in enumerate(entries):
                    l, k = pairs[e]
                    sums[place] = sums[place] + fold(v[l] * v[k])
            return tuple(sums)

        sums = lax.fori_loop(0, 8, body, tuple(jnp.zeros((8, 128), F32) for _ in entries))
        for place, e in enumerate(entries):
            prods[e] = sums[place]

    def corrections():
        sums = [jnp.zeros((8, 128), F32) for _ in range(4)]
        for at in range(0, 2 * YROWS, 8):
            add = yfix[at:at + 8, :]
            for l in range(3):
                sums[l] = sums[l] + yheld[l, at:at + 8, :] * add
            sums[3] = sums[3] + (2.0 * ypart[at:at + 8, :] + add) * add
        both = y_corners()
        for at in range(0, 64, 8):
            add = zfix[at:at + 8, :]
            for l in range(3):
                sums[l] = sums[l] + zheld[l, at:at + 8, :] * add
            sums[3] = sums[3] + (2.0 * (zpart[at:at + 8, :] + both[at:at + 8]) + add) * add
        for l in range(4):
            prods[6 + l] = prods[6 + l] + sums[l]

    yfix[...] = jnp.zeros(yfix.shape, F32)
    zfix[...] = jnp.zeros(zfix.shape, F32)
    corner[...] = jnp.zeros(corner.shape, F32)
    loads[1].wait()

    @functools.partial(each, 4)
    def _(k):
        par = k & 1
        pack()

        @pl.when(k == 3)
        def _():
            products((6, 7, 8, 9), 4)

        @pl.when(k > 0)
        def _():
            receive(1 - par)

        @pl.when(k == 3)
        def _():
            corrections()

        @pl.when(k < 3)
        def _():
            finish(k, par)

            @pl.when(k == 0)
            def _():
                pl.semaphore_wait(barrier, (ny - 1) + (nz - 1))

            send_halo(par)

            @pl.when(k == 0)
            def _():
                @functools.partial(each, nz, start=1)
                def _(delta):
                    pl.semaphore_signal(known_sem, inc=1, device_id={"gz": gz_at(delta)}, device_id_type=MESH)

            settle(k)

            @pl.when(k > 0)
            def _():
                pltpu.make_async_copy(basis.at[k], held_hbm.at[k - 1], out_sem).start()

            @pl.when(k == 0)
            def _():
                prepare()
                loads[2].wait()

            @pl.when(k == 1)
            def _():
                products((0, 1, 2), 2)
                rank_slots()

            @pl.when(k == 2)
            def _():
                dispatch()
                products((3, 4, 5), 3)

            sweep()

    sums = [prods[e] for e in range(10)]

    lane = iota((8, 128), 1)
    packed = jnp.zeros((8, 128), F32)
    for e, value in enumerate(sums):
        for shift in (64, 32, 16, 8):
            value = value + pltpu.roll(value, shift, axis=1)
        packed = jnp.where((lane >> 3) == e, value, packed)
    gsend[...] = jnp.sum(packed, axis=0, keepdims=True)

    pl.semaphore_wait(known_sem, nz - 1)

    def send_gram(a):
        row = gy_at(a)

        @functools.partial(each, nz, start=0 if a else 1, unroll=8 if a else 5)
        def _(b):
            pltpu.make_async_remote_copy(
                src_ref=gsend, dst_ref=grecv.at[pl.ds(a * nz + b, 1)], send_sem=g_sem.at[0], recv_sem=g_sem.at[1],
                device_id={"gy": row, "gz": gz_at(b)}, device_id_type=MESH).start()

    order = sorted(range(ny), key=lambda a: -min(a, ny - a))
    for a in order[:ny // 2]:
        send_gram(a)

    wait_all(recv1.at[pl.ds(1, ny - 1)], a1_sem.at[1])
    wait_all(recv1.at[pl.ds(1, ny - 1)], a1_sem.at[0])
    for g in range(nz):
        turned[g] = recv1[:, g, :]

    @functools.partial(each, nz, start=1)
    def _(delta):
        pltpu.make_async_remote_copy(
            src_ref=turned.at[gz_at(delta)], dst_ref=recv2.at[delta], send_sem=a2_sem.at[0], recv_sem=a2_sem.at[1],
            device_id={"gz": gz_at(delta)}, device_id_type=MESH).start()
    recv2[0] = turned[gz]

    for a in order[ny // 2:]:
        send_gram(a)

    wait_all(recv2.at[pl.ds(1, nz - 1)], a2_sem.at[1])
    wait_all(recv2.at[pl.ds(1, nz - 1)], a2_sem.at[0])
    picked[...] = recv2[...].reshape(number, 128).T
    digit = iota((16, 128), 0)
    left, right = [], []
    for r in range(SLOTS):
        number_r = picked[r:r + 1, :].astype(jnp.int32) - 1
        high = (number_r >> 4) == digit
        right.append(jnp.where((number_r & 15) == digit, 1.0, 0.0).astype(BF16))
        left.append(jnp.concatenate(
            [jnp.where(high, picked[SLOTS * (q + 1) + r:SLOTS * (q + 1) + r + 1, :], 0.0).astype(BF16) for q in range(6)], axis=0))
    bins = dot_nt(jnp.concatenate(left, axis=1), jnp.concatenate(right, axis=1))
    bins = bins[0:48] + bins[48:96]
    wide = jnp.where((iota((16, 256), 1) & 15) == iota((16, 256), 0), 1.0, 0.0).astype(BF16)
    bins = sum(dot(part_, wide) for part_ in pieces(bins))
    bins = jnp.where((iota((48, 256), 1) >> 4) == (iota((48, 256), 0) & 15), bins, 0.0)
    bin_sums = [jnp.sum(bins[16 * k:16 * k + 16], axis=0, keepdims=True) for k in range(3)]

    wait_all(grecv.at[pl.ds(1, number - 1)], g_sem.at[1])
    wait_all(grecv.at[pl.ds(1, number - 1)], g_sem.at[0])
    own = jnp.where(iota((8, 128), 0) == 0, gsend[...], grecv[0:8, :])
    for at in range(8, number, 8):
        own = own + grecv[at:at + 8, :]
    own = jnp.sum(own, axis=0, keepdims=True)
    for shift in (4, 2, 1):
        own = own + pltpu.roll(own, shift, axis=1)
    own = jnp.broadcast_to(own, (8, 128))
    splat = {}
    for e, (l, k) in enumerate(pairs):
        splat[l, k] = jnp.broadcast_to(own[:, 8 * e + 7:8 * e + 8], (8, 128))
    coeffs = solve([[splat[min(a, b), max(a, b)] for b in range(4)] for a in range(4)])

    sens = None
    for k in range(3):
        term = bin_sums[k] * jnp.concatenate([coeffs[k][0:1]] * (per_owner // 128), axis=1)
        sens = term if sens is None else sens + term
    small[0:1, :] = sens
    for k in range(3):
        small[8 + 8 * k:16 + 8 * k, :] = jnp.concatenate([coeffs[k]] * (per_owner // 128), axis=1)
    wait_all(basis.at[pl.ds(1, 2)], out_sem)


def combine(rs, held, small, adj_hbm, sens_hbm, result, sens, out_sem, sens_sem):
    sens[...] = small[0:1, :]
    put_sens = pltpu.make_async_copy(sens, sens_hbm, sens_sem)
    put_sens.start()
    full = [jnp.concatenate([small[8 + 8 * k:16 + 8 * k, :]] * 4, axis=0) for k in range(3)]

    def body(j, carry):
        for x in range(8):
            result[j, x] = full[0] * rs[j, x] + full[1] * held[0, j, x] + full[2] * held[1, j, x]
        pltpu.make_async_copy(result.at[j], adj_hbm.at[j], out_sem).start()
        return carry

    lax.fori_loop(0, VARS, body, 0)
    pltpu.make_async_copy(result, result, out_sem).wait()
    put_sens.wait()


def local(right_side, speeds, porosity, coupling, momentum, design_ids):
    ny = lax.axis_size("gy")
    nz = lax.axis_size("gz")
    _, nx, cy, cz = right_side.shape
    per_owner = design_ids.size // 4
    field = (VARS, nx, cy, cz)
    dma = pltpu.SemaphoreType.DMA
    hbm = pl.BlockSpec(memory_space=pltpu.HBM)
    held, small = pl.pallas_call(
        functools.partial(kernel, ny, nz, per_owner),
        out_shape=[jax.ShapeDtypeStruct((2,) + field, F32), jax.ShapeDtypeStruct((32, per_owner), F32)],
        in_specs=[hbm] * 6,
        out_specs=[pl.BlockSpec(memory_space=pl.ANY), pl.BlockSpec(memory_space=pltpu.VMEM)],
        scratch_shapes=[
            pltpu.VMEM((3,) + field, F32), pltpu.VMEM(field, F32), pltpu.VMEM(field, F32),
            pltpu.VMEM((3, nx, cy, cz), F32),
            pltpu.VMEM((nx, cy, cz), F32),
            pltpu.VMEM((3, nx, cy, cz), F32),
            pltpu.VMEM((240, 240), BF16),
            pltpu.VMEM((128, 128), F32),
            pltpu.VMEM((3 * VARS, cy, cz), F32), pltpu.VMEM((3 * VARS, cy, cz), F32),
            pltpu.VMEM((3, nx, cy, cz), F32), pltpu.VMEM((3, nx, cy, cz), F32),
            pltpu.VMEM((VARS, cy, cz), F32), pltpu.VMEM((VARS, cy, cz), F32),
            pltpu.VMEM((VARS, 2, 40, 128), F32), pltpu.VMEM((VARS, 2, 40, 128), F32),
            pltpu.VMEM((64, 128), F32),
            pltpu.VMEM((2, 224, 128), F32), pltpu.VMEM((2, 224, 128), F32), pltpu.VMEM((160, 128), F32), pltpu.VMEM((64, 128), F32),
            pltpu.VMEM((160, 128), F32), pltpu.VMEM((64, 128), F32), pltpu.VMEM((3, 160, 128), F32), pltpu.VMEM((3, 64, 128), F32),
            pltpu.VMEM((128, 128), F32), pltpu.VMEM((128, 128), F32),
            pltpu.VMEM((3, 2, cy, cz), F32),
            pltpu.VMEM((10, 8, 128), F32),
            pltpu.SMEM((VARS, 3, VARS), F32),
            pltpu.VMEM(design_ids.shape, jnp.int32),
            pltpu.VMEM((ny * nz, 1024), BF16),
            pltpu.VMEM((SLOTS, 1024), F32),
            pltpu.VMEM((8, 128), F32),
            pltpu.VMEM((8, 128), F32),
            pltpu.VMEM((128, 1024), BF16),
            pltpu.VMEM((ny, nz, 128), F32),
            pltpu.VMEM((ny, nz, 128), F32),
            pltpu.VMEM((nz, ny, 128), F32),
            pltpu.VMEM((nz, ny, 128), F32),
            pltpu.VMEM((128, 128), F32),
            pltpu.VMEM((1, 128), F32),
            pltpu.VMEM((ny * nz, 128), F32),
            dma((6,)), dma, dma((2, 4)), dma((2, 4)), dma((2,)), dma((2,)), dma((2,)), pltpu.SemaphoreType.REGULAR,
        ],
        compiler_params=pltpu.CompilerParams(
            collective_id=0, has_side_effects=True, vmem_limit_bytes=40 * 1024 * 1024),
    )(*[pltpu.with_memory_space_constraint(value, pltpu.HBM) for value in (
        right_side, speeds, porosity, coupling.transpose(1, 0, 2), momentum, design_ids)])
    adjoint, sensitivity = pl.pallas_call(
        combine,
        out_shape=[jax.ShapeDtypeStruct(field, F32), jax.ShapeDtypeStruct((1, per_owner), F32)],
        in_specs=[pl.BlockSpec(memory_space=pltpu.VMEM)] * 3,
        out_specs=[hbm, hbm],
        scratch_shapes=[pltpu.VMEM(field, F32), pltpu.VMEM((1, per_owner), F32), dma, dma],
        compiler_params=pltpu.CompilerParams(vmem_limit_bytes=24 * 1024 * 1024),
    )(right_side, held, small)
    return adjoint, sensitivity.reshape(per_owner)


def solution(mesh):
    in_specs = (
        P(None, None, "gy", "gz"),
        P(None, None, "gy", "gz"),
        P(None, "gy", "gz"),
        P(),
        P(None, None, "gy", "gz"),
        P(None, "gy", "gz"),
    )
    out_specs = (P(None, None, "gy", "gz"), P(("gy", "gz")))
    return jax.shard_map(local, mesh=mesh, in_specs=in_specs, out_specs=out_specs, check_vma=False)
```

```python
import functools

import jax
import jax.numpy as jnp
from jax import lax
from jax.experimental import pallas as pl
from jax.experimental.pallas import tpu as pltpu
from jax.sharding import PartitionSpec as P

PENALTY = 1.0
COURANT = 0.3
VARS = 5
SLOTS = 16
MESH = pl.DeviceIdType.MESH
F32 = jnp.float32
BF16 = jnp.bfloat16


def pieces(value):
    high = value.astype(BF16)
    rest = value - high.astype(F32)
    mid = rest.astype(BF16)
    low = (rest - mid.astype(F32)).astype(BF16)
    return high, mid, low


def dot(a, b):
    return jnp.dot(a, b, preferred_element_type=F32)


def dot_nt(a, b):
    return lax.dot_general(a, b, (((1,), (1,)), ((), ())), preferred_element_type=F32)


def iota(shape, axis):
    return lax.broadcasted_iota(jnp.int32, shape, axis)


def fold(product):
    rows = product[0:8] + product[8:16] + product[16:24] + product[24:32]
    return rows[:, 0:128] + rows[:, 128:256]


def solve(gram):
    low = [[None] * 4 for _ in range(4)]
    for col in range(4):
        diag = gram[col][col]
        for inner in range(col):
            diag = diag - low[col][inner] * low[col][inner]
        low[col][col] = jnp.sqrt(diag)
        for row in range(col + 1, 4):
            value = gram[row][col]
            for inner in range(col):
                value = value - low[row][inner] * low[col][inner]
            low[row][col] = value / low[col][col]
    zero = jnp.zeros_like(gram[0][0])
    upper = [[low[c][r] if c >= r else None for c in range(4)] for r in range(4)]

    def add(a, b):
        return b if a is None else (a if b is None else a + b)

    hess = [[add(upper[r][c + 1], upper[r][c]) for c in range(3)] for r in range(4)]

    def inner_sum(terms):
        total = None
        for a, b in terms:
            if a is not None and b is not None:
                total = add(total, a * b)
        return zero if total is None else total

    normal = [[inner_sum([(hess[r][a], hess[r][b]) for r in range(4)]) for b in range(3)] for a in range(3)]
    target = [inner_sum([(hess[r][a], upper[r][0]) for r in range(4)]) for a in range(3)]
    fac = [[None] * 3 for _ in range(3)]
    for col in range(3):
        diag = normal[col][col]
        for inner in range(col):
            diag = diag - fac[col][inner] * fac[col][inner]
        fac[col][col] = jnp.sqrt(diag)
        for row in range(col + 1, 3):
            value = normal[row][col]
            for inner in range(col):
                value = value - fac[row][inner] * fac[col][inner]
            fac[row][col] = value / fac[col][col]
    forward = []
    for place in range(3):
        value = target[place]
        for inner in range(place):
            value = value - fac[place][inner] * forward[inner]
        forward.append(value / fac[place][place])
    backward = [None] * 3
    for place in reversed(range(3)):
        value = forward[place]
        for inner in range(place + 1, 3):
            value = value - fac[inner][place] * backward[inner]
        backward[place] = value / fac[place][place]
    return backward


def kernel(ny, nz, per_owner,
           rs_hbm, sp_hbm, po_hbm, cp_hbm, mo_hbm, ids_hbm,
           held_hbm, small,
           basis, cur, nxt, sp, po, mo, wmat, wz, wa, wb, cpos, cneg, part, fprev, low_shift, high_shift, sface,
           halo_out, halo_in, yfix, zfix, ypart, zpart, yheld, zheld, corner, turn, block, prods, cp, ids_ref,
           owner_hot, rank_hot, owner_row, local_row, spread, dsend, recv1, turned, recv2, picked,
           gsend, grecv,
           in_sem, out_sem, halo_send, halo_recv, a1_sem, a2_sem, g_sem, known_sem):
    gy = lax.axis_index("gy")
    gz = lax.axis_index("gz")

    number = ny * nz

    def gy_at(delta):
        return (gy + (delta + ny)) & (ny - 1)

    def gz_at(delta):
        return (gz + (delta + nz)) & (nz - 1)

    def each(count, step, start=0, unroll=1):
        def body(t, carry):
            step(t)
            return carry
        lax.fori_loop(start, count, body, 0, unroll=unroll)

    barrier = pltpu.get_barrier_semaphore()

    def greet(target):
        pl.semaphore_signal(barrier, inc=1, device_id=target, device_id_type=MESH)

    for delta in (1, -1):
        greet({"gz": gz_at(delta)})
        greet({"gy": gy_at(delta)})

    loads = [pltpu.make_async_copy(src, dst, in_sem.at[place]) for place, (src, dst) in enumerate(
        [(sp_hbm, sp), (rs_hbm, nxt), (po_hbm, po), (mo_hbm, mo), (cp_hbm, cp), (ids_hbm, ids_ref)])]
    for place in (4, 5, 0, 1):
        loads[place].start()

    @functools.partial(each, ny - 1, start=2)
    def _(delta):
        greet({"gy": gy_at(delta)})

    @functools.partial(each, nz - 1, start=2)
    def _(delta):
        greet({"gz": gz_at(delta)})

    for place in (2, 3):
        loads[place].start()

    loads[4].wait()
    lane = iota((8, 128), 1)
    row = iota((8, 128), 0)
    wz[40:128, :] = jnp.zeros((88, 128), F32)

    @functools.partial(each, VARS)
    def _(i):
        value = jnp.zeros((8, 128), F32)
        for j in range(VARS):
            value = jnp.where((lane >> 3) == j, -COURANT * cp[i, 2, j], value)
        wz[pl.ds(pl.multiple_of(8 * i, 8), 8), :] = jnp.where((lane & 7) == row, value, 0.0)

    lane = iota((16, 256), 1)
    row = iota((16, 256), 0)
    group = lane >> 4
    piece = jnp.where(group >= 10, 2, jnp.where(group >= 5, 1, 0))
    which = group - 5 * piece
    same = (lane & 15) == row

    @functools.partial(each, 3 * VARS)
    def _(place):
        d = lax.div(place, VARS)
        j = place - d * VARS
        value = jnp.zeros((16, 256), F32)
        for i in range(VARS):
            value = jnp.where(which == i, COURANT * cp[i, d, j], value)
        high = value.astype(BF16).astype(F32)
        value = jnp.where(same, jnp.where(piece == 2, value - high, high), 0.0)
        wmat[pl.ds(pl.multiple_of(place * 16, 16), 16), :] = value[:, 0:240].astype(BF16)

    loads[5].wait()
    ids = jnp.concatenate([ids_ref[0], ids_ref[1]], axis=1)
    owners = lax.div(ids, per_owner)
    local_row[...] = (ids - owners * per_owner + 1).astype(F32)
    tri = jnp.where(iota((256, 128), 0) < jnp.where(iota((256, 128), 0) >= 128, 256, iota((256, 128), 1)), 1.0, 0.0).astype(BF16)
    sub = iota((number, 128), 0)
    before = jnp.zeros((number, 128), F32)
    for p in range(8):
        hot = jnp.where(sub == owners[p:p + 1, :], 1.0, 0.0)
        hot16 = hot.astype(BF16)
        count = dot(jnp.concatenate([hot16, before.astype(BF16)], axis=1), tri)
        before = before + hot
        owner_hot[:, p * 128:(p + 1) * 128] = hot16
        rank = jnp.sum(hot * count, axis=0, keepdims=True)
        rank_hot[:, p * 128:(p + 1) * 128] = jnp.where(rank == iota((SLOTS, 128), 0).astype(F32), 1.0, 0.0)

    loads[0].wait()

    lanes = iota((32, 128), 1)
    near = jnp.zeros((32, 128), F32)
    far = jnp.zeros((32, 128), F32)
    for x in range(8):
        ends = pltpu.roll(jnp.where(lanes == 0, sp[2, x, :, 0:128], sp[2, x, :, 128:256]), x + 1, axis=1)
        near = jnp.where(lanes == x + 1, ends, near)
        far = jnp.where(lanes == x, ends, far)
    near = pltpu.roll(near, 127, axis=1)
    for side, face in ((0, jnp.maximum(near, 0.0)), (1, jnp.maximum(-far, 0.0))):
        total = face
        for i in range(1, VARS):
            total = jnp.where((lanes >> 3) == i, pltpu.roll(face, 8 * i, axis=1), total)
        sface[32 * side:32 * side + 32, :] = jnp.where(lanes < 8 * VARS, total, 0.0)

    inside = (gy > 0, gy < ny - 1, gz > 0, gz < nz - 1)

    YROWS = VARS * 16
    ZAT = 2 * YROWS

    def y_at(side, j, half):
        return side * YROWS + j * 16 + half * 8

    def in_rows(place):
        return pl.ds(place * YROWS, YROWS) if place < 2 else pl.ds(ZAT + 32 * (place - 2), 32)

    def send_halo(par):
        for place, (axis, delta) in enumerate((("y", -1), ("y", 1), ("z", -1), ("z", 1))):
            rows = in_rows(place)
            target = {"gy": gy_at(delta)} if axis == "y" else {"gz": gz_at(delta)}
            copy = pltpu.make_async_remote_copy(
                src_ref=halo_out.at[par, rows], dst_ref=halo_in.at[par, in_rows(place ^ 1)],
                send_sem=halo_send.at[par, place], recv_sem=halo_recv.at[par, place ^ 1],
                device_id=target, device_id_type=MESH)
            pl.when(inside[place])(copy.start)

    for place in range(4):
        @pl.when(jnp.logical_not(inside[place]))
        def _():
            for par in range(2):
                halo_in[par, in_rows(place), :] = jnp.zeros((YROWS if place < 2 else 32, 128), F32)

    def wait_all(ref, sem):
        pltpu.make_async_copy(ref, ref, sem).wait()

    halves = (slice(0, 128), slice(128, 256))

    def pack():
        near = jnp.zeros((32, 128), F32)
        far = jnp.zeros((32, 128), F32)
        for i in range(VARS):
            for x in range(8):
                s = i * 8 + x
                ends = jnp.where(lanes == 0, nxt[i, x, :, 0:128], nxt[i, x, :, 128:256])
                ends = pltpu.roll(ends, s + 1, axis=1)
                near = jnp.where(lanes == s + 1, ends, near)
                far = jnp.where(lanes == s, ends, far)
        zpart[0:32, :] = pltpu.roll(near, 127, axis=1)
        zpart[32:64, :] = far
        for side, y in ((0, 0), (1, 31)):
            for half in range(2):
                for i in range(VARS):
                    at = y_at(side, i, half)
                    ypart[at:at + 8, :] = nxt[i, :, y, halves[half]]

    lane8 = iota((8, 128), 1)
    rows32 = iota((32, 128), 0)

    def y_corners():
        for side in range(2):
            for i in range(VARS):
                corner[side * 64 + i * 8:side * 64 + i * 8 + 8, :] = jnp.where(
                    lane8 == 0, yfix[y_at(side, i, 0):y_at(side, i, 0) + 8, :],
                    yfix[y_at(side, i, 1):y_at(side, i, 1) + 8, :])
        turn[...] = corner[...].T
        parts = []
        for at in (0, 127):
            both = jnp.broadcast_to(turn[at:at + 1, :], (32, 128))
            parts.append(jnp.where(rows32 == 0, both, jnp.where(rows32 == 31, pltpu.roll(both, 64, axis=1), 0.0)))
        return jnp.where(jnp.concatenate([lanes, lanes], axis=0) < 8 * VARS, jnp.concatenate(parts, axis=0), 0.0)

    def finish(k, par):
        faces = zpart[...] + zfix[...] + y_corners()
        zheld[k] = faces
        halo_out[par, ZAT:ZAT + 64, :] = jnp.dot(
            faces * sface[...], wz[...], preferred_element_type=F32, precision=lax.Precision.HIGHEST)
        turned_z = jnp.concatenate([zfix[...], jnp.zeros((64, 128), F32)], axis=0).T
        for side, y in ((0, 0), (1, 31)):
            for half in range(2):
                speed = sp[1, :, y, halves[half]]
                speed = jnp.maximum(speed, 0.0) if side == 0 else jnp.maximum(-speed, 0.0)
                flux = []
                for i in range(VARS):
                    extra = turned_z[8 * i:8 * i + 8]
                    shift = ((0, 95), (97, 64))[side][half]
                    extra = pltpu.roll(extra, shift, axis=1) if shift else extra
                    at = y_at(side, i, half)
                    value = ypart[at:at + 8, :] + yfix[at:at + 8, :] + jnp.where(lane8 == 127 * half, extra, 0.0)
                    yheld[k, at:at + 8, :] = value
                    flux.append(value * speed)
                for j in range(VARS):
                    total = flux[0] * (-COURANT * cp[0, 1, j])
                    for i in range(1, VARS):
                        total = total + flux[i] * (-COURANT * cp[i, 1, j])
                    at = y_at(side, j, half)
                    halo_out[par, at:at + 8, :] = total

    def settle(k):
        even = (lanes & 1) == 0
        near_columns = zfix[0:32, :]
        far_columns = pltpu.roll(zfix[32:64, :], 127, axis=1)
        columns = [jnp.where(even, near_columns, far_columns), jnp.where(even, far_columns, near_columns)]
        row8 = iota((8, 128), 0)
        for i in range(VARS):
            for x in range(8):
                s = i * 8 + x
                fix = pltpu.roll(columns[s & 1], 128 - s, axis=1) if s else columns[0]
                for half in range(2):
                    at = y_at(0, i, half) + x
                    top = jnp.where(row8 == 0, yfix[at:at + 1, :], 0.0)
                    at = y_at(1, i, half) + x
                    bottom = jnp.where(row8 == 7, yfix[at:at + 1, :], 0.0)
                    side = jnp.where(lanes == 127 * half, fix, 0.0)
                    value = jnp.concatenate([
                        nxt[i, x, 0:8, halves[half]] + top, nxt[i, x, 8:24, halves[half]],
                        nxt[i, x, 24:32, halves[half]] + bottom], axis=0) + side
                    cur[i, x, :, halves[half]] = value
                    basis[k, i, x, :, halves[half]] = value

    def receive(par):
        for place in range(4):
            @pl.when(inside[place])
            def _():
                ref = halo_in.at[par, in_rows(place)]
                wait_all(ref, halo_recv.at[par, place])
                wait_all(ref, halo_send.at[par, place])
        yfix[0:YROWS, :] = halo_in[par, 0:YROWS, :] - halo_out[par, YROWS:ZAT, :]
        yfix[YROWS:ZAT, :] = halo_in[par, YROWS:ZAT, :] - halo_out[par, 0:YROWS, :]
        zfix[0:32, :] = halo_in[par, ZAT:ZAT + 32, :] - halo_out[par, ZAT + 32:ZAT + 64, :]
        zfix[32:64, :] = halo_in[par, ZAT + 32:ZAT + 64, :] - halo_out[par, ZAT:ZAT + 32, :]

    def prepare():
        @functools.partial(each, 8)
        def _(x):
            for d in range(3):
                s = sp[d, x]
                cpos[d, x] = jnp.maximum(s, 0.0)
                cneg[d, x] = jnp.maximum(-s, 0.0)

    def couple(x, w):
        for h in (0, 16):
            high, low = [], []
            for i in range(VARS):
                v = cur[i, x, h:h + 16, :]
                top = v.astype(BF16)
                high.append(top)
                low.append((v - top.astype(F32)).astype(BF16))
            out = dot(wmat[...], jnp.concatenate(high + low + high, axis=0))
            for place in range(3 * VARS):
                w[place, h:h + 16, :] = out[place * 16:place * 16 + 16]

    def stencil(x, w):
        prior = jnp.maximum(x - 1, 0)
        for j in range(VARS):
            wx = w[j]
            flux = cpos[0, x] * wx - fprev[j]
            nxt[j, prior] = part[j] - flux
            fprev[j] = cneg[0, x] * wx
            acc = po[x] * cur[j, x] + flux
            wv = w[2 * VARS + j]
            flux = cpos[2, x] * wv - pltpu.roll(cneg[2, x] * wv, 1, axis=1)
            acc = acc + flux - pltpu.roll(flux, 255, axis=1)
            for half in range(2):
                at = halves[half]
                wy = w[VARS + j, :, at]
                minus = cneg[1, x, :, at] * wy
                low_shift[j, half, 8:40, :] = minus
                low_shift[j, half, 0:8, :] = minus[24:32]
                flux = cpos[1, x, :, at] * wy - low_shift[j, half, 7:39, :]
                high_shift[j, half, 0:32, :] = flux
                high_shift[j, half, 32:40, :] = flux[0:8]
                part[j, :, at] = acc[:, at] + flux - high_shift[j, half, 1:33, :]

    def sweep():
        fprev[...] = jnp.zeros(fprev.shape, F32)
        couple(0, wa)

        @functools.partial(each, 4)
        def _(t):
            x = 2 * t
            couple(x + 1, wb)
            stencil(x, wa)
            couple(jnp.minimum(x + 2, 7), wa)
            stencil(x + 1, wb)

        for j in range(VARS):
            nxt[j, 7] = part[j] + fprev[j]

    def dispatch():
        loads[3].wait()

        @functools.partial(each, 2)
        def _(half_x):
            for k in range(3):
                total = None
                for x in range(4):
                    for i in range(3):
                        term = basis[k, 1 + i, 4 * half_x + x] * mo[i, 4 * half_x + x]
                        total = term if total is None else total + term
                block[k, half_x] = total

        low8 = iota((16, 192), 0)
        col = iota((16, 192), 1)
        within = jnp.where(col >= 96, col - 96, col) & 31
        half = jnp.where(col >= 96, 1, 0)
        ysel = jnp.where((low8 >> 3 == half) & ((low8 & 7) == (within >> 2)), 1.0, 0.0).astype(BF16)
        zrow = iota((512, 128), 0)
        zsel = jnp.where(((zrow & 255) >> 2) + (zrow >> 8) * 64 == iota((512, 128), 1), 1.0, 0.0).astype(BF16)
        parts = []
        for k in range(3):
            t = dot(ysel, jnp.concatenate(list(pieces(block[k, 0])) + list(pieces(block[k, 1])), axis=0))
            for part_ in pieces(jnp.concatenate([t[0:8], t[8:16]], axis=1)):
                parts.append(part_.astype(F32))
        t = dot(jnp.concatenate(parts, axis=0).astype(BF16), zsel)
        values = [-PENALTY * (t[24 * k:24 * k + 8] + t[24 * k + 8:24 * k + 16] + t[24 * k + 16:24 * k + 24])
                  for k in range(3)]
        tops = [value.astype(BF16).astype(F32) for value in values]
        rests = [value - top for value, top in zip(values, tops)]
        empty = jnp.zeros((SLOTS, 128), BF16)
        for p in range(8):
            hot = rank_hot[:, p * 128:(p + 1) * 128]
            rows = [local_row[...]] + tops + rests
            rows = [(hot * value[p:p + 1, :]).astype(BF16) for value in rows]
            spread[:, p * 128:(p + 1) * 128] = jnp.concatenate(rows + [empty], axis=0)
        dsend[...] = dot_nt(owner_hot[...], spread[...]).reshape(ny, nz, 128)

        @functools.partial(each, ny, start=1)
        def _(delta):
            pltpu.make_async_remote_copy(
                src_ref=dsend.at[gy_at(delta)], dst_ref=recv1.at[delta],
                send_sem=a1_sem.at[0], recv_sem=a1_sem.at[1],
                device_id={"gy": gy_at(delta)}, device_id_type=MESH).start()
        recv1[0] = dsend[gy]

    pairs = [(l, k) for k in range(4) for l in range(k + 1)]

    def products(entries, vectors):
        def body(x, sums):
            sums = list(sums)
            for j in range(VARS):
                v = [nxt[j, x] if k == 3 else basis[k, j, x] for k in range(vectors)]
                for place, e in enumerate(entries):
                    l, k = pairs[e]
                    sums[place] = sums[place] + fold(v[l] * v[k])
            return tuple(sums)

        sums = lax.fori_loop(0, 8, body, tuple(jnp.zeros((8, 128), F32) for _ in entries))
        for place, e in enumerate(entries):
            prods[e] = sums[place]

    def corrections():
        sums = [jnp.zeros((8, 128), F32) for _ in range(4)]
        for at in range(0, 2 * YROWS, 8):
            add = yfix[at:at + 8, :]
            for l in range(3):
                sums[l] = sums[l] + yheld[l, at:at + 8, :] * add
            sums[3] = sums[3] + (2.0 * ypart[at:at + 8, :] + add) * add
        both = y_corners()
        for at in range(0, 64, 8):
            add = zfix[at:at + 8, :]
            for l in range(3):
                sums[l] = sums[l] + zheld[l, at:at + 8, :] * add
            sums[3] = sums[3] + (2.0 * (zpart[at:at + 8, :] + both[at:at + 8]) + add) * add
        for l in range(4):
            prods[6 + l] = prods[6 + l] + sums[l]

    yfix[...] = jnp.zeros(yfix.shape, F32)
    zfix[...] = jnp.zeros(zfix.shape, F32)
    corner[...] = jnp.zeros(corner.shape, F32)
    loads[1].wait()

    @functools.partial(each, 4)
    def _(k):
        par = k & 1
        pack()

        @pl.when(k == 3)
        def _():
            products((6, 7, 8, 9), 4)

        @pl.when(k > 0)
        def _():
            receive(1 - par)

        @pl.when(k == 3)
        def _():
            corrections()

        @pl.when(k < 3)
        def _():
            finish(k, par)

            @pl.when(k == 0)
            def _():
                pl.semaphore_wait(barrier, (ny - 1) + (nz - 1))

            send_halo(par)

            @pl.when(k == 0)
            def _():
                @functools.partial(each, nz, start=1)
                def _(delta):
                    pl.semaphore_signal(known_sem, inc=1, device_id={"gz": gz_at(delta)}, device_id_type=MESH)

            settle(k)

            @pl.when(k > 0)
            def _():
                pltpu.make_async_copy(basis.at[k], held_hbm.at[k - 1], out_sem).start()

            @pl.when(k == 0)
            def _():
                prepare()
                loads[2].wait()

            @pl.when(k == 1)
            def _():
                products((0, 1, 2), 2)

            @pl.when(k == 2)
            def _():
                dispatch()
                products((3, 4, 5), 3)

            sweep()

    sums = [prods[e] for e in range(10)]

    lane = iota((8, 128), 1)
    packed = jnp.zeros((8, 128), F32)
    for e, value in enumerate(sums):
        for shift in (64, 32, 16, 8):
            value = value + pltpu.roll(value, shift, axis=1)
        packed = jnp.where((lane >> 3) == e, value, packed)
    gsend[...] = jnp.sum(packed, axis=0, keepdims=True)

    pl.semaphore_wait(known_sem, nz - 1)

    def send_gram(a):
        row = gy_at(a)

        @functools.partial(each, nz, start=0 if a else 1, unroll=8 if a else 5)
        def _(b):
            pltpu.make_async_remote_copy(
                src_ref=gsend, dst_ref=grecv.at[pl.ds(a * nz + b, 1)], send_sem=g_sem.at[0], recv_sem=g_sem.at[1],
                device_id={"gy": row, "gz": gz_at(b)}, device_id_type=MESH).start()

    order = sorted(range(ny), key=lambda a: -min(a, ny - a))
    for a in order[:ny // 2]:
        send_gram(a)

    wait_all(recv1.at[pl.ds(1, ny - 1)], a1_sem.at[1])
    wait_all(recv1.at[pl.ds(1, ny - 1)], a1_sem.at[0])
    for g in range(nz):
        turned[g] = recv1[:, g, :]

    @functools.partial(each, nz, start=1)
    def _(delta):
        pltpu.make_async_remote_copy(
            src_ref=turned.at[gz_at(delta)], dst_ref=recv2.at[delta], send_sem=a2_sem.at[0], recv_sem=a2_sem.at[1],
            device_id={"gz": gz_at(delta)}, device_id_type=MESH).start()
    recv2[0] = turned[gz]

    for a in order[ny // 2:]:
        send_gram(a)

    wait_all(recv2.at[pl.ds(1, nz - 1)], a2_sem.at[1])
    wait_all(recv2.at[pl.ds(1, nz - 1)], a2_sem.at[0])
    picked[...] = recv2[...].reshape(number, 128).T
    digit = iota((16, 128), 0)
    left, right = [], []
    for r in range(SLOTS):
        number_r = picked[r:r + 1, :].astype(jnp.int32) - 1
        high = (number_r >> 4) == digit
        right.append(jnp.where((number_r & 15) == digit, 1.0, 0.0).astype(BF16))
        left.append(jnp.concatenate(
            [jnp.where(high, picked[SLOTS * (q + 1) + r:SLOTS * (q + 1) + r + 1, :], 0.0).astype(BF16) for q in range(6)], axis=0))
    bins = dot_nt(jnp.concatenate(left, axis=1), jnp.concatenate(right, axis=1))
    bins = bins[0:48] + bins[48:96]
    wide = jnp.where((iota((16, 256), 1) & 15) == iota((16, 256), 0), 1.0, 0.0).astype(BF16)
    bins = sum(dot(part_, wide) for part_ in pieces(bins))
    bins = jnp.where((iota((48, 256), 1) >> 4) == (iota((48, 256), 0) & 15), bins, 0.0)
    bin_sums = [jnp.sum(bins[16 * k:16 * k + 16], axis=0, keepdims=True) for k in range(3)]

    wait_all(grecv.at[pl.ds(1, number - 1)], g_sem.at[1])
    wait_all(grecv.at[pl.ds(1, number - 1)], g_sem.at[0])
    own = jnp.where(iota((8, 128), 0) == 0, gsend[...], grecv[0:8, :])
    for at in range(8, number, 8):
        own = own + grecv[at:at + 8, :]
    own = jnp.sum(own, axis=0, keepdims=True)
    for shift in (4, 2, 1):
        own = own + pltpu.roll(own, shift, axis=1)
    own = jnp.broadcast_to(own, (8, 128))
    splat = {}
    for e, (l, k) in enumerate(pairs):
        splat[l, k] = jnp.broadcast_to(own[:, 8 * e + 7:8 * e + 8], (8, 128))
    coeffs = solve([[splat[min(a, b), max(a, b)] for b in range(4)] for a in range(4)])

    sens = None
    for k in range(3):
        term = bin_sums[k] * jnp.concatenate([coeffs[k][0:1]] * (per_owner // 128), axis=1)
        sens = term if sens is None else sens + term
    small[0:1, :] = sens
    for k in range(3):
        small[8 + 8 * k:16 + 8 * k, :] = jnp.concatenate([coeffs[k]] * (per_owner // 128), axis=1)
    wait_all(basis.at[pl.ds(1, 2)], out_sem)


def combine(rs, held, small, adj_hbm, sens_hbm, result, sens, out_sem, sens_sem):
    sens[...] = small[0:1, :]
    put_sens = pltpu.make_async_copy(sens, sens_hbm, sens_sem)
    put_sens.start()
    full = [jnp.concatenate([small[8 + 8 * k:16 + 8 * k, :]] * 4, axis=0) for k in range(3)]

    def body(j, carry):
        for x in range(8):
            result[j, x] = full[0] * rs[j, x] + full[1] * held[0, j, x] + full[2] * held[1, j, x]
        pltpu.make_async_copy(result.at[j], adj_hbm.at[j], out_sem).start()
        return carry

    lax.fori_loop(0, VARS, body, 0)
    pltpu.make_async_copy(result, result, out_sem).wait()
    put_sens.wait()


def local(right_side, speeds, porosity, coupling, momentum, design_ids):
    ny = lax.axis_size("gy")
    nz = lax.axis_size("gz")
    _, nx, cy, cz = right_side.shape
    per_owner = design_ids.size // 4
    field = (VARS, nx, cy, cz)
    dma = pltpu.SemaphoreType.DMA
    hbm = pl.BlockSpec(memory_space=pltpu.HBM)
    held, small = pl.pallas_call(
        functools.partial(kernel, ny, nz, per_owner),
        out_shape=[jax.ShapeDtypeStruct((2,) + field, F32), jax.ShapeDtypeStruct((32, per_owner), F32)],
        in_specs=[hbm] * 6,
        out_specs=[pl.BlockSpec(memory_space=pl.ANY), pl.BlockSpec(memory_space=pltpu.VMEM)],
        scratch_shapes=[
            pltpu.VMEM((3,) + field, F32), pltpu.VMEM(field, F32), pltpu.VMEM(field, F32),
            pltpu.VMEM((3, nx, cy, cz), F32),
            pltpu.VMEM((nx, cy, cz), F32),
            pltpu.VMEM((3, nx, cy, cz), F32),
            pltpu.VMEM((240, 240), BF16),
            pltpu.VMEM((128, 128), F32),
            pltpu.VMEM((3 * VARS, cy, cz), F32), pltpu.VMEM((3 * VARS, cy, cz), F32),
            pltpu.VMEM((3, nx, cy, cz), F32), pltpu.VMEM((3, nx, cy, cz), F32),
            pltpu.VMEM((VARS, cy, cz), F32), pltpu.VMEM((VARS, cy, cz), F32),
            pltpu.VMEM((VARS, 2, 40, 128), F32), pltpu.VMEM((VARS, 2, 40, 128), F32),
            pltpu.VMEM((64, 128), F32),
            pltpu.VMEM((2, 224, 128), F32), pltpu.VMEM((2, 224, 128), F32), pltpu.VMEM((160, 128), F32), pltpu.VMEM((64, 128), F32),
            pltpu.VMEM((160, 128), F32), pltpu.VMEM((64, 128), F32), pltpu.VMEM((3, 160, 128), F32), pltpu.VMEM((3, 64, 128), F32),
            pltpu.VMEM((128, 128), F32), pltpu.VMEM((128, 128), F32),
            pltpu.VMEM((3, 2, cy, cz), F32),
            pltpu.VMEM((10, 8, 128), F32),
            pltpu.SMEM((VARS, 3, VARS), F32),
            pltpu.VMEM(design_ids.shape, jnp.int32),
            pltpu.VMEM((ny * nz, 1024), BF16),
            pltpu.VMEM((SLOTS, 1024), F32),
            pltpu.VMEM((8, 128), F32),
            pltpu.VMEM((8, 128), F32),
            pltpu.VMEM((128, 1024), BF16),
            pltpu.VMEM((ny, nz, 128), F32),
            pltpu.VMEM((ny, nz, 128), F32),
            pltpu.VMEM((nz, ny, 128), F32),
            pltpu.VMEM((nz, ny, 128), F32),
            pltpu.VMEM((128, 128), F32),
            pltpu.VMEM((1, 128), F32),
            pltpu.VMEM((ny * nz, 128), F32),
            dma((6,)), dma, dma((2, 4)), dma((2, 4)), dma((2,)), dma((2,)), dma((2,)), pltpu.SemaphoreType.REGULAR,
        ],
        compiler_params=pltpu.CompilerParams(
            collective_id=0, has_side_effects=True, vmem_limit_bytes=40 * 1024 * 1024),
    )(*[pltpu.with_memory_space_constraint(value, pltpu.HBM) for value in (
        right_side, speeds, porosity, coupling.transpose(1, 0, 2), momentum, design_ids)])
    adjoint, sensitivity = pl.pallas_call(
        combine,
        out_shape=[jax.ShapeDtypeStruct(field, F32), jax.ShapeDtypeStruct((1, per_owner), F32)],
        in_specs=[pl.BlockSpec(memory_space=pltpu.VMEM)] * 3,
        out_specs=[hbm, hbm],
        scratch_shapes=[pltpu.VMEM(field, F32), pltpu.VMEM((1, per_owner), F32), dma, dma],
        compiler_params=pltpu.CompilerParams(vmem_limit_bytes=24 * 1024 * 1024),
    )(right_side, held, small)
    return adjoint, sensitivity.reshape(per_owner)


def solution(mesh):
    in_specs = (
        P(None, None, "gy", "gz"),
        P(None, None, "gy", "gz"),
        P(None, "gy", "gz"),
        P(),
        P(None, None, "gy", "gz"),
        P(None, "gy", "gz"),
    )
    out_specs = (P(None, None, "gy", "gz"), P(("gy", "gz")))
    return jax.shard_map(local, mesh=mesh, in_specs=in_specs, out_specs=out_specs, check_vma=False)
```

```python
import functools

import jax
import jax.numpy as jnp
from jax import lax
from jax.experimental import pallas as pl
from jax.experimental.pallas import tpu as pltpu
from jax.sharding import PartitionSpec as P

PENALTY = 1.0
COURANT = 0.3
VARS = 5
SLOTS = 16
MESH = pl.DeviceIdType.MESH
F32 = jnp.float32
BF16 = jnp.bfloat16


def pieces(value):
    high = value.astype(BF16)
    rest = value - high.astype(F32)
    mid = rest.astype(BF16)
    low = (rest - mid.astype(F32)).astype(BF16)
    return high, mid, low


def dot(a, b):
    return jnp.dot(a, b, preferred_element_type=F32)


def dot_nt(a, b):
    return lax.dot_general(a, b, (((1,), (1,)), ((), ())), preferred_element_type=F32)


def iota(shape, axis):
    return lax.broadcasted_iota(jnp.int32, shape, axis)


def fold(product):
    rows = product[0:8] + product[8:16] + product[16:24] + product[24:32]
    return rows[:, 0:128] + rows[:, 128:256]


def solve(gram):
    low = [[None] * 4 for _ in range(4)]
    for col in range(4):
        diag = gram[col][col]
        for inner in range(col):
            diag = diag - low[col][inner] * low[col][inner]
        low[col][col] = jnp.sqrt(diag)
        for row in range(col + 1, 4):
            value = gram[row][col]
            for inner in range(col):
                value = value - low[row][inner] * low[col][inner]
            low[row][col] = value / low[col][col]
    zero = jnp.zeros_like(gram[0][0])
    upper = [[low[c][r] if c >= r else None for c in range(4)] for r in range(4)]

    def add(a, b):
        return b if a is None else (a if b is None else a + b)

    hess = [[add(upper[r][c + 1], upper[r][c]) for c in range(3)] for r in range(4)]

    def inner_sum(terms):
        total = None
        for a, b in terms:
            if a is not None and b is not None:
                total = add(total, a * b)
        return zero if total is None else total

    normal = [[inner_sum([(hess[r][a], hess[r][b]) for r in range(4)]) for b in range(3)] for a in range(3)]
    target = [inner_sum([(hess[r][a], upper[r][0]) for r in range(4)]) for a in range(3)]
    fac = [[None] * 3 for _ in range(3)]
    for col in range(3):
        diag = normal[col][col]
        for inner in range(col):
            diag = diag - fac[col][inner] * fac[col][inner]
        fac[col][col] = jnp.sqrt(diag)
        for row in range(col + 1, 3):
            value = normal[row][col]
            for inner in range(col):
                value = value - fac[row][inner] * fac[col][inner]
            fac[row][col] = value / fac[col][col]
    forward = []
    for place in range(3):
        value = target[place]
        for inner in range(place):
            value = value - fac[place][inner] * forward[inner]
        forward.append(value / fac[place][place])
    backward = [None] * 3
    for place in reversed(range(3)):
        value = forward[place]
        for inner in range(place + 1, 3):
            value = value - fac[inner][place] * backward[inner]
        backward[place] = value / fac[place][place]
    return backward


def kernel(ny, nz, per_owner,
           rs_hbm, sp_hbm, po_hbm, cp_hbm, mo_hbm, ids_hbm,
           held_hbm, small,
           basis, cur, nxt, sp, po, mo, wmat, wz, wa, wb, cpos, cneg, part, fprev, low_shift, high_shift, sface,
           halo_out, halo_in, yfix, zfix, ypart, zpart, yheld, zheld, corner, turn, block, prods, cp, ids_ref,
           owner_hot, rank_hot, owner_row, local_row, spread, dsend, recv1, turned, recv2, picked,
           gsend, grecv,
           in_sem, out_sem, halo_send, halo_recv, a1_sem, a2_sem, g_sem, known_sem):
    gy = lax.axis_index("gy")
    gz = lax.axis_index("gz")

    number = ny * nz

    def gy_at(delta):
        return (gy + (delta + ny)) & (ny - 1)

    def gz_at(delta):
        return (gz + (delta + nz)) & (nz - 1)

    def each(count, step, start=0, unroll=1):
        def body(t, carry):
            step(t)
            return carry
        lax.fori_loop(start, count, body, 0, unroll=unroll)

    barrier = pltpu.get_barrier_semaphore()

    def greet(target):
        pl.semaphore_signal(barrier, inc=1, device_id=target, device_id_type=MESH)

    for delta in (1, -1):
        greet({"gz": gz_at(delta)})
        greet({"gy": gy_at(delta)})

    loads = [pltpu.make_async_copy(src, dst, in_sem.at[place]) for place, (src, dst) in enumerate(
        [(sp_hbm, sp), (rs_hbm, basis.at[0]), (po_hbm, po), (mo_hbm, mo), (cp_hbm, cp), (ids_hbm, ids_ref)]
        + [(rs_hbm.at[i], cur.at[i]) for i in range(VARS)])]
    for place in [4, 5, 0] + list(range(6, 6 + VARS)):
        loads[place].start()

    @functools.partial(each, ny - 1, start=2)
    def _(delta):
        greet({"gy": gy_at(delta)})

    @functools.partial(each, nz - 1, start=2)
    def _(delta):
        greet({"gz": gz_at(delta)})

    for place in (2, 1, 3):
        loads[place].start()

    loads[4].wait()
    lane = iota((8, 128), 1)
    row = iota((8, 128), 0)
    wz[40:128, :] = jnp.zeros((88, 128), F32)

    @functools.partial(each, VARS)
    def _(i):
        value = jnp.zeros((8, 128), F32)
        for j in range(VARS):
            value = jnp.where((lane >> 3) == j, -COURANT * cp[i, 2, j], value)
        wz[pl.ds(pl.multiple_of(8 * i, 8), 8), :] = jnp.where((lane & 7) == row, value, 0.0)

    lane = iota((16, 256), 1)
    row = iota((16, 256), 0)
    group = lane >> 4
    piece = jnp.where(group >= 10, 2, jnp.where(group >= 5, 1, 0))
    which = group - 5 * piece
    same = (lane & 15) == row

    @functools.partial(each, 3 * VARS)
    def _(place):
        d = lax.div(place, VARS)
        j = place - d * VARS
        value = jnp.zeros((16, 256), F32)
        for i in range(VARS):
            value = jnp.where(which == i, COURANT * cp[i, d, j], value)
        high = value.astype(BF16).astype(F32)
        value = jnp.where(same, jnp.where(piece == 2, value - high, high), 0.0)
        wmat[pl.ds(pl.multiple_of(place * 16, 16), 16), :] = value[:, 0:240].astype(BF16)

    loads[5].wait()
    ids = jnp.concatenate([ids_ref[0], ids_ref[1]], axis=1)
    owners = lax.div(ids, per_owner)
    local_row[...] = (ids - owners * per_owner + 1).astype(F32)
    tri = jnp.where(iota((256, 128), 0) < jnp.where(iota((256, 128), 0) >= 128, 256, iota((256, 128), 1)), 1.0, 0.0).astype(BF16)
    sub = iota((number, 128), 0)
    before = jnp.zeros((number, 128), F32)
    for p in range(8):
        hot = jnp.where(sub == owners[p:p + 1, :], 1.0, 0.0)
        hot16 = hot.astype(BF16)
        count = dot(jnp.concatenate([hot16, before.astype(BF16)], axis=1), tri)
        before = before + hot
        owner_hot[:, p * 128:(p + 1) * 128] = hot16
        rank = jnp.sum(hot * count, axis=0, keepdims=True)
        rank_hot[:, p * 128:(p + 1) * 128] = jnp.where(rank == iota((SLOTS, 128), 0).astype(F32), 1.0, 0.0)

    loads[0].wait()

    lanes = iota((32, 128), 1)
    near = jnp.zeros((32, 128), F32)
    far = jnp.zeros((32, 128), F32)
    for x in range(8):
        ends = pltpu.roll(jnp.where(lanes == 0, sp[2, x, :, 0:128], sp[2, x, :, 128:256]), x + 1, axis=1)
        near = jnp.where(lanes == x + 1, ends, near)
        far = jnp.where(lanes == x, ends, far)
    near = pltpu.roll(near, 127, axis=1)
    for side, face in ((0, jnp.maximum(near, 0.0)), (1, jnp.maximum(-far, 0.0))):
        total = face
        for i in range(1, VARS):
            total = jnp.where((lanes >> 3) == i, pltpu.roll(face, 8 * i, axis=1), total)
        sface[32 * side:32 * side + 32, :] = jnp.where(lanes < 8 * VARS, total, 0.0)

    inside = (gy > 0, gy < ny - 1, gz > 0, gz < nz - 1)

    YROWS = VARS * 16
    ZAT = 2 * YROWS

    def y_at(side, j, half):
        return side * YROWS + j * 16 + half * 8

    def in_rows(place):
        return pl.ds(place * YROWS, YROWS) if place < 2 else pl.ds(ZAT + 32 * (place - 2), 32)

    def send_halo(par):
        for place, (axis, delta) in enumerate((("y", -1), ("y", 1), ("z", -1), ("z", 1))):
            rows = in_rows(place)
            target = {"gy": gy_at(delta)} if axis == "y" else {"gz": gz_at(delta)}
            copy = pltpu.make_async_remote_copy(
                src_ref=halo_out.at[par, rows], dst_ref=halo_in.at[par, in_rows(place ^ 1)],
                send_sem=halo_send.at[par, place], recv_sem=halo_recv.at[par, place ^ 1],
                device_id=target, device_id_type=MESH)
            pl.when(inside[place])(copy.start)

    for place in range(4):
        @pl.when(jnp.logical_not(inside[place]))
        def _():
            for par in range(2):
                halo_in[par, in_rows(place), :] = jnp.zeros((YROWS if place < 2 else 32, 128), F32)

    def wait_all(ref, sem):
        pltpu.make_async_copy(ref, ref, sem).wait()

    halves = (slice(0, 128), slice(128, 256))

    def pack(src, arrive=None):
        near = jnp.zeros((32, 128), F32)
        far = jnp.zeros((32, 128), F32)
        for i in range(VARS):
            if arrive is not None:
                arrive(i)
            for x in range(8):
                s = i * 8 + x
                ends = jnp.where(lanes == 0, src[i, x, :, 0:128], src[i, x, :, 128:256])
                ends = pltpu.roll(ends, s + 1, axis=1)
                near = jnp.where(lanes == s + 1, ends, near)
                far = jnp.where(lanes == s, ends, far)
        zpart[0:32, :] = pltpu.roll(near, 127, axis=1)
        zpart[32:64, :] = far
        for side, y in ((0, 0), (1, 31)):
            for half in range(2):
                for i in range(VARS):
                    at = y_at(side, i, half)
                    ypart[at:at + 8, :] = src[i, :, y, halves[half]]

    lane8 = iota((8, 128), 1)
    rows32 = iota((32, 128), 0)

    def y_corners():
        for side in range(2):
            for i in range(VARS):
                corner[side * 64 + i * 8:side * 64 + i * 8 + 8, :] = jnp.where(
                    lane8 == 0, yfix[y_at(side, i, 0):y_at(side, i, 0) + 8, :],
                    yfix[y_at(side, i, 1):y_at(side, i, 1) + 8, :])
        turn[...] = corner[...].T
        parts = []
        for at in (0, 127):
            both = jnp.broadcast_to(turn[at:at + 1, :], (32, 128))
            parts.append(jnp.where(rows32 == 0, both, jnp.where(rows32 == 31, pltpu.roll(both, 64, axis=1), 0.0)))
        return jnp.where(jnp.concatenate([lanes, lanes], axis=0) < 8 * VARS, jnp.concatenate(parts, axis=0), 0.0)

    def finish(k, par, fixed=True):
        faces = zpart[...] + zfix[...] + y_corners() if fixed else zpart[...]
        zheld[k] = faces
        halo_out[par, ZAT:ZAT + 64, :] = jnp.dot(
            faces * sface[...], wz[...], preferred_element_type=F32, precision=lax.Precision.HIGHEST)
        if fixed:
            turned_z = jnp.concatenate([zfix[...], jnp.zeros((64, 128), F32)], axis=0).T
        for side, y in ((0, 0), (1, 31)):
            for half in range(2):
                speed = sp[1, :, y, halves[half]]
                speed = jnp.maximum(speed, 0.0) if side == 0 else jnp.maximum(-speed, 0.0)
                flux = []
                for i in range(VARS):
                    at = y_at(side, i, half)
                    value = ypart[at:at + 8, :]
                    if fixed:
                        extra = turned_z[8 * i:8 * i + 8]
                        shift = ((0, 95), (97, 64))[side][half]
                        extra = pltpu.roll(extra, shift, axis=1) if shift else extra
                        value = value + yfix[at:at + 8, :] + jnp.where(lane8 == 127 * half, extra, 0.0)
                    yheld[k, at:at + 8, :] = value
                    flux.append(value * speed)
                for j in range(VARS):
                    total = flux[0] * (-COURANT * cp[0, 1, j])
                    for i in range(1, VARS):
                        total = total + flux[i] * (-COURANT * cp[i, 1, j])
                    at = y_at(side, j, half)
                    halo_out[par, at:at + 8, :] = total

    def settle(k):
        even = (lanes & 1) == 0
        near_columns = zfix[0:32, :]
        far_columns = pltpu.roll(zfix[32:64, :], 127, axis=1)
        columns = [jnp.where(even, near_columns, far_columns), jnp.where(even, far_columns, near_columns)]
        row8 = iota((8, 128), 0)
        for i in range(VARS):
            for x in range(8):
                s = i * 8 + x
                fix = pltpu.roll(columns[s & 1], 128 - s, axis=1) if s else columns[0]
                for half in range(2):
                    at = y_at(0, i, half) + x
                    top = jnp.where(row8 == 0, yfix[at:at + 1, :], 0.0)
                    at = y_at(1, i, half) + x
                    bottom = jnp.where(row8 == 7, yfix[at:at + 1, :], 0.0)
                    side = jnp.where(lanes == 127 * half, fix, 0.0)
                    value = jnp.concatenate([
                        nxt[i, x, 0:8, halves[half]] + top, nxt[i, x, 8:24, halves[half]],
                        nxt[i, x, 24:32, halves[half]] + bottom], axis=0) + side
                    cur[i, x, :, halves[half]] = value
                    basis[k, i, x, :, halves[half]] = value

    def receive(par):
        for place in range(4):
            @pl.when(inside[place])
            def _():
                ref = halo_in.at[par, in_rows(place)]
                wait_all(ref, halo_recv.at[par, place])
                wait_all(ref, halo_send.at[par, place])
        yfix[0:YROWS, :] = halo_in[par, 0:YROWS, :] - halo_out[par, YROWS:ZAT, :]
        yfix[YROWS:ZAT, :] = halo_in[par, YROWS:ZAT, :] - halo_out[par, 0:YROWS, :]
        zfix[0:32, :] = halo_in[par, ZAT:ZAT + 32, :] - halo_out[par, ZAT + 32:ZAT + 64, :]
        zfix[32:64, :] = halo_in[par, ZAT + 32:ZAT + 64, :] - halo_out[par, ZAT:ZAT + 32, :]

    def prepare():
        @functools.partial(each, 8)
        def _(x):
            for d in range(3):
                s = sp[d, x]
                cpos[d, x] = jnp.maximum(s, 0.0)
                cneg[d, x] = jnp.maximum(-s, 0.0)

    def couple(x, w):
        for h in (0, 16):
            high, low = [], []
            for i in range(VARS):
                v = cur[i, x, h:h + 16, :]
                top = v.astype(BF16)
                high.append(top)
                low.append((v - top.astype(F32)).astype(BF16))
            out = dot(wmat[...], jnp.concatenate(high + low + high, axis=0))
            for place in range(3 * VARS):
                w[place, h:h + 16, :] = out[place * 16:place * 16 + 16]

    def stencil(x, w):
        prior = jnp.maximum(x - 1, 0)
        tiles = [(slice(c, c + 8), half) for c in range(0, 32, 8) for half in range(2)]
        for rows, half in tiles:
            coefficient = cneg[1, x, rows, halves[half]]
            for j in range(VARS):
                minus = coefficient * w[VARS + j, rows, halves[half]]
                low_shift[j, half, rows.start + 8:rows.start + 16, :] = minus
                if rows.start == 24:
                    low_shift[j, half, 0:8, :] = minus
        for rows, half in tiles:
            coefficient = cpos[1, x, rows, halves[half]]
            for j in range(VARS):
                flux = coefficient * w[VARS + j, rows, halves[half]] - low_shift[j, half, rows.start + 7:rows.start + 15, :]
                high_shift[j, half, rows, :] = flux
                if rows.start == 0:
                    high_shift[j, half, 32:40, :] = flux
        for c in range(0, 32, 8):
            rows = slice(c, c + 8)
            z_pos, z_neg, solid = cpos[2, x, rows], cneg[2, x, rows], po[x, rows]
            x_pos, x_neg = cpos[0, x, rows], cneg[0, x, rows]
            for j in range(VARS):
                wx = w[j, rows]
                flux = x_pos * wx - fprev[j, rows]
                nxt[j, prior, rows] = part[j, rows] - flux
                fprev[j, rows] = x_neg * wx
                acc = solid * cur[j, x, rows] + flux
                wv = w[2 * VARS + j, rows]
                flux = z_pos * wv - pltpu.roll(z_neg * wv, 1, axis=1)
                acc = acc + flux - pltpu.roll(flux, 255, axis=1)
                for half in range(2):
                    at = halves[half]
                    part[j, rows, at] = acc[:, at] + (
                        high_shift[j, half, rows, :] - high_shift[j, half, c + 1:c + 9, :])

    def sweep():
        fprev[...] = jnp.zeros(fprev.shape, F32)
        couple(0, wa)

        @functools.partial(each, 4)
        def _(t):
            x = 2 * t
            couple(x + 1, wb)
            stencil(x, wa)
            couple(jnp.minimum(x + 2, 7), wa)
            stencil(x + 1, wb)

        for j in range(VARS):
            nxt[j, 7] = part[j] + fprev[j]

    def dispatch():
        loads[3].wait()

        @functools.partial(each, 2)
        def _(half_x):
            for k in range(3):
                total = None
                for x in range(4):
                    for i in range(3):
                        term = basis[k, 1 + i, 4 * half_x + x] * mo[i, 4 * half_x + x]
                        total = term if total is None else total + term
                block[k, half_x] = total

        low8 = iota((16, 192), 0)
        col = iota((16, 192), 1)
        within = jnp.where(col >= 96, col - 96, col) & 31
        half = jnp.where(col >= 96, 1, 0)
        ysel = jnp.where((low8 >> 3 == half) & ((low8 & 7) == (within >> 2)), 1.0, 0.0).astype(BF16)
        zrow = iota((512, 128), 0)
        zsel = jnp.where(((zrow & 255) >> 2) + (zrow >> 8) * 64 == iota((512, 128), 1), 1.0, 0.0).astype(BF16)
        parts = []
        for k in range(3):
            t = dot(ysel, jnp.concatenate(list(pieces(block[k, 0])) + list(pieces(block[k, 1])), axis=0))
            for part_ in pieces(jnp.concatenate([t[0:8], t[8:16]], axis=1)):
                parts.append(part_.astype(F32))
        t = dot(jnp.concatenate(parts, axis=0).astype(BF16), zsel)
        values = [-PENALTY * (t[24 * k:24 * k + 8] + t[24 * k + 8:24 * k + 16] + t[24 * k + 16:24 * k + 24])
                  for k in range(3)]
        tops = [value.astype(BF16).astype(F32) for value in values]
        rests = [value - top for value, top in zip(values, tops)]
        empty = jnp.zeros((SLOTS, 128), BF16)
        for p in range(8):
            hot = rank_hot[:, p * 128:(p + 1) * 128]
            rows = [local_row[...]] + tops + rests
            rows = [(hot * value[p:p + 1, :]).astype(BF16) for value in rows]
            spread[:, p * 128:(p + 1) * 128] = jnp.concatenate(rows + [empty], axis=0)
        dsend[...] = dot_nt(owner_hot[...], spread[...]).reshape(ny, nz, 128)

        @functools.partial(each, ny, start=1)
        def _(delta):
            pltpu.make_async_remote_copy(
                src_ref=dsend.at[gy_at(delta)], dst_ref=recv1.at[delta],
                send_sem=a1_sem.at[0], recv_sem=a1_sem.at[1],
                device_id={"gy": gy_at(delta)}, device_id_type=MESH).start()
        recv1[0] = dsend[gy]

    pairs = [(l, k) for k in range(4) for l in range(k + 1)]

    def products(entries, vectors):
        def body(x, sums):
            sums = list(sums)
            for j in range(VARS):
                v = [nxt[j, x] if k == 3 else basis[k, j, x] for k in range(vectors)]
                for place, e in enumerate(entries):
                    l, k = pairs[e]
                    sums[place] = sums[place] + fold(v[l] * v[k])
            return tuple(sums)

        sums = lax.fori_loop(0, 8, body, tuple(jnp.zeros((8, 128), F32) for _ in entries))
        for place, e in enumerate(entries):
            prods[e] = sums[place]

    def corrections():
        sums = [jnp.zeros((8, 128), F32) for _ in range(4)]
        for at in range(0, 2 * YROWS, 8):
            add = yfix[at:at + 8, :]
            for l in range(3):
                sums[l] = sums[l] + yheld[l, at:at + 8, :] * add
            sums[3] = sums[3] + (2.0 * ypart[at:at + 8, :] + add) * add
        both = y_corners()
        for at in range(0, 64, 8):
            add = zfix[at:at + 8, :]
            for l in range(3):
                sums[l] = sums[l] + zheld[l, at:at + 8, :] * add
            sums[3] = sums[3] + (2.0 * (zpart[at:at + 8, :] + both[at:at + 8]) + add) * add
        for l in range(4):
            prods[6 + l] = prods[6 + l] + sums[l]

    corner[...] = jnp.zeros(corner.shape, F32)
    pack(cur, lambda i: loads[6 + i].wait())
    finish(0, 0, fixed=False)
    pl.semaphore_wait(barrier, (ny - 1) + (nz - 1))
    send_halo(0)

    @functools.partial(each, nz, start=1)
    def _(delta):
        pl.semaphore_signal(known_sem, inc=1, device_id={"gz": gz_at(delta)}, device_id_type=MESH)

    prepare()
    loads[2].wait()
    loads[1].wait()

    @functools.partial(each, 4, start=1)
    def _(k):
        par = k & 1
        sweep()
        pack(nxt)

        @pl.when(k == 3)
        def _():
            products((6, 7, 8, 9), 4)

        receive(1 - par)

        @pl.when(k == 3)
        def _():
            corrections()

        @pl.when(k < 3)
        def _():
            finish(k, par)
            send_halo(par)
            settle(k)
            pltpu.make_async_copy(basis.at[k], held_hbm.at[k - 1], out_sem).start()

            @pl.when(k == 1)
            def _():
                products((0, 1, 2), 2)

            @pl.when(k == 2)
            def _():
                dispatch()
                products((3, 4, 5), 3)

    sums = [prods[e] for e in range(10)]

    lane = iota((8, 128), 1)
    packed = jnp.zeros((8, 128), F32)
    for e, value in enumerate(sums):
        for shift in (64, 32, 16, 8):
            value = value + pltpu.roll(value, shift, axis=1)
        packed = jnp.where((lane >> 3) == e, value, packed)
    gsend[...] = jnp.sum(packed, axis=0, keepdims=True)

    pl.semaphore_wait(known_sem, nz - 1)

    def send_gram(a):
        row = gy_at(a)

        @functools.partial(each, nz, start=0 if a else 1, unroll=8 if a else 5)
        def _(b):
            pltpu.make_async_remote_copy(
                src_ref=gsend, dst_ref=grecv.at[pl.ds(a * nz + b, 1)], send_sem=g_sem.at[0], recv_sem=g_sem.at[1],
                device_id={"gy": row, "gz": gz_at(b)}, device_id_type=MESH).start()

    order = sorted(range(ny), key=lambda a: -min(a, ny - a))
    for a in order[:ny // 2]:
        send_gram(a)

    wait_all(recv1.at[pl.ds(1, ny - 1)], a1_sem.at[1])
    wait_all(recv1.at[pl.ds(1, ny - 1)], a1_sem.at[0])
    for g in range(nz):
        turned[g] = recv1[:, g, :]

    @functools.partial(each, nz, start=1)
    def _(delta):
        pltpu.make_async_remote_copy(
            src_ref=turned.at[gz_at(delta)], dst_ref=recv2.at[delta], send_sem=a2_sem.at[0], recv_sem=a2_sem.at[1],
            device_id={"gz": gz_at(delta)}, device_id_type=MESH).start()
    recv2[0] = turned[gz]

    for a in order[ny // 2:]:
        send_gram(a)

    wait_all(recv2.at[pl.ds(1, nz - 1)], a2_sem.at[1])
    wait_all(recv2.at[pl.ds(1, nz - 1)], a2_sem.at[0])
    picked[...] = recv2[...].reshape(number, 128).T
    digit = iota((16, 128), 0)
    left, right = [], []
    for r in range(SLOTS):
        number_r = picked[r:r + 1, :].astype(jnp.int32) - 1
        high = (number_r >> 4) == digit
        right.append(jnp.where((number_r & 15) == digit, 1.0, 0.0).astype(BF16))
        left.append(jnp.concatenate(
            [jnp.where(high, picked[SLOTS * (q + 1) + r:SLOTS * (q + 1) + r + 1, :], 0.0).astype(BF16) for q in range(6)], axis=0))
    bins = dot_nt(jnp.concatenate(left, axis=1), jnp.concatenate(right, axis=1))
    bins = bins[0:48] + bins[48:96]
    wide = jnp.where((iota((16, 256), 1) & 15) == iota((16, 256), 0), 1.0, 0.0).astype(BF16)
    bins = sum(dot(part_, wide) for part_ in pieces(bins))
    bins = jnp.where((iota((48, 256), 1) >> 4) == (iota((48, 256), 0) & 15), bins, 0.0)
    bin_sums = [jnp.sum(bins[16 * k:16 * k + 16], axis=0, keepdims=True) for k in range(3)]

    wait_all(grecv.at[pl.ds(1, number - 1)], g_sem.at[1])
    wait_all(grecv.at[pl.ds(1, number - 1)], g_sem.at[0])
    own = jnp.where(iota((8, 128), 0) == 0, gsend[...], grecv[0:8, :])
    for at in range(8, number, 8):
        own = own + grecv[at:at + 8, :]
    own = jnp.sum(own, axis=0, keepdims=True)
    for shift in (4, 2, 1):
        own = own + pltpu.roll(own, shift, axis=1)
    own = jnp.broadcast_to(own, (8, 128))
    splat = {}
    for e, (l, k) in enumerate(pairs):
        splat[l, k] = jnp.broadcast_to(own[:, 8 * e + 7:8 * e + 8], (8, 128))
    coeffs = solve([[splat[min(a, b), max(a, b)] for b in range(4)] for a in range(4)])

    sens = None
    for k in range(3):
        term = bin_sums[k] * jnp.concatenate([coeffs[k][0:1]] * (per_owner // 128), axis=1)
        sens = term if sens is None else sens + term
    small[0:1, :] = sens
    for k in range(3):
        small[8 + 8 * k:16 + 8 * k, :] = jnp.concatenate([coeffs[k]] * (per_owner // 128), axis=1)
    wait_all(basis.at[pl.ds(1, 2)], out_sem)


def combine(rs, held, small, adj_hbm, sens_hbm, result, sens, out_sem, sens_sem):
    sens[...] = small[0:1, :]
    put_sens = pltpu.make_async_copy(sens, sens_hbm, sens_sem)
    put_sens.start()
    full = [jnp.concatenate([small[8 + 8 * k:16 + 8 * k, :]] * 4, axis=0) for k in range(3)]

    def body(j, carry):
        for x in range(8):
            result[j, x] = full[0] * rs[j, x] + full[1] * held[0, j, x] + full[2] * held[1, j, x]
        pltpu.make_async_copy(result.at[j], adj_hbm.at[j], out_sem).start()
        return carry

    lax.fori_loop(0, VARS, body, 0)
    pltpu.make_async_copy(result, result, out_sem).wait()
    put_sens.wait()


def local(right_side, speeds, porosity, coupling, momentum, design_ids):
    ny = lax.axis_size("gy")
    nz = lax.axis_size("gz")
    _, nx, cy, cz = right_side.shape
    per_owner = design_ids.size // 4
    field = (VARS, nx, cy, cz)
    dma = pltpu.SemaphoreType.DMA
    hbm = pl.BlockSpec(memory_space=pltpu.HBM)
    held, small = pl.pallas_call(
        functools.partial(kernel, ny, nz, per_owner),
        out_shape=[jax.ShapeDtypeStruct((2,) + field, F32), jax.ShapeDtypeStruct((32, per_owner), F32)],
        in_specs=[hbm] * 6,
        out_specs=[pl.BlockSpec(memory_space=pl.ANY), pl.BlockSpec(memory_space=pltpu.VMEM)],
        scratch_shapes=[
            pltpu.VMEM((3,) + field, F32), pltpu.VMEM(field, F32), pltpu.VMEM(field, F32),
            pltpu.VMEM((3, nx, cy, cz), F32),
            pltpu.VMEM((nx, cy, cz), F32),
            pltpu.VMEM((3, nx, cy, cz), F32),
            pltpu.VMEM((240, 240), BF16),
            pltpu.VMEM((128, 128), F32),
            pltpu.VMEM((3 * VARS, cy, cz), F32), pltpu.VMEM((3 * VARS, cy, cz), F32),
            pltpu.VMEM((3, nx, cy, cz), F32), pltpu.VMEM((3, nx, cy, cz), F32),
            pltpu.VMEM((VARS, cy, cz), F32), pltpu.VMEM((VARS, cy, cz), F32),
            pltpu.VMEM((VARS, 2, 40, 128), F32), pltpu.VMEM((VARS, 2, 40, 128), F32),
            pltpu.VMEM((64, 128), F32),
            pltpu.VMEM((2, 224, 128), F32), pltpu.VMEM((2, 224, 128), F32), pltpu.VMEM((160, 128), F32), pltpu.VMEM((64, 128), F32),
            pltpu.VMEM((160, 128), F32), pltpu.VMEM((64, 128), F32), pltpu.VMEM((3, 160, 128), F32), pltpu.VMEM((3, 64, 128), F32),
            pltpu.VMEM((128, 128), F32), pltpu.VMEM((128, 128), F32),
            pltpu.VMEM((3, 2, cy, cz), F32),
            pltpu.VMEM((10, 8, 128), F32),
            pltpu.SMEM((VARS, 3, VARS), F32),
            pltpu.VMEM(design_ids.shape, jnp.int32),
            pltpu.VMEM((ny * nz, 1024), BF16),
            pltpu.VMEM((SLOTS, 1024), F32),
            pltpu.VMEM((8, 128), F32),
            pltpu.VMEM((8, 128), F32),
            pltpu.VMEM((128, 1024), BF16),
            pltpu.VMEM((ny, nz, 128), F32),
            pltpu.VMEM((ny, nz, 128), F32),
            pltpu.VMEM((nz, ny, 128), F32),
            pltpu.VMEM((nz, ny, 128), F32),
            pltpu.VMEM((128, 128), F32),
            pltpu.VMEM((1, 128), F32),
            pltpu.VMEM((ny * nz, 128), F32),
            dma((6 + VARS,)), dma, dma((2, 4)), dma((2, 4)), dma((2,)), dma((2,)), dma((2,)), pltpu.SemaphoreType.REGULAR,
        ],
        compiler_params=pltpu.CompilerParams(
            collective_id=0, has_side_effects=True, vmem_limit_bytes=40 * 1024 * 1024),
    )(*[pltpu.with_memory_space_constraint(value, pltpu.HBM) for value in (
        right_side, speeds, porosity, coupling.transpose(1, 0, 2), momentum, design_ids)])
    adjoint, sensitivity = pl.pallas_call(
        combine,
        out_shape=[jax.ShapeDtypeStruct(field, F32), jax.ShapeDtypeStruct((1, per_owner), F32)],
        in_specs=[pl.BlockSpec(memory_space=pltpu.VMEM)] * 3,
        out_specs=[hbm, hbm],
        scratch_shapes=[pltpu.VMEM(field, F32), pltpu.VMEM((1, per_owner), F32), dma, dma],
        compiler_params=pltpu.CompilerParams(vmem_limit_bytes=24 * 1024 * 1024),
    )(right_side, held, small)
    return adjoint, sensitivity.reshape(per_owner)


def solution(mesh):
    in_specs = (
        P(None, None, "gy", "gz"),
        P(None, None, "gy", "gz"),
        P(None, "gy", "gz"),
        P(),
        P(None, None, "gy", "gz"),
        P(None, "gy", "gz"),
    )
    out_specs = (P(None, None, "gy", "gz"), P(("gy", "gz")))
    return jax.shard_map(local, mesh=mesh, in_specs=in_specs, out_specs=out_specs, check_vma=False)
```

```python
import functools

import jax
import jax.numpy as jnp
from jax import lax
from jax.experimental import pallas as pl
from jax.experimental.pallas import tpu as pltpu
from jax.sharding import PartitionSpec as P

PENALTY = 1.0
COURANT = 0.3
VARS = 5
SLOTS = 16
MESH = pl.DeviceIdType.MESH
F32 = jnp.float32
BF16 = jnp.bfloat16


def pieces(value):
    high = value.astype(BF16)
    rest = value - high.astype(F32)
    mid = rest.astype(BF16)
    low = (rest - mid.astype(F32)).astype(BF16)
    return high, mid, low


def dot(a, b):
    return jnp.dot(a, b, preferred_element_type=F32)


def dot_nt(a, b):
    return lax.dot_general(a, b, (((1,), (1,)), ((), ())), preferred_element_type=F32)


def iota(shape, axis):
    return lax.broadcasted_iota(jnp.int32, shape, axis)


def fold(product):
    rows = product[0:8] + product[8:16] + product[16:24] + product[24:32]
    return rows[:, 0:128] + rows[:, 128:256]


def solve(gram):
    low = [[None] * 4 for _ in range(4)]
    for col in range(4):
        diag = gram[col][col]
        for inner in range(col):
            diag = diag - low[col][inner] * low[col][inner]
        low[col][col] = jnp.sqrt(diag)
        for row in range(col + 1, 4):
            value = gram[row][col]
            for inner in range(col):
                value = value - low[row][inner] * low[col][inner]
            low[row][col] = value / low[col][col]
    zero = jnp.zeros_like(gram[0][0])
    upper = [[low[c][r] if c >= r else None for c in range(4)] for r in range(4)]

    def add(a, b):
        return b if a is None else (a if b is None else a + b)

    hess = [[add(upper[r][c + 1], upper[r][c]) for c in range(3)] for r in range(4)]

    def inner_sum(terms):
        total = None
        for a, b in terms:
            if a is not None and b is not None:
                total = add(total, a * b)
        return zero if total is None else total

    normal = [[inner_sum([(hess[r][a], hess[r][b]) for r in range(4)]) for b in range(3)] for a in range(3)]
    target = [inner_sum([(hess[r][a], upper[r][0]) for r in range(4)]) for a in range(3)]
    fac = [[None] * 3 for _ in range(3)]
    for col in range(3):
        diag = normal[col][col]
        for inner in range(col):
            diag = diag - fac[col][inner] * fac[col][inner]
        fac[col][col] = jnp.sqrt(diag)
        for row in range(col + 1, 3):
            value = normal[row][col]
            for inner in range(col):
                value = value - fac[row][inner] * fac[col][inner]
            fac[row][col] = value / fac[col][col]
    forward = []
    for place in range(3):
        value = target[place]
        for inner in range(place):
            value = value - fac[place][inner] * forward[inner]
        forward.append(value / fac[place][place])
    backward = [None] * 3
    for place in reversed(range(3)):
        value = forward[place]
        for inner in range(place + 1, 3):
            value = value - fac[inner][place] * backward[inner]
        backward[place] = value / fac[place][place]
    return backward


def kernel(ny, nz, per_owner,
           rs_hbm, sp_hbm, po_hbm, cp_hbm, mo_hbm, ids_hbm,
           held_hbm, small,
           basis, cur, nxt, sp, po, mo, wmat, wz, wa, wb, cpos, cneg, part, fprev, low_shift, high_shift, sface,
           halo_out, halo_in, yfix, zfix, ypart, zpart, yheld, zheld, corner, turn, block, prods, cp, ids_ref,
           owner_hot, rank_hot, owner_row, local_row, spread, dsend, recv1, turned, recv2, picked,
           gsend, grecv,
           in_sem, out_sem, halo_send, halo_recv, a1_sem, a2_sem, g_sem, known_sem):
    gy = lax.axis_index("gy")
    gz = lax.axis_index("gz")

    number = ny * nz

    def gy_at(delta):
        return (gy + (delta + ny)) & (ny - 1)

    def gz_at(delta):
        return (gz + (delta + nz)) & (nz - 1)

    def each(count, step, start=0, unroll=1):
        def body(t, carry):
            step(t)
            return carry
        lax.fori_loop(start, count, body, 0, unroll=unroll)

    barrier = pltpu.get_barrier_semaphore()

    def greet(target):
        pl.semaphore_signal(barrier, inc=1, device_id=target, device_id_type=MESH)

    for delta in (1, -1):
        greet({"gz": gz_at(delta)})
        greet({"gy": gy_at(delta)})

    loads = [pltpu.make_async_copy(src, dst, in_sem.at[place]) for place, (src, dst) in enumerate(
        [(sp_hbm, sp), (rs_hbm, basis.at[0]), (po_hbm, po), (mo_hbm, mo), (cp_hbm, cp), (ids_hbm, ids_ref)]
        + [(rs_hbm.at[i], cur.at[i]) for i in range(VARS)])]
    for place in [4, 5, 0] + list(range(6, 6 + VARS)):
        loads[place].start()

    @functools.partial(each, ny - 1, start=2)
    def _(delta):
        greet({"gy": gy_at(delta)})

    for place in (2, 1, 3):
        loads[place].start()

    loads[4].wait()
    lane = iota((8, 128), 1)
    row = iota((8, 128), 0)
    wz[40:128, :] = jnp.zeros((88, 128), F32)

    @functools.partial(each, VARS)
    def _(i):
        value = jnp.zeros((8, 128), F32)
        for j in range(VARS):
            value = jnp.where((lane >> 3) == j, -COURANT * cp[i, 2, j], value)
        wz[pl.ds(pl.multiple_of(8 * i, 8), 8), :] = jnp.where((lane & 7) == row, value, 0.0)

    lane = iota((16, 256), 1)
    row = iota((16, 256), 0)
    group = lane >> 4
    piece = jnp.where(group >= 10, 2, jnp.where(group >= 5, 1, 0))
    which = group - 5 * piece
    same = (lane & 15) == row

    @functools.partial(each, 3 * VARS)
    def _(place):
        d = lax.div(place, VARS)
        j = place - d * VARS
        value = jnp.zeros((16, 256), F32)
        for i in range(VARS):
            value = jnp.where(which == i, COURANT * cp[i, d, j], value)
        high = value.astype(BF16).astype(F32)
        value = jnp.where(same, jnp.where(piece == 2, value - high, high), 0.0)
        wmat[pl.ds(pl.multiple_of(place * 16, 16), 16), :] = value[:, 0:240].astype(BF16)

    loads[5].wait()
    ids = jnp.concatenate([ids_ref[0], ids_ref[1]], axis=1)
    owners = lax.div(ids, per_owner)
    local_row[...] = (ids - owners * per_owner + 1).astype(F32)
    tri = jnp.where(iota((256, 128), 0) < jnp.where(iota((256, 128), 0) >= 128, 256, iota((256, 128), 1)), 1.0, 0.0).astype(BF16)
    sub = iota((number, 128), 0)
    before = jnp.zeros((number, 128), F32)
    for p in range(8):
        hot = jnp.where(sub == owners[p:p + 1, :], 1.0, 0.0)
        hot16 = hot.astype(BF16)
        count = dot(jnp.concatenate([hot16, before.astype(BF16)], axis=1), tri)
        before = before + hot
        owner_hot[:, p * 128:(p + 1) * 128] = hot16
        rank = jnp.sum(hot * count, axis=0, keepdims=True)
        rank_hot[:, p * 128:(p + 1) * 128] = jnp.where(rank == iota((SLOTS, 128), 0).astype(F32), 1.0, 0.0)

    loads[0].wait()

    lanes = iota((32, 128), 1)
    near = jnp.zeros((32, 128), F32)
    far = jnp.zeros((32, 128), F32)
    for x in range(8):
        ends = pltpu.roll(jnp.where(lanes == 0, sp[2, x, :, 0:128], sp[2, x, :, 128:256]), x + 1, axis=1)
        near = jnp.where(lanes == x + 1, ends, near)
        far = jnp.where(lanes == x, ends, far)
    near = pltpu.roll(near, 127, axis=1)
    for side, face in ((0, jnp.maximum(near, 0.0)), (1, jnp.maximum(-far, 0.0))):
        total = face
        for i in range(1, VARS):
            total = jnp.where((lanes >> 3) == i, pltpu.roll(face, 8 * i, axis=1), total)
        sface[32 * side:32 * side + 32, :] = jnp.where(lanes < 8 * VARS, total, 0.0)

    inside = (gy > 0, gy < ny - 1, gz > 0, gz < nz - 1)

    YROWS = VARS * 16
    ZAT = 2 * YROWS

    def y_at(side, j, half):
        return side * YROWS + j * 16 + half * 8

    def in_rows(place):
        return pl.ds(place * YROWS, YROWS) if place < 2 else pl.ds(ZAT + 32 * (place - 2), 32)

    def send_halo(par):
        for place, (axis, delta) in enumerate((("y", -1), ("y", 1), ("z", -1), ("z", 1))):
            rows = in_rows(place)
            target = {"gy": gy_at(delta)} if axis == "y" else {"gz": gz_at(delta)}
            copy = pltpu.make_async_remote_copy(
                src_ref=halo_out.at[par, rows], dst_ref=halo_in.at[par, in_rows(place ^ 1)],
                send_sem=halo_send.at[par, place], recv_sem=halo_recv.at[par, place ^ 1],
                device_id=target, device_id_type=MESH)
            pl.when(inside[place])(copy.start)

    for place in range(4):
        @pl.when(jnp.logical_not(inside[place]))
        def _():
            for par in range(2):
                halo_in[par, in_rows(place), :] = jnp.zeros((YROWS if place < 2 else 32, 128), F32)

    def wait_all(ref, sem):
        pltpu.make_async_copy(ref, ref, sem).wait()

    halves = (slice(0, 128), slice(128, 256))

    def pack(src, arrive=None):
        near = jnp.zeros((32, 128), F32)
        far = jnp.zeros((32, 128), F32)
        for i in range(VARS):
            if arrive is not None:
                arrive(i)
            for x in range(8):
                s = i * 8 + x
                ends = jnp.where(lanes == 0, src[i, x, :, 0:128], src[i, x, :, 128:256])
                ends = pltpu.roll(ends, s + 1, axis=1)
                near = jnp.where(lanes == s + 1, ends, near)
                far = jnp.where(lanes == s, ends, far)
        zpart[0:32, :] = pltpu.roll(near, 127, axis=1)
        zpart[32:64, :] = far
        for side, y in ((0, 0), (1, 31)):
            for half in range(2):
                for i in range(VARS):
                    at = y_at(side, i, half)
                    ypart[at:at + 8, :] = src[i, :, y, halves[half]]

    lane8 = iota((8, 128), 1)
    rows32 = iota((32, 128), 0)

    def y_corners():
        for side in range(2):
            for i in range(VARS):
                corner[side * 64 + i * 8:side * 64 + i * 8 + 8, :] = jnp.where(
                    lane8 == 0, yfix[y_at(side, i, 0):y_at(side, i, 0) + 8, :],
                    yfix[y_at(side, i, 1):y_at(side, i, 1) + 8, :])
        turn[...] = corner[...].T
        parts = []
        for at in (0, 127):
            both = jnp.broadcast_to(turn[at:at + 1, :], (32, 128))
            parts.append(jnp.where(rows32 == 0, both, jnp.where(rows32 == 31, pltpu.roll(both, 64, axis=1), 0.0)))
        return jnp.where(jnp.concatenate([lanes, lanes], axis=0) < 8 * VARS, jnp.concatenate(parts, axis=0), 0.0)

    def finish(k, par, fixed=True):
        faces = zpart[...] + zfix[...] + y_corners() if fixed else zpart[...]
        zheld[k] = faces
        halo_out[par, ZAT:ZAT + 64, :] = jnp.dot(
            faces * sface[...], wz[...], preferred_element_type=F32, precision=lax.Precision.HIGHEST)
        if fixed:
            turned_z = jnp.concatenate([zfix[...], jnp.zeros((64, 128), F32)], axis=0).T
        for side, y in ((0, 0), (1, 31)):
            for half in range(2):
                speed = sp[1, :, y, halves[half]]
                speed = jnp.maximum(speed, 0.0) if side == 0 else jnp.maximum(-speed, 0.0)
                flux = []
                for i in range(VARS):
                    at = y_at(side, i, half)
                    value = ypart[at:at + 8, :]
                    if fixed:
                        extra = turned_z[8 * i:8 * i + 8]
                        shift = ((0, 95), (97, 64))[side][half]
                        extra = pltpu.roll(extra, shift, axis=1) if shift else extra
                        value = value + yfix[at:at + 8, :] + jnp.where(lane8 == 127 * half, extra, 0.0)
                    yheld[k, at:at + 8, :] = value
                    flux.append(value * speed)
                for j in range(VARS):
                    total = flux[0] * (-COURANT * cp[0, 1, j])
                    for i in range(1, VARS):
                        total = total + flux[i] * (-COURANT * cp[i, 1, j])
                    at = y_at(side, j, half)
                    halo_out[par, at:at + 8, :] = total

    def settle(k):
        even = (lanes & 1) == 0
        near_columns = zfix[0:32, :]
        far_columns = pltpu.roll(zfix[32:64, :], 127, axis=1)
        columns = [jnp.where(even, near_columns, far_columns), jnp.where(even, far_columns, near_columns)]
        row8 = iota((8, 128), 0)
        for i in range(VARS):
            for x in range(8):
                s = i * 8 + x
                fix = pltpu.roll(columns[s & 1], 128 - s, axis=1) if s else columns[0]
                for half in range(2):
                    at = y_at(0, i, half) + x
                    top = jnp.where(row8 == 0, yfix[at:at + 1, :], 0.0)
                    at = y_at(1, i, half) + x
                    bottom = jnp.where(row8 == 7, yfix[at:at + 1, :], 0.0)
                    side = jnp.where(lanes == 127 * half, fix, 0.0)
                    value = jnp.concatenate([
                        nxt[i, x, 0:8, halves[half]] + top, nxt[i, x, 8:24, halves[half]],
                        nxt[i, x, 24:32, halves[half]] + bottom], axis=0) + side
                    cur[i, x, :, halves[half]] = value
                    basis[k, i, x, :, halves[half]] = value

    def receive(par):
        for place in range(4):
            @pl.when(inside[place])
            def _():
                ref = halo_in.at[par, in_rows(place)]
                wait_all(ref, halo_recv.at[par, place])
                wait_all(ref, halo_send.at[par, place])
        yfix[0:YROWS, :] = halo_in[par, 0:YROWS, :] - halo_out[par, YROWS:ZAT, :]
        yfix[YROWS:ZAT, :] = halo_in[par, YROWS:ZAT, :] - halo_out[par, 0:YROWS, :]
        zfix[0:32, :] = halo_in[par, ZAT:ZAT + 32, :] - halo_out[par, ZAT + 32:ZAT + 64, :]
        zfix[32:64, :] = halo_in[par, ZAT + 32:ZAT + 64, :] - halo_out[par, ZAT:ZAT + 32, :]

    def prepare():
        @functools.partial(each, 8)
        def _(x):
            for d in range(3):
                s = sp[d, x]
                cpos[d, x] = jnp.maximum(s, 0.0)
                cneg[d, x] = jnp.maximum(-s, 0.0)

    def couple(x, w):
        for h in (0, 16):
            high, low = [], []
            for i in range(VARS):
                v = cur[i, x, h:h + 16, :]
                top = v.astype(BF16)
                high.append(top)
                low.append((v - top.astype(F32)).astype(BF16))
            out = dot(wmat[...], jnp.concatenate(high + low + high, axis=0))
            for place in range(3 * VARS):
                w[place, h:h + 16, :] = out[place * 16:place * 16 + 16]

    def stencil(x, w):
        prior = jnp.maximum(x - 1, 0)
        tiles = [(slice(c, c + 8), half) for c in range(0, 32, 8) for half in range(2)]
        for rows, half in tiles:
            coefficient = cneg[1, x, rows, halves[half]]
            for j in range(VARS):
                minus = coefficient * w[VARS + j, rows, halves[half]]
                low_shift[j, half, rows.start + 8:rows.start + 16, :] = minus
                if rows.start == 24:
                    low_shift[j, half, 0:8, :] = minus
        for rows, half in tiles:
            coefficient = cpos[1, x, rows, halves[half]]
            for j in range(VARS):
                flux = coefficient * w[VARS + j, rows, halves[half]] - low_shift[j, half, rows.start + 7:rows.start + 15, :]
                high_shift[j, half, rows, :] = flux
                if rows.start == 0:
                    high_shift[j, half, 32:40, :] = flux
        for c in range(0, 32, 8):
            rows = slice(c, c + 8)
            z_pos, z_neg, solid = cpos[2, x, rows], cneg[2, x, rows], po[x, rows]
            x_pos, x_neg = cpos[0, x, rows], cneg[0, x, rows]
            for j in range(VARS):
                wx = w[j, rows]
                flux = x_pos * wx - fprev[j, rows]
                nxt[j, prior, rows] = part[j, rows] - flux
                fprev[j, rows] = x_neg * wx
                acc = solid * cur[j, x, rows] + flux
                wv = w[2 * VARS + j, rows]
                flux = z_pos * wv - pltpu.roll(z_neg * wv, 1, axis=1)
                acc = acc + flux - pltpu.roll(flux, 255, axis=1)
                for half in range(2):
                    at = halves[half]
                    part[j, rows, at] = acc[:, at] + (
                        high_shift[j, half, rows, :] - high_shift[j, half, c + 1:c + 9, :])

    def sweep():
        fprev[...] = jnp.zeros(fprev.shape, F32)
        couple(0, wa)

        @functools.partial(each, 4)
        def _(t):
            x = 2 * t
            couple(x + 1, wb)
            stencil(x, wa)
            couple(jnp.minimum(x + 2, 7), wa)
            stencil(x + 1, wb)

        for j in range(VARS):
            nxt[j, 7] = part[j] + fprev[j]

    def dispatch():
        loads[3].wait()

        @functools.partial(each, 2)
        def _(half_x):
            for k in range(3):
                total = None
                for x in range(4):
                    for i in range(3):
                        term = basis[k, 1 + i, 4 * half_x + x] * mo[i, 4 * half_x + x]
                        total = term if total is None else total + term
                block[k, half_x] = total

        low8 = iota((16, 192), 0)
        col = iota((16, 192), 1)
        within = jnp.where(col >= 96, col - 96, col) & 31
        half = jnp.where(col >= 96, 1, 0)
        ysel = jnp.where((low8 >> 3 == half) & ((low8 & 7) == (within >> 2)), 1.0, 0.0).astype(BF16)
        zrow = iota((512, 128), 0)
        zsel = jnp.where(((zrow & 255) >> 2) + (zrow >> 8) * 64 == iota((512, 128), 1), 1.0, 0.0).astype(BF16)
        parts = []
        for k in range(3):
            t = dot(ysel, jnp.concatenate(list(pieces(block[k, 0])) + list(pieces(block[k, 1])), axis=0))
            for part_ in pieces(jnp.concatenate([t[0:8], t[8:16]], axis=1)):
                parts.append(part_.astype(F32))
        t = dot(jnp.concatenate(parts, axis=0).astype(BF16), zsel)
        values = [-PENALTY * (t[24 * k:24 * k + 8] + t[24 * k + 8:24 * k + 16] + t[24 * k + 16:24 * k + 24])
                  for k in range(3)]
        tops = [value.astype(BF16).astype(F32) for value in values]
        rests = [value - top for value, top in zip(values, tops)]
        empty = jnp.zeros((SLOTS, 128), BF16)
        for p in range(8):
            hot = rank_hot[:, p * 128:(p + 1) * 128]
            rows = [local_row[...]] + tops + rests
            rows = [(hot * value[p:p + 1, :]).astype(BF16) for value in rows]
            spread[:, p * 128:(p + 1) * 128] = jnp.concatenate(rows + [empty], axis=0)
        dsend[...] = dot_nt(owner_hot[...], spread[...]).reshape(ny, nz, 128)

        @functools.partial(each, ny, start=1)
        def _(delta):
            pltpu.make_async_remote_copy(
                src_ref=dsend.at[gy_at(delta)], dst_ref=recv1.at[delta],
                send_sem=a1_sem.at[0], recv_sem=a1_sem.at[1],
                device_id={"gy": gy_at(delta)}, device_id_type=MESH).start()
        recv1[0] = dsend[gy]

    pairs = [(l, k) for k in range(4) for l in range(k + 1)]

    def products(entries, vectors):
        def body(x, sums):
            sums = list(sums)
            for j in range(VARS):
                v = [nxt[j, x] if k == 3 else basis[k, j, x] for k in range(vectors)]
                for place, e in enumerate(entries):
                    l, k = pairs[e]
                    sums[place] = sums[place] + fold(v[l] * v[k])
            return tuple(sums)

        sums = lax.fori_loop(0, 8, body, tuple(jnp.zeros((8, 128), F32) for _ in entries))
        for place, e in enumerate(entries):
            prods[e] = sums[place]

    def corrections():
        sums = [jnp.zeros((8, 128), F32) for _ in range(4)]
        for at in range(0, 2 * YROWS, 8):
            add = yfix[at:at + 8, :]
            for l in range(3):
                sums[l] = sums[l] + yheld[l, at:at + 8, :] * add
            sums[3] = sums[3] + (2.0 * ypart[at:at + 8, :] + add) * add
        both = y_corners()
        for at in range(0, 64, 8):
            add = zfix[at:at + 8, :]
            for l in range(3):
                sums[l] = sums[l] + zheld[l, at:at + 8, :] * add
            sums[3] = sums[3] + (2.0 * (zpart[at:at + 8, :] + both[at:at + 8]) + add) * add
        for l in range(4):
            prods[6 + l] = prods[6 + l] + sums[l]

    corner[...] = jnp.zeros(corner.shape, F32)
    pack(cur, lambda i: loads[6 + i].wait())
    finish(0, 0, fixed=False)
    pl.semaphore_wait(barrier, (ny - 1) + 2)
    send_halo(0)

    def tell(k, distance):
        for delta in (distance, -distance):
            pl.semaphore_signal(known_sem.at[k], inc=1, device_id={"gz": gz_at(delta)}, device_id_type=MESH)

    tell(0, 1)
    prepare()
    loads[2].wait()
    loads[1].wait()

    @functools.partial(each, 4, start=1)
    def _(k):
        par = k & 1
        sweep()
        pl.semaphore_wait(known_sem.at[k - 1], 2)

        @pl.when(k < 3)
        def _():
            tell(k, 2 * k)

        @pl.when(k == 3)
        def _():
            pl.semaphore_signal(known_sem.at[3], inc=1, device_id={"gz": gz_at(nz // 2)}, device_id_type=MESH)

        pack(nxt)

        @pl.when(k == 3)
        def _():
            products((6, 7, 8, 9), 4)

        receive(1 - par)

        @pl.when(k == 3)
        def _():
            corrections()

        @pl.when(k < 3)
        def _():
            finish(k, par)
            send_halo(par)
            settle(k)
            pltpu.make_async_copy(basis.at[k], held_hbm.at[k - 1], out_sem).start()

            @pl.when(k == 1)
            def _():
                products((0, 1, 2), 2)

            @pl.when(k == 2)
            def _():
                dispatch()
                products((3, 4, 5), 3)

    sums = [prods[e] for e in range(10)]

    lane = iota((8, 128), 1)
    packed = jnp.zeros((8, 128), F32)
    for e, value in enumerate(sums):
        for shift in (64, 32, 16, 8):
            value = value + pltpu.roll(value, shift, axis=1)
        packed = jnp.where((lane >> 3) == e, value, packed)
    gsend[...] = jnp.sum(packed, axis=0, keepdims=True)

    def send_gram(a, start, count):
        row = gy_at(a)

        @functools.partial(each, start + count, start=start, unroll=count)
        def _(b):
            pltpu.make_async_remote_copy(
                src_ref=gsend, dst_ref=grecv.at[pl.ds(a * nz + b, 1)], send_sem=g_sem.at[0], recv_sem=g_sem.at[1],
                device_id={"gy": row, "gz": gz_at(b)}, device_id_type=MESH).start()

    def send_most(a):
        if a == 0:
            send_gram(0, 1, nz - 1)
        else:
            send_gram(a, 0, nz // 2)
            send_gram(a, nz // 2 + 1, nz // 2 - 1)

    order = sorted(range(ny), key=lambda a: -min(a, ny - a))
    for a in order[:ny // 2]:
        send_most(a)

    wait_all(recv1.at[pl.ds(1, ny - 1)], a1_sem.at[1])
    wait_all(recv1.at[pl.ds(1, ny - 1)], a1_sem.at[0])
    for g in range(nz):
        turned[g] = recv1[:, g, :]

    @functools.partial(each, nz, start=1)
    def _(delta):
        pltpu.make_async_remote_copy(
            src_ref=turned.at[gz_at(delta)], dst_ref=recv2.at[delta], send_sem=a2_sem.at[0], recv_sem=a2_sem.at[1],
            device_id={"gz": gz_at(delta)}, device_id_type=MESH).start()
    recv2[0] = turned[gz]

    for a in order[ny // 2:]:
        send_most(a)
    pl.semaphore_wait(known_sem.at[3], 1)
    for a in range(1, ny):
        send_gram(a, nz // 2, 1)

    wait_all(recv2.at[pl.ds(1, nz - 1)], a2_sem.at[1])
    wait_all(recv2.at[pl.ds(1, nz - 1)], a2_sem.at[0])
    picked[...] = recv2[...].reshape(number, 128).T
    digit = iota((16, 128), 0)
    left, right = [], []
    for r in range(SLOTS):
        number_r = picked[r:r + 1, :].astype(jnp.int32) - 1
        high = (number_r >> 4) == digit
        right.append(jnp.where((number_r & 15) == digit, 1.0, 0.0).astype(BF16))
        left.append(jnp.concatenate(
            [jnp.where(high, picked[SLOTS * (q + 1) + r:SLOTS * (q + 1) + r + 1, :], 0.0).astype(BF16) for q in range(6)], axis=0))
    bins = dot_nt(jnp.concatenate(left, axis=1), jnp.concatenate(right, axis=1))
    bins = bins[0:48] + bins[48:96]
    wide = jnp.where((iota((16, 256), 1) & 15) == iota((16, 256), 0), 1.0, 0.0).astype(BF16)
    bins = sum(dot(part_, wide) for part_ in pieces(bins))
    bins = jnp.where((iota((48, 256), 1) >> 4) == (iota((48, 256), 0) & 15), bins, 0.0)
    bin_sums = [jnp.sum(bins[16 * k:16 * k + 16], axis=0, keepdims=True) for k in range(3)]

    wait_all(grecv.at[pl.ds(1, number - 1)], g_sem.at[1])
    wait_all(grecv.at[pl.ds(1, number - 1)], g_sem.at[0])
    own = jnp.where(iota((8, 128), 0) == 0, gsend[...], grecv[0:8, :])
    for at in range(8, number, 8):
        own = own + grecv[at:at + 8, :]
    own = jnp.sum(own, axis=0, keepdims=True)
    for shift in (4, 2, 1):
        own = own + pltpu.roll(own, shift, axis=1)
    own = jnp.broadcast_to(own, (8, 128))
    splat = {}
    for e, (l, k) in enumerate(pairs):
        splat[l, k] = jnp.broadcast_to(own[:, 8 * e + 7:8 * e + 8], (8, 128))
    coeffs = solve([[splat[min(a, b), max(a, b)] for b in range(4)] for a in range(4)])

    sens = None
    for k in range(3):
        term = bin_sums[k] * jnp.concatenate([coeffs[k][0:1]] * (per_owner // 128), axis=1)
        sens = term if sens is None else sens + term
    small[0:1, :] = sens
    for k in range(3):
        small[8 + 8 * k:16 + 8 * k, :] = jnp.concatenate([coeffs[k]] * (per_owner // 128), axis=1)
    wait_all(basis.at[pl.ds(1, 2)], out_sem)


def combine(rs, held, small, adj_hbm, sens_hbm, result, sens, out_sem, sens_sem):
    sens[...] = small[0:1, :]
    put_sens = pltpu.make_async_copy(sens, sens_hbm, sens_sem)
    put_sens.start()
    full = [jnp.concatenate([small[8 + 8 * k:16 + 8 * k, :]] * 4, axis=0) for k in range(3)]

    def body(j, carry):
        for x in range(8):
            result[j, x] = full[0] * rs[j, x] + full[1] * held[0, j, x] + full[2] * held[1, j, x]
        pltpu.make_async_copy(result.at[j], adj_hbm.at[j], out_sem).start()
        return carry

    lax.fori_loop(0, VARS, body, 0)
    pltpu.make_async_copy(result, result, out_sem).wait()
    put_sens.wait()


def local(right_side, speeds, porosity, coupling, momentum, design_ids):
    ny = lax.axis_size("gy")
    nz = lax.axis_size("gz")
    _, nx, cy, cz = right_side.shape
    per_owner = design_ids.size // 4
    field = (VARS, nx, cy, cz)
    dma = pltpu.SemaphoreType.DMA
    hbm = pl.BlockSpec(memory_space=pltpu.HBM)
    held, small = pl.pallas_call(
        functools.partial(kernel, ny, nz, per_owner),
        out_shape=[jax.ShapeDtypeStruct((2,) + field, F32), jax.ShapeDtypeStruct((32, per_owner), F32)],
        in_specs=[hbm] * 6,
        out_specs=[pl.BlockSpec(memory_space=pl.ANY), pl.BlockSpec(memory_space=pltpu.VMEM)],
        scratch_shapes=[
            pltpu.VMEM((3,) + field, F32), pltpu.VMEM(field, F32), pltpu.VMEM(field, F32),
            pltpu.VMEM((3, nx, cy, cz), F32),
            pltpu.VMEM((nx, cy, cz), F32),
            pltpu.VMEM((3, nx, cy, cz), F32),
            pltpu.VMEM((240, 240), BF16),
            pltpu.VMEM((128, 128), F32),
            pltpu.VMEM((3 * VARS, cy, cz), F32), pltpu.VMEM((3 * VARS, cy, cz), F32),
            pltpu.VMEM((3, nx, cy, cz), F32), pltpu.VMEM((3, nx, cy, cz), F32),
            pltpu.VMEM((VARS, cy, cz), F32), pltpu.VMEM((VARS, cy, cz), F32),
            pltpu.VMEM((VARS, 2, 40, 128), F32), pltpu.VMEM((VARS, 2, 40, 128), F32),
            pltpu.VMEM((64, 128), F32),
            pltpu.VMEM((2, 224, 128), F32), pltpu.VMEM((2, 224, 128), F32), pltpu.VMEM((160, 128), F32), pltpu.VMEM((64, 128), F32),
            pltpu.VMEM((160, 128), F32), pltpu.VMEM((64, 128), F32), pltpu.VMEM((3, 160, 128), F32), pltpu.VMEM((3, 64, 128), F32),
            pltpu.VMEM((128, 128), F32), pltpu.VMEM((128, 128), F32),
            pltpu.VMEM((3, 2, cy, cz), F32),
            pltpu.VMEM((10, 8, 128), F32),
            pltpu.SMEM((VARS, 3, VARS), F32),
            pltpu.VMEM(design_ids.shape, jnp.int32),
            pltpu.VMEM((ny * nz, 1024), BF16),
            pltpu.VMEM((SLOTS, 1024), F32),
            pltpu.VMEM((8, 128), F32),
            pltpu.VMEM((8, 128), F32),
            pltpu.VMEM((128, 1024), BF16),
            pltpu.VMEM((ny, nz, 128), F32),
            pltpu.VMEM((ny, nz, 128), F32),
            pltpu.VMEM((nz, ny, 128), F32),
            pltpu.VMEM((nz, ny, 128), F32),
            pltpu.VMEM((128, 128), F32),
            pltpu.VMEM((1, 128), F32),
            pltpu.VMEM((ny * nz, 128), F32),
            dma((6 + VARS,)), dma, dma((2, 4)), dma((2, 4)), dma((2,)), dma((2,)), dma((2,)), pltpu.SemaphoreType.REGULAR((4,)),
        ],
        compiler_params=pltpu.CompilerParams(
            collective_id=0, has_side_effects=True, vmem_limit_bytes=40 * 1024 * 1024),
    )(*[pltpu.with_memory_space_constraint(value, pltpu.HBM) for value in (
        right_side, speeds, porosity, coupling.transpose(1, 0, 2), momentum, design_ids)])
    adjoint, sensitivity = pl.pallas_call(
        combine,
        out_shape=[jax.ShapeDtypeStruct(field, F32), jax.ShapeDtypeStruct((1, per_owner), F32)],
        in_specs=[pl.BlockSpec(memory_space=pltpu.VMEM)] * 3,
        out_specs=[hbm, hbm],
        scratch_shapes=[pltpu.VMEM(field, F32), pltpu.VMEM((1, per_owner), F32), dma, dma],
        compiler_params=pltpu.CompilerParams(vmem_limit_bytes=24 * 1024 * 1024),
    )(right_side, held, small)
    return adjoint, sensitivity.reshape(per_owner)


def solution(mesh):
    in_specs = (
        P(None, None, "gy", "gz"),
        P(None, None, "gy", "gz"),
        P(None, "gy", "gz"),
        P(),
        P(None, None, "gy", "gz"),
        P(None, "gy", "gz"),
    )
    out_specs = (P(None, None, "gy", "gz"), P(("gy", "gz")))
    return jax.shard_map(local, mesh=mesh, in_specs=in_specs, out_specs=out_specs, check_vma=False)
```

```python
import functools

import jax
import jax.numpy as jnp
from jax import lax
from jax.experimental import pallas as pl
from jax.experimental.pallas import tpu as pltpu
from jax.sharding import PartitionSpec as P

PENALTY = 1.0
COURANT = 0.3
VARS = 5
SLOTS = 16
MESH = pl.DeviceIdType.MESH
F32 = jnp.float32
BF16 = jnp.bfloat16


def pieces(value):
    high = value.astype(BF16)
    rest = value - high.astype(F32)
    mid = rest.astype(BF16)
    low = (rest - mid.astype(F32)).astype(BF16)
    return high, mid, low


def dot(a, b):
    return jnp.dot(a, b, preferred_element_type=F32)


def dot_nt(a, b):
    return lax.dot_general(a, b, (((1,), (1,)), ((), ())), preferred_element_type=F32)


def iota(shape, axis):
    return lax.broadcasted_iota(jnp.int32, shape, axis)


def fold(product):
    rows = product[0:8] + product[8:16] + product[16:24] + product[24:32]
    return rows[:, 0:128] + rows[:, 128:256]


def solve(gram):
    low = [[None] * 4 for _ in range(4)]
    for col in range(4):
        diag = gram[col][col]
        for inner in range(col):
            diag = diag - low[col][inner] * low[col][inner]
        low[col][col] = jnp.sqrt(diag)
        for row in range(col + 1, 4):
            value = gram[row][col]
            for inner in range(col):
                value = value - low[row][inner] * low[col][inner]
            low[row][col] = value / low[col][col]
    zero = jnp.zeros_like(gram[0][0])
    upper = [[low[c][r] if c >= r else None for c in range(4)] for r in range(4)]

    def add(a, b):
        return b if a is None else (a if b is None else a + b)

    hess = [[add(upper[r][c + 1], upper[r][c]) for c in range(3)] for r in range(4)]

    def inner_sum(terms):
        total = None
        for a, b in terms:
            if a is not None and b is not None:
                total = add(total, a * b)
        return zero if total is None else total

    normal = [[inner_sum([(hess[r][a], hess[r][b]) for r in range(4)]) for b in range(3)] for a in range(3)]
    target = [inner_sum([(hess[r][a], upper[r][0]) for r in range(4)]) for a in range(3)]
    fac = [[None] * 3 for _ in range(3)]
    for col in range(3):
        diag = normal[col][col]
        for inner in range(col):
            diag = diag - fac[col][inner] * fac[col][inner]
        fac[col][col] = jnp.sqrt(diag)
        for row in range(col + 1, 3):
            value = normal[row][col]
            for inner in range(col):
                value = value - fac[row][inner] * fac[col][inner]
            fac[row][col] = value / fac[col][col]
    forward = []
    for place in range(3):
        value = target[place]
        for inner in range(place):
            value = value - fac[place][inner] * forward[inner]
        forward.append(value / fac[place][place])
    backward = [None] * 3
    for place in reversed(range(3)):
        value = forward[place]
        for inner in range(place + 1, 3):
            value = value - fac[inner][place] * backward[inner]
        backward[place] = value / fac[place][place]
    return backward


def kernel(ny, nz, per_owner,
           rs_hbm, sp_hbm, po_hbm, cp_hbm, mo_hbm, ids_hbm,
           held_hbm, small,
           basis, cur, nxt, sp, po, mo, wmat, wz, wa, wb, cpos, cneg, part, fprev, low_shift, high_shift, sface,
           halo_out, halo_in, yfix, zfix, ypart, zpart, yheld, zheld, corner, turn, block, prods, cp, ids_ref,
           owner_hot, rank_hot, owner_row, local_row, spread, dsend, recv1, turned, recv2, picked,
           gsend, grecv,
           in_sem, out_sem, halo_send, halo_recv, a1_sem, a2_sem, g_sem, known_sem):
    gy = lax.axis_index("gy")
    gz = lax.axis_index("gz")

    number = ny * nz

    def gy_at(delta):
        return (gy + (delta + ny)) & (ny - 1)

    def gz_at(delta):
        return (gz + (delta + nz)) & (nz - 1)

    def each(count, step, start=0, unroll=1):
        def body(t, carry):
            step(t)
            return carry
        lax.fori_loop(start, count, body, 0, unroll=unroll)

    barrier = pltpu.get_barrier_semaphore()

    def greet(target):
        pl.semaphore_signal(barrier, inc=1, device_id=target, device_id_type=MESH)

    for delta in (1, -1):
        greet({"gz": gz_at(delta)})
        greet({"gy": gy_at(delta)})

    loads = [pltpu.make_async_copy(src, dst, in_sem.at[place]) for place, (src, dst) in enumerate(
        [(sp_hbm, sp), (rs_hbm, basis.at[0]), (po_hbm, po), (mo_hbm, mo), (cp_hbm, cp), (ids_hbm, ids_ref)]
        + [(rs_hbm.at[i], cur.at[i]) for i in range(VARS)])]
    for place in [4, 5, 0] + list(range(6, 6 + VARS)):
        loads[place].start()

    @functools.partial(each, ny - 1, start=2)
    def _(delta):
        greet({"gy": gy_at(delta)})

    for place in (2, 1, 3):
        loads[place].start()

    loads[4].wait()
    lane = iota((8, 128), 1)
    row = iota((8, 128), 0)
    wz[40:128, :] = jnp.zeros((88, 128), F32)

    @functools.partial(each, VARS)
    def _(i):
        value = jnp.zeros((8, 128), F32)
        for j in range(VARS):
            value = jnp.where((lane >> 3) == j, -COURANT * cp[i, 2, j], value)
        wz[pl.ds(pl.multiple_of(8 * i, 8), 8), :] = jnp.where((lane & 7) == row, value, 0.0)

    lane = iota((16, 256), 1)
    row = iota((16, 256), 0)
    group = lane >> 4
    piece = jnp.where(group >= 10, 2, jnp.where(group >= 5, 1, 0))
    which = group - 5 * piece
    same = (lane & 15) == row

    @functools.partial(each, 3 * VARS)
    def _(place):
        d = lax.div(place, VARS)
        j = place - d * VARS
        value = jnp.zeros((16, 256), F32)
        for i in range(VARS):
            value = jnp.where(which == i, COURANT * cp[i, d, j], value)
        high = value.astype(BF16).astype(F32)
        value = jnp.where(same, jnp.where(piece == 2, value - high, high), 0.0)
        wmat[pl.ds(pl.multiple_of(place * 16, 16), 16), :] = value[:, 0:240].astype(BF16)

    loads[5].wait()
    ids = jnp.concatenate([ids_ref[0], ids_ref[1]], axis=1)
    owners = lax.div(ids, per_owner)
    local_row[...] = (ids - owners * per_owner + 1).astype(F32)
    tri = jnp.where(iota((256, 128), 0) < jnp.where(iota((256, 128), 0) >= 128, 256, iota((256, 128), 1)), 1.0, 0.0).astype(BF16)
    sub = iota((number, 128), 0)
    before = jnp.zeros((number, 128), F32)
    for p in range(8):
        hot = jnp.where(sub == owners[p:p + 1, :], 1.0, 0.0)
        hot16 = hot.astype(BF16)
        count = dot(jnp.concatenate([hot16, before.astype(BF16)], axis=1), tri)
        before = before + hot
        owner_hot[:, p * 128:(p + 1) * 128] = hot16
        rank = jnp.sum(hot * count, axis=0, keepdims=True)
        rank_hot[:, p * 128:(p + 1) * 128] = jnp.where(rank == iota((SLOTS, 128), 0).astype(F32), 1.0, 0.0)

    loads[0].wait()

    lanes = iota((32, 128), 1)
    near = jnp.zeros((32, 128), F32)
    far = jnp.zeros((32, 128), F32)
    for x in range(8):
        ends = pltpu.roll(jnp.where(lanes == 0, sp[2, x, :, 0:128], sp[2, x, :, 128:256]), x + 1, axis=1)
        near = jnp.where(lanes == x + 1, ends, near)
        far = jnp.where(lanes == x, ends, far)
    near = pltpu.roll(near, 127, axis=1)
    for side, face in ((0, jnp.maximum(near, 0.0)), (1, jnp.maximum(-far, 0.0))):
        total = face
        for i in range(1, VARS):
            total = jnp.where((lanes >> 3) == i, pltpu.roll(face, 8 * i, axis=1), total)
        sface[32 * side:32 * side + 32, :] = jnp.where(lanes < 8 * VARS, total, 0.0)

    inside = (gy > 0, gy < ny - 1, gz > 0, gz < nz - 1)

    YROWS = VARS * 16
    ZAT = 2 * YROWS

    def y_at(side, j, half):
        return side * YROWS + j * 16 + half * 8

    def in_rows(place):
        return pl.ds(place * YROWS, YROWS) if place < 2 else pl.ds(ZAT + 32 * (place - 2), 32)

    def send_halo(par):
        for place, (axis, delta) in enumerate((("y", -1), ("y", 1), ("z", -1), ("z", 1))):
            rows = in_rows(place)
            target = {"gy": gy_at(delta)} if axis == "y" else {"gz": gz_at(delta)}
            copy = pltpu.make_async_remote_copy(
                src_ref=halo_out.at[par, rows], dst_ref=halo_in.at[par, in_rows(place ^ 1)],
                send_sem=halo_send.at[par, place], recv_sem=halo_recv.at[par, place ^ 1],
                device_id=target, device_id_type=MESH)
            pl.when(inside[place])(copy.start)

    for place in range(4):
        @pl.when(jnp.logical_not(inside[place]))
        def _():
            for par in range(2):
                halo_in[par, in_rows(place), :] = jnp.zeros((YROWS if place < 2 else 32, 128), F32)

    def wait_all(ref, sem):
        pltpu.make_async_copy(ref, ref, sem).wait()

    halves = (slice(0, 128), slice(128, 256))

    def pack(src, arrive=None):
        near = jnp.zeros((32, 128), F32)
        far = jnp.zeros((32, 128), F32)
        for i in range(VARS):
            if arrive is not None:
                arrive(i)
            for x in range(8):
                s = i * 8 + x
                ends = jnp.where(lanes == 0, src[i, x, :, 0:128], src[i, x, :, 128:256])
                ends = pltpu.roll(ends, s + 1, axis=1)
                near = jnp.where(lanes == s + 1, ends, near)
                far = jnp.where(lanes == s, ends, far)
        zpart[0:32, :] = pltpu.roll(near, 127, axis=1)
        zpart[32:64, :] = far
        for side, y in ((0, 0), (1, 31)):
            for half in range(2):
                for i in range(VARS):
                    at = y_at(side, i, half)
                    ypart[at:at + 8, :] = src[i, :, y, halves[half]]

    lane8 = iota((8, 128), 1)
    rows32 = iota((32, 128), 0)

    def y_corners():
        for side in range(2):
            for i in range(VARS):
                corner[side * 64 + i * 8:side * 64 + i * 8 + 8, :] = jnp.where(
                    lane8 == 0, yfix[y_at(side, i, 0):y_at(side, i, 0) + 8, :],
                    yfix[y_at(side, i, 1):y_at(side, i, 1) + 8, :])
        turn[...] = corner[...].T
        parts = []
        for at in (0, 127):
            both = jnp.broadcast_to(turn[at:at + 1, :], (32, 128))
            parts.append(jnp.where(rows32 == 0, both, jnp.where(rows32 == 31, pltpu.roll(both, 64, axis=1), 0.0)))
        return jnp.where(jnp.concatenate([lanes, lanes], axis=0) < 8 * VARS, jnp.concatenate(parts, axis=0), 0.0)

    def finish(k, par, fixed=True):
        faces = zpart[...] + zfix[...] + y_corners() if fixed else zpart[...]
        zheld[k] = faces
        halo_out[par, ZAT:ZAT + 64, :] = jnp.dot(
            faces * sface[...], wz[...], preferred_element_type=F32, precision=lax.Precision.HIGHEST)
        if fixed:
            turned_z = jnp.concatenate([zfix[...], jnp.zeros((64, 128), F32)], axis=0).T
        for side, y in ((0, 0), (1, 31)):
            for half in range(2):
                speed = sp[1, :, y, halves[half]]
                speed = jnp.maximum(speed, 0.0) if side == 0 else jnp.maximum(-speed, 0.0)
                flux = []
                for i in range(VARS):
                    at = y_at(side, i, half)
                    value = ypart[at:at + 8, :]
                    if fixed:
                        extra = turned_z[8 * i:8 * i + 8]
                        shift = ((0, 95), (97, 64))[side][half]
                        extra = pltpu.roll(extra, shift, axis=1) if shift else extra
                        value = value + yfix[at:at + 8, :] + jnp.where(lane8 == 127 * half, extra, 0.0)
                    yheld[k, at:at + 8, :] = value
                    flux.append(value * speed)
                for j in range(VARS):
                    total = flux[0] * (-COURANT * cp[0, 1, j])
                    for i in range(1, VARS):
                        total = total + flux[i] * (-COURANT * cp[i, 1, j])
                    at = y_at(side, j, half)
                    halo_out[par, at:at + 8, :] = total

    def settle(k):
        even = (lanes & 1) == 0
        near_columns = zfix[0:32, :]
        far_columns = pltpu.roll(zfix[32:64, :], 127, axis=1)
        columns = [jnp.where(even, near_columns, far_columns), jnp.where(even, far_columns, near_columns)]
        row8 = iota((8, 128), 0)
        for i in range(VARS):
            for x in range(8):
                s = i * 8 + x
                fix = pltpu.roll(columns[s & 1], 128 - s, axis=1) if s else columns[0]
                for half in range(2):
                    at = y_at(0, i, half) + x
                    top = jnp.where(row8 == 0, yfix[at:at + 1, :], 0.0)
                    at = y_at(1, i, half) + x
                    bottom = jnp.where(row8 == 7, yfix[at:at + 1, :], 0.0)
                    side = jnp.where(lanes == 127 * half, fix, 0.0)
                    value = jnp.concatenate([
                        nxt[i, x, 0:8, halves[half]] + top, nxt[i, x, 8:24, halves[half]],
                        nxt[i, x, 24:32, halves[half]] + bottom], axis=0) + side
                    cur[i, x, :, halves[half]] = value
                    basis[k, i, x, :, halves[half]] = value

    def receive(par):
        for place in range(4):
            @pl.when(inside[place])
            def _():
                ref = halo_in.at[par, in_rows(place)]
                wait_all(ref, halo_recv.at[par, place])
                wait_all(ref, halo_send.at[par, place])
        yfix[0:YROWS, :] = halo_in[par, 0:YROWS, :] - halo_out[par, YROWS:ZAT, :]
        yfix[YROWS:ZAT, :] = halo_in[par, YROWS:ZAT, :] - halo_out[par, 0:YROWS, :]
        zfix[0:32, :] = halo_in[par, ZAT:ZAT + 32, :] - halo_out[par, ZAT + 32:ZAT + 64, :]
        zfix[32:64, :] = halo_in[par, ZAT + 32:ZAT + 64, :] - halo_out[par, ZAT:ZAT + 32, :]

    def prepare():
        @functools.partial(each, 8)
        def _(x):
            for d in range(3):
                s = sp[d, x]
                cpos[d, x] = jnp.maximum(s, 0.0)
                cneg[d, x] = jnp.maximum(-s, 0.0)

    def couple(x, w):
        for h in (0, 16):
            high, low = [], []
            for i in range(VARS):
                v = cur[i, x, h:h + 16, :]
                top = v.astype(BF16)
                high.append(top)
                low.append((v - top.astype(F32)).astype(BF16))
            out = dot(wmat[...], jnp.concatenate(high + low + high, axis=0))
            for place in range(3 * VARS):
                w[place, h:h + 16, :] = out[place * 16:place * 16 + 16]

    def stencil(x, w):
        prior = jnp.maximum(x - 1, 0)
        tiles = [(slice(c, c + 8), half) for c in range(0, 32, 8) for half in range(2)]
        for rows, half in tiles:
            coefficient = cneg[1, x, rows, halves[half]]
            for j in range(VARS):
                minus = coefficient * w[VARS + j, rows, halves[half]]
                low_shift[j, half, rows.start + 8:rows.start + 16, :] = minus
                if rows.start == 24:
                    low_shift[j, half, 0:8, :] = minus
        for rows, half in tiles:
            coefficient = cpos[1, x, rows, halves[half]]
            for j in range(VARS):
                flux = coefficient * w[VARS + j, rows, halves[half]] - low_shift[j, half, rows.start + 7:rows.start + 15, :]
                high_shift[j, half, rows, :] = flux
                if rows.start == 0:
                    high_shift[j, half, 32:40, :] = flux
        for c in range(0, 32, 8):
            rows = slice(c, c + 8)
            z_pos, z_neg, solid = cpos[2, x, rows], cneg[2, x, rows], po[x, rows]
            x_pos, x_neg = cpos[0, x, rows], cneg[0, x, rows]
            for j in range(VARS):
                wx = w[j, rows]
                flux = x_pos * wx - fprev[j, rows]
                nxt[j, prior, rows] = part[j, rows] - flux
                fprev[j, rows] = x_neg * wx
                acc = solid * cur[j, x, rows] + flux
                wv = w[2 * VARS + j, rows]
                flux = z_pos * wv - pltpu.roll(z_neg * wv, 1, axis=1)
                acc = acc + flux - pltpu.roll(flux, 255, axis=1)
                for half in range(2):
                    at = halves[half]
                    part[j, rows, at] = acc[:, at] + (
                        high_shift[j, half, rows, :] - high_shift[j, half, c + 1:c + 9, :])

    def sweep():
        fprev[...] = jnp.zeros(fprev.shape, F32)
        couple(0, wa)

        @functools.partial(each, 4)
        def _(t):
            x = 2 * t
            couple(x + 1, wb)
            stencil(x, wa)
            couple(jnp.minimum(x + 2, 7), wa)
            stencil(x + 1, wb)

        for j in range(VARS):
            nxt[j, 7] = part[j] + fprev[j]

    def dispatch():
        loads[3].wait()

        @functools.partial(each, 2)
        def _(half_x):
            for k in range(3):
                total = None
                for x in range(4):
                    for i in range(3):
                        term = basis[k, 1 + i, 4 * half_x + x] * mo[i, 4 * half_x + x]
                        total = term if total is None else total + term
                block[k, half_x] = total

        low8 = iota((16, 192), 0)
        col = iota((16, 192), 1)
        within = jnp.where(col >= 96, col - 96, col) & 31
        half = jnp.where(col >= 96, 1, 0)
        ysel = jnp.where((low8 >> 3 == half) & ((low8 & 7) == (within >> 2)), 1.0, 0.0).astype(BF16)
        zrow = iota((512, 128), 0)
        zsel = jnp.where(((zrow & 255) >> 2) + (zrow >> 8) * 64 == iota((512, 128), 1), 1.0, 0.0).astype(BF16)
        parts = []
        for k in range(3):
            t = dot(ysel, jnp.concatenate(list(pieces(block[k, 0])) + list(pieces(block[k, 1])), axis=0))
            for part_ in pieces(jnp.concatenate([t[0:8], t[8:16]], axis=1)):
                parts.append(part_.astype(F32))
        t = dot(jnp.concatenate(parts, axis=0).astype(BF16), zsel)
        values = [-PENALTY * (t[24 * k:24 * k + 8] + t[24 * k + 8:24 * k + 16] + t[24 * k + 16:24 * k + 24])
                  for k in range(3)]
        tops = [value.astype(BF16).astype(F32) for value in values]
        rests = [value - top for value, top in zip(values, tops)]
        empty = jnp.zeros((SLOTS, 128), BF16)
        for p in range(8):
            hot = rank_hot[:, p * 128:(p + 1) * 128]
            rows = [local_row[...]] + tops + rests
            rows = [(hot * value[p:p + 1, :]).astype(BF16) for value in rows]
            spread[:, p * 128:(p + 1) * 128] = jnp.concatenate(rows + [empty], axis=0)
        dsend[...] = dot_nt(owner_hot[...], spread[...]).reshape(ny, nz, 128)

        @functools.partial(each, ny, start=1)
        def _(delta):
            pltpu.make_async_remote_copy(
                src_ref=dsend.at[gy_at(delta)], dst_ref=recv1.at[delta],
                send_sem=a1_sem.at[0], recv_sem=a1_sem.at[1],
                device_id={"gy": gy_at(delta)}, device_id_type=MESH).start()
        recv1[0] = dsend[gy]

    pairs = [(l, k) for k in range(4) for l in range(k + 1)]

    def products(entries, vectors):
        def body(x, sums):
            sums = list(sums)
            for j in range(VARS):
                v = [nxt[j, x] if k == 3 else basis[k, j, x] for k in range(vectors)]
                for place, e in enumerate(entries):
                    l, k = pairs[e]
                    sums[place] = sums[place] + fold(v[l] * v[k])
            return tuple(sums)

        sums = lax.fori_loop(0, 8, body, tuple(jnp.zeros((8, 128), F32) for _ in entries))
        for place, e in enumerate(entries):
            prods[e] = sums[place]

    def corrections():
        sums = [jnp.zeros((8, 128), F32) for _ in range(4)]
        for at in range(0, 2 * YROWS, 8):
            add = yfix[at:at + 8, :]
            for l in range(3):
                sums[l] = sums[l] + yheld[l, at:at + 8, :] * add
            sums[3] = sums[3] + (2.0 * ypart[at:at + 8, :] + add) * add
        both = y_corners()
        for at in range(0, 64, 8):
            add = zfix[at:at + 8, :]
            for l in range(3):
                sums[l] = sums[l] + zheld[l, at:at + 8, :] * add
            sums[3] = sums[3] + (2.0 * (zpart[at:at + 8, :] + both[at:at + 8]) + add) * add
        for l in range(4):
            prods[6 + l] = prods[6 + l] + sums[l]

    corner[...] = jnp.zeros(corner.shape, F32)
    pack(cur, lambda i: loads[6 + i].wait())
    finish(0, 0, fixed=False)
    pl.semaphore_wait(barrier, (ny - 1) + 2)
    send_halo(0)

    def tell(k, distance):
        for delta in (distance, -distance):
            pl.semaphore_signal(known_sem.at[k], inc=1, device_id={"gz": gz_at(delta)}, device_id_type=MESH)

    tell(0, 1)
    prepare()
    loads[2].wait()
    loads[1].wait()

    @functools.partial(each, 4, start=1)
    def _(k):
        par = k & 1
        sweep()
        pl.semaphore_wait(known_sem.at[k - 1], 2)

        @pl.when(k < 3)
        def _():
            tell(k, 2 * k)

        @pl.when(k == 3)
        def _():
            pl.semaphore_signal(known_sem.at[3], inc=1, device_id={"gz": gz_at(nz // 2)}, device_id_type=MESH)

        pack(nxt)

        @pl.when(k == 3)
        def _():
            products((6, 7, 8, 9), 4)

        receive(1 - par)

        @pl.when(k == 3)
        def _():
            corrections()

        @pl.when(k < 3)
        def _():
            finish(k, par)
            send_halo(par)
            settle(k)
            pltpu.make_async_copy(basis.at[k], held_hbm.at[k - 1], out_sem).start()

            @pl.when(k == 1)
            def _():
                products((0, 1, 2), 2)

            @pl.when(k == 2)
            def _():
                dispatch()
                products((3, 4, 5), 3)

    sums = [prods[e] for e in range(10)]

    row8 = iota((8, 128), 0)
    stacked = [jnp.zeros((8, 128), F32), jnp.zeros((8, 128), F32)]
    for e, value in enumerate(sums):
        stacked[e // 8] = jnp.where(row8 == e % 8, jnp.sum(value, axis=0, keepdims=True), stacked[e // 8])
    split = jnp.concatenate(pieces(jnp.concatenate(stacked, axis=0)), axis=0)
    totals = dot(split, jnp.ones((128, 128), BF16))
    totals = totals[0:16] + totals[16:32] + totals[32:48]
    packed = jnp.where((iota((16, 128), 1) >> 3) == iota((16, 128), 0), totals, 0.0)
    gsend[...] = jnp.sum(packed, axis=0, keepdims=True)

    def send_gram(a, b):
        pltpu.make_async_remote_copy(
            src_ref=gsend, dst_ref=grecv.at[pl.ds(a * nz + b, 1)], send_sem=g_sem.at[0], recv_sem=g_sem.at[1],
            device_id={"gy": gy_at(a), "gz": gz_at(b)}, device_id_type=MESH).start()

    def ring(offset, size):
        return min(offset % size, size - offset % size)

    def hops(place):
        a, b = place
        return ring(a, ny) / 2 + ring(b, 4) + ring(b // 4, nz // 4)

    places = [(a, b) for a in range(ny) for b in range(nz) if a + b and (a == 0 or b != nz // 2)]
    places = sorted(places, key=lambda place: -hops(place))
    for a, b in places[:number // 2]:
        send_gram(a, b)

    wait_all(recv1.at[pl.ds(1, ny - 1)], a1_sem.at[1])
    wait_all(recv1.at[pl.ds(1, ny - 1)], a1_sem.at[0])
    for g in range(nz):
        turned[g] = recv1[:, g, :]

    @functools.partial(each, nz, start=1)
    def _(delta):
        pltpu.make_async_remote_copy(
            src_ref=turned.at[gz_at(delta)], dst_ref=recv2.at[delta], send_sem=a2_sem.at[0], recv_sem=a2_sem.at[1],
            device_id={"gz": gz_at(delta)}, device_id_type=MESH).start()
    recv2[0] = turned[gz]

    for a, b in places[number // 2:]:
        send_gram(a, b)
    pl.semaphore_wait(known_sem.at[3], 1)
    for a in range(1, ny):
        send_gram(a, nz // 2)

    wait_all(recv2.at[pl.ds(1, nz - 1)], a2_sem.at[1])
    wait_all(recv2.at[pl.ds(1, nz - 1)], a2_sem.at[0])
    picked[...] = recv2[...].reshape(number, 128).T
    digit = iota((16, 128), 0)
    left, right = [], []
    for r in range(SLOTS):
        number_r = picked[r:r + 1, :].astype(jnp.int32) - 1
        high = (number_r >> 4) == digit
        right.append(jnp.where((number_r & 15) == digit, 1.0, 0.0).astype(BF16))
        left.append(jnp.concatenate(
            [jnp.where(high, picked[SLOTS * (q + 1) + r:SLOTS * (q + 1) + r + 1, :], 0.0).astype(BF16) for q in range(6)], axis=0))
    bins = dot_nt(jnp.concatenate(left, axis=1), jnp.concatenate(right, axis=1))
    bins = bins[0:48] + bins[48:96]
    wide = jnp.where((iota((16, 256), 1) & 15) == iota((16, 256), 0), 1.0, 0.0).astype(BF16)
    bins = sum(dot(part_, wide) for part_ in pieces(bins))
    bins = jnp.where((iota((48, 256), 1) >> 4) == (iota((48, 256), 0) & 15), bins, 0.0)
    bin_sums = [jnp.sum(bins[16 * k:16 * k + 16], axis=0, keepdims=True) for k in range(3)]

    wait_all(grecv.at[pl.ds(1, number - 1)], g_sem.at[1])
    wait_all(grecv.at[pl.ds(1, number - 1)], g_sem.at[0])
    own = jnp.where(iota((8, 128), 0) == 0, gsend[...], grecv[0:8, :])
    for at in range(8, number, 8):
        own = own + grecv[at:at + 8, :]
    own = jnp.sum(own, axis=0, keepdims=True)
    own = jnp.broadcast_to(own, (8, 128))
    splat = {}
    for e, (l, k) in enumerate(pairs):
        splat[l, k] = jnp.broadcast_to(own[:, 8 * e + 7:8 * e + 8], (8, 128))
    coeffs = solve([[splat[min(a, b), max(a, b)] for b in range(4)] for a in range(4)])

    sens = None
    for k in range(3):
        term = bin_sums[k] * jnp.concatenate([coeffs[k][0:1]] * (per_owner // 128), axis=1)
        sens = term if sens is None else sens + term
    small[0:1, :] = sens
    for k in range(3):
        small[8 + 8 * k:16 + 8 * k, :] = jnp.concatenate([coeffs[k]] * (per_owner // 128), axis=1)
    wait_all(basis.at[pl.ds(1, 2)], out_sem)


def combine(rs, held, small, adj_hbm, sens_hbm, result, sens, out_sem, sens_sem):
    sens[...] = small[0:1, :]
    put_sens = pltpu.make_async_copy(sens, sens_hbm, sens_sem)
    put_sens.start()
    full = [jnp.concatenate([small[8 + 8 * k:16 + 8 * k, :]] * 4, axis=0) for k in range(3)]

    def body(j, carry):
        for x in range(8):
            result[j, x] = full[0] * rs[j, x] + full[1] * held[0, j, x] + full[2] * held[1, j, x]
        pltpu.make_async_copy(result.at[j], adj_hbm.at[j], out_sem).start()
        return carry

    lax.fori_loop(0, VARS, body, 0)
    pltpu.make_async_copy(result, result, out_sem).wait()
    put_sens.wait()


def local(right_side, speeds, porosity, coupling, momentum, design_ids):
    ny = lax.axis_size("gy")
    nz = lax.axis_size("gz")
    _, nx, cy, cz = right_side.shape
    per_owner = design_ids.size // 4
    field = (VARS, nx, cy, cz)
    dma = pltpu.SemaphoreType.DMA
    hbm = pl.BlockSpec(memory_space=pltpu.HBM)
    held, small = pl.pallas_call(
        functools.partial(kernel, ny, nz, per_owner),
        out_shape=[jax.ShapeDtypeStruct((2,) + field, F32), jax.ShapeDtypeStruct((32, per_owner), F32)],
        in_specs=[hbm] * 6,
        out_specs=[pl.BlockSpec(memory_space=pl.ANY), pl.BlockSpec(memory_space=pltpu.VMEM)],
        scratch_shapes=[
            pltpu.VMEM((3,) + field, F32), pltpu.VMEM(field, F32), pltpu.VMEM(field, F32),
            pltpu.VMEM((3, nx, cy, cz), F32),
            pltpu.VMEM((nx, cy, cz), F32),
            pltpu.VMEM((3, nx, cy, cz), F32),
            pltpu.VMEM((240, 240), BF16),
            pltpu.VMEM((128, 128), F32),
            pltpu.VMEM((3 * VARS, cy, cz), F32), pltpu.VMEM((3 * VARS, cy, cz), F32),
            pltpu.VMEM((3, nx, cy, cz), F32), pltpu.VMEM((3, nx, cy, cz), F32),
            pltpu.VMEM((VARS, cy, cz), F32), pltpu.VMEM((VARS, cy, cz), F32),
            pltpu.VMEM((VARS, 2, 40, 128), F32), pltpu.VMEM((VARS, 2, 40, 128), F32),
            pltpu.VMEM((64, 128), F32),
            pltpu.VMEM((2, 224, 128), F32), pltpu.VMEM((2, 224, 128), F32), pltpu.VMEM((160, 128), F32), pltpu.VMEM((64, 128), F32),
            pltpu.VMEM((160, 128), F32), pltpu.VMEM((64, 128), F32), pltpu.VMEM((3, 160, 128), F32), pltpu.VMEM((3, 64, 128), F32),
            pltpu.VMEM((128, 128), F32), pltpu.VMEM((128, 128), F32),
            pltpu.VMEM((3, 2, cy, cz), F32),
            pltpu.VMEM((10, 8, 128), F32),
            pltpu.SMEM((VARS, 3, VARS), F32),
            pltpu.VMEM(design_ids.shape, jnp.int32),
            pltpu.VMEM((ny * nz, 1024), BF16),
            pltpu.VMEM((SLOTS, 1024), F32),
            pltpu.VMEM((8, 128), F32),
            pltpu.VMEM((8, 128), F32),
            pltpu.VMEM((128, 1024), BF16),
            pltpu.VMEM((ny, nz, 128), F32),
            pltpu.VMEM((ny, nz, 128), F32),
            pltpu.VMEM((nz, ny, 128), F32),
            pltpu.VMEM((nz, ny, 128), F32),
            pltpu.VMEM((128, 128), F32),
            pltpu.VMEM((1, 128), F32),
            pltpu.VMEM((ny * nz, 128), F32),
            dma((6 + VARS,)), dma, dma((2, 4)), dma((2, 4)), dma((2,)), dma((2,)), dma((2,)), pltpu.SemaphoreType.REGULAR((4,)),
        ],
        compiler_params=pltpu.CompilerParams(
            collective_id=0, has_side_effects=True, vmem_limit_bytes=40 * 1024 * 1024),
    )(*[pltpu.with_memory_space_constraint(value, pltpu.HBM) for value in (
        right_side, speeds, porosity, coupling.transpose(1, 0, 2), momentum, design_ids)])
    adjoint, sensitivity = pl.pallas_call(
        combine,
        out_shape=[jax.ShapeDtypeStruct(field, F32), jax.ShapeDtypeStruct((1, per_owner), F32)],
        in_specs=[pl.BlockSpec(memory_space=pltpu.VMEM)] * 3,
        out_specs=[hbm, hbm],
        scratch_shapes=[pltpu.VMEM(field, F32), pltpu.VMEM((1, per_owner), F32), dma, dma],
        compiler_params=pltpu.CompilerParams(vmem_limit_bytes=24 * 1024 * 1024),
    )(right_side, held, small)
    return adjoint, sensitivity.reshape(per_owner)


def solution(mesh):
    in_specs = (
        P(None, None, "gy", "gz"),
        P(None, None, "gy", "gz"),
        P(None, "gy", "gz"),
        P(),
        P(None, None, "gy", "gz"),
        P(None, "gy", "gz"),
    )
    out_specs = (P(None, None, "gy", "gz"), P(("gy", "gz")))
    return jax.shard_map(local, mesh=mesh, in_specs=in_specs, out_specs=out_specs, check_vma=False)
```

```python
import functools

import jax
import jax.numpy as jnp
from jax import lax
from jax.experimental import pallas as pl
from jax.experimental.pallas import tpu as pltpu
from jax.sharding import PartitionSpec as P

PENALTY = 1.0
COURANT = 0.3
VARS = 5
SLOTS = 16
MESH = pl.DeviceIdType.MESH
F32 = jnp.float32
BF16 = jnp.bfloat16


def pieces(value):
    high = value.astype(BF16)
    rest = value - high.astype(F32)
    mid = rest.astype(BF16)
    low = (rest - mid.astype(F32)).astype(BF16)
    return high, mid, low


def dot(a, b):
    return jnp.dot(a, b, preferred_element_type=F32)


def dot_nt(a, b):
    return lax.dot_general(a, b, (((1,), (1,)), ((), ())), preferred_element_type=F32)


def iota(shape, axis):
    return lax.broadcasted_iota(jnp.int32, shape, axis)


def fold(product):
    rows = product[0:8] + product[8:16] + product[16:24] + product[24:32]
    return rows[:, 0:128] + rows[:, 128:256]


def solve(gram):
    low = [[None] * 4 for _ in range(4)]
    for col in range(4):
        diag = gram[col][col]
        for inner in range(col):
            diag = diag - low[col][inner] * low[col][inner]
        low[col][col] = jnp.sqrt(diag)
        for row in range(col + 1, 4):
            value = gram[row][col]
            for inner in range(col):
                value = value - low[row][inner] * low[col][inner]
            low[row][col] = value / low[col][col]
    zero = jnp.zeros_like(gram[0][0])
    upper = [[low[c][r] if c >= r else None for c in range(4)] for r in range(4)]

    def add(a, b):
        return b if a is None else (a if b is None else a + b)

    hess = [[add(upper[r][c + 1], upper[r][c]) for c in range(3)] for r in range(4)]

    def inner_sum(terms):
        total = None
        for a, b in terms:
            if a is not None and b is not None:
                total = add(total, a * b)
        return zero if total is None else total

    normal = [[inner_sum([(hess[r][a], hess[r][b]) for r in range(4)]) for b in range(3)] for a in range(3)]
    target = [inner_sum([(hess[r][a], upper[r][0]) for r in range(4)]) for a in range(3)]
    fac = [[None] * 3 for _ in range(3)]
    for col in range(3):
        diag = normal[col][col]
        for inner in range(col):
            diag = diag - fac[col][inner] * fac[col][inner]
        fac[col][col] = jnp.sqrt(diag)
        for row in range(col + 1, 3):
            value = normal[row][col]
            for inner in range(col):
                value = value - fac[row][inner] * fac[col][inner]
            fac[row][col] = value / fac[col][col]
    forward = []
    for place in range(3):
        value = target[place]
        for inner in range(place):
            value = value - fac[place][inner] * forward[inner]
        forward.append(value / fac[place][place])
    backward = [None] * 3
    for place in reversed(range(3)):
        value = forward[place]
        for inner in range(place + 1, 3):
            value = value - fac[inner][place] * backward[inner]
        backward[place] = value / fac[place][place]
    return backward


def kernel(ny, nz, per_owner,
           rs_hbm, sp_hbm, po_hbm, cp_hbm, mo_hbm, ids_hbm,
           held_hbm, small,
           basis, cur, nxt, sp, po, mo, wmat, wz, wa, wb, cpos, cneg, part, fprev, low_shift, high_shift, sface,
           halo_out, halo_in, yfix, zfix, ypart, zpart, yheld, zheld, corner, turn, block, prods, cp, ids_ref,
           owner_hot, rank_hot, owner_row, local_row, spread, dsend, recv1, turned, recv2, picked,
           gsend, grecv,
           in_sem, out_sem, halo_send, halo_recv, a1_sem, a2_sem, g_sem, known_sem):
    gy = lax.axis_index("gy")
    gz = lax.axis_index("gz")

    number = ny * nz

    def gy_at(delta):
        return (gy + (delta + ny)) & (ny - 1)

    def gz_at(delta):
        return (gz + (delta + nz)) & (nz - 1)

    def each(count, step, start=0, unroll=1):
        def body(t, carry):
            step(t)
            return carry
        lax.fori_loop(start, count, body, 0, unroll=unroll)

    barrier = pltpu.get_barrier_semaphore()

    def greet(target):
        pl.semaphore_signal(barrier, inc=1, device_id=target, device_id_type=MESH)

    for delta in (1, -1):
        greet({"gz": gz_at(delta)})
        greet({"gy": gy_at(delta)})

    loads = [pltpu.make_async_copy(src, dst, in_sem.at[place]) for place, (src, dst) in enumerate(
        [(sp_hbm, sp), (rs_hbm, basis.at[0]), (po_hbm, po), (mo_hbm, mo), (cp_hbm, cp), (ids_hbm, ids_ref)]
        + [(rs_hbm.at[i], cur.at[i]) for i in range(VARS)])]
    for place in [4, 5, 0] + list(range(6, 6 + VARS)):
        loads[place].start()

    @functools.partial(each, ny - 1, start=2)
    def _(delta):
        greet({"gy": gy_at(delta)})

    for place in (2, 1, 3):
        loads[place].start()

    loads[4].wait()
    lane = iota((8, 128), 1)
    row = iota((8, 128), 0)
    wz[40:128, :] = jnp.zeros((88, 128), F32)

    @functools.partial(each, VARS)
    def _(i):
        value = jnp.zeros((8, 128), F32)
        for j in range(VARS):
            value = jnp.where((lane >> 3) == j, -COURANT * cp[i, 2, j], value)
        wz[pl.ds(pl.multiple_of(8 * i, 8), 8), :] = jnp.where((lane & 7) == row, value, 0.0)

    lane = iota((16, 256), 1)
    row = iota((16, 256), 0)
    group = lane >> 4
    piece = jnp.where(group >= 10, 2, jnp.where(group >= 5, 1, 0))
    which = group - 5 * piece
    same = (lane & 15) == row

    @functools.partial(each, 3 * VARS)
    def _(place):
        d = lax.div(place, VARS)
        j = place - d * VARS
        value = jnp.zeros((16, 256), F32)
        for i in range(VARS):
            value = jnp.where(which == i, COURANT * cp[i, d, j], value)
        high = value.astype(BF16).astype(F32)
        value = jnp.where(same, jnp.where(piece == 2, value - high, high), 0.0)
        wmat[pl.ds(pl.multiple_of(place * 16, 16), 16), :] = value[:, 0:240].astype(BF16)

    loads[5].wait()
    ids = jnp.concatenate([ids_ref[0], ids_ref[1]], axis=1)
    owners = lax.div(ids, per_owner)
    local_row[...] = (ids - owners * per_owner + 1).astype(F32)
    tri = jnp.where(iota((256, 128), 0) < jnp.where(iota((256, 128), 0) >= 128, 256, iota((256, 128), 1)), 1.0, 0.0).astype(BF16)
    sub = iota((number, 128), 0)
    before = jnp.zeros((number, 128), F32)
    for p in range(8):
        hot = jnp.where(sub == owners[p:p + 1, :], 1.0, 0.0)
        hot16 = hot.astype(BF16)
        count = dot(jnp.concatenate([hot16, before.astype(BF16)], axis=1), tri)
        before = before + hot
        owner_hot[:, p * 128:(p + 1) * 128] = hot16
        rank = jnp.sum(hot * count, axis=0, keepdims=True)
        rank_hot[:, p * 128:(p + 1) * 128] = jnp.where(rank == iota((SLOTS, 128), 0).astype(F32), 1.0, 0.0)

    loads[0].wait()

    lanes = iota((32, 128), 1)
    near = jnp.zeros((32, 128), F32)
    far = jnp.zeros((32, 128), F32)
    for x in range(8):
        ends = pltpu.roll(jnp.where(lanes == 0, sp[2, x, :, 0:128], sp[2, x, :, 128:256]), x + 1, axis=1)
        near = jnp.where(lanes == x + 1, ends, near)
        far = jnp.where(lanes == x, ends, far)
    near = pltpu.roll(near, 127, axis=1)
    for side, face in ((0, jnp.maximum(near, 0.0)), (1, jnp.maximum(-far, 0.0))):
        total = face
        for i in range(1, VARS):
            total = jnp.where((lanes >> 3) == i, pltpu.roll(face, 8 * i, axis=1), total)
        sface[32 * side:32 * side + 32, :] = jnp.where(lanes < 8 * VARS, total, 0.0)

    inside = (gy > 0, gy < ny - 1, gz > 0, gz < nz - 1)

    YROWS = VARS * 16
    ZAT = 2 * YROWS

    def y_at(side, j, half):
        return side * YROWS + j * 16 + half * 8

    def in_rows(place):
        return pl.ds(place * YROWS, YROWS) if place < 2 else pl.ds(ZAT + 32 * (place - 2), 32)

    def send_halo(par):
        for place, (axis, delta) in enumerate((("y", -1), ("y", 1), ("z", -1), ("z", 1))):
            rows = in_rows(place)
            target = {"gy": gy_at(delta)} if axis == "y" else {"gz": gz_at(delta)}
            copy = pltpu.make_async_remote_copy(
                src_ref=halo_out.at[par, rows], dst_ref=halo_in.at[par, in_rows(place ^ 1)],
                send_sem=halo_send.at[par, place], recv_sem=halo_recv.at[par, place ^ 1],
                device_id=target, device_id_type=MESH)
            pl.when(inside[place])(copy.start)

    for place in range(4):
        @pl.when(jnp.logical_not(inside[place]))
        def _():
            for par in range(2):
                halo_in[par, in_rows(place), :] = jnp.zeros((YROWS if place < 2 else 32, 128), F32)

    def wait_all(ref, sem):
        pltpu.make_async_copy(ref, ref, sem).wait()

    halves = (slice(0, 128), slice(128, 256))

    def pack(src, arrive=None):
        near = jnp.zeros((32, 128), F32)
        far = jnp.zeros((32, 128), F32)
        for i in range(VARS):
            if arrive is not None:
                arrive(i)
            for x in range(8):
                s = i * 8 + x
                ends = jnp.where(lanes == 0, src[i, x, :, 0:128], src[i, x, :, 128:256])
                ends = pltpu.roll(ends, s + 1, axis=1)
                near = jnp.where(lanes == s + 1, ends, near)
                far = jnp.where(lanes == s, ends, far)
        zpart[0:32, :] = pltpu.roll(near, 127, axis=1)
        zpart[32:64, :] = far
        for side, y in ((0, 0), (1, 31)):
            for half in range(2):
                for i in range(VARS):
                    at = y_at(side, i, half)
                    ypart[at:at + 8, :] = src[i, :, y, halves[half]]

    lane8 = iota((8, 128), 1)
    rows32 = iota((32, 128), 0)

    def y_corners():
        for side in range(2):
            for i in range(VARS):
                corner[side * 64 + i * 8:side * 64 + i * 8 + 8, :] = jnp.where(
                    lane8 == 0, yfix[y_at(side, i, 0):y_at(side, i, 0) + 8, :],
                    yfix[y_at(side, i, 1):y_at(side, i, 1) + 8, :])
        turn[...] = corner[...].T
        parts = []
        for at in (0, 127):
            both = jnp.broadcast_to(turn[at:at + 1, :], (32, 128))
            parts.append(jnp.where(rows32 == 0, both, jnp.where(rows32 == 31, pltpu.roll(both, 64, axis=1), 0.0)))
        return jnp.where(jnp.concatenate([lanes, lanes], axis=0) < 8 * VARS, jnp.concatenate(parts, axis=0), 0.0)

    def couple_faces(flux):
        top = flux.astype(BF16)
        rest = (flux - top.astype(F32)).astype(BF16)
        heavy = wz[...].astype(BF16)
        light = (wz[...] - heavy.astype(F32)).astype(BF16)
        return dot(top, heavy) + (dot(rest, heavy) + dot(top, light))

    def finish(k, par, fixed=True):
        faces = zpart[...] + zfix[...] + y_corners() if fixed else zpart[...]
        zheld[k] = faces
        halo_out[par, ZAT:ZAT + 64, :] = couple_faces(faces * sface[...])
        if fixed:
            turned_z = jnp.concatenate([zfix[...], jnp.zeros((64, 128), F32)], axis=0).T
        for side, y in ((0, 0), (1, 31)):
            for half in range(2):
                speed = sp[1, :, y, halves[half]]
                speed = jnp.maximum(speed, 0.0) if side == 0 else jnp.maximum(-speed, 0.0)
                flux = []
                for i in range(VARS):
                    at = y_at(side, i, half)
                    value = ypart[at:at + 8, :]
                    if fixed:
                        extra = turned_z[8 * i:8 * i + 8]
                        shift = ((0, 95), (97, 64))[side][half]
                        extra = pltpu.roll(extra, shift, axis=1) if shift else extra
                        value = value + yfix[at:at + 8, :] + jnp.where(lane8 == 127 * half, extra, 0.0)
                    yheld[k, at:at + 8, :] = value
                    flux.append(value * speed)
                for j in range(VARS):
                    total = flux[0] * (-COURANT * cp[0, 1, j])
                    for i in range(1, VARS):
                        total = total + flux[i] * (-COURANT * cp[i, 1, j])
                    at = y_at(side, j, half)
                    halo_out[par, at:at + 8, :] = total

    def settle(k):
        even = (lanes & 1) == 0
        near_columns = zfix[0:32, :]
        far_columns = pltpu.roll(zfix[32:64, :], 127, axis=1)
        columns = [jnp.where(even, near_columns, far_columns), jnp.where(even, far_columns, near_columns)]
        row8 = iota((8, 128), 0)
        for i in range(VARS):
            for x in range(8):
                s = i * 8 + x
                fix = pltpu.roll(columns[s & 1], 128 - s, axis=1) if s else columns[0]
                for half in range(2):
                    at = y_at(0, i, half) + x
                    top = jnp.where(row8 == 0, yfix[at:at + 1, :], 0.0)
                    at = y_at(1, i, half) + x
                    bottom = jnp.where(row8 == 7, yfix[at:at + 1, :], 0.0)
                    side = jnp.where(lanes == 127 * half, fix, 0.0)
                    value = jnp.concatenate([
                        nxt[i, x, 0:8, halves[half]] + top, nxt[i, x, 8:24, halves[half]],
                        nxt[i, x, 24:32, halves[half]] + bottom], axis=0) + side
                    cur[i, x, :, halves[half]] = value
                    basis[k, i, x, :, halves[half]] = value

    def receive(par):
        for place in range(4):
            @pl.when(inside[place])
            def _():
                ref = halo_in.at[par, in_rows(place)]
                wait_all(ref, halo_recv.at[par, place])
                wait_all(ref, halo_send.at[par, place])
        yfix[0:YROWS, :] = halo_in[par, 0:YROWS, :] - halo_out[par, YROWS:ZAT, :]
        yfix[YROWS:ZAT, :] = halo_in[par, YROWS:ZAT, :] - halo_out[par, 0:YROWS, :]
        zfix[0:32, :] = halo_in[par, ZAT:ZAT + 32, :] - halo_out[par, ZAT + 32:ZAT + 64, :]
        zfix[32:64, :] = halo_in[par, ZAT + 32:ZAT + 64, :] - halo_out[par, ZAT:ZAT + 32, :]

    def prepare():
        @functools.partial(each, 8)
        def _(x):
            for d in range(3):
                s = sp[d, x]
                cpos[d, x] = jnp.maximum(s, 0.0)
                cneg[d, x] = jnp.maximum(-s, 0.0)

    def couple(x, w):
        for h in (0, 16):
            high, low = [], []
            for i in range(VARS):
                v = cur[i, x, h:h + 16, :]
                top = v.astype(BF16)
                high.append(top)
                low.append((v - top.astype(F32)).astype(BF16))
            out = dot(wmat[...], jnp.concatenate(high + low + high, axis=0))
            for place in range(3 * VARS):
                w[place, h:h + 16, :] = out[place * 16:place * 16 + 16]

    def stencil(x, w):
        prior = jnp.maximum(x - 1, 0)
        tiles = [(slice(c, c + 8), half) for c in range(0, 32, 8) for half in range(2)]
        for rows, half in tiles:
            coefficient = cneg[1, x, rows, halves[half]]
            for j in range(VARS):
                minus = coefficient * w[VARS + j, rows, halves[half]]
                low_shift[j, half, rows.start + 8:rows.start + 16, :] = minus
                if rows.start == 24:
                    low_shift[j, half, 0:8, :] = minus
        for rows, half in tiles:
            coefficient = cpos[1, x, rows, halves[half]]
            for j in range(VARS):
                flux = coefficient * w[VARS + j, rows, halves[half]] - low_shift[j, half, rows.start + 7:rows.start + 15, :]
                high_shift[j, half, rows, :] = flux
                if rows.start == 0:
                    high_shift[j, half, 32:40, :] = flux
        for c in range(0, 32, 8):
            rows = slice(c, c + 8)
            z_pos, z_neg, solid = cpos[2, x, rows], cneg[2, x, rows], po[x, rows]
            x_pos, x_neg = cpos[0, x, rows], cneg[0, x, rows]
            for j in range(VARS):
                wx = w[j, rows]
                flux = x_pos * wx - fprev[j, rows]
                nxt[j, prior, rows] = part[j, rows] - flux
                fprev[j, rows] = x_neg * wx
                acc = solid * cur[j, x, rows] + flux
                wv = w[2 * VARS + j, rows]
                flux = z_pos * wv - pltpu.roll(z_neg * wv, 1, axis=1)
                acc = acc + flux - pltpu.roll(flux, 255, axis=1)
                for half in range(2):
                    at = halves[half]
                    part[j, rows, at] = acc[:, at] + (
                        high_shift[j, half, rows, :] - high_shift[j, half, c + 1:c + 9, :])

    def sweep():
        fprev[...] = jnp.zeros(fprev.shape, F32)
        couple(0, wa)

        @functools.partial(each, 4)
        def _(t):
            x = 2 * t
            couple(x + 1, wb)
            stencil(x, wa)
            couple(jnp.minimum(x + 2, 7), wa)
            stencil(x + 1, wb)

        for j in range(VARS):
            nxt[j, 7] = part[j] + fprev[j]

    def dispatch():
        loads[3].wait()

        @functools.partial(each, 2)
        def _(half_x):
            for k in range(3):
                total = None
                for x in range(4):
                    for i in range(3):
                        term = basis[k, 1 + i, 4 * half_x + x] * mo[i, 4 * half_x + x]
                        total = term if total is None else total + term
                block[k, half_x] = total

        low8 = iota((16, 192), 0)
        col = iota((16, 192), 1)
        within = jnp.where(col >= 96, col - 96, col) & 31
        half = jnp.where(col >= 96, 1, 0)
        ysel = jnp.where((low8 >> 3 == half) & ((low8 & 7) == (within >> 2)), 1.0, 0.0).astype(BF16)
        zrow = iota((512, 128), 0)
        zsel = jnp.where(((zrow & 255) >> 2) + (zrow >> 8) * 64 == iota((512, 128), 1), 1.0, 0.0).astype(BF16)
        parts = []
        for k in range(3):
            t = dot(ysel, jnp.concatenate(list(pieces(block[k, 0])) + list(pieces(block[k, 1])), axis=0))
            for part_ in pieces(jnp.concatenate([t[0:8], t[8:16]], axis=1)):
                parts.append(part_.astype(F32))
        t = dot(jnp.concatenate(parts, axis=0).astype(BF16), zsel)
        values = [-PENALTY * (t[24 * k:24 * k + 8] + t[24 * k + 8:24 * k + 16] + t[24 * k + 16:24 * k + 24])
                  for k in range(3)]
        tops = [value.astype(BF16).astype(F32) for value in values]
        rests = [value - top for value, top in zip(values, tops)]
        empty = jnp.zeros((SLOTS, 128), BF16)
        for p in range(8):
            hot = rank_hot[:, p * 128:(p + 1) * 128]
            rows = [local_row[...]] + tops + rests
            rows = [(hot * value[p:p + 1, :]).astype(BF16) for value in rows]
            spread[:, p * 128:(p + 1) * 128] = jnp.concatenate(rows + [empty], axis=0)
        dsend[...] = dot_nt(owner_hot[...], spread[...]).reshape(ny, nz, 128)

        @functools.partial(each, ny, start=1)
        def _(delta):
            pltpu.make_async_remote_copy(
                src_ref=dsend.at[gy_at(delta)], dst_ref=recv1.at[delta],
                send_sem=a1_sem.at[0], recv_sem=a1_sem.at[1],
                device_id={"gy": gy_at(delta)}, device_id_type=MESH).start()
        recv1[0] = dsend[gy]

    pairs = [(l, k) for k in range(4) for l in range(k + 1)]

    def products(entries, vectors):
        def body(x, sums):
            sums = list(sums)
            for j in range(VARS):
                v = [nxt[j, x] if k == 3 else basis[k, j, x] for k in range(vectors)]
                for place, e in enumerate(entries):
                    l, k = pairs[e]
                    sums[place] = sums[place] + fold(v[l] * v[k])
            return tuple(sums)

        sums = lax.fori_loop(0, 8, body, tuple(jnp.zeros((8, 128), F32) for _ in entries))
        for place, e in enumerate(entries):
            prods[e] = sums[place]

    def corrections():
        sums = [jnp.zeros((8, 128), F32) for _ in range(4)]
        for at in range(0, 2 * YROWS, 8):
            add = yfix[at:at + 8, :]
            for l in range(3):
                sums[l] = sums[l] + yheld[l, at:at + 8, :] * add
            sums[3] = sums[3] + (2.0 * ypart[at:at + 8, :] + add) * add
        both = y_corners()
        for at in range(0, 64, 8):
            add = zfix[at:at + 8, :]
            for l in range(3):
                sums[l] = sums[l] + zheld[l, at:at + 8, :] * add
            sums[3] = sums[3] + (2.0 * (zpart[at:at + 8, :] + both[at:at + 8]) + add) * add
        for l in range(4):
            prods[6 + l] = prods[6 + l] + sums[l]

    corner[...] = jnp.zeros(corner.shape, F32)
    pack(cur, lambda i: loads[6 + i].wait())
    finish(0, 0, fixed=False)
    pl.semaphore_wait(barrier, (ny - 1) + 2)
    send_halo(0)

    def tell(k, distance):
        for delta in (distance, -distance):
            pl.semaphore_signal(known_sem.at[k], inc=1, device_id={"gz": gz_at(delta)}, device_id_type=MESH)

    tell(0, 1)
    prepare()
    loads[2].wait()
    loads[1].wait()

    @functools.partial(each, 4, start=1)
    def _(k):
        par = k & 1
        sweep()
        pl.semaphore_wait(known_sem.at[k - 1], 2)

        @pl.when(k < 3)
        def _():
            tell(k, 2 * k)

        @pl.when(k == 3)
        def _():
            pl.semaphore_signal(known_sem.at[3], inc=1, device_id={"gz": gz_at(nz // 2)}, device_id_type=MESH)

        pack(nxt)

        @pl.when(k == 3)
        def _():
            products((6, 7, 8, 9), 4)

        receive(1 - par)

        @pl.when(k == 3)
        def _():
            corrections()

        @pl.when(k < 3)
        def _():
            finish(k, par)
            send_halo(par)
            settle(k)
            pltpu.make_async_copy(basis.at[k], held_hbm.at[k - 1], out_sem).start()

            @pl.when(k == 1)
            def _():
                products((0, 1, 2), 2)

            @pl.when(k == 2)
            def _():
                dispatch()
                products((3, 4, 5), 3)

    sums = [prods[e] for e in range(10)]

    row8 = iota((8, 128), 0)
    stacked = [jnp.zeros((8, 128), F32), jnp.zeros((8, 128), F32)]
    for e, value in enumerate(sums):
        stacked[e // 8] = jnp.where(row8 == e % 8, jnp.sum(value, axis=0, keepdims=True), stacked[e // 8])
    split = jnp.concatenate(pieces(jnp.concatenate(stacked, axis=0)), axis=0)
    totals = dot(split, jnp.ones((128, 128), BF16))
    totals = totals[0:16] + totals[16:32] + totals[32:48]
    packed = jnp.where((iota((16, 128), 1) >> 3) == iota((16, 128), 0), totals, 0.0)
    gsend[...] = jnp.sum(packed, axis=0, keepdims=True)

    def send_gram(a, b):
        pltpu.make_async_remote_copy(
            src_ref=gsend, dst_ref=grecv.at[pl.ds(a * nz + b, 1)], send_sem=g_sem.at[0], recv_sem=g_sem.at[1],
            device_id={"gy": gy_at(a), "gz": gz_at(b)}, device_id_type=MESH).start()

    def ring(offset, size):
        return min(offset % size, size - offset % size)

    def hops(place):
        a, b = place
        return ring(a, ny) / 2 + ring(b, 4) + ring(b // 4, nz // 4)

    places = [(a, b) for a in range(ny) for b in range(nz) if a + b and (a == 0 or b != nz // 2)]
    places = sorted(places, key=lambda place: -hops(place))
    for a, b in places[:96]:
        send_gram(a, b)

    wait_all(recv1.at[pl.ds(1, ny - 1)], a1_sem.at[1])
    wait_all(recv1.at[pl.ds(1, ny - 1)], a1_sem.at[0])
    for g in range(nz):
        turned[g] = recv1[:, g, :]

    @functools.partial(each, nz, start=1)
    def _(delta):
        pltpu.make_async_remote_copy(
            src_ref=turned.at[gz_at(delta)], dst_ref=recv2.at[delta], send_sem=a2_sem.at[0], recv_sem=a2_sem.at[1],
            device_id={"gz": gz_at(delta)}, device_id_type=MESH).start()
    recv2[0] = turned[gz]

    for a, b in places[96:]:
        send_gram(a, b)
    pl.semaphore_wait(known_sem.at[3], 1)
    for a in range(1, ny):
        send_gram(a, nz // 2)

    wait_all(recv2.at[pl.ds(1, nz - 1)], a2_sem.at[1])
    wait_all(recv2.at[pl.ds(1, nz - 1)], a2_sem.at[0])
    picked[...] = recv2[...].reshape(number, 128).T
    digit = iota((16, 128), 0)
    left, right = [], []
    for r in range(SLOTS):
        number_r = picked[r:r + 1, :].astype(jnp.int32) - 1
        high = (number_r >> 4) == digit
        right.append(jnp.where((number_r & 15) == digit, 1.0, 0.0).astype(BF16))
        left.append(jnp.concatenate(
            [jnp.where(high, picked[SLOTS * (q + 1) + r:SLOTS * (q + 1) + r + 1, :], 0.0).astype(BF16) for q in range(6)], axis=0))
    bins = dot_nt(jnp.concatenate(left, axis=1), jnp.concatenate(right, axis=1))
    bins = bins[0:48] + bins[48:96]
    wide = jnp.where((iota((16, 256), 1) & 15) == iota((16, 256), 0), 1.0, 0.0).astype(BF16)
    bins = sum(dot(part_, wide) for part_ in pieces(bins))
    bins = jnp.where((iota((48, 256), 1) >> 4) == (iota((48, 256), 0) & 15), bins, 0.0)
    bin_sums = [jnp.sum(bins[16 * k:16 * k + 16], axis=0, keepdims=True) for k in range(3)]

    wait_all(grecv.at[pl.ds(1, number - 1)], g_sem.at[1])
    wait_all(grecv.at[pl.ds(1, number - 1)], g_sem.at[0])
    own = jnp.where(iota((8, 128), 0) == 0, gsend[...], grecv[0:8, :])
    for at in range(8, number, 8):
        own = own + grecv[at:at + 8, :]
    own = jnp.sum(own, axis=0, keepdims=True)
    own = jnp.broadcast_to(own, (8, 128))
    splat = {}
    for e, (l, k) in enumerate(pairs):
        splat[l, k] = jnp.broadcast_to(own[:, 8 * e + 7:8 * e + 8], (8, 128))
    coeffs = solve([[splat[min(a, b), max(a, b)] for b in range(4)] for a in range(4)])

    sens = None
    for k in range(3):
        term = bin_sums[k] * jnp.concatenate([coeffs[k][0:1]] * (per_owner // 128), axis=1)
        sens = term if sens is None else sens + term
    small[0:1, :] = sens
    for k in range(3):
        small[8 + 8 * k:16 + 8 * k, :] = jnp.concatenate([coeffs[k]] * (per_owner // 128), axis=1)
    wait_all(basis.at[pl.ds(1, 2)], out_sem)


def combine(rs, held, small, adj_hbm, sens_hbm, result, sens, out_sem, sens_sem):
    sens[...] = small[0:1, :]
    put_sens = pltpu.make_async_copy(sens, sens_hbm, sens_sem)
    put_sens.start()
    full = [jnp.concatenate([small[8 + 8 * k:16 + 8 * k, :]] * 4, axis=0) for k in range(3)]

    def body(j, carry):
        for x in range(8):
            result[j, x] = full[0] * rs[j, x] + full[1] * held[0, j, x] + full[2] * held[1, j, x]
        pltpu.make_async_copy(result.at[j], adj_hbm.at[j], out_sem).start()
        return carry

    lax.fori_loop(0, VARS, body, 0)
    pltpu.make_async_copy(result, result, out_sem).wait()
    put_sens.wait()


def local(right_side, speeds, porosity, coupling, momentum, design_ids):
    ny = lax.axis_size("gy")
    nz = lax.axis_size("gz")
    _, nx, cy, cz = right_side.shape
    per_owner = design_ids.size // 4
    field = (VARS, nx, cy, cz)
    dma = pltpu.SemaphoreType.DMA
    hbm = pl.BlockSpec(memory_space=pltpu.HBM)
    held, small = pl.pallas_call(
        functools.partial(kernel, ny, nz, per_owner),
        out_shape=[jax.ShapeDtypeStruct((2,) + field, F32), jax.ShapeDtypeStruct((32, per_owner), F32)],
        in_specs=[hbm] * 6,
        out_specs=[pl.BlockSpec(memory_space=pl.ANY), pl.BlockSpec(memory_space=pltpu.VMEM)],
        scratch_shapes=[
            pltpu.VMEM((3,) + field, F32), pltpu.VMEM(field, F32), pltpu.VMEM(field, F32),
            pltpu.VMEM((3, nx, cy, cz), F32),
            pltpu.VMEM((nx, cy, cz), F32),
            pltpu.VMEM((3, nx, cy, cz), F32),
            pltpu.VMEM((240, 240), BF16),
            pltpu.VMEM((128, 128), F32),
            pltpu.VMEM((3 * VARS, cy, cz), F32), pltpu.VMEM((3 * VARS, cy, cz), F32),
            pltpu.VMEM((3, nx, cy, cz), F32), pltpu.VMEM((3, nx, cy, cz), F32),
            pltpu.VMEM((VARS, cy, cz), F32), pltpu.VMEM((VARS, cy, cz), F32),
            pltpu.VMEM((VARS, 2, 40, 128), F32), pltpu.VMEM((VARS, 2, 40, 128), F32),
            pltpu.VMEM((64, 128), F32),
            pltpu.VMEM((2, 224, 128), F32), pltpu.VMEM((2, 224, 128), F32), pltpu.VMEM((160, 128), F32), pltpu.VMEM((64, 128), F32),
            pltpu.VMEM((160, 128), F32), pltpu.VMEM((64, 128), F32), pltpu.VMEM((3, 160, 128), F32), pltpu.VMEM((3, 64, 128), F32),
            pltpu.VMEM((128, 128), F32), pltpu.VMEM((128, 128), F32),
            pltpu.VMEM((3, 2, cy, cz), F32),
            pltpu.VMEM((10, 8, 128), F32),
            pltpu.SMEM((VARS, 3, VARS), F32),
            pltpu.VMEM(design_ids.shape, jnp.int32),
            pltpu.VMEM((ny * nz, 1024), BF16),
            pltpu.VMEM((SLOTS, 1024), F32),
            pltpu.VMEM((8, 128), F32),
            pltpu.VMEM((8, 128), F32),
            pltpu.VMEM((128, 1024), BF16),
            pltpu.VMEM((ny, nz, 128), F32),
            pltpu.VMEM((ny, nz, 128), F32),
            pltpu.VMEM((nz, ny, 128), F32),
            pltpu.VMEM((nz, ny, 128), F32),
            pltpu.VMEM((128, 128), F32),
            pltpu.VMEM((1, 128), F32),
            pltpu.VMEM((ny * nz, 128), F32),
            dma((6 + VARS,)), dma, dma((2, 4)), dma((2, 4)), dma((2,)), dma((2,)), dma((2,)), pltpu.SemaphoreType.REGULAR((4,)),
        ],
        compiler_params=pltpu.CompilerParams(
            collective_id=0, has_side_effects=True, vmem_limit_bytes=40 * 1024 * 1024),
    )(*[pltpu.with_memory_space_constraint(value, pltpu.HBM) for value in (
        right_side, speeds, porosity, coupling.transpose(1, 0, 2), momentum, design_ids)])
    adjoint, sensitivity = pl.pallas_call(
        combine,
        out_shape=[jax.ShapeDtypeStruct(field, F32), jax.ShapeDtypeStruct((1, per_owner), F32)],
        in_specs=[pl.BlockSpec(memory_space=pltpu.VMEM)] * 3,
        out_specs=[hbm, hbm],
        scratch_shapes=[pltpu.VMEM(field, F32), pltpu.VMEM((1, per_owner), F32), dma, dma],
        compiler_params=pltpu.CompilerParams(vmem_limit_bytes=24 * 1024 * 1024),
    )(right_side, held, small)
    return adjoint, sensitivity.reshape(per_owner)


def solution(mesh):
    in_specs = (
        P(None, None, "gy", "gz"),
        P(None, None, "gy", "gz"),
        P(None, "gy", "gz"),
        P(),
        P(None, None, "gy", "gz"),
        P(None, "gy", "gz"),
    )
    out_specs = (P(None, None, "gy", "gz"), P(("gy", "gz")))
    return jax.shard_map(local, mesh=mesh, in_specs=in_specs, out_specs=out_specs, check_vma=False)
```
